32 devices in a mesh: branch: 4 (over y, x), seq: 8 (over z, core).
Axes of the slice: x: 2, y: 2, z: 4, core: 2. Of those that a mesh axis runs over, the one named last changes fastest.
Arguments:
- x_in: bfloat16 [4096, 1024], P(('seq', 'branch')), may hold values from -6 to 6
- lengths: int32 [5], replicated, may hold values from 64 to 3712, as said below
- norm1_gain: float32 [1024], replicated, may hold values from 0.5 to 1.5
- w_mix_in: bfloat16 [1024, 3584], P('seq', 'branch'), may hold values from -0.1875 to 0.1875
- w_dt: bfloat16 [1024, 24], P('seq', 'branch'), may hold values from -0.1875 to 0.1875
- w_shared: bfloat16 [1024, 512], P('seq'), may hold values from -0.1875 to 0.1875
- conv_x: float32 [4, 1536], P(None, 'branch'), may hold values from -3 to 3
- conv_bc: float32 [4, 256], replicated, may hold values from -3 to 3
- a_log: float32 [24], P('branch'), may hold values from -3 to 1
- dt_bias: float32 [24], P('branch'), may hold values from -8 to -2
- d_skip: float32 [24], P('branch'), may hold values from 0.5 to 1.5
- gate_gain: float32 [1536], replicated, may hold values from 0.5 to 1.5
- w_out: bfloat16 [2048, 1024], P('seq'), may hold values from -0.1875 to 0.1875
- norm2_gain: float32 [1024], replicated, may hold values from 0.5 to 1.5
- w_gate: bfloat16 [1024, 2048], P('seq'), may hold values from -0.1875 to 0.1875
- w_up: bfloat16 [1024, 2048], P('seq'), may hold values from -0.1875 to 0.1875
- w_down: bfloat16 [2048, 1024], P('seq'), may hold values from -0.125 to 0.125
- d_out: bfloat16 [4096, 1024], P(('seq', 'branch')), may hold values from -6 to 6
Outputs:
- y_out: bfloat16 [4096, 1024], P(('seq', 'branch'))
- grad_x: float32 [4096, 1024], P(('seq', 'branch'))
- grad_norm1_gain: float32 [1024], P(('branch', 'seq'))
- grad_w_mix_in: float32 [1024, 3584], P('seq', 'branch')
- grad_w_dt: float32 [1024, 24], P('seq', 'branch')
- grad_w_shared: float32 [1024, 512], P(('branch', 'seq'))
- grad_conv_x: float32 [4, 1536], P(None, ('branch', 'seq'))
- grad_conv_bc: float32 [4, 256], P(None, ('branch', 'seq'))
- grad_a_log: float32 [24], P('branch')
- grad_dt_bias: float32 [24], P('branch')
- grad_d_skip: float32 [24], P('branch')
- grad_gate_gain: float32 [1536], P(('branch', 'seq'))
- grad_w_out: float32 [2048, 1024], P(('branch', 'seq'))
- grad_norm2_gain: float32 [1024], P(('branch', 'seq'))
- grad_w_gate: float32 [1024, 2048], P(('branch', 'seq'))
- grad_w_up: float32 [1024, 2048], P(('branch', 'seq'))
- grad_w_down: float32 [2048, 1024], P(('branch', 'seq'))
The draws below stay inside these ranges and needn't reach their ends.
Inputs may be any that keep to these rules, and one draw needn't show every extreme that they name: The 5 lengths sum to 4096. One sequence, at a place among them drawn from the seed, begins within the first 512 rows and ends within the last 512 rows; every other one has from an eighth to a quarter of 512 rows.
All inputs are finite; a program needn't handle non-finite values.
Results may differ from the reference program's by a relative error of at most 0.024.
Values may be sent and summed in bfloat16 or wider, within the bound.
No kernel may reach another device: no remote copies, remote signals or barrier semaphores. Data moves between devices by JAX's collectives and lax.ppermute only.
A program may use at most 448 MiB of HBM per device.

```python
import jax
import jax.numpy as jnp
from jax import lax

D = 1024
FF = 2048
HEADS_ATT = 8
KV = 2
HEAD = 64
HEADS_SSM = 24
NSTATE = 128
CONV = 4
SPAN = 128
SEQS = 5
SEQ_ROWS = 512
TOKENS = 4096
N_BRANCH = 4


def draw_lengths(key, part):
    key = jax.random.fold_in(key, 7)
    pair_key, order_key, slot_key = jax.random.split(key, 3)
    eighth = SEQ_ROWS // 8
    middle_len = jax.random.randint(pair_key, (), eighth, 2 * eighth + 1, dtype=jnp.int32)
    shorts = jnp.stack([jnp.int32(eighth), jnp.int32(2 * eighth), middle_len, (3 * eighth - middle_len).astype(jnp.int32)]).astype(jnp.int32)
    shorts = jax.random.permutation(order_key, shorts).astype(jnp.int32)
    longest = (TOKENS - jnp.sum(shorts)).astype(jnp.int32)
    long_slot = jax.random.randint(slot_key, (), 0, SEQS, dtype=jnp.int32)
    slot_ids = jnp.arange(SEQS, dtype=jnp.int32)
    padded = jnp.concatenate([shorts, jnp.zeros((1,), jnp.int32)])
    picked = padded[jnp.where(slot_ids < long_slot, slot_ids, slot_ids - 1)]
    return jnp.where(slot_ids == long_slot, longest, picked).astype(jnp.int32)


def levels(rng, extent, cuts, low, largest):
    def one(dim, parts):
        steps = jax.random.uniform(jax.random.fold_in(jax.random.fold_in(rng, 6), dim), (parts,), jnp.float32, low / len(cuts), largest / len(cuts))
        return jnp.repeat(jnp.exp(steps), extent[dim] // parts).reshape((-1,) + (1,) * (len(extent) - dim - 1))

    gain = one(*cuts[0])
    for cut in cuts[1:]:
        gain = gain * one(*cut)
    return gain


def noise(rng, shape, scale, bound, shards=(), kind=jnp.bfloat16):
    entries = jax.random.normal(rng, shape, jnp.float32) * scale
    if len(shards) > 0:
        entries = levels(rng, shape, shards, -0.22, 0.18) * entries
    return jnp.clip(entries, min=-bound, max=bound).astype(kind)


def setup_inputs(seed: int = 0) -> dict:
    seeds = jax.random.split(jax.random.key(seed), 19)
    return {
        "x_in": noise(seeds[0], (TOKENS, D), 1.0, 6.0, ((0, 32),)),
        "lengths": draw_lengths(jax.random.fold_in(seeds[18], 71), 0),
        "norm1_gain": jnp.clip(1.0 + 0.1 * jax.random.normal(seeds[2], (D,), jnp.float32), 0.5, 1.5),
        "w_mix_in": noise(seeds[3], (D, N_BRANCH * ((HEADS_ATT + 2 * HEADS_SSM) * HEAD // N_BRANCH)), D ** -0.5, 0.1875, ((0, 8), (1, 4))),
        "w_dt": noise(seeds[4], (D, HEADS_SSM), D ** -0.5, 0.1875, ((0, 8), (1, 4))),
        "w_shared": noise(seeds[5], (D, 2 * KV * HEAD + 2 * NSTATE), D ** -0.5, 0.1875, ((0, 8),)),
        "conv_x": noise(seeds[6], (CONV, HEADS_SSM * HEAD), CONV ** -0.5, 3.0, ((1, 4),), jnp.float32),
        "conv_bc": noise(seeds[7], (CONV, 2 * NSTATE), CONV ** -0.5, 3.0, (), jnp.float32),
        "a_log": jnp.clip(-3.0 + 4.0 * jax.random.uniform(seeds[8], (HEADS_SSM,), jnp.float32) ** levels(seeds[8], (HEADS_SSM,), ((0, 4),), -0.2, 0.2), -3.0, 1.0),
        "dt_bias": jnp.clip(-8.0 + 6.0 * jax.random.uniform(seeds[9], (HEADS_SSM,), jnp.float32) ** levels(seeds[9], (HEADS_SSM,), ((0, 4),), -0.2, 0.2), -8.0, -2.0),
        "d_skip": jnp.clip(0.5 + 1.0 * jax.random.uniform(seeds[10], (HEADS_SSM,), jnp.float32) ** levels(seeds[10], (HEADS_SSM,), ((0, 4),), -0.2, 0.2), 0.5, 1.5),
        "gate_gain": jnp.clip(1.0 + 0.1 * jax.random.normal(seeds[11], (HEADS_SSM * HEAD,), jnp.float32), 0.5, 1.5),
        "w_out": noise(seeds[12], ((HEADS_ATT + HEADS_SSM) * HEAD, D), D ** -0.5, 0.1875, ((0, 8),)),
        "norm2_gain": jnp.clip(1.0 + 0.1 * jax.random.normal(seeds[13], (D,), jnp.float32), 0.5, 1.5),
        "w_gate": noise(seeds[14], (D, FF), D ** -0.5, 0.1875, ((0, 8),)),
        "w_up": noise(seeds[15], (D, FF), D ** -0.5, 0.1875, ((0, 8),)),
        "w_down": noise(seeds[16], (FF, D), FF ** -0.5, 0.125, ((0, 8),)),
        "d_out": noise(seeds[17], (TOKENS, D), 1.0, 6.0, ((0, 32),)),
    }


HIGHEST = lax.Precision.HIGHEST
EPSILON = 1e-06
SCORE_SCALE = 0.125
ROPE_BASE = 1000000.0

@jax.custom_vjp
def low(v):
    return lax.optimization_barrier(v.astype(jnp.bfloat16)).astype(jnp.float32)

@jax.custom_vjp
def low_back(v):
    return v

def low_keep(v):
    return (low(v), None)

def low_pass(kept, grad):
    return (grad,)

def back_keep(v):
    return (v, None)

def back_low(kept, grad):
    return (low(grad),)
low.defvjp(low_keep, low_pass)
low_back.defvjp(back_keep, back_low)

def rounded_both(value):
    return low_back(low(value))

def rms_norm(value, gain_vec):
    scaled = value * lax.rsqrt(lax.optimization_barrier(jnp.mean(value * value, axis=-1, keepdims=True)) + EPSILON)
    return scaled * gain_vec

def rotate(values_in, position, direction):
    half_dim = values_in.shape[-1] // 2
    inverse = ROPE_BASE ** (-jnp.arange(half_dim, dtype=jnp.float32) / half_dim)
    angles = position.astype(jnp.float32)[:, None] * inverse[None, :]
    cosine = jnp.cos(angles)[:, None, :]
    sine_dir = direction * jnp.sin(angles)[:, None, :]
    front_half = values_in[..., :half_dim]
    back_half = values_in[..., half_dim:]
    return jnp.concatenate([front_half * cosine - back_half * sine_dir, front_half * sine_dir + back_half * cosine], axis=-1)

def row_layout(lengths, first_row, amount):
    seq_ends = jnp.cumsum(lengths).astype(jnp.int32)
    starts = (seq_ends - lengths).astype(jnp.int32)
    row_ids = (first_row + jnp.arange(amount, dtype=jnp.int32)).astype(jnp.int32)
    segment = lax.optimization_barrier(jnp.sum((row_ids[:, None] >= seq_ends[None, :]).astype(jnp.int32), axis=1)).astype(jnp.int32)
    segment = jnp.where(row_ids < 0, jnp.int32(-1), segment).astype(jnp.int32)
    picked = segment[:, None] == jnp.arange(lengths.shape[0], dtype=jnp.int32)[None, :]
    begins = lax.optimization_barrier(jnp.sum(jnp.where(picked, starts[None, :], 0), axis=1)).astype(jnp.int32)
    return (row_ids, segment, (row_ids - begins).astype(jnp.int32))

def conv_masks(segment_ext, taps):
    amount = segment_ext.shape[0] - taps + 1
    target = segment_ext[taps - 1:]
    return jnp.stack([(segment_ext[offset:offset + amount] == target).astype(jnp.float32) for offset in range(taps)])

def causal_conv(extended, weight, tap_masks):
    amount = extended.shape[0] - weight.shape[0] + 1
    summed = jnp.zeros((amount, extended.shape[1]), jnp.float32)
    for offset in range(weight.shape[0]):
        summed = summed + extended[offset:offset + amount] * weight[offset][None, :] * tap_masks[offset][:, None]
    return summed

def ssm_prepare(x_ext, bc_ext, dt_raw, conv_x, conv_bc, dt_bias, a_log, tap_masks):
    amount = dt_raw.shape[0]
    heads_here = dt_raw.shape[1]
    mixed_x = jax.nn.silu(causal_conv(x_ext, conv_x, tap_masks)).reshape(amount, heads_here, -1)
    mixed_bc = jax.nn.silu(causal_conv(bc_ext, conv_bc, tap_masks))
    state_dim = mixed_bc.shape[1] // 2
    steps_dt = jax.nn.softplus(dt_raw + dt_bias[None, :])
    decay_rate = -jnp.exp(a_log)
    return (mixed_x, mixed_bc[:, :state_dim], mixed_bc[:, state_dim:], steps_dt, decay_rate)

def span_terms(mixed_x, b_rows, c_rows, steps_dt, decay_rate, segment, segment_prev):
    log_decay = steps_dt * decay_rate[None, :]
    cumulative = jnp.cumsum(log_decay, axis=0)
    positions = jnp.arange(segment.shape[0])
    lower_tri = (positions[:, None] >= positions[None, :]) & (segment[:, None] == segment[None, :])
    lower_cube = lower_tri[:, :, None]
    spread = jnp.where(lower_cube, cumulative[:, None, :] - cumulative[None, :, :], 0.0)
    decays = jnp.where(lower_cube, jnp.exp(spread), 0.0)
    inner_cb = jnp.dot(c_rows, b_rows.T, precision=HIGHEST)
    weights = decays * inner_cb[:, :, None] * steps_dt[None, :, :]
    intra_out = jnp.einsum('ijh,jhp->ihp', weights, mixed_x, precision=HIGHEST)
    carried = (segment == segment_prev).astype(jnp.float32)
    entering = jnp.exp(cumulative) * carried[:, None]
    closing = (segment == segment[-1]).astype(jnp.float32)
    to_end = jnp.exp(cumulative[-1][None, :] - cumulative) * closing[:, None] * steps_dt
    span_state = jnp.einsum('jh,jhp,jn->hpn', to_end, mixed_x, b_rows, precision=HIGHEST)
    span_decay = jnp.exp(cumulative[-1]) * (segment[-1] == segment_prev).astype(jnp.float32)
    return (intra_out, entering, span_decay, span_state)

def ssm_reference(mixed_x, b_rows, c_rows, steps_dt, decay_rate, segment):
    total_rows, heads_all, head_dim = mixed_x.shape
    blocks = total_rows // SPAN
    previous = jnp.concatenate([jnp.full((1,), -1, jnp.int32), segment[:-1]]).astype(jnp.int32)

    def advance(carry_state, inputs):
        x_blk, b_blk, c_blk, dt_blk, seg_blk, prev_blk = inputs
        intra_out, entering, span_decay, span_state = span_terms(x_blk, b_blk, c_blk, dt_blk, decay_rate, seg_blk, prev_blk[0])
        output = intra_out + jnp.einsum('ih,in,hpn->ihp', entering, c_blk, carry_state, precision=HIGHEST)
        return (span_decay[:, None, None] * carry_state + span_state, output)
    inputs = (mixed_x.reshape(blocks, SPAN, heads_all, head_dim), b_rows.reshape(blocks, SPAN, -1), c_rows.reshape(blocks, SPAN, -1), steps_dt.reshape(blocks, SPAN, -1), segment.reshape(blocks, SPAN), previous.reshape(blocks, SPAN))
    initial = jnp.zeros((heads_all, head_dim, b_rows.shape[1]), jnp.float32)
    final_state, outputs = lax.scan(jax.checkpoint(advance), initial, inputs)
    return outputs.reshape(total_rows, heads_all, head_dim)

def attention_reference(queries, keys_rot, values_in, row_ids, segment):
    total_rows = queries.shape[0]
    group_size = HEADS_ATT // KV
    keys_all = jnp.repeat(keys_rot, group_size, axis=1)
    values_all = jnp.repeat(values_in, group_size, axis=1)
    block_rows = min(512, total_rows)

    def one_block(inputs):
        q_blk, row_blk, seg_blk = inputs
        scores = low_back(SCORE_SCALE * jnp.einsum('bhd,nhd->bhn', q_blk, keys_all, precision=HIGHEST))
        visible = ((row_ids[None, :] <= row_blk[:, None]) & (segment[None, :] == seg_blk[:, None]))[:, None, :]
        masked = jnp.where(visible, scores, -1e+30)
        log_total = jax.nn.logsumexp(masked, axis=-1)
        probability = low(jnp.where(visible, jnp.exp(masked - log_total[..., None]), 0.0))
        return jnp.einsum('bhn,nhd->bhd', probability, values_all, precision=HIGHEST)
    blocks = total_rows // block_rows
    outputs = lax.map(jax.checkpoint(one_block), (queries.reshape(blocks, block_rows, HEADS_ATT, HEAD), row_ids.reshape(blocks, block_rows), segment.reshape(blocks, block_rows)))
    return outputs.reshape(total_rows, HEADS_ATT * HEAD)

def layer_forward(x_rows, norm1_gain, w_mix_in, w_dt, w_shared, conv_x, conv_bc, a_log, dt_bias, d_skip, gate_gain, w_out, norm2_gain, w_gate, w_up, w_down, row_ids, segment, position, tap_masks):
    total_rows = x_rows.shape[0]
    normed = low(rms_norm(x_rows, norm1_gain))
    blocked = w_mix_in.reshape(D, N_BRANCH, -1)
    query_cols = HEADS_ATT * HEAD // N_BRANCH
    ssm_cols = HEADS_SSM * HEAD // N_BRANCH
    w_query = blocked[:, :, :query_cols].reshape(D, -1)
    w_zgate = blocked[:, :, query_cols:query_cols + ssm_cols].reshape(D, -1)
    w_input = blocked[:, :, query_cols + ssm_cols:].reshape(D, -1)
    kv_cols = KV * HEAD
    q_raw = low_back(jnp.dot(normed, w_query, precision=HIGHEST))
    queries = low(rotate(q_raw.reshape(total_rows, HEADS_ATT, HEAD), position, 1.0))
    k_raw = jnp.dot(normed, w_shared[:, :kv_cols], precision=HIGHEST)
    keys_rot = low(rotate(k_raw.reshape(total_rows, KV, HEAD), position, 1.0))
    values_in = low(jnp.dot(normed, w_shared[:, kv_cols:2 * kv_cols], precision=HIGHEST)).reshape(total_rows, KV, HEAD)
    bc_pre = jnp.dot(normed, w_shared[:, 2 * kv_cols:], precision=HIGHEST)
    z_pre = low_back(jnp.dot(normed, w_zgate, precision=HIGHEST))
    x_pre = low_back(jnp.dot(normed, w_input, precision=HIGHEST))
    dt_raw = low_back(jnp.dot(normed, w_dt, precision=HIGHEST))
    attention = rounded_both(attention_reference(queries, keys_rot, values_in, row_ids, segment))
    x_ext = jnp.concatenate([jnp.zeros((CONV - 1, x_pre.shape[1]), jnp.float32), x_pre], axis=0)
    bc_ext = jnp.concatenate([jnp.zeros((CONV - 1, bc_pre.shape[1]), jnp.float32), bc_pre], axis=0)
    mixed_x, b_rows, c_rows, steps_dt, decay_rate = ssm_prepare(x_ext, bc_ext, dt_raw, conv_x, conv_bc, dt_bias, a_log, tap_masks)
    ssm_out = ssm_reference(mixed_x, b_rows, c_rows, steps_dt, decay_rate, segment)
    gated = (ssm_out + d_skip[None, :, None] * mixed_x) * jax.nn.silu(z_pre.reshape(total_rows, HEADS_SSM, HEAD))
    gated = rounded_both(gated.reshape(total_rows, -1))
    gnormed = low(rms_norm(gated, gate_gain))
    projected = low_back(jnp.dot(jnp.concatenate([attention, gnormed], axis=1), w_out, precision=HIGHEST))
    middle = x_rows + projected
    normed2 = low(rms_norm(middle, norm2_gain))
    gate_val = low_back(jnp.dot(normed2, w_gate, precision=HIGHEST))
    up_val = low_back(jnp.dot(normed2, w_up, precision=HIGHEST))
    hidden = low(jax.nn.silu(gate_val) * up_val)
    return middle + jnp.dot(hidden, w_down, precision=HIGHEST)

def reference(x_in, lengths, norm1_gain, w_mix_in, w_dt, w_shared, conv_x, conv_bc, a_log, dt_bias, d_skip, gate_gain, w_out, norm2_gain, w_gate, w_up, w_down, d_out):
    row_ids, segment, position = row_layout(lengths, jnp.int32(0), TOKENS)
    segment_ext = jnp.concatenate([jnp.full((CONV - 1,), -1, jnp.int32), segment]).astype(jnp.int32)
    tap_masks = conv_masks(segment_ext, CONV)
    floats = tuple((array_in.astype(jnp.float32) for array_in in (x_in, norm1_gain, w_mix_in, w_dt, w_shared, conv_x, conv_bc, a_log, dt_bias, d_skip, gate_gain, w_out, norm2_gain, w_gate, w_up, w_down)))

    def forward_only(*arrays):
        return layer_forward(*arrays, row_ids, segment, position, tap_masks)
    result, pullback = jax.vjp(forward_only, *floats)
    grads = pullback(d_out.astype(jnp.float32))
    return (result.astype(jnp.bfloat16), grads[0], grads[1], grads[2], grads[3], grads[4], grads[5], grads[6], grads[7], grads[8], grads[9], grads[10], grads[11], grads[12], grads[13], grads[14], grads[15])
```

```python
import jax
import jax.numpy as jnp
from jax import lax
from jax.sharding import PartitionSpec as P

HEADS_ATT = 8
KV = 2
HEAD = 64
CONV = 4
SPAN = 128


HIGHEST = lax.Precision.HIGHEST
EPSILON = 1e-06
SCORE_SCALE = 0.125
ROPE_BASE = 1000000.0


def from_behind(block, axis, distance):
    devices = range(lax.axis_size(axis))
    route = [(i - distance, i) for i in devices if i - distance in devices]
    return lax.ppermute(block, axis, route)


def entering_2(shard, axis, combine, identity):
    count, position = (lax.axis_size(axis), lax.axis_index(axis))
    everything = jax.tree.map(
        lambda part, kind: lax.all_gather(part.astype(kind), axis),
        shard,
        (jnp.bfloat16, jnp.bfloat16),
    )
    start = jax.tree.map(
        lambda part, zero: jnp.broadcast_to(jnp.asarray(zero, part.dtype), part.shape),
        shard,
        identity,
    )

    def turn(k, before):
        reached = k < position
        new = combine(
            before, jax.tree.map(lambda part, own: part[k].astype(own.dtype), everything, shard)
        )
        return jax.tree.map(lambda a, b: jnp.where(reached, a, b), new, before)

    return lax.fori_loop(0, count, turn, start)


def entering_3(shard, axis, combine, identity):
    count, position = (lax.axis_size(axis), lax.axis_index(axis))
    everything = jax.tree.map(
        lambda part, kind: lax.all_gather(part.astype(kind), axis),
        shard,
        jax.tree.map(lambda a: jnp.bfloat16 if a.dtype == jnp.float32 else a.dtype, shard),
    )
    start = jax.tree.map(
        lambda part, zero: jnp.broadcast_to(jnp.asarray(zero, part.dtype), part.shape),
        shard,
        identity,
    )

    def turn(k, before):
        at = count - 1 - k
        reached = at > position
        new = combine(
            before, jax.tree.map(lambda part, own: part[at].astype(own.dtype), everything, shard)
        )
        return jax.tree.map(lambda a, b: jnp.where(reached, a, b), new, before)

    return lax.fori_loop(0, count, turn, start)


def split_up(shard, dim, count):
    before, after = (shard.shape[:dim], shard.shape[dim + 1 :])
    return jnp.moveaxis(shard.reshape(*before, count, -1, *after), dim, 0)


def sent_and_summed(shard, axis, dim):
    count = lax.axis_size(axis)
    blocks = lax.all_to_all(split_up(shard, dim, count), axis, 0, 0, tiled=True)
    return jnp.sum(blocks.astype(jnp.float32), axis=0)


def side_by_side(arrays, axis, dim, along):
    widths = [a.shape[along] for a in arrays]
    both = jnp.concatenate(arrays, axis=along)
    result = sent_and_summed(both, axis, dim)
    return tuple(jnp.split(result, [sum(widths[:k]) for k in range(1, len(widths))], axis=along))


def rms_parts(value):
    inverse = lax.rsqrt(jnp.mean(value * value, axis=-1, keepdims=True) + EPSILON)
    return (value * inverse, inverse)


def rms_backward(grad_out, scaled, inverse, gain_vec):
    grad_scaled = grad_out * gain_vec
    grad_in = inverse * (
        grad_scaled - scaled * jnp.mean(grad_scaled * scaled, axis=-1, keepdims=True)
    )
    return (grad_in, jnp.sum(grad_out * scaled, axis=0))


def rotate(values_in, position, direction):
    half_dim = values_in.shape[-1] // 2
    inverse = ROPE_BASE ** (-jnp.arange(half_dim, dtype=jnp.float32) / half_dim)
    angles = position.astype(jnp.float32)[:, None] * inverse[None, :]
    cosine = jnp.cos(angles)[:, None, :]
    sine_dir = direction * jnp.sin(angles)[:, None, :]
    front_half = values_in[..., :half_dim]
    back_half = values_in[..., half_dim:]
    return jnp.concatenate(
        [front_half * cosine - back_half * sine_dir, front_half * sine_dir + back_half * cosine],
        axis=-1,
    )


def row_layout(lengths, first_row, amount):
    seq_ends = jnp.cumsum(lengths)
    starts = seq_ends - lengths
    row_ids = first_row + jnp.arange(amount, dtype=jnp.int32)
    segment = jnp.sum((row_ids[:, None] >= seq_ends[None, :]).astype(jnp.int32), axis=1)
    segment = jnp.where(row_ids < 0, jnp.int32(-1), segment)
    picked = segment[:, None] == jnp.arange(lengths.shape[0], dtype=jnp.int32)[None, :]
    begins = jnp.sum(jnp.where(picked, starts[None, :], 0), axis=1)
    return (row_ids, segment, row_ids - begins)


def conv_masks(segment_ext, taps):
    amount = segment_ext.shape[0] - taps + 1
    target = segment_ext[taps - 1 :]
    return jnp.stack(
        [
            (segment_ext[offset : offset + amount] == target).astype(jnp.float32)
            for offset in range(taps)
        ]
    )


def causal_conv(extended, weight, tap_masks):
    amount = extended.shape[0] - weight.shape[0] + 1
    summed = jnp.zeros((amount, extended.shape[1]), jnp.float32)
    for offset in range(weight.shape[0]):
        summed = (
            summed
            + extended[offset : offset + amount]
            * weight[offset][None, :]
            * tap_masks[offset][:, None]
        )
    return summed


def ssm_prepare(x_ext, bc_ext, dt_raw, conv_x, conv_bc, dt_bias, a_log, tap_masks):
    amount = dt_raw.shape[0]
    heads_here = dt_raw.shape[1]
    mixed_x = jax.nn.silu(causal_conv(x_ext, conv_x, tap_masks)).reshape(amount, heads_here, -1)
    mixed_bc = jax.nn.silu(causal_conv(bc_ext, conv_bc, tap_masks))
    state_dim = mixed_bc.shape[1] // 2
    steps_dt = jax.nn.softplus(dt_raw + dt_bias[None, :])
    decay_rate = -jnp.exp(a_log)
    return (mixed_x, mixed_bc[:, :state_dim], mixed_bc[:, state_dim:], steps_dt, decay_rate)


def span_terms(mixed_x, b_rows, c_rows, steps_dt, decay_rate, segment, segment_prev):
    log_decay = steps_dt * decay_rate[None, :]
    cumulative = jnp.cumsum(log_decay, axis=0)
    positions = jnp.arange(segment.shape[0])
    lower_tri = (positions[:, None] >= positions[None, :]) & (segment[:, None] == segment[None, :])
    lower_cube = lower_tri[:, :, None]
    spread = jnp.where(lower_cube, cumulative[:, None, :] - cumulative[None, :, :], 0.0)
    decays = jnp.where(lower_cube, jnp.exp(spread), 0.0)
    inner_cb = jnp.dot(c_rows, b_rows.T, precision=HIGHEST)
    weights = decays * inner_cb[:, :, None] * steps_dt[None, :, :]
    intra_out = jnp.einsum("ijh,jhp->ihp", weights, mixed_x, precision=HIGHEST)
    carried = (segment == segment_prev).astype(jnp.float32)
    entering = jnp.exp(cumulative) * carried[:, None]
    closing = (segment == segment[-1]).astype(jnp.float32)
    to_end = jnp.exp(cumulative[-1][None, :] - cumulative) * closing[:, None] * steps_dt
    span_state = jnp.einsum("jh,jhp,jn->hpn", to_end, mixed_x, b_rows, precision=HIGHEST)
    span_decay = jnp.exp(cumulative[-1]) * (segment[-1] == segment_prev).astype(jnp.float32)
    return (intra_out, entering, span_decay, span_state)


def to_blocks(array_in, blocks):
    return array_in.reshape((blocks, SPAN) + array_in.shape[1:])


def span_all(mixed_x, b_rows, c_rows, steps_dt, decay_rate, segment, segment_prev):
    amount, heads_here, head_dim = mixed_x.shape
    blocks = amount // SPAN
    firsts = segment_prev.reshape(blocks, SPAN)[:, 0]
    intra_out, entering, span_decay, span_state = jax.vmap(
        span_terms, in_axes=(0, 0, 0, 0, None, 0, 0)
    )(
        to_blocks(mixed_x, blocks),
        to_blocks(b_rows, blocks),
        to_blocks(c_rows, blocks),
        to_blocks(steps_dt, blocks),
        decay_rate,
        to_blocks(segment, blocks),
        firsts,
    )

    def compose(running, inputs):
        decay_now, state_now = running
        decay_blk, state_blk = inputs
        return ((decay_now * decay_blk, decay_blk[:, None, None] * state_now + state_blk), None)

    initial = (jnp.ones((heads_here,), jnp.float32), jnp.zeros(span_state.shape[1:], jnp.float32))
    composed, unused = lax.scan(compose, initial, (span_decay, span_state))
    return (intra_out, entering, span_decay, span_state, composed[0], composed[1])


def span_finish(
    state_in, intra_out, entering, span_decay, span_state, c_rows, mixed_x, z_pre, d_skip
):
    blocks = intra_out.shape[0]

    def advance(running, inputs):
        decay_blk, state_blk = inputs
        return (decay_blk[:, None, None] * running + state_blk, running)

    unused, incoming = lax.scan(advance, state_in, (span_decay, span_state))
    c_blocks = c_rows.reshape(blocks, SPAN, -1)
    ssm_out = intra_out + jnp.einsum(
        "cih,cin,chpn->cihp", entering, c_blocks, incoming, precision=HIGHEST
    )
    ssm_out = ssm_out.reshape(mixed_x.shape)
    gated = (ssm_out + d_skip[None, :, None] * mixed_x) * jax.nn.silu(z_pre.reshape(mixed_x.shape))
    return gated.reshape(mixed_x.shape[0], -1)


def chain_forward(earlier, later):
    return (earlier[0] * later[0], later[0][:, None, None] * earlier[1] + later[1])


def chain_backward(earlier, later):
    return (earlier[0] * later[0], later[1] + later[0][:, None, None] * earlier[1])


def keep_block(current):
    return current


def shards(
    x_in,
    lengths,
    norm1_gain,
    w_mix_in,
    w_dt,
    w_shared,
    conv_x,
    conv_bc,
    a_log,
    dt_bias,
    d_skip,
    gate_gain,
    w_out,
    norm2_gain,
    w_gate,
    w_up,
    w_down,
    d_out,
):
    tok_rows = x_in.shape[0]
    groups = lax.axis_size("branch")
    branch_id = lax.axis_index("branch")
    seq_id = lax.axis_index("seq")
    seq_rows = tok_rows * groups
    group_first = seq_id * seq_rows
    att_heads = HEADS_ATT // groups
    att_cols = att_heads * HEAD
    ssm_heads = w_dt.shape[1]
    ssm_cols = ssm_heads * HEAD
    kv_cols = KV * HEAD
    rim_rows = CONV - 1
    att_all = HEADS_ATT * HEAD
    f32 = jnp.float32
    bf16 = jnp.bfloat16
    dim = x_in.shape[1]
    parts = lax.axis_size("seq")
    chunk = w_out.shape[0] // groups
    att_chunks = parts * att_cols // (att_cols + ssm_cols)
    ssm_chunks = parts - att_chunks
    strip = dim // (groups * parts)
    hidden_all = w_gate.shape[1]
    hidden_a = hidden_all * att_cols // ((att_cols + ssm_cols) * groups)
    hidden_s = hidden_all // groups - hidden_a
    hidden_b = hidden_a + hidden_s

    def spot(c):
        first = groups * att_chunks
        if c < first:
            return (c // att_chunks) * parts + c % att_chunks
        return ((c - first) // ssm_chunks) * parts + att_chunks + (c - first) % ssm_chunks

    to_heads = [((c % groups) * parts + c // groups, spot(c)) for c in range(groups * parts)]
    from_heads = [(spot(c), c) for c in range(groups * parts)]

    def branch_sum(part):
        total = part
        for k in range(1, groups):
            route = [(i, (i + k) % groups) for i in range(groups)]
            total = total + lax.ppermute(part, "branch", route)
        return total

    def branch_gather(part):
        copies = jnp.broadcast_to(part[None], (groups,) + part.shape)
        return lax.all_to_all(copies, "branch", 0, 0, tiled=True).reshape(
            (groups * part.shape[0],) + part.shape[1:]
        )

    def branch_scatter(terms):
        blocks = terms.astype(bf16).reshape((groups, -1) + terms.shape[1:])
        return jnp.sum(lax.all_to_all(blocks, "branch", 0, 0, tiled=True).astype(f32), axis=0)

    kv_head = branch_id * att_heads // (HEADS_ATT // KV)
    dt_pad = 128
    w1_part = jnp.concatenate(
        [
            w_mix_in[:, :att_cols],
            lax.dynamic_slice_in_dim(w_shared, kv_head * HEAD, HEAD, 1),
            lax.dynamic_slice_in_dim(w_shared, kv_cols + kv_head * HEAD, HEAD, 1),
            w_mix_in[:, att_cols:],
            w_shared[:, 2 * kv_cols :],
            jnp.pad(w_dt, ((0, 0), (0, dt_pad - ssm_heads))),
        ],
        axis=1,
    )
    w1 = lax.all_gather(w1_part, "seq", axis=0, tiled=True)

    def own_columns(w):
        return [
            lax.dynamic_slice_in_dim(w, branch_id * hidden_a, hidden_a, 1),
            lax.dynamic_slice_in_dim(w, groups * hidden_a + branch_id * hidden_s, hidden_s, 1),
        ]

    row_part = jnp.concatenate(
        [
            lax.dynamic_slice_in_dim(w_out, branch_id * chunk, chunk, 0),
            lax.dynamic_slice_in_dim(w_down, branch_id * chunk, chunk, 0),
        ],
        axis=0,
    )
    row_part = lax.ppermute(row_part, ("branch", "seq"), to_heads)
    w2_part = jnp.concatenate(
        [row_part, jnp.concatenate(own_columns(w_gate) + own_columns(w_up), axis=1)], axis=0
    )
    w2 = lax.all_gather(w2_part, "seq", axis=0)
    w_out_b = w2[:, :chunk].reshape(parts * chunk, dim)
    w_down_b = w2[:, chunk : 2 * chunk].reshape(parts * chunk, dim)
    w_gu = w2[:, 2 * chunk :].reshape(dim, 2 * hidden_b)
    x_rows = x_in.astype(f32)
    scaled1, inverse1 = rms_parts(x_rows)
    normed1 = (scaled1 * norm1_gain).astype(bf16)
    group_in = branch_gather(normed1)
    d_out_g = branch_gather(d_out)
    row_ids, segment, position = row_layout(lengths, group_first, seq_rows)
    ext_ids, segment_ext, unused_pos = row_layout(
        lengths, group_first - rim_rows, seq_rows + rim_rows
    )
    tap_masks = conv_masks(segment_ext, CONV)
    segment_prev = segment_ext[rim_rows - 1 : rim_rows - 1 + seq_rows]
    pre = jnp.dot(group_in, w1, preferred_element_type=f32)
    at_k = att_cols
    at_z = at_k + 2 * HEAD
    at_x = at_z + ssm_cols
    at_bc = at_x + ssm_cols
    at_dt = at_bc + w_shared.shape[1] - 2 * kv_cols
    q_raw = pre[:, :at_k]
    side_pre = pre[:, at_k:at_z]
    z_pre = pre[:, at_z:at_x]
    x_pre = pre[:, at_x:at_bc]
    bc_pre = pre[:, at_bc:at_dt]
    dt_raw = pre[:, at_dt : at_dt + ssm_heads]
    queries = rotate(q_raw.reshape(seq_rows, att_heads, HEAD), position, 1.0).astype(bf16)
    keys_rot = (
        rotate(side_pre[:, :HEAD].reshape(seq_rows, 1, HEAD), position, 1.0)
        .reshape(seq_rows, HEAD)
        .astype(bf16)
    )
    values_b = side_pre[:, HEAD : 2 * HEAD].astype(bf16)
    row_last = group_first + seq_rows - 1
    seq_begin = group_first - position[0]

    def key_visible(first_key, amount):
        key_ids, key_seg, unused = row_layout(lengths, first_key, amount)
        return ((key_ids[None, :] <= row_ids[:, None]) & (key_seg[None, :] == segment[:, None]))[
            :, None, :
        ]

    def reachable(first_key, amount):
        return (first_key <= row_last) & (first_key + amount > seq_begin)

    kv_all = lax.all_gather(
        jnp.concatenate([keys_rot, values_b], axis=1), "seq", axis=0, tiled=True
    )
    piece_keys, piece_values = (kv_all[:, :HEAD], kv_all[:, HEAD:])

    def over_keys(fold_fn, initial):
        return fold_fn(initial, (piece_keys, piece_values), jnp.int32(0))

    def raw_scores(piece_keys):
        return (
            jnp.einsum("rhd,nd->rhn", queries, piece_keys, preferred_element_type=f32) * SCORE_SCALE
        )

    def max_sum(running, pieces, first_key):
        piece_keys, piece_values = pieces
        amount = piece_keys.shape[0]

        def max_compute_block(current):
            top_now, total_now = current
            visible = key_visible(first_key, amount)
            scores = jnp.where(visible, raw_scores(piece_keys), -1e30)
            top_new = jnp.maximum(top_now, jnp.max(scores, axis=-1))
            total_new = jnp.sum(
                jnp.where(visible, jnp.exp(scores - top_new[..., None]), 0.0), axis=-1
            )
            return (top_new, total_new)

        return lax.cond(reachable(first_key, amount), max_compute_block, keep_block, running)

    top_all, total_all = over_keys(
        max_sum,
        (jnp.full((seq_rows, att_heads), -1e30, f32), jnp.zeros((seq_rows, att_heads), f32)),
    )
    log_total = top_all + jnp.log(total_all)

    def probabilities(piece_keys, first_key):
        visible = key_visible(first_key, piece_keys.shape[0])
        return jnp.where(visible, jnp.exp(raw_scores(piece_keys) - log_total[..., None]), 0.0)

    def weighted_values(running, pieces, first_key):
        piece_keys, piece_values = pieces

        def weighted_compute_block(current):
            probs_f = probabilities(piece_keys, first_key)
            probs_b = probs_f.astype(bf16)
            leftover = (probs_f - probs_b.astype(f32)).astype(bf16)
            summed = jnp.einsum("rhn,nd->rhd", probs_b, piece_values, preferred_element_type=f32)
            remainder = jnp.einsum(
                "rhn,nd->rhd", leftover, piece_values, preferred_element_type=f32
            )
            return (summed, remainder)

        return lax.cond(
            reachable(first_key, piece_keys.shape[0]), weighted_compute_block, keep_block, running
        )

    empty3 = jnp.zeros((seq_rows, att_heads, HEAD), f32)
    attn_sum, attn_rest = over_keys(weighted_values, (empty3, empty3))
    attn_out = attn_sum.reshape(seq_rows, att_cols).astype(bf16)
    rim = from_behind(pre[seq_rows - rim_rows :, at_x:at_dt], "seq", 1)
    rim_x, rim_bc = (rim[:, :ssm_cols], rim[:, ssm_cols:])
    x_ext = jnp.concatenate([rim_x, x_pre], axis=0)
    bc_ext = jnp.concatenate([rim_bc, bc_pre], axis=0)

    def prepare(x_ext, bc_ext, dt_raw, conv_x, conv_bc, dt_bias, a_log):
        return ssm_prepare(x_ext, bc_ext, dt_raw, conv_x, conv_bc, dt_bias, a_log, tap_masks)

    prepared, prepare_back = jax.vjp(
        prepare, x_ext, bc_ext, dt_raw, conv_x, conv_bc, dt_bias, a_log
    )
    mixed_x, b_rows, c_rows, steps_dt, decay_rate = prepared

    def decompose(mixed_x, b_rows, c_rows, steps_dt, decay_rate):
        return span_all(mixed_x, b_rows, c_rows, steps_dt, decay_rate, segment, segment_prev)

    spanned, span_back = jax.vjp(decompose, mixed_x, b_rows, c_rows, steps_dt, decay_rate)
    intra_out, entering, span_decay, span_state, device_decay, device_state = spanned
    chain_identity = (jnp.ones_like(device_decay), jnp.zeros_like(device_state))
    prefix = entering_2((device_decay, device_state), "seq", chain_forward, chain_identity)
    state_in = prefix[1]
    gated_f, finish_back = jax.vjp(
        span_finish,
        state_in,
        intra_out,
        entering,
        span_decay,
        span_state,
        c_rows,
        mixed_x,
        z_pre,
        d_skip,
    )
    gated_b = gated_f.astype(bf16)
    gated_r = gated_b.astype(f32)
    gain_b = lax.dynamic_slice_in_dim(gate_gain, branch_id * ssm_cols, ssm_cols, 0)
    ssm_all = gate_gain.shape[0]
    squares = branch_sum(jnp.sum(gated_r * gated_r, axis=1))
    inverse_g = lax.rsqrt(squares / ssm_all + EPSILON)[:, None]
    scaled_g = gated_r * inverse_g
    mixed_out = jnp.concatenate([attn_out, (scaled_g * gain_b).astype(bf16)], axis=1)
    projected = branch_scatter(jnp.dot(mixed_out, w_out_b, preferred_element_type=f32))
    middle = x_rows + projected
    scaled2, inverse2 = rms_parts(middle)
    normed2 = branch_gather((scaled2 * norm2_gain).astype(bf16))
    gate_up = jnp.dot(normed2, w_gu, preferred_element_type=f32)
    gate_val = gate_up[:, :hidden_b]
    up_val = gate_up[:, hidden_b:]
    sig_gate = jax.nn.sigmoid(gate_val)
    silu_gate = gate_val * sig_gate
    hidden = (silu_gate * up_val).astype(bf16)
    grad_hidden = lax.dot_general(
        d_out_g, w_down_b, (((1,), (1,)), ((), ())), preferred_element_type=f32
    )
    grad_gate = (grad_hidden * up_val * sig_gate * (1.0 + gate_val * (1.0 - sig_gate))).astype(bf16)
    grad_up = (grad_hidden * silu_gate).astype(bf16)
    grad_gu = jnp.concatenate([grad_gate, grad_up], axis=1)
    grad_normed2 = branch_scatter(
        lax.dot_general(grad_gu, w_gu, (((1,), (1,)), ((), ())), preferred_element_type=f32)
    )
    y_out = (
        middle + branch_scatter(jnp.dot(hidden, w_down_b, preferred_element_type=f32))
    ).astype(bf16)
    grad_middle, grad_n2 = rms_backward(grad_normed2, scaled2, inverse2, norm2_gain)
    grad_middle = grad_middle + d_out.astype(f32)
    grad_proj = branch_gather(grad_middle.astype(bf16))
    grad_mixed = lax.dot_general(
        grad_proj, w_out_b, (((1,), (1,)), ((), ())), preferred_element_type=f32
    )
    back_att = grad_mixed[:, :att_cols].astype(bf16)
    grad_gnormed = grad_mixed[:, att_cols:]
    grad_scaled = grad_gnormed * gain_b
    mean_g = branch_sum(jnp.sum(grad_scaled * scaled_g, axis=1))[:, None] / ssm_all
    back_ssm = (inverse_g * (grad_scaled - scaled_g * mean_g)).astype(bf16)
    grad_gate_gain = jnp.sum(grad_gnormed * scaled_g, axis=0)

    def over_rows(left, right):
        return lax.dot_general(
            left, right, (((0,), (0,)), ((), ())), preferred_element_type=f32
        ).astype(bf16)

    def strips(rows_all):
        wide = rows_all.reshape((groups, parts, strip) + rows_all.shape[1:])
        return jnp.swapaxes(wide, 0, 1).reshape((parts, groups * strip) + rows_all.shape[1:])

    terms2 = jnp.concatenate(
        [
            over_rows(mixed_out, grad_proj).reshape(parts, chunk, dim),
            over_rows(hidden, d_out_g).reshape(parts, chunk, dim),
            strips(over_rows(normed2, grad_gu)),
        ],
        axis=1,
    )
    own2 = lax.psum_scatter(terms2, "seq", scatter_dimension=0)
    own_rows = lax.ppermute(own2[: 2 * chunk], ("branch", "seq"), from_heads).astype(f32)
    grad_w_out = own_rows[:chunk]
    grad_w_down = own_rows[chunk:]
    own_gu = lax.all_to_all(
        own2[2 * chunk :].reshape(groups, strip, 2 * hidden_b), "branch", 0, 0, tiled=True
    ).astype(f32)

    def all_columns(blocks):
        blocks = jnp.swapaxes(blocks, 0, 1)
        return jnp.concatenate(
            [blocks[:, :, :hidden_a].reshape(strip, -1), blocks[:, :, hidden_a:].reshape(strip, -1)],
            axis=1,
        )

    grad_w_gate = all_columns(own_gu[:, :, :hidden_b])
    grad_w_up = all_columns(own_gu[:, :, hidden_b:])
    (
        grad_state_in,
        grad_intra,
        grad_enter,
        grad_cdecay,
        grad_cstate,
        grad_c_fin,
        grad_x_fin,
        grad_z,
        grad_skip,
    ) = finish_back(back_ssm.astype(f32))
    suffix = entering_3((device_decay, grad_state_in), "seq", chain_backward, chain_identity)
    grad_out_state = suffix[1]
    grad_dev_decay = jnp.sum(grad_out_state * state_in, axis=(1, 2))
    grad_x_span, grad_b, grad_c_span, grad_dt, grad_rate = span_back(
        (grad_intra, grad_enter, grad_cdecay, grad_cstate, grad_dev_decay, grad_out_state)
    )
    grad_x_ext, grad_bc_ext, grad_dt_raw, grad_conv_x, grad_conv_bc, grad_dt_bias, grad_a_log = (
        prepare_back(
            (grad_x_fin + grad_x_span, grad_b, grad_c_fin + grad_c_span, grad_dt, grad_rate)
        )
    )
    rim_back = from_behind(
        jnp.concatenate([grad_x_ext[:rim_rows], grad_bc_ext[:rim_rows]], axis=1), "seq", -1
    )
    rim_back_x, rim_back_bc = (rim_back[:, :ssm_cols], rim_back[:, ssm_cols:])
    grad_x_pre = grad_x_ext[rim_rows:].at[seq_rows - rim_rows :].add(rim_back_x)
    grad_bc_pre = grad_bc_ext[rim_rows:].at[seq_rows - rim_rows :].add(rim_back_bc)
    grad_att_rows = back_att.reshape(seq_rows, att_heads, HEAD)
    delta_rows = jnp.sum(grad_att_rows.astype(f32) * (attn_sum + attn_rest), axis=-1)

    def score_grads(piece_keys, piece_values, first_key):
        probs_f = probabilities(piece_keys, first_key)
        grad_p = jnp.einsum("rhd,nd->rhn", grad_att_rows, piece_values, preferred_element_type=f32)
        return (probs_f, (probs_f * (grad_p - delta_rows[..., None])).astype(bf16))

    seq_ends = jnp.cumsum(lengths)
    last_end = jnp.sum(jnp.where(jnp.arange(lengths.shape[0]) == segment[-1], seq_ends, 0))
    empty_keys = jnp.zeros((seq_rows, HEAD), f32)
    first_row = jnp.int32(0)
    piece_q = lax.all_gather(queries, "seq", axis=0, tiled=True)
    piece_grad = lax.all_gather(grad_att_rows, "seq", axis=0, tiled=True)
    piece_lse = lax.all_gather(log_total.astype(jnp.bfloat16), "seq", axis=0, tiled=True).astype(
        jnp.float32
    )
    piece_delta = lax.all_gather(delta_rows.astype(jnp.bfloat16), "seq", axis=0, tiled=True).astype(
        jnp.float32
    )
    amount = piece_q.shape[0]
    grad_q_now = empty3
    grad_k_now = empty_keys
    grad_v_now = empty_keys

    def query_block(current):
        probs_f, grad_s = score_grads(piece_keys, piece_values, first_row)
        return SCORE_SCALE * jnp.einsum(
            "rhn,nd->rhd", grad_s, piece_keys, preferred_element_type=f32
        )

    def key_block(current):
        query_ids, query_seg, unused = row_layout(lengths, first_row, amount)
        visible = (
            (row_ids[None, :] <= query_ids[:, None]) & (segment[None, :] == query_seg[:, None])
        )[:, None, :]
        scores = (
            jnp.einsum("nhd,rd->nhr", piece_q, keys_rot, preferred_element_type=f32) * SCORE_SCALE
        )
        probs_f = jnp.where(visible, jnp.exp(scores - piece_lse[..., None]), 0.0)
        grad_p = jnp.einsum("nhd,rd->nhr", piece_grad, values_b, preferred_element_type=f32)
        grad_s = (probs_f * (grad_p - piece_delta[..., None])).astype(bf16)
        grad_k = SCORE_SCALE * jnp.einsum(
            "nhr,nhd->rd", grad_s, piece_q, preferred_element_type=f32
        )
        grad_v = jnp.einsum(
            "nhr,nhd->rd", probs_f.astype(bf16), piece_grad, preferred_element_type=f32
        )
        return (grad_k, grad_v)

    grad_q_now = lax.cond(reachable(first_row, amount), query_block, keep_block, grad_q_now)
    near_enough = (first_row + amount > group_first) & (first_row < last_end)
    grad_k_now, grad_v_now = lax.cond(near_enough, key_block, keep_block, (grad_k_now, grad_v_now))
    grad_q_raw = rotate(grad_q_now, position, -1.0).reshape(seq_rows, att_cols).astype(bf16)
    grad_k_raw = rotate(grad_k_now.reshape(seq_rows, 1, HEAD), position, -1.0).reshape(
        seq_rows, HEAD
    )
    pad_cols = dt_pad - ssm_heads
    grad_pre = jnp.concatenate(
        [
            grad_q_raw,
            grad_k_raw.astype(bf16),
            grad_v_now.astype(bf16),
            grad_z.astype(bf16),
            grad_x_pre.astype(bf16),
            grad_bc_pre.astype(bf16),
            jnp.pad(grad_dt_raw, ((0, 0), (0, pad_cols))).astype(bf16),
        ],
        axis=1,
    )
    grad_group = lax.dot_general(
        grad_pre, w1, (((1,), (1,)), ((), ())), preferred_element_type=f32
    )
    grad_n1 = jnp.sum(grad_group * group_in.astype(f32), axis=0) / norm1_gain
    grad_w1 = over_rows(group_in, grad_pre)
    tall = groups * strip

    def to_column(vector, rows_each):
        padded = jnp.pad(vector.reshape(parts, rows_each), ((0, 0), (0, tall - rows_each)))
        return padded[:, :, None]

    def to_columns(matrix, rows_each):
        wide = jnp.swapaxes(matrix.reshape(matrix.shape[0], parts, rows_each), 0, 1)
        wide = jnp.pad(wide, ((0, 0), (0, 0), (0, tall - rows_each)))
        return jnp.swapaxes(wide, 1, 2)

    bc_each = conv_bc.shape[1] // (groups * parts)
    x_each = ssm_cols // parts
    bc_wide = grad_conv_bc.reshape(CONV, groups, parts, bc_each)
    bc_wide = jnp.pad(bc_wide, ((0, 0), (0, 0), (0, 0), (0, strip - bc_each)))
    bc_wide = jnp.transpose(bc_wide, (2, 1, 3, 0)).reshape(parts, tall, CONV)
    heads3 = jnp.concatenate([grad_a_log, grad_dt_bias, grad_skip])
    heads3 = jnp.broadcast_to(heads3[None, None, :], (parts, tall, 3 * ssm_heads))
    small = jnp.concatenate(
        [
            strips(jnp.stack([grad_n1, grad_n2], axis=1)),
            bc_wide,
            to_column(grad_gate_gain, x_each),
            to_columns(grad_conv_x, x_each),
            heads3,
        ],
        axis=2,
    )
    small = jnp.pad(small, ((0, 0), (0, 0), (0, pad_cols - small.shape[2]))).astype(bf16)

    def plain(rows_all):
        return rows_all.reshape(parts, tall, rows_all.shape[1])

    terms1 = jnp.concatenate(
        [
            plain(grad_w1[:, :at_k]),
            strips(grad_w1[:, at_k:at_z]),
            plain(grad_w1[:, at_z:at_bc]),
            strips(grad_w1[:, at_bc:at_dt]),
            plain(grad_w1[:, at_dt : at_dt + ssm_heads]),
            small,
        ],
        axis=2,
    )
    grad_normed1 = branch_scatter(grad_group)
    own1 = lax.psum_scatter(terms1, "seq", scatter_dimension=0)
    at_s = at_dt + ssm_heads
    own_f = own1.astype(f32)
    grad_mix = jnp.concatenate([own_f[:, :at_k], own_f[:, at_z:at_bc]], axis=1)
    grad_dt_w = own_f[:, at_dt:at_s]
    shared_part = jnp.concatenate(
        [own1[:, at_k:at_z], own1[:, at_bc:at_dt], own1[:, at_s : at_s + 2 + CONV]], axis=1
    ).reshape(groups, strip, -1)
    blocks = lax.all_to_all(shared_part, "branch", 0, 0, tiled=True).astype(f32)
    per_kv = groups // KV
    bc_cols = at_dt - at_bc
    grad_shared = jnp.concatenate(
        [
            jnp.sum(blocks[h * per_kv : (h + 1) * per_kv, :, at : at + HEAD], axis=0)
            for at in (0, HEAD)
            for h in range(KV)
        ]
        + [jnp.sum(blocks[:, :, 2 * HEAD : 2 * HEAD + bc_cols], axis=0)],
        axis=1,
    )
    gains = jnp.sum(blocks[:, :, 2 * HEAD + bc_cols :], axis=0)
    at_g = at_s + 2 + CONV
    grad_gain_g = own_f[:x_each, at_g]
    grad_cx = own_f[:x_each, at_g + 1 : at_g + 1 + CONV].T
    at_h = at_g + 1 + CONV
    grad_x1, unused_n1 = rms_backward(grad_normed1, scaled1, inverse1, norm1_gain)
    return (
        y_out,
        grad_middle + grad_x1,
        gains[:, 0],
        grad_mix,
        grad_dt_w,
        grad_shared,
        grad_cx,
        gains[:bc_each, 2:].T,
        own_f[0, at_h : at_h + ssm_heads],
        own_f[0, at_h + ssm_heads : at_h + 2 * ssm_heads],
        own_f[0, at_h + 2 * ssm_heads : at_h + 3 * ssm_heads],
        grad_gain_g,
        grad_w_out,
        gains[:, 1],
        grad_w_gate,
        grad_w_up,
        grad_w_down,
    )


def solution(mesh):
    in_specs = (
        P(("seq", "branch"), None),
        P(),
        P(),
        P("seq", "branch"),
        P("seq", "branch"),
        P("seq", None),
        P(None, "branch"),
        P(),
        P("branch"),
        P("branch"),
        P("branch"),
        P(),
        P("seq", None),
        P(),
        P("seq", None),
        P("seq", None),
        P("seq", None),
        P(("seq", "branch"), None),
    )
    out_specs = (
        P(("seq", "branch"), None),
        P(("seq", "branch"), None),
        P(("branch", "seq")),
        P("seq", "branch"),
        P("seq", "branch"),
        P(("branch", "seq"), None),
        P(None, ("branch", "seq")),
        P(None, ("branch", "seq")),
        P("branch"),
        P("branch"),
        P("branch"),
        P(("branch", "seq")),
        P(("branch", "seq"), None),
        P(("branch", "seq")),
        P(("branch", "seq"), None),
        P(("branch", "seq"), None),
        P(("branch", "seq"), None),
    )
    return jax.shard_map(shards, mesh=mesh, in_specs=in_specs, out_specs=out_specs, check_vma=False)
```

```python
import functools

import jax
import jax.numpy as jnp
from jax import lax
from jax.experimental import pallas as pl
from jax.experimental.pallas import tpu as pltpu
from jax.sharding import PartitionSpec as P

HEADS_ATT = 8
KV = 2
HEAD = 64
CONV = 4
LANES = 128
TILE = 128
MASKED = -1e30
HIGHEST = lax.Precision.HIGHEST
EPSILON = 1e-06
SCORE_SCALE = 0.125
ROPE_BASE = 1000000.0
F32 = jnp.float32
B16 = jnp.bfloat16
LANE_DOT = (((1,), (1,)), ((), ()))
ROW_DOT = (((0,), (0,)), ((), ()))


VMEM_SPEC = pl.BlockSpec(memory_space=pltpu.VMEM)
SMEM_SPEC = pl.BlockSpec(memory_space=pltpu.SMEM)


def from_behind(block, axis, distance):
    devices = range(lax.axis_size(axis))
    route = [(i - distance, i) for i in devices if i - distance in devices]
    return lax.ppermute(block, axis, route)


def rms_parts(value):
    inverse = lax.rsqrt(jnp.mean(value * value, axis=-1, keepdims=True) + EPSILON)
    return (value * inverse, inverse)


def rms_backward(grad_out, scaled, inverse, gain_vec):
    grad_scaled = grad_out * gain_vec
    grad_in = inverse * (
        grad_scaled - scaled * jnp.mean(grad_scaled * scaled, axis=-1, keepdims=True)
    )
    return (grad_in, jnp.sum(grad_out * scaled, axis=0))


def rotate(values_in, position, direction):
    half_dim = values_in.shape[-1] // 2
    inverse = ROPE_BASE ** (-jnp.arange(half_dim, dtype=jnp.float32) / half_dim)
    angles = position.astype(jnp.float32)[:, None] * inverse[None, :]
    cosine = jnp.cos(angles)[:, None, :]
    sine_dir = direction * jnp.sin(angles)[:, None, :]
    front_half = values_in[..., :half_dim]
    back_half = values_in[..., half_dim:]
    return jnp.concatenate(
        [front_half * cosine - back_half * sine_dir, front_half * sine_dir + back_half * cosine],
        axis=-1,
    )


def attend_kernel(bounds, begin_ref, q_ref, kv_ref, out_ref, lse_ref, top, acc, *, heads, block, keys):
    rows = q_ref.shape[0]
    first_row = bounds[2]
    top[...] = jnp.full_like(top, MASKED)
    acc[...] = jnp.zeros_like(acc)
    row_ids = first_row + lax.broadcasted_iota(jnp.int32, (1, rows), 1)
    begins = begin_ref[...]
    ones = (lax.broadcasted_iota(jnp.int32, (keys, HEAD), 1) == 0).astype(jnp.bfloat16)

    def step(n, masked):
        at = n * keys
        kv = kv_ref[pl.ds(pl.multiple_of(at, keys), keys), :]
        k = kv[:, :HEAD]
        v = jnp.concatenate([kv[:, HEAD:], ones], axis=1).T
        if masked:
            key_ids = at + lax.broadcasted_iota(jnp.int32, (keys, rows), 0)
            seen = (key_ids <= row_ids) & (key_ids >= begins)
        for h in range(heads):
            q = q_ref[:, h * HEAD : (h + 1) * HEAD]
            s = lax.dot_general(k, q, (((1,), (1,)), ((), ())), preferred_element_type=jnp.float32)
            if masked:
                s = jnp.where(seen, s, MASKED)
            old = top[h : h + 1, :]
            new = jnp.maximum(old, jnp.max(s, axis=0, keepdims=True))
            p = jnp.exp(s - new).astype(jnp.bfloat16)
            scale = jnp.exp(old - new)
            add = jnp.dot(v, p, preferred_element_type=jnp.float32)
            acc[h] = acc[h] * scale + add
            top[h : h + 1, :] = new

    pl.loop(bounds[0], bounds[1])(lambda n: step(n, True))
    pl.loop(bounds[1], bounds[3])(lambda n: step(n, False))
    pl.loop(bounds[3], bounds[4])(lambda n: step(n, True))
    for h in range(heads):
        total = acc[h, HEAD : HEAD + 1, :]
        out_ref[:, h * HEAD : (h + 1) * HEAD] = (acc[h, :HEAD, :] / total).T.astype(jnp.bfloat16)
        lse_ref[h : h + 1, :] = top[h : h + 1, :] + jnp.log(total)


def attend(queries, kv_all, begins, bounds, heads, keys):
    rows = queries.shape[0]
    vm = pl.BlockSpec(memory_space=pltpu.VMEM)
    return pl.pallas_call(
        functools.partial(attend_kernel, heads=heads, block=rows, keys=keys),
        out_shape=(jax.ShapeDtypeStruct((rows, heads * HEAD), jnp.bfloat16), jax.ShapeDtypeStruct((8, rows), jnp.float32)),
        in_specs=[pl.BlockSpec(memory_space=pltpu.SMEM), vm, vm, vm],
        out_specs=(vm, vm),
        scratch_shapes=[pltpu.VMEM((8, rows), jnp.float32), pltpu.VMEM((heads, LANES, rows), jnp.float32)],
        compiler_params=pltpu.CompilerParams(vmem_limit_bytes=48 << 20),
        name="attend",
    )(bounds, begins, queries, kv_all)


def query_grad_kernel(bounds, begin_ref, q_ref, g_ref, kv_ref, out_ref, acc, *, heads, keys):
    rows = q_ref.shape[0]
    acc[...] = jnp.zeros_like(acc)
    row_ids = bounds[2] + lax.broadcasted_iota(jnp.int32, (rows, keys), 0)
    begins = begin_ref[...]
    minus = jnp.where(lax.broadcasted_iota(jnp.int32, (keys, HEAD), 1) < 2, -1.0, 0.0).astype(jnp.bfloat16)

    def step(n, masked):
        at = n * keys
        kv = kv_ref[pl.ds(pl.multiple_of(at, keys), keys), :]
        k = jnp.concatenate([kv[:, :HEAD], minus], axis=1)
        v = jnp.concatenate([kv[:, HEAD:], minus], axis=1)
        if masked:
            key_ids = at + lax.broadcasted_iota(jnp.int32, (rows, keys), 1)
            seen = (key_ids <= row_ids) & (key_ids >= begins)
        for h in range(heads):
            q = q_ref[:, h * LANES : (h + 1) * LANES]
            g = g_ref[:, h * LANES : (h + 1) * LANES]
            s = lax.dot_general(q, k, (((1,), (1,)), ((), ())), preferred_element_type=jnp.float32)
            if masked:
                s = jnp.where(seen, s, MASKED)
            gp = lax.dot_general(g, v, (((1,), (1,)), ((), ())), preferred_element_type=jnp.float32)
            ds = (jnp.exp(s) * gp).astype(jnp.bfloat16)
            acc[h] += jnp.dot(ds, k, preferred_element_type=jnp.float32)

    pl.loop(bounds[0], bounds[1])(lambda n: step(n, True))
    pl.loop(bounds[1], bounds[3])(lambda n: step(n, False))
    pl.loop(bounds[3], bounds[4])(lambda n: step(n, True))
    for h in range(heads):
        out_ref[:, h * HEAD : (h + 1) * HEAD] = acc[h, :, :HEAD] * SCORE_SCALE


def query_grad(q_pack, g_pack, kv_all, begins, bounds, heads, keys):
    rows = q_pack.shape[0]
    vm = pl.BlockSpec(memory_space=pltpu.VMEM)
    return pl.pallas_call(
        functools.partial(query_grad_kernel, heads=heads, keys=keys),
        out_shape=jax.ShapeDtypeStruct((rows, heads * HEAD), jnp.float32),
        in_specs=[pl.BlockSpec(memory_space=pltpu.SMEM), vm, vm, vm, vm],
        out_specs=vm,
        scratch_shapes=[pltpu.VMEM((heads, rows, LANES), jnp.float32)],
        compiler_params=pltpu.CompilerParams(vmem_limit_bytes=48 << 20),
        name="query_grad",
    )(bounds, begins, q_pack, g_pack, kv_all)


def key_grad_kernel(bounds, end_ref, kv_ref, q_ref, g_ref, out_ref, acc_k, acc_v, *, heads, keys):
    rows = kv_ref.shape[0]
    acc_k[...] = jnp.zeros_like(acc_k)
    acc_v[...] = jnp.zeros_like(acc_v)
    key_ids = bounds[2] + lax.broadcasted_iota(jnp.int32, (rows, keys), 0)
    ends = end_ref[...]
    minus = jnp.where(lax.broadcasted_iota(jnp.int32, (rows, HEAD), 1) < 2, -1.0, 0.0).astype(jnp.bfloat16)
    k = jnp.concatenate([kv_ref[:, :HEAD], minus], axis=1)
    v = jnp.concatenate([kv_ref[:, HEAD:], minus], axis=1)

    def step(n, masked):
        at = n * keys
        at_al = pl.ds(pl.multiple_of(at, keys), keys)
        if masked:
            row_ids = at + lax.broadcasted_iota(jnp.int32, (rows, keys), 1)
            seen = (key_ids <= row_ids) & (row_ids < ends)
        for h in range(heads):
            q = q_ref[at_al, h * LANES : (h + 1) * LANES]
            g = g_ref[at_al, h * LANES : (h + 1) * LANES]
            s = lax.dot_general(k, q, (((1,), (1,)), ((), ())), preferred_element_type=jnp.float32)
            if masked:
                s = jnp.where(seen, s, MASKED)
            p = jnp.exp(s)
            gp = lax.dot_general(v, g, (((1,), (1,)), ((), ())), preferred_element_type=jnp.float32)
            ds = (p * gp).astype(jnp.bfloat16)
            acc_k[...] += jnp.dot(ds, q, preferred_element_type=jnp.float32)
            acc_v[...] += jnp.dot(p.astype(jnp.bfloat16), g, preferred_element_type=jnp.float32)

    pl.loop(bounds[0], bounds[1])(lambda n: step(n, True))
    pl.loop(bounds[1], bounds[3])(lambda n: step(n, False))
    pl.loop(bounds[3], bounds[4])(lambda n: step(n, True))
    out_ref[:, :HEAD] = acc_k[:, :HEAD]
    out_ref[:, HEAD:] = acc_v[:, :HEAD]


def key_grad(kv_own, q_all, g_all, ends, bounds, heads, keys):
    rows = kv_own.shape[0]
    vm = pl.BlockSpec(memory_space=pltpu.VMEM)
    return pl.pallas_call(
        functools.partial(key_grad_kernel, heads=heads, keys=keys),
        out_shape=jax.ShapeDtypeStruct((rows, LANES), jnp.float32),
        in_specs=[pl.BlockSpec(memory_space=pltpu.SMEM), vm, vm, vm, vm],
        out_specs=vm,
        scratch_shapes=[pltpu.VMEM((rows, LANES), jnp.float32)] * 2,
        compiler_params=pltpu.CompilerParams(vmem_limit_bytes=56 << 20),
        name="key_grad",
    )(bounds, ends, kv_own, q_all, g_all)


def iota(shape, dim):
    return lax.broadcasted_iota(jnp.int32, shape, dim)


def per_head(columns, pair):
    shape = (columns.shape[0], LANES)
    return jnp.where(
        iota(shape, 1) < HEAD, columns[:, 2 * pair : 2 * pair + 1], columns[:, 2 * pair + 1 : 2 * pair + 2]
    )


def one_head(values, head):
    keep = (iota(values.shape, 1) < HEAD) == (head % 2 == 0)
    return jnp.where(keep, values, jnp.zeros_like(values))


def into_lane(columns, head, column):
    return jnp.where(iota(columns.shape, 1) == head, column, columns)


def silu_slope(v, sig):
    return sig * (1.0 + v * (1.0 - sig))


def tap_window(ext_ref, tap, first, amount, places):
    return ext_ref[first + 8 - (CONV - 1) + tap : first + 8 - (CONV - 1) + tap + amount, :]


def span_kernel(places, begin_ref, pre_ref, rim_ref, taps_ref, params_ref, u_ref, intra_ref, cum_ref, state_ref, ext, xb, *, heads, at_x, at_dt, nstate):
    rows = pre_ref.shape[0]
    cols = heads * HEAD
    first_row, last_begin = places[0], places[1]
    ext[0:8, :] = rim_ref[...]
    ext[8 : 8 + rows, :] = pre_ref[:, at_x:at_dt]
    local = begin_ref[...] - first_row
    row_ids = iota((rows, 1), 0)
    for i in range(0, rows, TILE):
        total = jnp.zeros((TILE, ext.shape[1]), F32)
        for tap in range(CONV):
            seen = row_ids[i : i + TILE] - (CONV - 1) + tap >= local[i : i + TILE]
            window = tap_window(ext, tap, i, TILE, places)
            total = total + jnp.where(seen, window, 0.0) * taps_ref[tap : tap + 1, :]
        u_ref[i : i + TILE, :] = total
        xb[i : i + TILE, :] = (total * jax.nn.sigmoid(total)).astype(B16)
    raw = pre_ref[:, at_dt : at_dt + LANES] + params_ref[0:1, :]
    dt = jnp.maximum(raw, 0.0) + jnp.log1p(jnp.exp(-jnp.abs(raw)))
    lower = (iota((rows, rows), 0) >= iota((rows, rows), 1)).astype(F32)
    cum = jnp.dot(lower, dt * params_ref[1:2, :], precision=HIGHEST, preferred_element_type=F32)
    cum_ref[:, :LANES] = cum
    cum_ref[:, LANES:] = dt
    cum_t, dt_t = cum.T, dt.T
    last = cum[rows - 1 : rows, :]
    closing = row_ids + first_row >= last_begin
    to_end = jnp.where(closing, jnp.exp(last - cum) * dt, 0.0)
    for i in range(0, rows, TILE):
        width = i + TILE
        c = xb[i : i + TILE, cols + nstate : cols + 2 * nstate]
        b = xb[:width, cols : cols + nstate]
        inner = lax.dot_general(c, b, LANE_DOT, preferred_element_type=F32)
        key = iota((TILE, width), 1)
        seen = (key <= iota((TILE, width), 0) + i) & (key >= local[i : i + TILE])
        for pair in range(heads // 2):
            out = []
            for h in (2 * pair, 2 * pair + 1):
                spread = jnp.where(seen, cum[i : i + TILE, h : h + 1] - cum_t[h : h + 1, :width], MASKED)
                weights = (jnp.exp(spread) * inner * dt_t[h : h + 1, :width]).astype(B16)
                out.append(jnp.dot(weights, xb[:width, pair * LANES : (pair + 1) * LANES], preferred_element_type=F32))
            intra_ref[i : i + TILE, pair * LANES : (pair + 1) * LANES] = jnp.where(iota((TILE, LANES), 1) < HEAD, out[0], out[1])
    b_all = xb[:, cols : cols + nstate]
    for pair in range(heads // 2):
        at = slice(pair * LANES, (pair + 1) * LANES)
        closed = (xb[:, at].astype(F32) * per_head(to_end, pair)).astype(B16)
        state_ref[at, :] = lax.dot_general(closed, b_all, ROW_DOT, preferred_element_type=F32).astype(B16)
    decay = jnp.where(last_begin < first_row, jnp.exp(last), 0.0)
    high = decay.astype(B16)
    low = (decay - high.astype(F32)).astype(B16)
    both = jnp.concatenate([jnp.broadcast_to(high.astype(F32), (LANES // 2, LANES)), jnp.broadcast_to(low.astype(F32), (LANES // 2, LANES))], axis=0)
    state_ref[cols : cols + LANES, :] = both.T.astype(B16)


def call(kernel, name, args, outs, scratch):
    return pl.pallas_call(
        kernel,
        out_shape=tuple(jax.ShapeDtypeStruct(s, d) for s, d in outs),
        in_specs=[SMEM_SPEC] + [VMEM_SPEC] * (len(args) - 1),
        out_specs=tuple(VMEM_SPEC for _ in outs),
        scratch_shapes=[pltpu.VMEM(s, d) for s, d in scratch],
        compiler_params=pltpu.CompilerParams(vmem_limit_bytes=56 << 20),
        name=name,
    )(*args)


def span_forward(places, begins, pre, rim, taps, params, heads, at_x, at_dt, nstate):
    rows = pre.shape[0]
    wide = at_dt - at_x
    cols = heads * HEAD
    return call(
        functools.partial(span_kernel, heads=heads, at_x=at_x, at_dt=at_dt, nstate=nstate),
        "span_forward",
        (places, begins, pre, rim, taps, params),
        (((rows, wide), F32), ((rows, cols), F32), ((rows, 2 * LANES), F32), ((cols + LANES, nstate), B16)),
        (((rows + 8, wide), F32), ((rows, wide), B16)),
    )


def decay_of(states_ref, k, head, cols):
    tail = states_ref[k, cols + head - head % 8 : cols + head - head % 8 + 8, :].astype(F32)
    row = tail[head % 8 : head % 8 + 1, :]
    return row[:, 0:1] + row[:, LANES // 2 : LANES // 2 + 1]


def finish_kernel(places, begin_ref, states_ref, u_ref, intra_ref, cum_ref, pre_ref, params_ref, gated_ref, v_ref, state_ref, squares_ref, *, heads, at_z, nstate):
    rows = u_ref.shape[0]
    cols = heads * HEAD
    state_ref[...] = jnp.zeros_like(state_ref)

    def fold(k):
        for h in range(heads):
            at = slice(h * HEAD, (h + 1) * HEAD)
            state_ref[at, :] = state_ref[at, :] * decay_of(states_ref, k, h, cols) + states_ref[k, at, :].astype(F32)

    pl.loop(0, places[2])(fold)
    carried = begin_ref[...] < places[0]
    for i in range(0, rows, TILE):
        r = slice(i, i + TILE)
        enter = jnp.where(carried[r], jnp.exp(cum_ref[r, :LANES]), 0.0)
        uc = u_ref[r, cols + nstate : cols + 2 * nstate]
        c = (uc * jax.nn.sigmoid(uc)).astype(B16)
        total = jnp.zeros((8, TILE), F32)
        for pair in range(heads // 2):
            at = slice(pair * LANES, (pair + 1) * LANES)
            y = lax.dot_general(c, state_ref[at, :].astype(B16), LANE_DOT, preferred_element_type=F32)
            ux = u_ref[r, at]
            x = ux * jax.nn.sigmoid(ux)
            skip = per_head(params_ref[2:3, :], pair)
            v = intra_ref[r, at] + per_head(enter, pair) * y + skip * x
            z = pre_ref[r, at_z + pair * LANES : at_z + (pair + 1) * LANES]
            gated = (v * (z * jax.nn.sigmoid(z))).astype(B16)
            v_ref[r, at] = v
            gated_ref[r, at] = gated
            g = gated.astype(F32)
            total = total + lax.dot_general(jnp.ones((8, LANES), F32), g * g, LANE_DOT, precision=HIGHEST, preferred_element_type=F32)
        squares_ref[:, r] = total


def span_finish(places, begins, states, u, intra, cum, pre, params, heads, at_z, nstate):
    rows = u.shape[0]
    cols = heads * HEAD
    return call(
        functools.partial(finish_kernel, heads=heads, at_z=at_z, nstate=nstate),
        "span_finish",
        (places, begins, states, u, intra, cum, pre, params),
        (((rows, cols), B16), ((rows, cols), F32), ((cols, nstate), F32), ((8, rows), F32)),
        (),
    )


def gate_back_kernel(places, begin_ref, g_ref, u_ref, cum_ref, pre_ref, v_ref, dz_ref, state_ref, eg, *, heads, at_z, nstate):
    rows = u_ref.shape[0]
    cols = heads * HEAD
    carried = begin_ref[...] < places[0]
    uc = u_ref[:, cols + nstate : cols + 2 * nstate]
    c = (uc * jax.nn.sigmoid(uc)).astype(B16)
    for i in range(0, rows, TILE):
        r = slice(i, i + TILE)
        enter = jnp.where(carried[r], jnp.exp(cum_ref[r, :LANES]), 0.0)
        for pair in range(heads // 2):
            at = slice(pair * LANES, (pair + 1) * LANES)
            z = pre_ref[r, at_z + pair * LANES : at_z + (pair + 1) * LANES]
            sig = jax.nn.sigmoid(z)
            gg = g_ref[r, at].astype(F32)
            dz_ref[r, at] = (gg * v_ref[r, at] * silu_slope(z, sig)).astype(B16)
            eg[r, at] = (gg * (z * sig) * per_head(enter, pair)).astype(B16)
    state_ref[:cols, :] = lax.dot_general(eg[...], c, ROW_DOT, preferred_element_type=F32).astype(B16)
    state_ref[cols:, :] = jnp.zeros((LANES, nstate), B16)


def gate_back(places, begins, back, u, cum, pre, v, heads, at_z, nstate):
    rows = u.shape[0]
    cols = heads * HEAD
    return call(
        functools.partial(gate_back_kernel, heads=heads, at_z=at_z, nstate=nstate),
        "gate_back",
        (places, begins, back, u, cum, pre, v),
        (((rows, cols), B16), ((cols + LANES, nstate), B16)),
        (((rows, cols), B16),),
    )


def back_kernel(places, begin_ref, g_ref, pre_ref, rim_ref, u_ref, cum_ref, state_ref, states_ref, grads_ref, taps_ref, params_ref, gx_ref, gdt_ref, rim_out, taps_out, small_out, ext, gext, xb, gb, later, dxb, lane_sum, cols_sum, *, heads, at_z, at_x, at_dt, nstate):
    rows = u_ref.shape[0]
    cols = heads * HEAD
    wide = at_dt - at_x
    count = states_ref.shape[0]
    pairs = heads // 2
    first_row, last_begin, mine = places[0], places[1], places[2]
    later[...] = jnp.zeros_like(later)

    def fold(n):
        k = count - 1 - n
        for h in range(heads):
            at = slice(h * HEAD, (h + 1) * HEAD)
            later[at, :] = later[at, :] * decay_of(states_ref, k, h, cols) + grads_ref[k, at, :].astype(F32)

    pl.loop(0, count - 1 - mine)(fold)
    local = begin_ref[...] - first_row
    row_ids = iota((rows, 1), 0)
    cum = cum_ref[:, :LANES]
    dt = cum_ref[:, LANES:]
    cum_t, dt_t = cum.T, dt.T
    last = cum[rows - 1 : rows, :]
    leave = jnp.where(row_ids + first_row >= last_begin, jnp.exp(last - cum), 0.0)
    enter = jnp.where(begin_ref[...] < first_row, jnp.exp(cum), 0.0)
    to_end = leave * dt
    for i in range(0, rows, TILE):
        r = slice(i, i + TILE)
        u = u_ref[r, :]
        xb[r, :] = (u * jax.nn.sigmoid(u)).astype(B16)
        z = pre_ref[r, at_z : at_z + cols]
        gb[r, :] = (g_ref[r, :].astype(F32) * (z * jax.nn.sigmoid(z))).astype(B16)
    dxb[...] = jnp.zeros_like(dxb)
    cols_sum[...] = jnp.zeros_like(cols_sum)
    b_at = slice(cols, cols + nstate)
    c_at = slice(cols + nstate, cols + 2 * nstate)
    for i in range(0, rows, TILE):
        width = i + TILE
        r = slice(i, i + TILE)
        inner = lax.dot_general(xb[r, c_at], xb[:width, b_at], LANE_DOT, preferred_element_type=F32)
        key = iota((TILE, width), 1)
        seen = (key <= iota((TILE, width), 0) + i) & (key >= local[r])
        grad_inner = jnp.zeros((TILE, width), F32)
        sums = jnp.zeros((TILE, LANES), F32)
        for h in range(heads):
            at = slice(h // 2 * LANES, (h // 2 + 1) * LANES)
            g = one_head(gb[r, at], h)
            spread = jnp.where(seen, cum[r, h : h + 1] - cum_t[h : h + 1, :width], MASKED)
            decays = jnp.exp(spread)
            steps = dt_t[h : h + 1, :width]
            pairing = lax.dot_general(g, xb[:width, at], LANE_DOT, preferred_element_type=F32)
            paired = pairing * decays
            grad_inner = grad_inner + paired * steps
            both = paired * inner
            cols_sum[h : h + 1, :width] += jnp.sum(both, axis=0, keepdims=True)
            sums = into_lane(sums, h, jnp.sum(both * steps, axis=1, keepdims=True))
            weights = (decays * inner * steps).astype(B16)
            dxb[:width, at] += lax.dot_general(weights, g, ROW_DOT, preferred_element_type=F32)
        lane_sum[r, :] = sums
        grad_inner = grad_inner.astype(B16)
        dxb[r, c_at] += jnp.dot(grad_inner, xb[:width, b_at], preferred_element_type=F32)
        dxb[:width, b_at] += lax.dot_general(grad_inner, xb[r, c_at], ROW_DOT, preferred_element_type=F32)
    from_cols = jnp.concatenate([cols_sum[...], jnp.zeros((LANES - 8, rows), F32)], axis=0).T
    state_b = state_ref[...].astype(B16)
    later_b = later[...].astype(B16)
    entered = jnp.zeros((rows, LANES), F32)
    closed = jnp.zeros((rows, LANES), F32)
    skips = jnp.zeros((1, LANES), F32)
    chained = jnp.zeros((1, LANES), F32)
    for pair in range(pairs):
        at = slice(pair * LANES, (pair + 1) * LANES)
        x = xb[:, at].astype(F32)
        g = gb[:, at].astype(F32)
        y = lax.dot_general(xb[:, c_at], state_b[at, :], LANE_DOT, preferred_element_type=F32)
        q = lax.dot_general(xb[:, b_at], later_b[at, :], LANE_DOT, preferred_element_type=F32)
        ends = per_head(to_end, pair)
        dxb[:, c_at] += jnp.dot((g * per_head(enter, pair)).astype(B16), state_b[at, :], preferred_element_type=F32)
        dxb[:, b_at] += jnp.dot((x * ends).astype(B16), later_b[at, :], preferred_element_type=F32)
        dxb[:, at] += ends * q + g * per_head(params_ref[2:3, :], pair)
        gy, xq, gx = g * y, x * q, jnp.sum(g * x, axis=0, keepdims=True)
        kept = jnp.sum(later[at, :] * state_ref[at, :], axis=1, keepdims=True)
        for h in (2 * pair, 2 * pair + 1):
            entered = into_lane(entered, h, jnp.sum(one_head(gy, h), axis=1, keepdims=True))
            closed = into_lane(closed, h, jnp.sum(one_head(xq, h), axis=1, keepdims=True))
            skips = into_lane(skips, h, jnp.sum(one_head(gx, h), axis=1, keepdims=True))
            half = slice(h % 2 * HEAD, (h % 2 + 1) * HEAD)
            chained = into_lane(chained, h, jnp.sum(kept[half], axis=0, keepdims=True))
    decay = jnp.where(last_begin < first_row, jnp.exp(last), 0.0)
    ended = closed * to_end
    grad_cum = lane_sum[...] - from_cols * dt + entered * enter - ended
    at_last = jnp.sum(ended, axis=0, keepdims=True) + decay * chained
    grad_cum = grad_cum + jnp.where(row_ids == rows - 1, at_last, 0.0)
    upper = (iota((rows, rows), 0) <= iota((rows, rows), 1)).astype(F32)
    grad_log = jnp.dot(upper, grad_cum, precision=HIGHEST, preferred_element_type=F32)
    rate = params_ref[1:2, :]
    grad_dt = from_cols + closed * leave + grad_log * rate
    grad_raw = grad_dt * jax.nn.sigmoid(pre_ref[:, at_dt : at_dt + LANES] + params_ref[0:1, :])
    grad_raw = jnp.where(iota((rows, LANES), 1) < heads, grad_raw, 0.0)
    gdt_ref[...] = grad_raw.astype(B16)
    small_out[0:1, :] = jnp.sum(grad_log * dt, axis=0, keepdims=True) * rate
    small_out[1:2, :] = jnp.sum(grad_raw, axis=0, keepdims=True)
    small_out[2:3, :] = skips
    small_out[3:8, :] = jnp.zeros((5, LANES), F32)
    ext[0:8, :] = rim_ref[...]
    ext[8 : 8 + rows, :] = pre_ref[:, at_x:at_dt]
    gext[...] = jnp.zeros_like(gext)
    taps_out[...] = jnp.zeros_like(taps_out)
    for i in range(0, rows, TILE):
        r = slice(i, i + TILE)
        u = u_ref[r, :]
        du = dxb[r, :] * silu_slope(u, jax.nn.sigmoid(u))
        for tap in range(CONV):
            seen = row_ids[r] - (CONV - 1) + tap >= local[r]
            part = jnp.where(seen, du, 0.0)
            taps_out[tap : tap + 1, :] += jnp.sum(part * tap_window(ext, tap, i, TILE, places), axis=0, keepdims=True)
            at = 8 - (CONV - 1) + tap + i
            gext[at : at + TILE, :] += part * taps_ref[tap : tap + 1, :]
    rim_out[...] = gext[0:8, :]
    gx_ref[...] = gext[8:, :]


def span_back(places, begins, back, pre, rim, u, cum, state, states, grads, taps, params, heads, at_z, at_x, at_dt, nstate):
    rows = u.shape[0]
    cols = heads * HEAD
    wide = at_dt - at_x
    return call(
        functools.partial(back_kernel, heads=heads, at_z=at_z, at_x=at_x, at_dt=at_dt, nstate=nstate),
        "span_back",
        (places, begins, back, pre, rim, u, cum, state, states, grads, taps, params),
        (((rows, wide), F32), ((rows, LANES), B16), ((8, wide), F32), ((8, wide), F32), ((8, LANES), F32)),
        (((rows + 8, wide), F32), ((rows + 8, wide), F32), ((rows, wide), B16), ((rows, cols), B16),
         ((cols, nstate), F32), ((rows, wide), F32), ((rows, LANES), F32), ((8, rows), F32)),
    )


def shards(
    x_in,
    lengths,
    norm1_gain,
    w_mix_in,
    w_dt,
    w_shared,
    conv_x,
    conv_bc,
    a_log,
    dt_bias,
    d_skip,
    gate_gain,
    w_out,
    norm2_gain,
    w_gate,
    w_up,
    w_down,
    d_out,
):
    tok_rows = x_in.shape[0]
    groups = lax.axis_size("branch")
    branch_id = lax.axis_index("branch")
    seq_id = lax.axis_index("seq")
    seq_rows = tok_rows * groups
    group_first = seq_id * seq_rows
    att_heads = HEADS_ATT // groups
    att_cols = att_heads * HEAD
    ssm_heads = w_dt.shape[1]
    ssm_cols = ssm_heads * HEAD
    kv_cols = KV * HEAD
    rim_rows = CONV - 1
    att_all = HEADS_ATT * HEAD
    f32 = jnp.float32
    bf16 = jnp.bfloat16
    dim = x_in.shape[1]
    parts = lax.axis_size("seq")
    chunk = w_out.shape[0] // groups
    att_chunks = parts * att_cols // (att_cols + ssm_cols)
    ssm_chunks = parts - att_chunks
    strip = dim // (groups * parts)
    hidden_all = w_gate.shape[1]
    hidden_a = hidden_all * att_cols // ((att_cols + ssm_cols) * groups)
    hidden_s = hidden_all // groups - hidden_a
    hidden_b = hidden_a + hidden_s

    def spot(c):
        first = groups * att_chunks
        if c < first:
            return (c // att_chunks) * parts + c % att_chunks
        return ((c - first) // ssm_chunks) * parts + att_chunks + (c - first) % ssm_chunks

    to_heads = [((c % groups) * parts + c // groups, spot(c)) for c in range(groups * parts)]
    from_heads = [(spot(c), c) for c in range(groups * parts)]

    def branch_sum(part):
        total = part
        for k in range(1, groups):
            route = [(i, (i + k) % groups) for i in range(groups)]
            total = total + lax.ppermute(part, "branch", route)
        return total

    def branch_gather(part):
        copies = jnp.broadcast_to(part[None], (groups,) + part.shape)
        return lax.all_to_all(copies, "branch", 0, 0, tiled=True).reshape(
            (groups * part.shape[0],) + part.shape[1:]
        )

    def branch_scatter(terms):
        blocks = terms.astype(bf16).reshape((groups, -1) + terms.shape[1:])
        return jnp.sum(lax.all_to_all(blocks, "branch", 0, 0, tiled=True).astype(f32), axis=0)

    kv_head = branch_id * att_heads // (HEADS_ATT // KV)
    dt_pad = 128
    w1_part = jnp.concatenate(
        [
            w_mix_in[:, :att_cols],
            lax.dynamic_slice_in_dim(w_shared, kv_head * HEAD, HEAD, 1),
            lax.dynamic_slice_in_dim(w_shared, kv_cols + kv_head * HEAD, HEAD, 1),
            w_mix_in[:, att_cols:],
            w_shared[:, 2 * kv_cols :],
            jnp.pad(w_dt, ((0, 0), (0, dt_pad - ssm_heads))),
        ],
        axis=1,
    )
    w1 = lax.all_gather(w1_part, "seq", axis=0, tiled=True)

    def own_columns(w):
        return [
            lax.dynamic_slice_in_dim(w, branch_id * hidden_a, hidden_a, 1),
            lax.dynamic_slice_in_dim(w, groups * hidden_a + branch_id * hidden_s, hidden_s, 1),
        ]

    row_part = jnp.concatenate(
        [
            lax.dynamic_slice_in_dim(w_out, branch_id * chunk, chunk, 0),
            lax.dynamic_slice_in_dim(w_down, branch_id * chunk, chunk, 0),
        ],
        axis=0,
    )
    row_part = lax.ppermute(row_part, ("branch", "seq"), to_heads)
    w2_part = jnp.concatenate(
        [row_part, jnp.concatenate(own_columns(w_gate) + own_columns(w_up), axis=1)], axis=0
    )
    w2 = lax.all_gather(w2_part, "seq", axis=0)
    w_out_b = w2[:, :chunk].reshape(parts * chunk, dim)
    w_down_b = w2[:, chunk : 2 * chunk].reshape(parts * chunk, dim)
    w_gu = w2[:, 2 * chunk :].reshape(dim, 2 * hidden_b)
    x_rows = x_in.astype(f32)
    scaled1, inverse1 = rms_parts(x_rows)
    normed1 = (scaled1 * norm1_gain).astype(bf16)
    group_in = branch_gather(normed1)
    d_out_g = branch_gather(d_out)
    row_ids = group_first + jnp.arange(seq_rows, dtype=jnp.int32)
    seq_ends = jnp.cumsum(lengths)

    def begin_of(ids):
        return jnp.max(jnp.where(seq_ends <= ids[..., None], seq_ends, 0), axis=-1)

    def end_of(ids):
        return jnp.min(jnp.where(seq_ends > ids[..., None], seq_ends, seq_rows * parts), axis=-1)

    begins = begin_of(row_ids)
    ends = end_of(row_ids)
    position = row_ids - begins
    row_last = group_first + seq_rows - 1
    begin_first, begin_last = (begin_of(group_first), begin_of(row_last))
    end_first, end_last = (end_of(group_first), end_of(row_last))
    here = seq_id
    query_lo = begin_first // seq_rows
    query_clear = jnp.minimum(jnp.maximum(query_lo, -(-begin_last // seq_rows)), here)
    query_bounds = jnp.stack([query_lo, query_clear, group_first, here, here + 1])
    key_hi = -(-end_last // seq_rows)
    key_clear = jnp.maximum(here + 1, jnp.minimum(end_first // seq_rows, key_hi))
    key_bounds = jnp.stack([here, here + 1, group_first, key_clear, key_hi])
    places = jnp.stack([group_first, begin_last, seq_id])
    begins_col, begins_row, ends_col = (begins[:, None], begins[None, :], ends[:, None])
    pre = jnp.dot(group_in, w1, preferred_element_type=f32)
    at_k = att_cols
    at_z = at_k + 2 * HEAD
    at_x = at_z + ssm_cols
    at_bc = at_x + ssm_cols
    at_dt = at_bc + w_shared.shape[1] - 2 * kv_cols
    q_raw = pre[:, :at_k]
    side_pre = pre[:, at_k:at_z]
    queries = rotate(q_raw.reshape(seq_rows, att_heads, HEAD), position, 1.0).astype(bf16)
    queries = (queries * SCORE_SCALE).astype(bf16).reshape(seq_rows, att_cols)
    keys_rot = (
        rotate(side_pre[:, :HEAD].reshape(seq_rows, 1, HEAD), position, 1.0)
        .reshape(seq_rows, HEAD)
        .astype(bf16)
    )
    kv_own = jnp.concatenate([keys_rot, side_pre[:, HEAD:].astype(bf16)], axis=1)
    kv_all = lax.all_gather(kv_own, "seq", axis=0, tiled=True)
    nstate = conv_bc.shape[1] // 2
    rim = from_behind(pre[seq_rows - 8 :, at_x:at_dt], "seq", 1)
    taps = jnp.pad(jnp.concatenate([conv_x, conv_bc], axis=1), ((0, 8 - CONV), (0, 0)))
    rate = -jnp.exp(a_log)
    params = jnp.pad(jnp.stack([dt_bias, rate, d_skip]), ((0, 5), (0, LANES - ssm_heads)))
    u, intra, cum, state = span_forward(
        places, begins_col, pre, rim, taps, params, ssm_heads, at_x, at_dt, nstate
    )
    states = lax.all_gather(state, "seq", axis=0)
    attn_out, lse = attend(queries, kv_all, begins_row, query_bounds, att_heads, seq_rows)
    gated_b, gated_v, state_in, squares = span_finish(
        places, begins_col, states, u, intra, cum, pre, params, ssm_heads, at_z, nstate
    )

    def pack(values, columns):
        high = columns.astype(bf16)
        low = (columns - high.astype(f32)).astype(bf16)
        extra = jnp.zeros((seq_rows, LANES - HEAD - 2), bf16)
        pieces = []
        for h in range(att_heads):
            pieces += [values[:, h * HEAD : (h + 1) * HEAD], high[:, h : h + 1], low[:, h : h + 1], extra]
        return jnp.concatenate(pieces, axis=1)

    q_pack = pack(queries, lse[:att_heads].T)
    q_all = lax.all_gather(q_pack, "seq", axis=0, tiled=True)
    gated_r = gated_b.astype(f32)
    gain_b = lax.dynamic_slice_in_dim(gate_gain, branch_id * ssm_cols, ssm_cols, 0)
    ssm_all = gate_gain.shape[0]
    squares = branch_sum(squares[0])
    inverse_g = lax.rsqrt(squares / ssm_all + EPSILON)[:, None]
    scaled_g = gated_r * inverse_g
    mixed_out = jnp.concatenate([attn_out, (scaled_g * gain_b).astype(bf16)], axis=1)
    projected = branch_scatter(jnp.dot(mixed_out, w_out_b, preferred_element_type=f32))
    middle = x_rows + projected
    scaled2, inverse2 = rms_parts(middle)
    normed2 = branch_gather((scaled2 * norm2_gain).astype(bf16))
    gate_up = jnp.dot(normed2, w_gu, preferred_element_type=f32)
    gate_val = gate_up[:, :hidden_b]
    up_val = gate_up[:, hidden_b:]
    sig_gate = jax.nn.sigmoid(gate_val)
    silu_gate = gate_val * sig_gate
    hidden = (silu_gate * up_val).astype(bf16)
    grad_hidden = lax.dot_general(
        d_out_g, w_down_b, (((1,), (1,)), ((), ())), preferred_element_type=f32
    )
    grad_gate = (grad_hidden * up_val * sig_gate * (1.0 + gate_val * (1.0 - sig_gate))).astype(bf16)
    grad_up = (grad_hidden * silu_gate).astype(bf16)
    grad_gu = jnp.concatenate([grad_gate, grad_up], axis=1)
    grad_normed2 = branch_scatter(
        lax.dot_general(grad_gu, w_gu, (((1,), (1,)), ((), ())), preferred_element_type=f32)
    )
    y_out = (
        middle + branch_scatter(jnp.dot(hidden, w_down_b, preferred_element_type=f32))
    ).astype(bf16)
    grad_middle, grad_n2 = rms_backward(grad_normed2, scaled2, inverse2, norm2_gain)
    grad_middle = grad_middle + d_out.astype(f32)
    grad_proj = branch_gather(grad_middle.astype(bf16))
    grad_mixed = lax.dot_general(
        grad_proj, w_out_b, (((1,), (1,)), ((), ())), preferred_element_type=f32
    )
    back_att = grad_mixed[:, :att_cols].astype(bf16)
    grad_gnormed = grad_mixed[:, att_cols:]
    grad_scaled = grad_gnormed * gain_b
    mean_g = branch_sum(jnp.sum(grad_scaled * scaled_g, axis=1))[:, None] / ssm_all
    back_ssm = (inverse_g * (grad_scaled - scaled_g * mean_g)).astype(bf16)
    grad_gate_gain = jnp.sum(grad_gnormed * scaled_g, axis=0)

    def over_rows(left, right):
        return lax.dot_general(
            left, right, (((0,), (0,)), ((), ())), preferred_element_type=f32
        ).astype(bf16)

    def strips(rows_all):
        wide = rows_all.reshape((groups, parts, strip) + rows_all.shape[1:])
        return jnp.swapaxes(wide, 0, 1).reshape((parts, groups * strip) + rows_all.shape[1:])

    terms2 = jnp.concatenate(
        [
            over_rows(mixed_out, grad_proj).reshape(parts, chunk, dim),
            over_rows(hidden, d_out_g).reshape(parts, chunk, dim),
            strips(over_rows(normed2, grad_gu)),
        ],
        axis=1,
    )
    own2 = lax.psum_scatter(terms2, "seq", scatter_dimension=0)
    own_rows = lax.ppermute(own2[: 2 * chunk], ("branch", "seq"), from_heads).astype(f32)
    grad_w_out = own_rows[:chunk]
    grad_w_down = own_rows[chunk:]
    own_gu = lax.all_to_all(
        own2[2 * chunk :].reshape(groups, strip, 2 * hidden_b), "branch", 0, 0, tiled=True
    ).astype(f32)

    def all_columns(blocks):
        blocks = jnp.swapaxes(blocks, 0, 1)
        return jnp.concatenate(
            [blocks[:, :, :hidden_a].reshape(strip, -1), blocks[:, :, hidden_a:].reshape(strip, -1)],
            axis=1,
        )

    grad_w_gate = all_columns(own_gu[:, :, :hidden_b])
    grad_w_up = all_columns(own_gu[:, :, hidden_b:])
    grad_z, grad_state = gate_back(
        places, begins_col, back_ssm, u, cum, pre, gated_v, ssm_heads, at_z, nstate
    )
    grad_states = lax.all_gather(grad_state, "seq", axis=0)
    delta = jnp.sum(
        (back_att.astype(f32) * attn_out.astype(f32)).reshape(seq_rows, att_heads, HEAD), axis=-1
    )
    g_pack = pack(back_att, delta)
    g_all = lax.all_gather(g_pack, "seq", axis=0, tiled=True)
    grad_q = query_grad(q_pack, g_pack, kv_all, begins_col, query_bounds, att_heads, seq_rows)
    grad_xbc, grad_dt, rim_back, grad_taps, grad_small = span_back(
        places,
        begins_col,
        back_ssm,
        pre,
        rim,
        u,
        cum,
        state_in,
        states,
        grad_states,
        taps,
        params,
        ssm_heads,
        at_z,
        at_x,
        at_dt,
        nstate,
    )
    rim_back = from_behind(rim_back, "seq", -1)
    grad_xbc = grad_xbc.at[seq_rows - 8 :].add(rim_back)
    grad_kv = key_grad(kv_own, q_all, g_all, ends_col, key_bounds, att_heads, seq_rows)
    grad_q_raw = rotate(grad_q.reshape(seq_rows, att_heads, HEAD), position, -1.0)
    grad_k_raw = rotate(grad_kv[:, :HEAD].reshape(seq_rows, 1, HEAD), position, -1.0)
    grad_conv_x, grad_conv_bc = (grad_taps[:CONV, :ssm_cols], grad_taps[:CONV, ssm_cols:])
    pad_cols = dt_pad - ssm_heads
    grad_pre = jnp.concatenate(
        [
            grad_q_raw.reshape(seq_rows, att_cols).astype(bf16),
            grad_k_raw.reshape(seq_rows, HEAD).astype(bf16),
            grad_kv[:, HEAD:].astype(bf16),
            grad_z,
            grad_xbc.astype(bf16),
            grad_dt,
        ],
        axis=1,
    )
    grad_group = lax.dot_general(
        grad_pre, w1, (((1,), (1,)), ((), ())), preferred_element_type=f32
    )
    grad_n1 = jnp.sum(grad_group * group_in.astype(f32), axis=0) / norm1_gain
    grad_w1 = over_rows(group_in, grad_pre)
    tall = groups * strip

    def to_column(vector, rows_each):
        padded = jnp.pad(vector.reshape(parts, rows_each), ((0, 0), (0, tall - rows_each)))
        return padded[:, :, None]

    def to_columns(matrix, rows_each):
        wide = jnp.swapaxes(matrix.reshape(matrix.shape[0], parts, rows_each), 0, 1)
        wide = jnp.pad(wide, ((0, 0), (0, 0), (0, tall - rows_each)))
        return jnp.swapaxes(wide, 1, 2)

    bc_each = conv_bc.shape[1] // (groups * parts)
    x_each = ssm_cols // parts
    bc_wide = grad_conv_bc.reshape(CONV, groups, parts, bc_each)
    bc_wide = jnp.pad(bc_wide, ((0, 0), (0, 0), (0, 0), (0, strip - bc_each)))
    bc_wide = jnp.transpose(bc_wide, (2, 1, 3, 0)).reshape(parts, tall, CONV)
    heads3 = grad_small[:3, :ssm_heads].reshape(3 * ssm_heads)
    heads3 = jnp.broadcast_to(heads3[None, None, :], (parts, tall, 3 * ssm_heads))
    small = jnp.concatenate(
        [
            strips(jnp.stack([grad_n1, grad_n2], axis=1)),
            bc_wide,
            to_column(grad_gate_gain, x_each),
            to_columns(grad_conv_x, x_each),
            heads3,
        ],
        axis=2,
    )
    small = jnp.pad(small, ((0, 0), (0, 0), (0, pad_cols - small.shape[2]))).astype(bf16)

    def plain(rows_all):
        return rows_all.reshape(parts, tall, rows_all.shape[1])

    terms1 = jnp.concatenate(
        [
            plain(grad_w1[:, :at_k]),
            strips(grad_w1[:, at_k:at_z]),
            plain(grad_w1[:, at_z:at_bc]),
            strips(grad_w1[:, at_bc:at_dt]),
            plain(grad_w1[:, at_dt : at_dt + ssm_heads]),
            small,
        ],
        axis=2,
    )
    grad_normed1 = branch_scatter(grad_group)
    own1 = lax.psum_scatter(terms1, "seq", scatter_dimension=0)
    at_s = at_dt + ssm_heads
    own_f = own1.astype(f32)
    grad_mix = jnp.concatenate([own_f[:, :at_k], own_f[:, at_z:at_bc]], axis=1)
    grad_dt_w = own_f[:, at_dt:at_s]
    shared_part = jnp.concatenate(
        [own1[:, at_k:at_z], own1[:, at_bc:at_dt], own1[:, at_s : at_s + 2 + CONV]], axis=1
    ).reshape(groups, strip, -1)
    blocks = lax.all_to_all(shared_part, "branch", 0, 0, tiled=True).astype(f32)
    per_kv = groups // KV
    bc_cols = at_dt - at_bc
    grad_shared = jnp.concatenate(
        [
            jnp.sum(blocks[h * per_kv : (h + 1) * per_kv, :, at : at + HEAD], axis=0)
            for at in (0, HEAD)
            for h in range(KV)
        ]
        + [jnp.sum(blocks[:, :, 2 * HEAD : 2 * HEAD + bc_cols], axis=0)],
        axis=1,
    )
    gains = jnp.sum(blocks[:, :, 2 * HEAD + bc_cols :], axis=0)
    at_g = at_s + 2 + CONV
    grad_gain_g = own_f[:x_each, at_g]
    grad_cx = own_f[:x_each, at_g + 1 : at_g + 1 + CONV].T
    at_h = at_g + 1 + CONV
    grad_x1, unused_n1 = rms_backward(grad_normed1, scaled1, inverse1, norm1_gain)
    return (
        y_out,
        grad_middle + grad_x1,
        gains[:, 0],
        grad_mix,
        grad_dt_w,
        grad_shared,
        grad_cx,
        gains[:bc_each, 2:].T,
        own_f[0, at_h : at_h + ssm_heads],
        own_f[0, at_h + ssm_heads : at_h + 2 * ssm_heads],
        own_f[0, at_h + 2 * ssm_heads : at_h + 3 * ssm_heads],
        grad_gain_g,
        grad_w_out,
        gains[:, 1],
        grad_w_gate,
        grad_w_up,
        grad_w_down,
    )


def solution(mesh):
    in_specs = (
        P(("seq", "branch"), None),
        P(),
        P(),
        P("seq", "branch"),
        P("seq", "branch"),
        P("seq", None),
        P(None, "branch"),
        P(),
        P("branch"),
        P("branch"),
        P("branch"),
        P(),
        P("seq", None),
        P(),
        P("seq", None),
        P("seq", None),
        P("seq", None),
        P(("seq", "branch"), None),
    )
    out_specs = (
        P(("seq", "branch"), None),
        P(("seq", "branch"), None),
        P(("branch", "seq")),
        P("seq", "branch"),
        P("seq", "branch"),
        P(("branch", "seq"), None),
        P(None, ("branch", "seq")),
        P(None, ("branch", "seq")),
        P("branch"),
        P("branch"),
        P("branch"),
        P(("branch", "seq")),
        P(("branch", "seq"), None),
        P(("branch", "seq")),
        P(("branch", "seq"), None),
        P(("branch", "seq"), None),
        P(("branch", "seq"), None),
    )
    return jax.shard_map(shards, mesh=mesh, in_specs=in_specs, out_specs=out_specs, check_vma=False)
```

```python
import functools

import jax
import jax.numpy as jnp
from jax import lax
from jax.experimental import pallas as pl
from jax.experimental.pallas import tpu as pltpu
from jax.sharding import PartitionSpec as P

HEADS_ATT = 8
KV = 2
HEAD = 64
CONV = 4
LANES = 128
TILE = 128
MASKED = -1e30
HIGHEST = lax.Precision.HIGHEST
EPSILON = 1e-06
SCORE_SCALE = 0.125
ROPE_BASE = 1000000.0
F32 = jnp.float32
B16 = jnp.bfloat16
LANE_DOT = (((1,), (1,)), ((), ()))
ROW_DOT = (((0,), (0,)), ((), ()))


VMEM_SPEC = pl.BlockSpec(memory_space=pltpu.VMEM)
SMEM_SPEC = pl.BlockSpec(memory_space=pltpu.SMEM)
ANY_SPEC = pl.BlockSpec(memory_space=pl.ANY)


def from_behind(block, axis, distance):
    devices = range(lax.axis_size(axis))
    route = [(i - distance, i) for i in devices if i - distance in devices]
    return lax.ppermute(block, axis, route)


def rms_parts(value):
    inverse = lax.rsqrt(jnp.mean(value * value, axis=-1, keepdims=True) + EPSILON)
    return (value * inverse, inverse)


def rms_backward(grad_out, scaled, inverse, gain_vec):
    grad_scaled = grad_out * gain_vec
    grad_in = inverse * (
        grad_scaled - scaled * jnp.mean(grad_scaled * scaled, axis=-1, keepdims=True)
    )
    return (grad_in, jnp.sum(grad_out * scaled, axis=0))


def rotate_tables(position):
    half = HEAD // 2
    inverse = ROPE_BASE ** (-jnp.arange(half, dtype=jnp.float32) / half)
    angles = position.astype(jnp.float32)[:, None] * inverse[None, :]
    cosine, sine = (jnp.cos(angles), jnp.sin(angles))
    return (
        jnp.concatenate([cosine] * (LANES // half), axis=1),
        jnp.concatenate([-sine, sine] * (LANES // HEAD), axis=1),
    )


def swap_halves(values):
    half = HEAD // 2
    lane = lax.broadcasted_iota(jnp.int32, values.shape, 1)
    return jnp.where(
        lane % HEAD < half, pltpu.roll(values, LANES - half, 1), pltpu.roll(values, half, 1)
    )


def call(kernel, name, micros, args, outs, scratch, waits=()):
    given, held = (len(args), len(waits))

    def body(*refs):
        kernel(*refs[:given], *refs[given + held :])

    result = pl.pallas_call(
        body,
        out_shape=tuple(jax.ShapeDtypeStruct(s, d) for s, d in outs),
        in_specs=[SMEM_SPEC] + [VMEM_SPEC] * (given - 1) + [ANY_SPEC] * held,
        out_specs=tuple(VMEM_SPEC for _ in outs),
        scratch_shapes=[pltpu.VMEM(s, d) for s, d in scratch],
        compiler_params=pltpu.CompilerParams(vmem_limit_bytes=56 << 20),
        cost_estimate=pl.CostEstimate(
            flops=micros * 1000000, bytes_accessed=micros * 3600000, transcendentals=micros * 100000
        ),
        name=name,
    )(*args, *waits)
    return result


def extra_rows(values, heads):
    pieces = []
    for h in range(heads):
        row = values[h : h + 1, :]
        high = row.astype(B16).astype(F32)
        for part in (high, row - high):
            pieces += [part[:, at : at + LANES] for at in range(0, row.shape[1], LANES)]
    return jnp.concatenate(pieces, axis=0)


def extra_row(rows, head, count):
    at = 2 * head * count
    high = jnp.concatenate([rows[at + n : at + n + 1] for n in range(count)], axis=1)
    low = jnp.concatenate([rows[at + count + n : at + count + n + 1] for n in range(count)], axis=1)
    return high + low


def attend_kernel(
    bounds, begin_ref, own_ref, all_ref, out_ref, lse_ref, send_ref, top, acc, *, heads, keys
):
    rows = own_ref.shape[0]
    top[...] = jnp.full_like(top, MASKED)
    acc[...] = jnp.zeros_like(acc)
    row_ids = bounds[2] + iota((1, rows), 1)
    begins = begin_ref[...]
    ones = (iota((keys, HEAD), 1) == 0).astype(B16)

    def step(n, masked):
        at = n * keys
        kv = all_ref[pl.ds(pl.multiple_of(at, keys), keys), :]
        k = kv[:, :HEAD]
        v = jnp.concatenate([kv[:, HEAD:], ones], axis=1).T
        if masked:
            key_ids = at + iota((keys, rows), 0)
            seen = (key_ids <= row_ids) & (key_ids >= begins)
        for h in range(heads):
            q = own_ref[:, h * HEAD : (h + 1) * HEAD]
            s = lax.dot_general(k, q, LANE_DOT, preferred_element_type=F32)
            if masked:
                s = jnp.where(seen, s, MASKED)
            old = top[h : h + 1, :]
            new = jnp.maximum(old, jnp.max(s, axis=0, keepdims=True))
            p = jnp.exp(s - new).astype(B16)
            scale = jnp.exp(old - new)
            add = jnp.dot(v, p, preferred_element_type=F32)
            acc[h] = acc[h] * scale + add
            top[h : h + 1, :] = new

    pl.loop(bounds[0], bounds[1])(lambda n: step(n, True))
    pl.loop(bounds[1], bounds[3])(lambda n: step(n, False))
    pl.loop(bounds[3], bounds[4])(lambda n: step(n, True))
    for h in range(heads):
        total = acc[h, HEAD : HEAD + 1, :]
        out_ref[:, h * HEAD : (h + 1) * HEAD] = (acc[h, :HEAD, :] / total).T.astype(B16)
        lse_ref[h : h + 1, :] = top[h : h + 1, :] + jnp.log(total)
    send_ref[:rows, :] = own_ref[...]
    send_ref[rows:, :] = extra_rows(lse_ref[...], heads).astype(B16)


def attend(own, everything, begins, bounds, heads, keys):
    rows = own.shape[0]
    return call(
        functools.partial(attend_kernel, heads=heads, keys=keys),
        "attend",
        12,
        (bounds, begins, own, everything),
        (((rows, heads * HEAD), B16), ((8, rows), F32), ((rows + 2 * heads * rows // LANES, LANES), B16)),
        (((8, rows), F32), ((heads, LANES, rows), F32)),
    )


def minus_ones(lane, base, first):
    at = base + first
    return jnp.where((lane == at) | (lane == at + 1), -1.0, 0.0).astype(B16)


def key_sides(kv, heads):
    turned = jnp.concatenate([kv[:, HEAD:], kv[:, :HEAD]], axis=1)
    lane = iota(kv.shape, 1)
    zero = jnp.zeros_like(kv)
    sides = []
    for h in range(heads):
        mine = lane < HEAD if h == 0 else lane >= HEAD
        base = HEAD * (1 - h)
        keys_h = jnp.where(mine, kv if h == 0 else turned, zero)
        values_h = jnp.where(mine, turned if h == 0 else kv, minus_ones(lane, base, 0))
        both = jnp.concatenate([keys_h, minus_ones(lane, base, 2)], axis=1)
        sides.append((keys_h, values_h, both))
    return sides


def query_grad_kernel(
    bounds, begin_ref, own_ref, g_ref, all_ref, out_ref, acc, *, heads, keys
):
    rows = own_ref.shape[0]
    acc[...] = jnp.zeros_like(acc)
    row_ids = bounds[2] + iota((rows, keys), 0)
    begins = begin_ref[...]

    def step(n, masked):
        at = n * keys
        kv = all_ref[pl.ds(pl.multiple_of(at, keys), keys), :]
        sides = key_sides(kv, heads)
        if masked:
            key_ids = at + iota((rows, keys), 1)
            seen = (key_ids <= row_ids) & (key_ids >= begins)
        total = acc[...]
        for h in range(heads):
            k, v, both = sides[h]
            g = g_ref[:, h * LANES : (h + 1) * LANES]
            q = jnp.concatenate([own_ref[...], g], axis=1)
            s = lax.dot_general(q, both, LANE_DOT, preferred_element_type=F32)
            if masked:
                s = jnp.where(seen, s, MASKED)
            gp = lax.dot_general(g, v, LANE_DOT, preferred_element_type=F32)
            ds = (jnp.exp(s) * gp).astype(B16)
            total = total + jnp.dot(ds, k, preferred_element_type=F32)
        acc[...] = total

    pl.loop(bounds[0], bounds[1])(lambda n: step(n, True))
    pl.loop(bounds[1], bounds[3])(lambda n: step(n, False))
    pl.loop(bounds[3], bounds[4])(lambda n: step(n, True))
    out_ref[...] = acc[...] * SCORE_SCALE


def query_grad(own, g_pack, everything, begins, bounds, heads, keys, waits):
    rows = own.shape[0]
    return call(
        functools.partial(query_grad_kernel, heads=heads, keys=keys),
        "query_grad",
        11,
        (bounds, begins, own, g_pack, everything),
        (((rows, LANES), F32),),
        (((rows, LANES), F32),),
        waits,
    )[0]


def key_grad_kernel(
    bounds, end_ref, own_ref, all_ref, g_ref, out_ref, acc_k, acc_v, *, heads, keys, at_g
):
    rows = own_ref.shape[0]
    acc_k[...] = jnp.zeros_like(acc_k)
    acc_v[...] = jnp.zeros_like(acc_v)
    key_ids = bounds[2] + iota((rows, keys), 0)
    ends = end_ref[...]
    kv = own_ref[...]
    turned = jnp.concatenate([kv[:, HEAD:], kv[:, :HEAD]], axis=1)
    first = iota(kv.shape, 1) < HEAD
    zero = jnp.zeros_like(kv)
    count = keys // LANES

    def step(n, masked):
        at = n * keys
        if masked:
            row_ids = at + iota((rows, keys), 1)
            seen = (key_ids <= row_ids) & (row_ids < ends)
        q = all_ref[n, :keys, :]
        g = g_ref[n, at_g : at_g + keys, :]
        lse_rows = all_ref[n, keys:, :].astype(F32)
        delta_rows = g_ref[n, at_g + keys :, :].astype(F32)
        for h in range(heads):
            mine = first if h == 0 else jnp.logical_not(first)
            k = jnp.where(mine, kv if h == 0 else turned, zero)
            v = jnp.where(mine, turned if h == 0 else kv, zero)
            s = lax.dot_general(k, q, LANE_DOT, preferred_element_type=F32)
            s = s - extra_row(lse_rows, h, count)
            if masked:
                s = jnp.where(seen, s, MASKED)
            p = jnp.exp(s)
            gp = lax.dot_general(v, g, LANE_DOT, preferred_element_type=F32)
            ds = (p * (gp - extra_row(delta_rows, h, count))).astype(B16)
            acc_k[h] += jnp.dot(ds, q, preferred_element_type=F32)
            acc_v[h] += jnp.dot(p.astype(B16), g, preferred_element_type=F32)

    pl.loop(bounds[0], bounds[1])(lambda n: step(n, True))
    pl.loop(bounds[1], bounds[3])(lambda n: step(n, False))
    pl.loop(bounds[3], bounds[4])(lambda n: step(n, True))
    out_ref[:, :HEAD] = acc_k[0, :, :HEAD] + acc_k[1, :, HEAD:]
    out_ref[:, HEAD:] = acc_v[0, :, :HEAD] + acc_v[1, :, HEAD:]


def key_grad(own, everything, g_all, at_g, ends, bounds, heads, keys, waits):
    rows = own.shape[0]
    return call(
        functools.partial(key_grad_kernel, heads=heads, keys=keys, at_g=at_g),
        "key_grad",
        12,
        (bounds, ends, own, everything, g_all),
        (((rows, LANES), F32),),
        (((heads, rows, LANES), F32), ((heads, rows, LANES), F32)),
        waits,
    )[0]


def assemble_kernel(picks, mix_ref, shared_ref, dt_ref, out_ref, *, att_cols, turned):
    kv_cols = KV * HEAD
    wide = mix_ref.shape[1]
    first = picks[0] == 0
    at = att_cols
    out_ref[:, :at] = mix_ref[:, :at]
    for part in range(2):
        tile = shared_ref[:, part * kv_cols : (part + 1) * kv_cols]
        out_ref[:, at : at + HEAD] = jnp.where(first, tile[:, :HEAD], tile[:, HEAD:])
        at += HEAD
    out_ref[:, at : at + wide - att_cols] = mix_ref[:, att_cols:]
    at += wide - att_cols
    out_ref[:, at : at + shared_ref.shape[1] - 2 * kv_cols] = shared_ref[:, 2 * kv_cols :]
    at += shared_ref.shape[1] - 2 * kv_cols
    if turned:
        heads, rows = dt_ref.shape
        steps = jnp.concatenate([dt_ref[...].astype(F32), jnp.zeros((LANES - heads, rows), F32)], axis=0)
        out_ref[:, at:] = steps.T.astype(B16)
    else:
        out_ref[:, at:] = jnp.zeros((out_ref.shape[0], LANES), B16)
        out_ref[:, at : at + dt_ref.shape[1]] = dt_ref[...]


def project_kernel(
    places, both_ref, before_ref, w_ref, cos_ref, sin_ref, q_ref, kv_ref, z_ref, pre_ref, rim_ref
):
    rows = both_ref.shape[0]
    dim = w_ref.shape[0]
    at_z = 2 * LANES
    at_x = at_z + z_ref.shape[1]
    step = 2 * TILE
    for i in range(0, rows, step):
        r = slice(i, i + step)
        x = both_ref[r, :dim]
        t = jnp.dot(x, w_ref[:, :at_z], preferred_element_type=F32)
        cosine, sine = cos_ref[r, :], sin_ref[r, :]
        q, kv = t[:, :LANES], t[:, LANES:]
        q = (q * cosine + swap_halves(q) * sine).astype(B16)
        q_ref[r, :] = (q.astype(F32) * SCORE_SCALE).astype(B16)
        turned = kv * cosine + swap_halves(kv) * sine
        kv_ref[r, :] = jnp.where(iota(kv.shape, 1) < HEAD, turned, kv).astype(B16)
        z_ref[r, :] = jnp.dot(x, w_ref[:, at_z:at_x], preferred_element_type=F32)
        pre_ref[r, :] = jnp.dot(x, w_ref[:, at_x:], preferred_element_type=F32)
    wide = rim_ref.shape[1]
    rim = jnp.dot(before_ref[...], w_ref[:, at_x : at_x + wide], preferred_element_type=F32)
    rim_ref[...] = rim[before_ref.shape[0] - 8 :, :]


def mix_out_kernel(places, attn_ref, gated_ref, gain_ref, w_ref, *refs, ssm_all):
    mixed_ref, part_ref, total_ref = refs[-3:]
    rows = attn_ref.shape[0]
    att_cols = attn_ref.shape[1]
    total = refs[0][...]
    for ref in refs[1:-3]:
        total = total + ref[...]
    total_ref[...] = total
    squares = total.T
    for i in range(0, rows, TILE):
        r = slice(i, i + TILE)
        inverse = lax.rsqrt(squares[r, 0:1] / ssm_all + EPSILON)
        gnormed = (gated_ref[r, :].astype(F32) * inverse * gain_ref[...]).astype(B16)
        mixed_ref[r, :att_cols] = attn_ref[r, :]
        mixed_ref[r, att_cols:] = gnormed
    for i in range(0, rows, 2 * TILE):
        r = slice(i, i + 2 * TILE)
        part_ref[r, :] = jnp.dot(mixed_ref[r, :], w_ref[...], preferred_element_type=F32).astype(B16)


def mix_back_kernel(
    places, grad_ref, w_ref, attn_ref, lse_ref, gated_ref, squares_ref, gain_ref,
    pack_ref, send_ref, scaled_ref, stat_ref, gain_out, deltas, *, heads, ssm_all,
):
    rows = attn_ref.shape[0]
    att_cols = attn_ref.shape[1]
    squares = squares_ref[...].T
    lse = lse_ref[...].T
    total = jnp.zeros((1, gated_ref.shape[1]), F32)
    ones = jnp.ones((8, gated_ref.shape[1]), F32)
    for i in range(0, rows, TILE):
        r = slice(i, i + TILE)
        mixed = lax.dot_general(grad_ref[r, :], w_ref[...], LANE_DOT, preferred_element_type=F32)
        back = mixed[:, :att_cols].astype(B16).astype(F32)
        product = back * attn_ref[r, :].astype(F32)
        lane = iota(back.shape, 1)
        send_ref[r, :] = back.astype(B16)
        packed = jnp.zeros((TILE, LANES), F32)
        for h in range(heads):
            base = HEAD * (1 - h)
            tile = one_head(back, h)
            delta = jnp.sum(one_head(product, h), axis=1, keepdims=True)
            packed = into_lane(packed, h, delta)
            for n, column in enumerate((delta, lse[r, h : h + 1])):
                high = column.astype(B16).astype(F32)
                tile = jnp.where(lane == base + 2 * n, high, tile)
                tile = jnp.where(lane == base + 2 * n + 1, column - high, tile)
            pack_ref[r, h * LANES : (h + 1) * LANES] = tile.astype(B16)
        deltas[r, :] = packed
        grad = mixed[:, att_cols:]
        scaled = gated_ref[r, :].astype(F32) * lax.rsqrt(squares[r, 0:1] / ssm_all + EPSILON)
        grad_scaled = grad * gain_ref[...]
        scaled_ref[r, :] = grad_scaled
        stat_ref[:, r] = lax.dot_general(
            ones, grad_scaled * scaled, LANE_DOT, precision=HIGHEST, preferred_element_type=F32
        )
        total = total + jnp.sum(grad * scaled, axis=0, keepdims=True)
    gain_out[...] = jnp.broadcast_to(total, gain_out.shape)
    send_ref[rows:, :] = extra_rows(deltas[...].T, heads).astype(B16)


def rows_of(ref, first, last):
    return jnp.concatenate([ref[k, first:last, :] for k in range(ref.shape[0])], axis=0)


def mlp_kernel(places, in_ref, out_ref, *refs, chunk, groups):
    if chunk:
        all_ref, hidden_ref, weights_ref, terms_ref, gu_ref, down_ref, grad_ref = refs
        down_ref[...] = rows_of(all_ref, 0, chunk)
        gu_ref[...] = rows_of(all_ref, chunk, all_ref.shape[1])
    else:
        gu_ref, down_ref, hidden_ref, grad_ref, terms_ref = refs
    rows = in_ref.shape[0]
    half = hidden_ref.shape[1]
    dim = in_ref.shape[1]
    step = 2 * TILE
    for i in range(0, rows, step):
        r = slice(i, i + step)
        both = jnp.dot(in_ref[r, :], gu_ref[...], preferred_element_type=F32)
        back = lax.dot_general(out_ref[r, dim:], down_ref[...], LANE_DOT, preferred_element_type=F32)
        gate, up = both[:, :half], both[:, half:]
        sig = jax.nn.sigmoid(gate)
        soft = gate * sig
        hidden_ref[r, :] = (soft * up).astype(B16)
        grad_ref[r, :half] = (back * up * sig * (1.0 + gate * (1.0 - sig))).astype(B16)
        grad_ref[r, half:] = (back * soft).astype(B16)
        terms_ref[r, :] = lax.dot_general(
            grad_ref[r, :], gu_ref[...], LANE_DOT, preferred_element_type=F32
        ).astype(B16)
    if chunk:
        parts, tall = weights_ref.shape[0], weights_ref.shape[1] - chunk
        strip = tall // groups
        for i in range(0, half, step):
            down = lax.dot_general(
                hidden_ref[:, i : i + step], out_ref[:, dim:], ROW_DOT, preferred_element_type=F32
            ).astype(B16)
            for n in range(step // chunk):
                weights_ref[i // chunk + n, :chunk, :] = down[n * chunk : (n + 1) * chunk]
        for i in range(0, dim, step):
            both = lax.dot_general(
                in_ref[:, i : i + step], grad_ref[...], ROW_DOT, preferred_element_type=F32
            ).astype(B16)
            for n in range(step // strip):
                b, s = divmod(i // strip + n, parts)
                at = chunk + b * strip
                weights_ref[s, at : at + strip, :] = both[n * strip : (n + 1) * strip]


def down_kernel(places, hidden_ref, w_ref, out_ref, *, chunk):
    w = rows_of(w_ref, 0, chunk) if chunk else w_ref[...]
    out_ref[...] = jnp.dot(hidden_ref[...], w, preferred_element_type=F32).astype(B16)


def add_blocks_kernel(places, blocks_ref, middle_ref, out_ref):
    total = blocks_ref[0].astype(F32)
    for n in range(1, blocks_ref.shape[0]):
        total = total + blocks_ref[n].astype(F32)
    out_ref[...] = (middle_ref[...] + total).astype(B16)


def group_back_kernel(places, grad_ref, w_ref, early_ref, out_ref, kept_ref):
    rows = grad_ref.shape[0]
    step = 2 * TILE
    for i in range(0, rows, step):
        r = slice(i, i + step)
        out_ref[r, :] = lax.dot_general(
            grad_ref[r, :], w_ref[...], LANE_DOT, preferred_element_type=F32
        ).astype(B16)
    kept_ref[...] = early_ref[...]


def norm_back_kernel(places, blocks_ref, middle_ref, grad_ref, gain_ref, total_ref, copies_ref, gain_out):
    grad = blocks_ref[0].astype(F32)
    for n in range(1, blocks_ref.shape[0]):
        grad = grad + blocks_ref[n].astype(F32)
    middle = middle_ref[...]
    inverse = lax.rsqrt(jnp.mean(middle * middle, axis=1, keepdims=True) + EPSILON)
    scaled = middle * inverse
    grad_scaled = grad * gain_ref[...]
    mean = jnp.mean(grad_scaled * scaled, axis=1, keepdims=True)
    total = inverse * (grad_scaled - scaled * mean) + grad_ref[...].astype(F32)
    total_ref[...] = total
    for n in range(copies_ref.shape[0]):
        copies_ref[n] = total.astype(B16)
    gain_out[...] = jnp.broadcast_to(jnp.sum(grad * scaled, axis=0, keepdims=True), gain_out.shape)


def turned_rows(values):
    rows = values.shape[0]
    if rows < LANES:
        values = jnp.concatenate([values, jnp.zeros((LANES - rows, LANES), F32)], axis=0)
    return values.T


def own_kernel(places, own_ref, early_ref, mixed_ref, dt_ref, gain_ref, taps_ref, *head_refs, heads, half):
    rows = own_ref.shape[0]
    cols = early_ref.shape[1] - half
    mixed_ref[:, :LANES] = own_ref[:, :LANES].astype(F32)
    mixed_ref[:, LANES : LANES + cols] = early_ref[:, half:].astype(F32)
    mixed_ref[:, LANES + cols :] = own_ref[:, LANES : LANES + cols].astype(F32)
    tail = own_ref[:, own_ref.shape[1] - LANES :].astype(F32)
    turned = turned_rows(tail)
    at_gain = heads + 2 + CONV
    each = gain_ref.shape[1]
    dt_ref[...] = turned[:heads, :rows]
    gain_ref[...] = turned[at_gain : at_gain + 1, :each]
    taps_ref[...] = turned[at_gain + 1 : at_gain + 1 + CONV, :each]
    at = at_gain + 1 + CONV
    for n, ref in enumerate(head_refs):
        ref[...] = tail[0:1, at + n * heads : at + (n + 1) * heads]


def side_kernel(places, blocks_ref, gain_ref, shared_ref, first_ref, second_ref, taps_ref, *, heads):
    groups, strip, wide = blocks_ref.shape
    per_kv = groups // KV
    blocks = [blocks_ref[b].astype(F32) for b in range(groups)]
    sums = []
    for h in range(KV):
        total = blocks[h * per_kv][:, : 2 * HEAD]
        for b in range(h * per_kv + 1, (h + 1) * per_kv):
            total = total + blocks[b][:, : 2 * HEAD]
        sums.append(total)
    rest = blocks[0]
    for b in range(1, groups):
        rest = rest + blocks[b]
    for part in range(2):
        for h in range(KV):
            at = (part * KV + h) * HEAD
            shared_ref[:, at : at + HEAD] = sums[h][:, part * HEAD : (part + 1) * HEAD]
    shared_ref[:, 2 * KV * HEAD :] = rest[:, 2 * HEAD : wide - LANES]
    turned = turned_rows(rest[:, wide - LANES :])
    first_ref[...] = turned[heads : heads + 1, :strip] / gain_ref[...]
    second_ref[...] = turned[heads + 1 : heads + 2, :strip]
    taps_ref[...] = turned[heads + 2 : heads + 2 + CONV, : taps_ref.shape[1]]


def early_kernel(places, mixed_ref, grad_ref, both_ref, dz_ref, w_ref, terms_ref, gain_ref, *, parts):
    dim = grad_ref.shape[1]
    half = dim // 2
    rows = mixed_ref.shape[1]
    chunk = rows // parts
    tall = dim // parts
    at_z = 2 * LANES
    cols = dz_ref.shape[1]
    step = 2 * TILE
    for i in range(0, rows, step):
        out = lax.dot_general(
            mixed_ref[:, i : i + step], grad_ref[...], ROW_DOT, preferred_element_type=F32
        ).astype(B16)
        for n in range(step // chunk):
            at = (i // chunk + n) * tall
            piece = out[n * chunk : (n + 1) * chunk]
            terms_ref[at : at + chunk, :half] = piece[:, :half]
            terms_ref[at + chunk : at + tall, :half] = piece[:, half:]
    for i in range(0, dim, step):
        r = slice(i, i + step)
        grad = lax.dot_general(both_ref[:, r], dz_ref[...], ROW_DOT, preferred_element_type=F32)
        terms_ref[r, half:] = grad.astype(B16)
        gain_ref[r, :] = jnp.sum(grad * w_ref[r, at_z : at_z + cols].astype(F32), axis=1, keepdims=True)


def small_columns(tile, gain_ref, taps_ref, heads_ref, second_ref, *, heads, groups, parts):
    dim = second_ref.shape[1]
    cols = gain_ref.shape[1]
    wide = taps_ref.shape[1]
    tall = dim // parts
    strip = tall // groups
    at_gain = heads + 2 + CONV
    at = at_gain + 1 + CONV
    lane = iota((8, LANES), 1)
    values = jnp.where(lane < heads, heads_ref[...], 0.0)
    base = pltpu.roll(values, at, 1)[0:1]
    for n in (1, 2):
        base = base + pltpu.roll(values, at + n * heads, 1)[n : n + 1]
    tile[...] = jnp.broadcast_to(base, tile.shape)

    def columns(first, rows, width):
        pieces = [jnp.zeros((first, width), F32)] + rows
        left = LANES - first - sum(row.shape[0] for row in rows)
        return jnp.concatenate(pieces + [jnp.zeros((left, width), F32)], axis=0).T

    own = columns(at_gain, [gain_ref[0:1, :], taps_ref[:CONV, :cols]], cols)
    each = cols // parts
    for s in range(parts):
        tile[s * tall : s * tall + each, :] += own[s * each : (s + 1) * each]
    side = columns(heads + 2, [taps_ref[:CONV, cols:]], wide - cols)
    each = (wide - cols) // (groups * parts)
    second = columns(heads + 1, [second_ref[0:1, :]], dim)
    for b in range(groups):
        for s in range(parts):
            there = s * tall + b * strip
            n = b * parts + s
            tile[there : there + each, :] += side[n * each : (n + 1) * each]
            tile[there : there + strip, :] += second[n * strip : (n + 1) * strip]


def weight_grad_kernel(
    places, q_ref, kv_ref, z_ref, x_ref, rim_ref, dt_ref, cos_ref, sin_ref, w_ref, both_ref, early_ref,
    *refs, heads, groups, parts, in_strips,
):
    if in_strips:
        small_refs, (pre_ref, terms_ref, tile) = refs[:4], refs[4:]
        small_columns(tile, *small_refs, heads=heads, groups=groups, parts=parts)
    else:
        tile, pre_ref, terms_ref = refs
    rows = q_ref.shape[0]
    dim = w_ref.shape[0]
    cols = heads * HEAD
    wide = x_ref.shape[1]
    at_z = 2 * LANES
    at_x = at_z + cols
    at_dt = at_x + wide
    for i in range(0, rows, TILE):
        r = slice(i, i + TILE)
        cosine, sine = cos_ref[r, :], sin_ref[r, :]
        q, kv = q_ref[r, :], kv_ref[r, :]
        pre_ref[r, :LANES] = (q * cosine - swap_halves(q) * sine).astype(B16)
        turned = kv * cosine - swap_halves(kv) * sine
        pre_ref[r, LANES : 2 * LANES] = jnp.where(iota(kv.shape, 1) < HEAD, turned, kv).astype(B16)
        pre_ref[r, at_z:at_x] = z_ref[r, :]
        x = x_ref[r, :]
        if i + TILE == rows:
            x = jnp.concatenate([x[: TILE - 8], x[TILE - 8 :] + rim_ref[...]], axis=0)
        pre_ref[r, at_x:at_dt] = x.astype(B16)
        pre_ref[r, at_dt:] = dt_ref[r, :]
    block = dim // groups
    strip = block // parts
    mixed = LANES + cols
    sides = slice(mixed + LANES, mixed + 3 * LANES)
    ends = slice(mixed + 3 * LANES, mixed + 4 * LANES)
    lane = iota((block, LANES), 1)
    for b in range(groups):
        r = slice(b * block, (b + 1) * block)
        x = both_ref[:, r]
        near = lax.dot_general(x, pre_ref[:, :at_z], ROW_DOT, preferred_element_type=F32)
        far = lax.dot_general(x, pre_ref[:, at_x:], ROW_DOT, preferred_element_type=F32)
        gain = jnp.sum(near * w_ref[r, :at_z].astype(F32), axis=1, keepdims=True)
        gain = gain + jnp.sum(far * w_ref[r, at_x:].astype(F32), axis=1, keepdims=True)
        gain = gain + early_ref[r, :]
        terms_ref[r, :LANES] = near[:, :LANES].astype(B16)
        terms_ref[r, LANES:mixed] = far[:, :cols].astype(B16)
        if in_strips:
            for s in range(parts):
                here = slice(s * strip, (s + 1) * strip)
                first = s * groups * strip + b * strip
                there = slice(first, first + strip)
                terms_ref[there, mixed : mixed + LANES] = near[here, LANES:].astype(B16)
                terms_ref[there, sides] = far[here, cols:wide].astype(B16)
                at_gain = iota((strip, LANES), 1) == heads
                tile[there, :] = jnp.where(at_gain, gain[here], tile[there, :])
            tile[r, :] = jnp.where(lane < heads, far[:, wide:], tile[r, :])
        else:
            terms_ref[r, mixed : mixed + LANES] = near[:, LANES:].astype(B16)
            terms_ref[r, sides] = far[:, cols:wide].astype(B16)
            tail = jnp.where(lane < heads, far[:, wide:], tile[r, :])
            terms_ref[r, ends] = jnp.where(lane == heads, gain, tail).astype(B16)
    if in_strips:
        terms_ref[:, ends] = tile[...].astype(B16)


def iota(shape, dim):
    return lax.broadcasted_iota(jnp.int32, shape, dim)


def per_head(columns, pair):
    shape = (columns.shape[0], LANES)
    return jnp.where(
        iota(shape, 1) < HEAD, columns[:, 2 * pair : 2 * pair + 1], columns[:, 2 * pair + 1 : 2 * pair + 2]
    )


def one_head(values, head):
    keep = (iota(values.shape, 1) < HEAD) == (head % 2 == 0)
    return jnp.where(keep, values, jnp.zeros_like(values))


def into_lane(columns, head, column):
    return jnp.where(iota(columns.shape, 1) == head, column, columns)


def silu_slope(v, sig):
    return sig * (1.0 + v * (1.0 - sig))


def tap_window(ext_ref, tap, first, amount, places):
    return ext_ref[first + 8 - (CONV - 1) + tap : first + 8 - (CONV - 1) + tap + amount, :]


def span_kernel(places, begin_ref, pre_ref, rim_ref, taps_ref, params_ref, u_ref, intra_ref, cum_ref, state_ref, ext, xb, *, heads, at_x, at_dt, nstate):
    rows = pre_ref.shape[0]
    cols = heads * HEAD
    first_row, last_begin = places[0], places[1]
    ext[0:8, :] = rim_ref[...]
    ext[8 : 8 + rows, :] = pre_ref[:, at_x:at_dt]
    local = begin_ref[...] - first_row
    row_ids = iota((rows, 1), 0)
    for i in range(0, rows, TILE):
        total = jnp.zeros((TILE, ext.shape[1]), F32)
        for tap in range(CONV):
            seen = row_ids[i : i + TILE] - (CONV - 1) + tap >= local[i : i + TILE]
            window = tap_window(ext, tap, i, TILE, places)
            total = total + jnp.where(seen, window, 0.0) * taps_ref[tap : tap + 1, :]
        u_ref[i : i + TILE, :] = total
        xb[i : i + TILE, :] = (total * jax.nn.sigmoid(total)).astype(B16)
    raw = pre_ref[:, at_dt : at_dt + LANES] + params_ref[0:1, :]
    dt = jnp.maximum(raw, 0.0) + jnp.log1p(jnp.exp(-jnp.abs(raw)))
    lower = (iota((rows, rows), 0) >= iota((rows, rows), 1)).astype(F32)
    cum = jnp.dot(lower, dt * params_ref[1:2, :], precision=HIGHEST, preferred_element_type=F32)
    cum_ref[:, :LANES] = cum
    cum_ref[:, LANES:] = dt
    cum_t, dt_t = cum.T, dt.T
    last = cum[rows - 1 : rows, :]
    closing = row_ids + first_row >= last_begin
    to_end = jnp.where(closing, jnp.exp(last - cum) * dt, 0.0)
    for i in range(0, rows, TILE):
        width = i + TILE
        c = xb[i : i + TILE, cols + nstate : cols + 2 * nstate]
        b = xb[:width, cols : cols + nstate]
        inner = lax.dot_general(c, b, LANE_DOT, preferred_element_type=F32)
        key = iota((TILE, width), 1)
        seen = (key <= iota((TILE, width), 0) + i) & (key >= local[i : i + TILE])
        for pair in range(heads // 2):
            out = []
            for h in (2 * pair, 2 * pair + 1):
                spread = jnp.where(seen, cum[i : i + TILE, h : h + 1] - cum_t[h : h + 1, :width], MASKED)
                weights = (jnp.exp(spread) * inner * dt_t[h : h + 1, :width]).astype(B16)
                out.append(jnp.dot(weights, xb[:width, pair * LANES : (pair + 1) * LANES], preferred_element_type=F32))
            intra_ref[i : i + TILE, pair * LANES : (pair + 1) * LANES] = jnp.where(iota((TILE, LANES), 1) < HEAD, out[0], out[1])
    b_all = xb[:, cols : cols + nstate]
    for pair in range(heads // 2):
        at = slice(pair * LANES, (pair + 1) * LANES)
        closed = (xb[:, at].astype(F32) * per_head(to_end, pair)).astype(B16)
        state_ref[at, :] = lax.dot_general(closed, b_all, ROW_DOT, preferred_element_type=F32).astype(B16)
    decay = jnp.where(last_begin < first_row, jnp.exp(last), 0.0)
    high = decay.astype(B16)
    low = (decay - high.astype(F32)).astype(B16)
    both = jnp.concatenate([jnp.broadcast_to(high.astype(F32), (LANES // 2, LANES)), jnp.broadcast_to(low.astype(F32), (LANES // 2, LANES))], axis=0)
    state_ref[cols : cols + 16, :] = both.T[:16, :].astype(B16)


def span_forward(places, begins, pre, rim, taps, params, heads, at_x, at_dt, nstate):
    rows = pre.shape[0]
    wide = at_dt - at_x
    cols = heads * HEAD
    return call(
        functools.partial(span_kernel, heads=heads, at_x=at_x, at_dt=at_dt, nstate=nstate),
        "span_forward",
        8,
        (places, begins, pre, rim, taps, params),
        (((rows, wide), F32), ((rows, cols), F32), ((rows, 2 * LANES), F32), ((cols + 16, nstate), B16)),
        (((rows + 8, wide), F32), ((rows, wide), B16)),
    )


def decay_of(states_ref, k, head, cols):
    tail = states_ref[k, cols + head - head % 8 : cols + head - head % 8 + 8, :].astype(F32)
    row = tail[head % 8 : head % 8 + 1, :]
    return row[:, 0:1] + row[:, LANES // 2 : LANES // 2 + 1]


def finish_kernel(places, begin_ref, states_ref, u_ref, intra_ref, cum_ref, z_ref, params_ref, gated_ref, v_ref, state_ref, squares_ref, *, heads, nstate):
    rows = u_ref.shape[0]
    cols = heads * HEAD
    state_ref[...] = jnp.zeros_like(state_ref)

    def fold(k):
        for h in range(heads):
            at = slice(h * HEAD, (h + 1) * HEAD)
            state_ref[at, :] = state_ref[at, :] * decay_of(states_ref, k, h, cols) + states_ref[k, at, :].astype(F32)

    pl.loop(0, places[2])(fold)
    carried = begin_ref[...] < places[0]
    for i in range(0, rows, TILE):
        r = slice(i, i + TILE)
        enter = jnp.where(carried[r], jnp.exp(cum_ref[r, :LANES]), 0.0)
        uc = u_ref[r, cols + nstate : cols + 2 * nstate]
        c = (uc * jax.nn.sigmoid(uc)).astype(B16)
        total = jnp.zeros((8, TILE), F32)
        for pair in range(heads // 2):
            at = slice(pair * LANES, (pair + 1) * LANES)
            y = lax.dot_general(c, state_ref[at, :].astype(B16), LANE_DOT, preferred_element_type=F32)
            ux = u_ref[r, at]
            x = ux * jax.nn.sigmoid(ux)
            skip = per_head(params_ref[2:3, :], pair)
            v = intra_ref[r, at] + per_head(enter, pair) * y + skip * x
            z = z_ref[r, at]
            gated = (v * (z * jax.nn.sigmoid(z))).astype(B16)
            v_ref[r, at] = v
            gated_ref[r, at] = gated
            g = gated.astype(F32)
            total = total + lax.dot_general(jnp.ones((8, LANES), F32), g * g, LANE_DOT, precision=HIGHEST, preferred_element_type=F32)
        squares_ref[:, r] = total


def span_finish(places, begins, states, u, intra, cum, z, params, heads, nstate):
    rows = u.shape[0]
    cols = heads * HEAD
    return call(
        functools.partial(finish_kernel, heads=heads, nstate=nstate),
        "span_finish",
        7,
        (places, begins, states, u, intra, cum, z, params),
        (((rows, cols), B16), ((rows, cols), F32), ((cols, nstate), F32), ((8, rows), F32)),
        (),
    )


def gate_back_kernel(places, begin_ref, scaled_ref, gated_ref, squares_ref, u_ref, cum_ref, z_ref, v_ref, send_ref, *refs, heads, nstate, ssm_all):
    back_ref, dz_ref, state_ref, eg = refs[-4:]
    total = refs[0][...]
    for ref in refs[1:-4]:
        total = total + ref[...]
    rows = u_ref.shape[0]
    cols = heads * HEAD
    carried = begin_ref[...] < places[0]
    squares, stat = squares_ref[...].T, total.T
    uc = u_ref[:, cols + nstate : cols + 2 * nstate]
    c = (uc * jax.nn.sigmoid(uc)).astype(B16)
    for i in range(0, rows, TILE):
        r = slice(i, i + TILE)
        enter = jnp.where(carried[r], jnp.exp(cum_ref[r, :LANES]), 0.0)
        inverse = lax.rsqrt(squares[r, 0:1] / ssm_all + EPSILON)
        mean = stat[r, 0:1] / ssm_all
        for pair in range(heads // 2):
            at = slice(pair * LANES, (pair + 1) * LANES)
            z = z_ref[r, at]
            sig = jax.nn.sigmoid(z)
            scaled = gated_ref[r, at].astype(F32) * inverse
            gg = (inverse * (scaled_ref[r, at] - scaled * mean)).astype(B16)
            back_ref[r, at] = gg
            gg = gg.astype(F32)
            dz_ref[r, at] = (gg * v_ref[r, at] * silu_slope(z, sig)).astype(B16)
            eg[r, at] = (gg * (z * sig) * per_head(enter, pair)).astype(B16)
    state_ref[:cols, :] = lax.dot_general(eg[...], c, ROW_DOT, preferred_element_type=F32).astype(B16)
    state_ref[cols:, :] = send_ref[...]


def gate_back(places, begins, scaled, gated, squares, stats, u, cum, z, v, send, heads, nstate, ssm_all):
    rows = u.shape[0]
    cols = heads * HEAD
    return call(
        functools.partial(gate_back_kernel, heads=heads, nstate=nstate, ssm_all=ssm_all),
        "gate_back",
        5,
        (places, begins, scaled, gated, squares, u, cum, z, v, send) + stats,
        (((rows, cols), B16), ((rows, cols), B16), ((cols + send.shape[0], nstate), B16)),
        (((rows, cols), B16),),
    )


def back_kernel(places, begin_ref, g_ref, z_ref, pre_ref, rim_ref, u_ref, cum_ref, state_ref, states_ref, grads_ref, taps_ref, params_ref, gx_ref, gdt_ref, rim_out, taps_out, small_out, ext, gext, xb, gb, later, dxb, lane_sum, cols_sum, *, heads, at_x, at_dt, nstate):
    rows = u_ref.shape[0]
    cols = heads * HEAD
    wide = at_dt - at_x
    count = states_ref.shape[0]
    pairs = heads // 2
    first_row, last_begin, mine = places[0], places[1], places[2]
    later[...] = jnp.zeros_like(later)

    def fold(n):
        k = count - 1 - n
        for h in range(heads):
            at = slice(h * HEAD, (h + 1) * HEAD)
            later[at, :] = later[at, :] * decay_of(states_ref, k, h, cols) + grads_ref[k, at, :].astype(F32)

    pl.loop(0, count - 1 - mine)(fold)
    local = begin_ref[...] - first_row
    row_ids = iota((rows, 1), 0)
    cum = cum_ref[:, :LANES]
    dt = cum_ref[:, LANES:]
    cum_t, dt_t = cum.T, dt.T
    last = cum[rows - 1 : rows, :]
    leave = jnp.where(row_ids + first_row >= last_begin, jnp.exp(last - cum), 0.0)
    enter = jnp.where(begin_ref[...] < first_row, jnp.exp(cum), 0.0)
    to_end = leave * dt
    for i in range(0, rows, TILE):
        r = slice(i, i + TILE)
        u = u_ref[r, :]
        xb[r, :] = (u * jax.nn.sigmoid(u)).astype(B16)
        z = z_ref[r, :]
        gb[r, :] = (g_ref[r, :].astype(F32) * (z * jax.nn.sigmoid(z))).astype(B16)
    dxb[...] = jnp.zeros_like(dxb)
    cols_sum[...] = jnp.zeros_like(cols_sum)
    b_at = slice(cols, cols + nstate)
    c_at = slice(cols + nstate, cols + 2 * nstate)
    for i in range(0, rows, TILE):
        width = i + TILE
        r = slice(i, i + TILE)
        inner = lax.dot_general(xb[r, c_at], xb[:width, b_at], LANE_DOT, preferred_element_type=F32)
        key = iota((TILE, width), 1)
        seen = (key <= iota((TILE, width), 0) + i) & (key >= local[r])
        grad_inner = jnp.zeros((TILE, width), F32)
        sums = jnp.zeros((TILE, LANES), F32)
        for h in range(heads):
            at = slice(h // 2 * LANES, (h // 2 + 1) * LANES)
            g = one_head(gb[r, at], h)
            spread = jnp.where(seen, cum[r, h : h + 1] - cum_t[h : h + 1, :width], MASKED)
            decays = jnp.exp(spread)
            steps = dt_t[h : h + 1, :width]
            pairing = lax.dot_general(g, xb[:width, at], LANE_DOT, preferred_element_type=F32)
            paired = pairing * decays
            grad_inner = grad_inner + paired * steps
            both = paired * inner
            cols_sum[h : h + 1, :width] += jnp.sum(both, axis=0, keepdims=True)
            sums = into_lane(sums, h, jnp.sum(both * steps, axis=1, keepdims=True))
            weights = (decays * inner * steps).astype(B16)
            dxb[:width, at] += lax.dot_general(weights, g, ROW_DOT, preferred_element_type=F32)
        lane_sum[r, :] = sums
        grad_inner = grad_inner.astype(B16)
        dxb[r, c_at] += jnp.dot(grad_inner, xb[:width, b_at], preferred_element_type=F32)
        dxb[:width, b_at] += lax.dot_general(grad_inner, xb[r, c_at], ROW_DOT, preferred_element_type=F32)
    from_cols = jnp.concatenate([cols_sum[...], jnp.zeros((LANES - 8, rows), F32)], axis=0).T
    state_b = state_ref[...].astype(B16)
    later_b = later[...].astype(B16)
    entered = jnp.zeros((rows, LANES), F32)
    closed = jnp.zeros((rows, LANES), F32)
    skips = jnp.zeros((1, LANES), F32)
    chained = jnp.zeros((1, LANES), F32)
    for pair in range(pairs):
        at = slice(pair * LANES, (pair + 1) * LANES)
        x = xb[:, at].astype(F32)
        g = gb[:, at].astype(F32)
        y = lax.dot_general(xb[:, c_at], state_b[at, :], LANE_DOT, preferred_element_type=F32)
        q = lax.dot_general(xb[:, b_at], later_b[at, :], LANE_DOT, preferred_element_type=F32)
        ends = per_head(to_end, pair)
        dxb[:, c_at] += jnp.dot((g * per_head(enter, pair)).astype(B16), state_b[at, :], preferred_element_type=F32)
        dxb[:, b_at] += jnp.dot((x * ends).astype(B16), later_b[at, :], preferred_element_type=F32)
        dxb[:, at] += ends * q + g * per_head(params_ref[2:3, :], pair)
        gy, xq, gx = g * y, x * q, jnp.sum(g * x, axis=0, keepdims=True)
        kept = jnp.sum(later[at, :] * state_ref[at, :], axis=1, keepdims=True)
        for h in (2 * pair, 2 * pair + 1):
            entered = into_lane(entered, h, jnp.sum(one_head(gy, h), axis=1, keepdims=True))
            closed = into_lane(closed, h, jnp.sum(one_head(xq, h), axis=1, keepdims=True))
            skips = into_lane(skips, h, jnp.sum(one_head(gx, h), axis=1, keepdims=True))
            half = slice(h % 2 * HEAD, (h % 2 + 1) * HEAD)
            chained = into_lane(chained, h, jnp.sum(kept[half], axis=0, keepdims=True))
    decay = jnp.where(last_begin < first_row, jnp.exp(last), 0.0)
    ended = closed * to_end
    grad_cum = lane_sum[...] - from_cols * dt + entered * enter - ended
    at_last = jnp.sum(ended, axis=0, keepdims=True) + decay * chained
    grad_cum = grad_cum + jnp.where(row_ids == rows - 1, at_last, 0.0)
    upper = (iota((rows, rows), 0) <= iota((rows, rows), 1)).astype(F32)
    grad_log = jnp.dot(upper, grad_cum, precision=HIGHEST, preferred_element_type=F32)
    rate = params_ref[1:2, :]
    grad_dt = from_cols + closed * leave + grad_log * rate
    grad_raw = grad_dt * jax.nn.sigmoid(pre_ref[:, at_dt : at_dt + LANES] + params_ref[0:1, :])
    grad_raw = jnp.where(iota((rows, LANES), 1) < heads, grad_raw, 0.0)
    gdt_ref[...] = grad_raw.astype(B16)
    small_out[0:1, :] = jnp.sum(grad_log * dt, axis=0, keepdims=True) * rate
    small_out[1:2, :] = jnp.sum(grad_raw, axis=0, keepdims=True)
    small_out[2:3, :] = skips
    small_out[3:8, :] = jnp.zeros((5, LANES), F32)
    ext[0:8, :] = rim_ref[...]
    ext[8 : 8 + rows, :] = pre_ref[:, at_x:at_dt]
    gext[...] = jnp.zeros_like(gext)
    taps_out[...] = jnp.zeros_like(taps_out)
    for i in range(0, rows, TILE):
        r = slice(i, i + TILE)
        u = u_ref[r, :]
        du = dxb[r, :] * silu_slope(u, jax.nn.sigmoid(u))
        for tap in range(CONV):
            seen = row_ids[r] - (CONV - 1) + tap >= local[r]
            part = jnp.where(seen, du, 0.0)
            taps_out[tap : tap + 1, :] += jnp.sum(part * tap_window(ext, tap, i, TILE, places), axis=0, keepdims=True)
            at = 8 - (CONV - 1) + tap + i
            gext[at : at + TILE, :] += part * taps_ref[tap : tap + 1, :]
    rim_out[...] = gext[0:8, :]
    gx_ref[...] = gext[8:, :]


def span_back(places, begins, back, z, pre, rim, u, cum, state, states, grads, taps, params, heads, at_x, at_dt, nstate, waits):
    rows = u.shape[0]
    cols = heads * HEAD
    wide = at_dt - at_x
    return call(
        functools.partial(back_kernel, heads=heads, at_x=at_x, at_dt=at_dt, nstate=nstate),
        "span_back",
        16,
        (places, begins, back, z, pre, rim, u, cum, state, states, grads, taps, params),
        (((rows, wide), F32), ((rows, LANES), B16), ((8, wide), F32), ((8, wide), F32), ((8, LANES), F32)),
        (((rows + 8, wide), F32), ((rows + 8, wide), F32), ((rows, wide), B16), ((rows, cols), B16),
         ((cols, nstate), F32), ((rows, wide), F32), ((rows, LANES), F32), ((8, rows), F32)),
        waits,
    )


def shards(
    x_in,
    lengths,
    norm1_gain,
    w_mix_in,
    w_dt,
    w_shared,
    conv_x,
    conv_bc,
    a_log,
    dt_bias,
    d_skip,
    gate_gain,
    w_out,
    norm2_gain,
    w_gate,
    w_up,
    w_down,
    d_out,
):
    tok_rows = x_in.shape[0]
    groups = lax.axis_size("branch")
    branch_id = lax.axis_index("branch")
    seq_id = lax.axis_index("seq")
    seq_rows = tok_rows * groups
    group_first = seq_id * seq_rows
    att_heads = HEADS_ATT // groups
    att_cols = att_heads * HEAD
    ssm_heads = w_dt.shape[1]
    ssm_cols = ssm_heads * HEAD
    kv_cols = KV * HEAD
    f32 = jnp.float32
    bf16 = jnp.bfloat16
    dim = x_in.shape[1]
    parts = lax.axis_size("seq")
    chunk = w_out.shape[0] // groups
    att_chunks = parts * att_cols // (att_cols + ssm_cols)
    ssm_chunks = parts - att_chunks
    strip = dim // (groups * parts)
    hidden_all = w_gate.shape[1]
    hidden_a = hidden_all * att_cols // ((att_cols + ssm_cols) * groups)
    hidden_s = hidden_all // groups - hidden_a
    hidden_b = hidden_a + hidden_s

    def spot(c):
        first = groups * att_chunks
        if c < first:
            return (c // att_chunks) * parts + c % att_chunks
        return ((c - first) // ssm_chunks) * parts + att_chunks + (c - first) % ssm_chunks

    to_heads = [((c % groups) * parts + c // groups, spot(c)) for c in range(groups * parts)]
    from_heads = [(spot(c), c) for c in range(groups * parts)]

    def branch_parts(part):
        routes = [[(i, i ^ k) for i in range(groups)] for k in range(1, groups)]
        return (part,) + tuple(lax.ppermute(part, "branch", route) for route in routes)

    def branch_exchange(blocks):
        return lax.all_to_all(blocks, "branch", 0, 0, tiled=True)

    def branch_gather(part):
        copies = branch_exchange(jnp.broadcast_to(part[None], (groups,) + part.shape))
        return copies.reshape((groups * part.shape[0],) + part.shape[1:])

    def branch_scatter(terms):
        blocks = terms.astype(bf16).reshape((groups, -1) + terms.shape[1:])
        return jnp.sum(lax.all_to_all(blocks, "branch", 0, 0, tiled=True).astype(f32), axis=0)

    kv_head = branch_id * att_heads // (HEADS_ATT // KV)
    side_cols = w_shared.shape[1] - 2 * kv_cols
    w1_cols = w_mix_in.shape[1] + 2 * HEAD + side_cols + LANES
    turned = w_dt.shape[0] % LANES == 0
    w1_part = call(
        functools.partial(assemble_kernel, att_cols=att_cols, turned=turned),
        "assemble",
        1,
        (kv_head[None], w_mix_in, w_shared, w_dt.T if turned else w_dt),
        (((w_mix_in.shape[0], w1_cols), B16),),
        (),
    )[0]
    w1 = lax.all_gather(w1_part, "seq", axis=0, tiled=True)

    def own_columns(w):
        return [
            lax.dynamic_slice_in_dim(w, branch_id * hidden_a, hidden_a, 1),
            lax.dynamic_slice_in_dim(w, groups * hidden_a + branch_id * hidden_s, hidden_s, 1),
        ]

    row_part = jnp.concatenate(
        [
            lax.dynamic_slice_in_dim(w_out, branch_id * chunk, chunk, 0),
            lax.dynamic_slice_in_dim(w_down, branch_id * chunk, chunk, 0),
        ],
        axis=0,
    )
    row_part = lax.ppermute(row_part, ("branch", "seq"), to_heads)
    out_part = row_part[:chunk]
    mlp_part = jnp.concatenate(
        [row_part[chunk:], jnp.concatenate(own_columns(w_gate) + own_columns(w_up), axis=1)], axis=0
    )
    x_rows = x_in.astype(f32)
    scaled1, inverse1 = rms_parts(x_rows)
    normed1 = (scaled1 * norm1_gain).astype(bf16)
    both_in = branch_gather(jnp.concatenate([normed1, d_out], axis=1))
    d_out_g = both_in[:, dim:]
    before = from_behind(both_in[seq_rows - 16 :, :dim], "seq", 1)
    row_ids = group_first + jnp.arange(seq_rows, dtype=jnp.int32)
    seq_ends = jnp.cumsum(lengths)

    def begin_of(ids):
        return jnp.max(jnp.where(seq_ends <= ids[..., None], seq_ends, 0), axis=-1)

    def end_of(ids):
        return jnp.min(jnp.where(seq_ends > ids[..., None], seq_ends, seq_rows * parts), axis=-1)

    begins = begin_of(row_ids)
    ends = end_of(row_ids)
    position = row_ids - begins
    row_last = group_first + seq_rows - 1
    begin_first, begin_last = (begin_of(group_first), begin_of(row_last))
    end_first, end_last = (end_of(group_first), end_of(row_last))
    here = seq_id
    query_lo = begin_first // seq_rows
    query_clear = jnp.minimum(jnp.maximum(query_lo, -(-begin_last // seq_rows)), here)
    query_bounds = jnp.stack([query_lo, query_clear, group_first, here, here + 1])
    key_hi = -(-end_last // seq_rows)
    key_clear = jnp.maximum(here + 1, jnp.minimum(end_first // seq_rows, key_hi))
    key_bounds = jnp.stack([here, here + 1, group_first, key_clear, key_hi])
    places = jnp.stack([group_first, begin_last, seq_id])
    begins_col, begins_row, ends_col = (begins[:, None], begins[None, :], ends[:, None])
    at_dt = ssm_cols + side_cols
    nstate = conv_bc.shape[1] // 2
    taps = jnp.pad(jnp.concatenate([conv_x, conv_bc], axis=1), ((0, 8 - CONV), (0, 0)))
    params = jnp.stack([dt_bias, -jnp.exp(a_log), d_skip])
    params = jnp.pad(params, ((0, 5), (0, LANES - ssm_heads)))
    ssm_all = gate_gain.shape[0]
    gain_row = lax.dynamic_slice_in_dim(gate_gain, branch_id * ssm_cols, ssm_cols, 0)[None, :]
    cosine, sine = rotate_tables(position)
    queries, kv, z_pre, pre, rim = call(
        project_kernel,
        "project",
        5,
        (places, both_in, before, w1, cosine, sine),
        (
            ((seq_rows, LANES), B16),
            ((seq_rows, LANES), B16),
            ((seq_rows, ssm_cols), F32),
            ((seq_rows, at_dt + LANES), F32),
            ((8, at_dt), F32),
        ),
        (),
        (
            begins_col,
            begins_row,
            ends_col,
            query_bounds,
            key_bounds,
            taps,
            params,
            gain_row,
            out_part,
            mlp_part,
        ),
    )
    kv_all = lax.all_gather(kv, "seq", axis=0, tiled=True)
    w_out_b = lax.all_gather(out_part, "seq", axis=0, tiled=True)
    mlp_all = lax.all_gather(mlp_part, "seq", axis=0)
    packed = chunk if chunk % 16 == 0 and strip % 16 == 0 else 0
    if packed:
        mlp_weights, down_weights = ((mlp_all,), mlp_all)
        mlp_scratch = (
            ((dim, 2 * hidden_b), B16),
            ((parts * chunk, dim), B16),
            ((seq_rows, 2 * hidden_b), B16),
        )
    else:
        down_weights = mlp_all[:, :chunk].reshape(parts * chunk, dim)
        mlp_weights = (mlp_all[:, chunk:].reshape(dim, 2 * hidden_b), down_weights)
        mlp_scratch = ()
    u, intra, cum, state = span_forward(
        places, begins_col, pre, rim, taps, params, ssm_heads, 0, at_dt, nstate
    )
    states = lax.all_gather(state, "seq", axis=0)
    attn_out, lse, q_send = attend(
        queries, kv_all, begins_row, query_bounds, att_heads, seq_rows
    )
    q_all = lax.all_gather(q_send, "seq", axis=0)
    gated_b, gated_v, state_in, squares = span_finish(
        places, begins_col, states, u, intra, cum, z_pre, params, ssm_heads, nstate
    )

    mixed_out, out_terms, squares = call(
        functools.partial(mix_out_kernel, ssm_all=ssm_all),
        "mix_out",
        3,
        (places, attn_out, gated_b, gain_row, w_out_b) + branch_parts(squares),
        (((seq_rows, att_cols + ssm_cols), B16), ((seq_rows, dim), B16), ((8, seq_rows), F32)),
        (),
    )
    projected = branch_scatter(out_terms)
    middle = x_rows + projected
    scaled2, inverse2 = rms_parts(middle)
    normed2 = branch_gather((scaled2 * norm2_gain).astype(bf16))
    middle_shape = (parts, chunk + dim // parts, dim) if packed else (seq_rows, 2 * hidden_b)
    hidden, mlp_middle, mlp_back = call(
        functools.partial(mlp_kernel, chunk=packed, groups=groups),
        "mlp",
        11,
        (places, normed2, both_in) + mlp_weights,
        (
            ((seq_rows, hidden_b), B16),
            (middle_shape, B16),
            ((seq_rows, dim), B16),
        ),
        mlp_scratch,
    )
    def over_rows(left, right):
        return lax.dot_general(
            left, right, (((0,), (0,)), ((), ())), preferred_element_type=f32
        ).astype(bf16)

    def strips(rows_all):
        wide = rows_all.reshape((groups, parts, strip) + rows_all.shape[1:])
        return jnp.swapaxes(wide, 0, 1).reshape((parts, groups * strip) + rows_all.shape[1:])

    if packed:
        mlp_terms = mlp_middle
    else:
        mlp_terms = jnp.concatenate(
            [
                over_rows(hidden, d_out_g).reshape(parts, chunk, dim),
                strips(over_rows(normed2, mlp_middle)),
            ],
            axis=1,
        )
    mlp_own = lax.psum_scatter(mlp_terms, "seq", scatter_dimension=0)
    grad_middle, grad_copies, grad_n2 = call(
        norm_back_kernel,
        "norm_back",
        2,
        (
            places,
            branch_exchange(mlp_back.reshape(groups, tok_rows, dim)),
            middle,
            d_out,
            norm2_gain[None, :],
        ),
        (((tok_rows, dim), F32), ((groups, tok_rows, dim), B16), ((8, dim), F32)),
        (),
        (q_all,),
    )
    grad_proj = branch_exchange(grad_copies).reshape(seq_rows, dim)
    g_pack, g_send, grad_scaled, stat, grad_gain = call(
        functools.partial(mix_back_kernel, heads=att_heads, ssm_all=ssm_all),
        "mix_back",
        5,
        (places, grad_proj, w_out_b, attn_out, lse, gated_b, squares, gain_row),
        (
            ((seq_rows, att_heads * LANES), B16),
            (q_send.shape, B16),
            ((seq_rows, ssm_cols), F32),
            ((8, seq_rows), F32),
            ((8, ssm_cols), F32),
        ),
        (((seq_rows, LANES), F32),),
    )
    stats = branch_parts(stat)
    grad_gate_gain = grad_gain[0]

    def all_columns(blocks):
        blocks = jnp.swapaxes(blocks, 0, 1)
        return jnp.concatenate(
            [blocks[:, :, :hidden_a].reshape(strip, -1), blocks[:, :, hidden_a:].reshape(strip, -1)],
            axis=1,
        )

    back_ssm, grad_z, grad_state = gate_back(
        places, begins_col, grad_scaled, gated_b, squares, stats, u, cum, z_pre, gated_v, g_send, ssm_heads, nstate, ssm_all
    )
    grad_states = lax.all_gather(grad_state, "seq", axis=0)
    grad_q = query_grad(
        queries, g_pack, kv_all, begins_col, query_bounds, att_heads, seq_rows, (grad_state, mlp_own)
    )
    y_terms = call(
        functools.partial(down_kernel, chunk=packed),
        "down",
        3,
        (places, hidden, down_weights),
        (((seq_rows, dim), B16),),
        (),
        (grad_state,),
    )[0]
    y_blocks = branch_exchange(y_terms.reshape(groups, tok_rows, dim))
    if packed:
        early_terms, early_gain = call(
            functools.partial(early_kernel, parts=parts),
            "early",
            3,
            (places, mixed_out, grad_proj, both_in, grad_z, w1),
            (((dim, dim // 2 + ssm_cols), B16), ((dim, 1), F32)),
            (),
        )
        early_terms = early_terms.reshape(parts, dim // parts, dim // 2 + ssm_cols)
    else:
        out_rows = over_rows(mixed_out, grad_proj).reshape(parts, chunk, dim)
        z_grad = lax.dot_general(both_in[:, :dim], grad_z, ROW_DOT, preferred_element_type=f32)
        at_z = 2 * LANES
        z_weight = w1[:, at_z : at_z + ssm_cols].astype(f32)
        early_gain = jnp.sum(z_grad * z_weight, axis=1, keepdims=True)
        early_terms = jnp.concatenate(
            [
                jnp.concatenate([out_rows[:, :, : dim // 2], out_rows[:, :, dim // 2 :]], axis=1),
                z_grad.astype(bf16).reshape(parts, dim // parts, ssm_cols),
            ],
            axis=2,
        )
    early_own = lax.psum_scatter(early_terms, "seq", scatter_dimension=0)
    grad_w_down = lax.ppermute(mlp_own[:chunk], ("branch", "seq"), from_heads)
    own_gu = branch_exchange(mlp_own[chunk:].reshape(groups, strip, 2 * hidden_b))
    grad_w_gate = all_columns(own_gu[:, :, :hidden_b]).astype(f32)
    grad_w_up = all_columns(own_gu[:, :, hidden_b:]).astype(f32)
    grad_xbc, grad_dt, rim_back, grad_taps, grad_small = span_back(
        places,
        begins_col,
        back_ssm,
        z_pre,
        pre,
        rim,
        u,
        cum,
        state_in,
        states,
        grad_states,
        taps,
        params,
        ssm_heads,
        0,
        at_dt,
        nstate,
        (grad_q, early_terms, y_terms),
    )
    rim_back = from_behind(rim_back, "seq", -1)
    grad_kv = key_grad(
        kv, q_all, grad_states, ssm_cols, ends_col, key_bounds, att_heads, seq_rows, (grad_dt,)
    )
    tall = groups * strip
    bc_each = conv_bc.shape[1] // (groups * parts)
    x_each = ssm_cols // parts
    in_strips = strip % 16 == 0
    if in_strips:
        small = (grad_gain, grad_taps, grad_small, grad_n2)
    else:
        grad_conv_x, grad_conv_bc = (grad_taps[:CONV, :ssm_cols], grad_taps[:CONV, ssm_cols:])
        def to_column(vector, rows_each):
            padded = jnp.pad(vector.reshape(parts, rows_each), ((0, 0), (0, tall - rows_each)))
            return padded[:, :, None]

        def to_columns(matrix, rows_each):
            wide = jnp.swapaxes(matrix.reshape(matrix.shape[0], parts, rows_each), 0, 1)
            wide = jnp.pad(wide, ((0, 0), (0, 0), (0, tall - rows_each)))
            return jnp.swapaxes(wide, 1, 2)

        bc_wide = grad_conv_bc.reshape(CONV, groups, parts, bc_each)
        bc_wide = jnp.pad(bc_wide, ((0, 0), (0, 0), (0, 0), (0, strip - bc_each)))
        bc_wide = jnp.transpose(bc_wide, (2, 1, 3, 0)).reshape(parts, tall, CONV)
        heads3 = grad_small[:3, :ssm_heads].reshape(3 * ssm_heads)
        heads3 = jnp.broadcast_to(heads3[None, None, :], (parts, tall, 3 * ssm_heads))
        small = jnp.concatenate(
            [
                jnp.zeros((parts, tall, ssm_heads + 1), f32),
                strips(grad_n2[0][:, None]),
                bc_wide,
                to_column(grad_gate_gain, x_each),
                to_columns(grad_conv_x, x_each),
                heads3,
            ],
            axis=2,
        )
        small = jnp.pad(small, ((0, 0), (0, 0), (0, LANES - small.shape[2]))).reshape(dim, LANES)
        small = (small,)
    late_cols = w1_cols - ssm_cols
    grad_pre, terms1 = call(
        functools.partial(
            weight_grad_kernel, heads=ssm_heads, groups=groups, parts=parts, in_strips=in_strips
        ),
        "weight_grad",
        7,
        (places, grad_q, grad_kv, grad_z, grad_xbc, rim_back, grad_dt, cosine, sine, w1, both_in, early_gain)
        + small,
        (((seq_rows, w1_cols), B16), ((dim, late_cols), B16)),
        (((dim, LANES), F32),) if in_strips else (),
        (own_gu, grad_w_down),
    )
    mixed_cols = att_cols + ssm_cols
    at_s = mixed_cols + 2 * HEAD + side_cols
    if in_strips:
        terms1 = terms1.reshape(parts, tall, late_cols)
    else:
        tail = terms1[:, at_s:].reshape(parts, tall, LANES)
        gain_column = strips(terms1[:, at_s + ssm_heads][:, None])
        lane = jnp.arange(LANES)
        terms1 = jnp.concatenate(
            [
                terms1[:, :mixed_cols].reshape(parts, tall, mixed_cols),
                strips(terms1[:, mixed_cols:at_s]),
                jnp.where(lane == ssm_heads, gain_column, tail),
            ],
            axis=2,
        )
    own1 = lax.psum_scatter(terms1, "seq", scatter_dimension=0)
    group_terms, early_own = call(
        group_back_kernel,
        "group_back",
        4,
        (places, grad_pre, w1, early_own),
        (((seq_rows, dim), B16), (early_own.shape, B16)),
        (),
    )
    grad_normed1 = branch_scatter(group_terms)
    y_out = call(
        add_blocks_kernel,
        "add_blocks",
        1,
        (places, y_blocks, middle),
        (((tok_rows, dim), B16),),
        (),
        (group_terms,),
    )[0]
    out_own = jnp.concatenate(
        [early_own[:chunk, : dim // 2], early_own[chunk:, : dim // 2]], axis=1
    )
    grad_w_out = lax.ppermute(out_own, ("branch", "seq"), from_heads).astype(f32)
    own_gain = lax.dynamic_slice_in_dim(norm1_gain, (branch_id * parts + seq_id) * strip, strip, 0)
    side_blocks = branch_exchange(own1[:, mixed_cols:].reshape(groups, strip, -1))
    head_row = ((1, ssm_heads), F32)
    grad_mix, grad_dt_w, grad_gain_g, grad_cx, grad_a_log, grad_dt_bias, grad_skip = call(
        functools.partial(own_kernel, heads=ssm_heads, half=dim // 2),
        "own",
        2,
        (places, own1, early_own),
        (
            ((tall, w_mix_in.shape[1]), F32),
            ((ssm_heads, tall), F32),
            ((1, x_each), F32),
            ((CONV, x_each), F32),
            head_row,
            head_row,
            head_row,
        ),
        (),
    )
    grad_shared, first_gain, second_gain, grad_cbc = call(
        functools.partial(side_kernel, heads=ssm_heads),
        "side",
        1,
        (places, side_blocks, own_gain[None, :]),
        (
            ((strip, w_shared.shape[1]), F32),
            ((1, strip), F32),
            ((1, strip), F32),
            ((CONV, bc_each), F32),
        ),
        (),
    )
    grad_x1, unused_n1 = rms_backward(grad_normed1, scaled1, inverse1, norm1_gain)
    return (
        y_out,
        grad_middle + grad_x1,
        first_gain[0],
        grad_mix,
        grad_dt_w.T,
        grad_shared,
        grad_cx,
        grad_cbc,
        grad_a_log[0],
        grad_dt_bias[0],
        grad_skip[0],
        grad_gain_g[0],
        grad_w_out,
        second_gain[0],
        grad_w_gate,
        grad_w_up,
        grad_w_down.astype(f32),
    )


def solution(mesh):
    in_specs = (
        P(("seq", "branch"), None),
        P(),
        P(),
        P("seq", "branch"),
        P("seq", "branch"),
        P("seq", None),
        P(None, "branch"),
        P(),
        P("branch"),
        P("branch"),
        P("branch"),
        P(),
        P("seq", None),
        P(),
        P("seq", None),
        P("seq", None),
        P("seq", None),
        P(("seq", "branch"), None),
    )
    out_specs = (
        P(("seq", "branch"), None),
        P(("seq", "branch"), None),
        P(("branch", "seq")),
        P("seq", "branch"),
        P("seq", "branch"),
        P(("branch", "seq"), None),
        P(None, ("branch", "seq")),
        P(None, ("branch", "seq")),
        P("branch"),
        P("branch"),
        P("branch"),
        P(("branch", "seq")),
        P(("branch", "seq"), None),
        P(("branch", "seq")),
        P(("branch", "seq"), None),
        P(("branch", "seq"), None),
        P(("branch", "seq"), None),
    )
    return jax.shard_map(shards, mesh=mesh, in_specs=in_specs, out_specs=out_specs, check_vma=False)
```

```python
import functools

import jax
import jax.numpy as jnp
from jax import lax
from jax.experimental import pallas as pl
from jax.experimental.pallas import tpu as pltpu
from jax.sharding import PartitionSpec as P

HEADS_ATT = 8
KV = 2
HEAD = 64
CONV = 4
LANES = 128
TILE = 128
MASKED = -1e30
HIGHEST = lax.Precision.HIGHEST
EPSILON = 1e-06
SCORE_SCALE = 0.125
ROPE_BASE = 1000000.0
F32 = jnp.float32
B16 = jnp.bfloat16
LANE_DOT = (((1,), (1,)), ((), ()))
ROW_DOT = (((0,), (0,)), ((), ()))


VMEM_SPEC = pl.BlockSpec(memory_space=pltpu.VMEM)
SMEM_SPEC = pl.BlockSpec(memory_space=pltpu.SMEM)
ANY_SPEC = pl.BlockSpec(memory_space=pl.ANY)


def from_behind(block, axis, distance):
    devices = range(lax.axis_size(axis))
    route = [(i - distance, i) for i in devices if i - distance in devices]
    return lax.ppermute(block, axis, route)


def rms_parts(value):
    inverse = lax.rsqrt(jnp.mean(value * value, axis=-1, keepdims=True) + EPSILON)
    return (value * inverse, inverse)


def rms_backward(grad_out, scaled, inverse, gain_vec):
    grad_scaled = grad_out * gain_vec
    grad_in = inverse * (
        grad_scaled - scaled * jnp.mean(grad_scaled * scaled, axis=-1, keepdims=True)
    )
    return (grad_in, jnp.sum(grad_out * scaled, axis=0))


def rotate_tables(position):
    half = HEAD // 2
    inverse = ROPE_BASE ** (-jnp.arange(half, dtype=jnp.float32) / half)
    angles = position.astype(jnp.float32)[:, None] * inverse[None, :]
    cosine, sine = (jnp.cos(angles), jnp.sin(angles))
    return (
        jnp.concatenate([cosine] * (LANES // half), axis=1),
        jnp.concatenate([-sine, sine] * (LANES // HEAD), axis=1),
    )


def swap_halves(values):
    half = HEAD // 2
    lane = lax.broadcasted_iota(jnp.int32, values.shape, 1)
    return jnp.where(
        lane % HEAD < half, pltpu.roll(values, LANES - half, 1), pltpu.roll(values, half, 1)
    )


def call(kernel, name, micros, args, outs, scratch, waits=()):
    given, held = (len(args), len(waits))

    def body(*refs):
        kernel(*refs[:given], *refs[given + held :])

    def padded(shape, kind):
        shape = (1,) * (2 - len(shape)) + tuple(shape)
        wide = -(-shape[-1] // LANES) * LANES
        tall = -(-shape[-2] // 16) * 16
        return functools.reduce(lambda a, b: a * b, shape[:-2], 1) * tall * wide * jnp.dtype(kind).itemsize

    held_bytes = [padded(a.shape, a.dtype) for a in args[1:]]
    held_bytes += [padded(s, d) for s, d in tuple(outs) + tuple(scratch)]
    limit = 56 << 20
    if name in ("span_finish", "attend", "mix_out", "mlp", "norm_back", "mix_back", "gate_back"):
        limit = min(limit, sum(held_bytes) + (8 << 20))
    result = pl.pallas_call(
        body,
        out_shape=tuple(jax.ShapeDtypeStruct(s, d) for s, d in outs),
        in_specs=[SMEM_SPEC] + [VMEM_SPEC] * (given - 1) + [ANY_SPEC] * held,
        out_specs=tuple(VMEM_SPEC for _ in outs),
        scratch_shapes=[pltpu.VMEM(s, d) for s, d in scratch],
        compiler_params=pltpu.CompilerParams(vmem_limit_bytes=limit),
        cost_estimate=pl.CostEstimate(
            flops=micros * 1000000, bytes_accessed=micros * 3600000, transcendentals=micros * 100000
        ),
        name=name,
    )(*args, *waits)
    return result


def extra_rows(values, heads):
    pieces = []
    for h in range(heads):
        row = values[h : h + 1, :]
        high = row.astype(B16).astype(F32)
        for part in (high, row - high):
            pieces += [part[:, at : at + LANES] for at in range(0, row.shape[1], LANES)]
    return jnp.concatenate(pieces, axis=0)


def extra_row(rows, head, count):
    at = 2 * head * count
    high = jnp.concatenate([rows[at + n : at + n + 1] for n in range(count)], axis=1)
    low = jnp.concatenate([rows[at + count + n : at + count + n + 1] for n in range(count)], axis=1)
    return high + low


def attend_kernel(
    bounds, begin_ref, own_ref, all_ref, out_ref, lse_ref, send_ref, top, acc, *, heads, keys
):
    rows = own_ref.shape[0]
    top[...] = jnp.full_like(top, MASKED)
    acc[...] = jnp.zeros_like(acc)
    row_ids = bounds[2] + iota((1, rows), 1)
    begins = begin_ref[...]
    ones = (iota((keys, HEAD), 1) == 0).astype(B16)

    def step(n, masked):
        at = n * keys
        kv = all_ref[n, :keys, :]
        k = kv[:, :HEAD]
        v = jnp.concatenate([kv[:, HEAD:], ones], axis=1).T
        if masked:
            key_ids = at + iota((keys, rows), 0)
            seen = (key_ids <= row_ids) & (key_ids >= begins)
        for h in range(heads):
            q = own_ref[:, h * HEAD : (h + 1) * HEAD]
            s = lax.dot_general(k, q, LANE_DOT, preferred_element_type=F32)
            if masked:
                s = jnp.where(seen, s, MASKED)
            old = top[h : h + 1, :]
            new = jnp.maximum(old, jnp.max(s, axis=0, keepdims=True))
            p = jnp.exp(s - new).astype(B16)
            scale = jnp.exp(old - new)
            add = jnp.dot(v, p, preferred_element_type=F32)
            acc[h] = acc[h] * scale + add
            top[h : h + 1, :] = new

    pl.loop(bounds[0], bounds[1])(lambda n: step(n, True))
    pl.loop(bounds[1], bounds[3])(lambda n: step(n, False))
    pl.loop(bounds[3], bounds[4])(lambda n: step(n, True))
    for h in range(heads):
        total = acc[h, HEAD : HEAD + 1, :]
        out_ref[:, h * HEAD : (h + 1) * HEAD] = (acc[h, :HEAD, :] / total).T.astype(B16)
        lse_ref[h : h + 1, :] = top[h : h + 1, :] + jnp.log(total)
    send_ref[:rows, :] = own_ref[...]
    send_ref[rows:, :] = extra_rows(lse_ref[...], heads).astype(B16)


def attend(own, everything, begins, bounds, heads, keys):
    rows = own.shape[0]
    return call(
        functools.partial(attend_kernel, heads=heads, keys=keys),
        "attend",
        12,
        (bounds, begins, own, everything),
        (((rows, heads * HEAD), B16), ((8, rows), F32), ((rows + 2 * heads * rows // LANES, LANES), B16)),
        (((8, rows), F32), ((heads, LANES, rows), F32)),
    )


def minus_ones(lane, base, first):
    at = base + first
    return jnp.where((lane == at) | (lane == at + 1), -1.0, 0.0).astype(B16)


def key_sides(kv, heads):
    turned = jnp.concatenate([kv[:, HEAD:], kv[:, :HEAD]], axis=1)
    lane = iota(kv.shape, 1)
    zero = jnp.zeros_like(kv)
    sides = []
    for h in range(heads):
        mine = lane < HEAD if h == 0 else lane >= HEAD
        base = HEAD * (1 - h)
        keys_h = jnp.where(mine, kv if h == 0 else turned, zero)
        values_h = jnp.where(mine, turned if h == 0 else kv, minus_ones(lane, base, 0))
        both = jnp.concatenate([keys_h, minus_ones(lane, base, 2)], axis=1)
        sides.append((keys_h, values_h, both))
    return sides


def query_grad_kernel(
    bounds, begin_ref, own_ref, g_ref, all_ref, out_ref, acc, *, heads, keys
):
    rows = own_ref.shape[0]
    acc[...] = jnp.zeros_like(acc)
    row_ids = bounds[2] + iota((rows, keys), 0)
    begins = begin_ref[...]

    def step(n, masked):
        at = n * keys
        kv = all_ref[n, :keys, :]
        sides = key_sides(kv, heads)
        if masked:
            key_ids = at + iota((rows, keys), 1)
            seen = (key_ids <= row_ids) & (key_ids >= begins)
        total = acc[...]
        for h in range(heads):
            k, v, both = sides[h]
            g = g_ref[:, h * LANES : (h + 1) * LANES]
            q = jnp.concatenate([own_ref[...], g], axis=1)
            s = lax.dot_general(q, both, LANE_DOT, preferred_element_type=F32)
            if masked:
                s = jnp.where(seen, s, MASKED)
            gp = lax.dot_general(g, v, LANE_DOT, preferred_element_type=F32)
            ds = (jnp.exp(s) * gp).astype(B16)
            total = total + jnp.dot(ds, k, preferred_element_type=F32)
        acc[...] = total

    pl.loop(bounds[0], bounds[1])(lambda n: step(n, True))
    pl.loop(bounds[1], bounds[3])(lambda n: step(n, False))
    pl.loop(bounds[3], bounds[4])(lambda n: step(n, True))
    out_ref[...] = acc[...] * SCORE_SCALE


def query_grad(own, g_pack, everything, begins, bounds, heads, keys, waits):
    rows = own.shape[0]
    return call(
        functools.partial(query_grad_kernel, heads=heads, keys=keys),
        "query_grad",
        11,
        (bounds, begins, own, g_pack, everything),
        (((rows, LANES), F32),),
        (((rows, LANES), F32),),
        waits,
    )[0]


def key_grad_kernel(
    bounds, end_ref, own_ref, all_ref, g_ref, out_ref, acc_k, acc_v, *, heads, keys, at_g
):
    rows = out_ref.shape[0]
    acc_k[...] = jnp.zeros_like(acc_k)
    acc_v[...] = jnp.zeros_like(acc_v)
    key_ids = bounds[2] + iota((rows, keys), 0)
    ends = end_ref[...]
    kv = own_ref[:rows, :]
    turned = jnp.concatenate([kv[:, HEAD:], kv[:, :HEAD]], axis=1)
    first = iota(kv.shape, 1) < HEAD
    zero = jnp.zeros_like(kv)
    count = keys // LANES
    sides = []
    for h in range(heads):
        mine = first if h == 0 else jnp.logical_not(first)
        k = jnp.where(mine, kv if h == 0 else turned, zero)
        sides.append((k, jnp.where(mine, turned if h == 0 else kv, zero)))

    def step(n, masked):
        at = n * keys
        if masked:
            row_ids = at + iota((rows, keys), 1)
            seen = (key_ids <= row_ids) & (row_ids < ends)
        q = all_ref[n, :keys, :]
        g = g_ref[n, at_g : at_g + keys, :]
        lse_rows = all_ref[n, keys:, :].astype(F32)
        delta_rows = g_ref[n, at_g + keys :, :].astype(F32)
        for h in range(heads):
            k, v = sides[h]
            s = lax.dot_general(k, q, LANE_DOT, preferred_element_type=F32)
            s = s - extra_row(lse_rows, h, count)
            if masked:
                s = jnp.where(seen, s, MASKED)
            p = jnp.exp(s)
            gp = lax.dot_general(v, g, LANE_DOT, preferred_element_type=F32)
            ds = (p * (gp - extra_row(delta_rows, h, count))).astype(B16)
            acc_k[h] += jnp.dot(ds, q, preferred_element_type=F32)
            acc_v[h] += jnp.dot(p.astype(B16), g, preferred_element_type=F32)

    pl.loop(bounds[0], bounds[1])(lambda n: step(n, True))
    pl.loop(bounds[1], bounds[3])(lambda n: step(n, False))
    pl.loop(bounds[3], bounds[4])(lambda n: step(n, True))
    out_ref[:, :HEAD] = acc_k[0, :, :HEAD] + acc_k[1, :, HEAD:]
    out_ref[:, HEAD:] = acc_v[0, :, :HEAD] + acc_v[1, :, HEAD:]


def key_grad(own, everything, g_all, at_g, ends, bounds, heads, keys, waits):
    rows = ends.shape[0]
    return call(
        functools.partial(key_grad_kernel, heads=heads, keys=keys, at_g=at_g),
        "key_grad",
        12,
        (bounds, ends, own, everything, g_all),
        (((rows, LANES), F32),),
        (((heads, rows, LANES), F32), ((heads, rows, LANES), F32)),
        waits,
    )[0]


def assemble_kernel(picks, mix_ref, shared_ref, dt_ref, out_ref, *, att_cols, turned):
    kv_cols = KV * HEAD
    wide = mix_ref.shape[1]
    first = picks[0] == 0
    at = att_cols
    out_ref[:, :at] = mix_ref[:, :at]
    for part in range(2):
        tile = shared_ref[:, part * kv_cols : (part + 1) * kv_cols]
        out_ref[:, at : at + HEAD] = jnp.where(first, tile[:, :HEAD], tile[:, HEAD:])
        at += HEAD
    out_ref[:, at : at + wide - att_cols] = mix_ref[:, att_cols:]
    at += wide - att_cols
    out_ref[:, at : at + shared_ref.shape[1] - 2 * kv_cols] = shared_ref[:, 2 * kv_cols :]
    at += shared_ref.shape[1] - 2 * kv_cols
    if turned:
        heads, rows = dt_ref.shape
        steps = jnp.concatenate([dt_ref[...].astype(F32), jnp.zeros((LANES - heads, rows), F32)], axis=0)
        out_ref[:, at:] = steps.T.astype(B16)
    else:
        out_ref[:, at:] = jnp.zeros((out_ref.shape[0], LANES), B16)
        out_ref[:, at : at + dt_ref.shape[1]] = dt_ref[...]


def project_kernel(
    places, both_ref, before_ref, w_ref, cos_ref, sin_ref, out_ref, q_ref, kv_ref, z_ref, pre_ref, rim_ref
):
    rows = both_ref.shape[0]
    dim = w_ref.shape[0]
    at_z = 2 * LANES
    at_x = at_z + z_ref.shape[1]
    step = 2 * TILE
    for i in range(0, rows, step):
        r = slice(i, i + step)
        x = both_ref[r, :dim]
        t = jnp.dot(x, w_ref[:, :at_z], preferred_element_type=F32)
        cosine, sine = cos_ref[r, :], sin_ref[r, :]
        q, kv = t[:, :LANES], t[:, LANES:]
        q = (q * cosine + swap_halves(q) * sine).astype(B16)
        q_ref[r, :] = (q.astype(F32) * SCORE_SCALE).astype(B16)
        turned = kv * cosine + swap_halves(kv) * sine
        kv_ref[r, :] = jnp.where(iota(kv.shape, 1) < HEAD, turned, kv).astype(B16)
        z_ref[r, :] = jnp.dot(x, w_ref[:, at_z:at_x], preferred_element_type=F32)
        pre_ref[r, :] = jnp.dot(x, w_ref[:, at_x:], preferred_element_type=F32)
    wide = rim_ref.shape[1]
    rim = jnp.dot(before_ref[...], w_ref[:, at_x : at_x + wide], preferred_element_type=F32)
    rim_ref[...] = rim[before_ref.shape[0] - 8 :, :]
    if kv_ref.shape[0] > rows:
        chunk = out_ref.shape[0]
        for n in range(dim // LANES):
            at = rows + n * chunk
            kv_ref[at : at + chunk, :] = out_ref[:, n * LANES : (n + 1) * LANES]


def out_weights(all_ref, w_ref, first, chunk):
    for s in range(all_ref.shape[0]):
        for n in range(w_ref.shape[1] // LANES):
            at = first + n * chunk
            piece = all_ref[s, at : at + chunk, :]
            w_ref[s * chunk : (s + 1) * chunk, n * LANES : (n + 1) * LANES] = piece


def mix_out_kernel(places, attn_ref, gated_ref, gain_ref, all_ref, *refs, ssm_all, chunk):
    if chunk:
        mixed_ref, part_ref, total_ref, w_ref = refs[-4:]
        refs = refs[:-1]
        out_weights(all_ref, w_ref, attn_ref.shape[0], chunk)
    else:
        mixed_ref, part_ref, total_ref = refs[-3:]
        w_ref = all_ref
    rows = attn_ref.shape[0]
    att_cols = attn_ref.shape[1]
    total = refs[0][...]
    for ref in refs[1:-3]:
        total = total + ref[...]
    total_ref[...] = total
    squares = total.T
    for i in range(0, rows, TILE):
        r = slice(i, i + TILE)
        inverse = lax.rsqrt(squares[r, 0:1] / ssm_all + EPSILON)
        gnormed = (gated_ref[r, :].astype(F32) * inverse * gain_ref[...]).astype(B16)
        mixed_ref[r, :att_cols] = attn_ref[r, :]
        mixed_ref[r, att_cols:] = gnormed
    for i in range(0, rows, 2 * TILE):
        r = slice(i, i + 2 * TILE)
        part_ref[r, :] = jnp.dot(mixed_ref[r, :], w_ref[...], preferred_element_type=F32).astype(B16)


def mix_back_kernel(
    places, grad_ref, w_ref, attn_ref, lse_ref, gated_ref, squares_ref, gain_ref,
    pack_ref, send_ref, scaled_ref, stat_ref, gain_out, deltas, *, heads, ssm_all,
):
    rows = attn_ref.shape[0]
    att_cols = attn_ref.shape[1]
    squares = squares_ref[...].T
    lse = lse_ref[...].T
    total = jnp.zeros((1, gated_ref.shape[1]), F32)
    ones = jnp.ones((8, gated_ref.shape[1]), F32)
    for i in range(0, rows, TILE):
        r = slice(i, i + TILE)
        mixed = lax.dot_general(grad_ref[r, :], w_ref[...], LANE_DOT, preferred_element_type=F32)
        back = mixed[:, :att_cols].astype(B16).astype(F32)
        product = back * attn_ref[r, :].astype(F32)
        lane = iota(back.shape, 1)
        send_ref[r, :] = back.astype(B16)
        packed = jnp.zeros((TILE, LANES), F32)
        for h in range(heads):
            base = HEAD * (1 - h)
            tile = one_head(back, h)
            delta = jnp.sum(one_head(product, h), axis=1, keepdims=True)
            packed = into_lane(packed, h, delta)
            for n, column in enumerate((delta, lse[r, h : h + 1])):
                high = column.astype(B16).astype(F32)
                tile = jnp.where(lane == base + 2 * n, high, tile)
                tile = jnp.where(lane == base + 2 * n + 1, column - high, tile)
            pack_ref[r, h * LANES : (h + 1) * LANES] = tile.astype(B16)
        deltas[r, :] = packed
        grad = mixed[:, att_cols:]
        scaled = gated_ref[r, :].astype(F32) * lax.rsqrt(squares[r, 0:1] / ssm_all + EPSILON)
        grad_scaled = grad * gain_ref[...]
        scaled_ref[r, :] = grad_scaled
        stat_ref[:, r] = lax.dot_general(
            ones, grad_scaled * scaled, LANE_DOT, precision=HIGHEST, preferred_element_type=F32
        )
        total = total + jnp.sum(grad * scaled, axis=0, keepdims=True)
    gain_out[...] = jnp.broadcast_to(total, gain_out.shape)
    send_ref[rows:, :] = extra_rows(deltas[...].T, heads).astype(B16)


def rows_of(ref, first, last):
    return jnp.concatenate([ref[k, first:last, :] for k in range(ref.shape[0])], axis=0)


def mlp_kernel(places, in_ref, out_ref, *refs, chunk, groups):
    if chunk:
        all_ref, hidden_ref, weights_ref, terms_ref, gu_ref, down_ref, grad_ref = refs
        down_ref[...] = rows_of(all_ref, 0, chunk)
        gu_ref[...] = rows_of(all_ref, chunk, all_ref.shape[1])
    else:
        gu_ref, down_ref, hidden_ref, grad_ref, terms_ref = refs
    rows = in_ref.shape[0]
    half = hidden_ref.shape[1]
    dim = in_ref.shape[1]
    step = 2 * TILE
    for i in range(0, rows, step):
        r = slice(i, i + step)
        both = jnp.dot(in_ref[r, :], gu_ref[...], preferred_element_type=F32)
        back = lax.dot_general(out_ref[r, dim:], down_ref[...], LANE_DOT, preferred_element_type=F32)
        gate, up = both[:, :half], both[:, half:]
        sig = jax.nn.sigmoid(gate)
        soft = gate * sig
        hidden_ref[r, :] = (soft * up).astype(B16)
        grad_ref[r, :half] = (back * up * sig * (1.0 + gate * (1.0 - sig))).astype(B16)
        grad_ref[r, half:] = (back * soft).astype(B16)
        terms_ref[r, :] = lax.dot_general(
            grad_ref[r, :], gu_ref[...], LANE_DOT, preferred_element_type=F32
        ).astype(B16)
    if chunk:
        parts, tall = weights_ref.shape[0], weights_ref.shape[1] - chunk
        strip = tall // groups
        for i in range(0, half, step):
            down = lax.dot_general(
                hidden_ref[:, i : i + step], out_ref[:, dim:], ROW_DOT, preferred_element_type=F32
            ).astype(B16)
            for n in range(step // chunk):
                weights_ref[i // chunk + n, :chunk, :] = down[n * chunk : (n + 1) * chunk]
        for i in range(0, dim, step):
            both = lax.dot_general(
                in_ref[:, i : i + step], grad_ref[...], ROW_DOT, preferred_element_type=F32
            ).astype(B16)
            for n in range(step // strip):
                b, s = divmod(i // strip + n, parts)
                at = chunk + b * strip
                weights_ref[s, at : at + strip, :] = both[n * strip : (n + 1) * strip]


def down_kernel(places, hidden_ref, w_ref, out_ref, *, chunk):
    w = rows_of(w_ref, 0, chunk) if chunk else w_ref[...]
    out_ref[...] = jnp.dot(hidden_ref[...], w, preferred_element_type=F32).astype(B16)


def add_blocks_kernel(places, blocks_ref, middle_ref, out_ref):
    total = blocks_ref[0].astype(F32)
    for n in range(1, blocks_ref.shape[0]):
        total = total + blocks_ref[n].astype(F32)
    out_ref[...] = (middle_ref[...] + total).astype(B16)


def group_back_kernel(places, grad_ref, w_ref, early_ref, out_ref, kept_ref):
    rows = grad_ref.shape[0]
    step = 2 * TILE
    for i in range(0, rows, step):
        r = slice(i, i + step)
        out_ref[r, :] = lax.dot_general(
            grad_ref[r, :], w_ref[...], LANE_DOT, preferred_element_type=F32
        ).astype(B16)
    kept_ref[...] = early_ref[...]


def norm_back_kernel(places, blocks_ref, middle_ref, grad_ref, gain_ref, total_ref, copies_ref, gain_out):
    grad = blocks_ref[0].astype(F32)
    for n in range(1, blocks_ref.shape[0]):
        grad = grad + blocks_ref[n].astype(F32)
    middle = middle_ref[...]
    inverse = lax.rsqrt(jnp.mean(middle * middle, axis=1, keepdims=True) + EPSILON)
    scaled = middle * inverse
    grad_scaled = grad * gain_ref[...]
    mean = jnp.mean(grad_scaled * scaled, axis=1, keepdims=True)
    total = inverse * (grad_scaled - scaled * mean) + grad_ref[...].astype(F32)
    total_ref[...] = total
    for n in range(copies_ref.shape[0]):
        copies_ref[n] = total.astype(B16)
    gain_out[...] = jnp.broadcast_to(jnp.sum(grad * scaled, axis=0, keepdims=True), gain_out.shape)


def turned_rows(values):
    rows = values.shape[0]
    if rows < LANES:
        values = jnp.concatenate([values, jnp.zeros((LANES - rows, LANES), F32)], axis=0)
    return values.T


def own_kernel(places, own_ref, early_ref, mixed_ref, dt_ref, gain_ref, taps_ref, *head_refs, heads, half, apart):
    rows = own_ref.shape[0]
    cols = early_ref.shape[1] - half
    mixed_ref[:, :LANES] = own_ref[:, :LANES].astype(F32)
    mixed_ref[:, LANES : LANES + cols] = early_ref[:, half:].astype(F32)
    mixed_ref[:, LANES + cols :] = own_ref[:, LANES : LANES + cols].astype(F32)
    tail = own_ref[:, own_ref.shape[1] - LANES :].astype(F32)
    turned = turned_rows(tail)
    at_gain = heads + 2 + CONV
    each = gain_ref.shape[1]
    dt_ref[...] = turned[:heads, :rows]
    gain_ref[...] = turned[at_gain : at_gain + 1, :each]
    taps_ref[...] = turned[at_gain + 1 : at_gain + 1 + CONV, :each]
    at = at_gain + 1 + CONV
    sums = jnp.sum(tail, axis=0, keepdims=True) if apart else tail[0:1]
    count = len(head_refs)
    for n, ref in enumerate(head_refs):
        total = sums[:, at + n * heads : at + (n + 1) * heads]
        if apart:
            total = total + sums[:, at + (count + n) * heads : at + (count + n + 1) * heads]
        ref[...] = total


def side_kernel(places, blocks_ref, gain_ref, shared_ref, first_ref, second_ref, taps_ref, *, heads):
    groups, strip, wide = blocks_ref.shape
    per_kv = groups // KV
    blocks = [blocks_ref[b].astype(F32) for b in range(groups)]
    sums = []
    for h in range(KV):
        total = blocks[h * per_kv][:, : 2 * HEAD]
        for b in range(h * per_kv + 1, (h + 1) * per_kv):
            total = total + blocks[b][:, : 2 * HEAD]
        sums.append(total)
    rest = blocks[0]
    for b in range(1, groups):
        rest = rest + blocks[b]
    for part in range(2):
        for h in range(KV):
            at = (part * KV + h) * HEAD
            shared_ref[:, at : at + HEAD] = sums[h][:, part * HEAD : (part + 1) * HEAD]
    shared_ref[:, 2 * KV * HEAD :] = rest[:, 2 * HEAD : wide - LANES]
    turned = turned_rows(rest[:, wide - LANES :])
    first_ref[...] = turned[heads : heads + 1, :strip] / gain_ref[...]
    second_ref[...] = turned[heads + 1 : heads + 2, :strip]
    taps_ref[...] = turned[heads + 2 : heads + 2 + CONV, : taps_ref.shape[1]]


def early_kernel(places, mixed_ref, grad_ref, both_ref, dz_ref, w_ref, terms_ref, gain_ref, *, parts):
    dim = grad_ref.shape[1]
    half = dim // 2
    rows = mixed_ref.shape[1]
    chunk = rows // parts
    tall = dim // parts
    at_z = 2 * LANES
    cols = dz_ref.shape[1]
    step = 2 * TILE
    for i in range(0, rows, step):
        out = lax.dot_general(
            mixed_ref[:, i : i + step], grad_ref[...], ROW_DOT, preferred_element_type=F32
        ).astype(B16)
        for n in range(step // chunk):
            at = (i // chunk + n) * tall
            piece = out[n * chunk : (n + 1) * chunk]
            terms_ref[at : at + chunk, :half] = piece[:, :half]
            terms_ref[at + chunk : at + tall, :half] = piece[:, half:]
    for i in range(0, dim, step):
        r = slice(i, i + step)
        grad = lax.dot_general(both_ref[:, r], dz_ref[...], ROW_DOT, preferred_element_type=F32)
        terms_ref[r, half:] = grad.astype(B16)
        gain_ref[r, :] = jnp.sum(grad * w_ref[r, at_z : at_z + cols].astype(F32), axis=1, keepdims=True)


def small_columns(tile, mine, gain_ref, taps_ref, heads_ref, second_ref, *, heads, groups, parts):
    dim = second_ref.shape[1]
    cols = gain_ref.shape[1]
    wide = taps_ref.shape[1]
    tall = dim // parts
    strip = tall // groups
    at_gain = heads + 2 + CONV
    at = at_gain + 1 + CONV
    lane = iota((8, LANES), 1)
    values = jnp.where(lane < heads, heads_ref[...], 0.0)
    high = values.astype(B16).astype(F32)
    base = jnp.zeros((1, LANES), F32)
    for n in range(3):
        base = base + pltpu.roll(high, at + n * heads, 1)[n : n + 1]
        base = base + pltpu.roll(values - high, at + (3 + n) * heads, 1)[n : n + 1]
    own_row = iota(tile.shape, 0) % tall == mine
    tile[...] = jnp.where(own_row, base, 0.0)

    def columns(first, rows, width):
        pieces = [jnp.zeros((first, width), F32)] + rows
        left = LANES - first - sum(row.shape[0] for row in rows)
        return jnp.concatenate(pieces + [jnp.zeros((left, width), F32)], axis=0).T

    own = columns(at_gain, [gain_ref[0:1, :], taps_ref[:CONV, :cols]], cols)
    each = cols // parts
    for s in range(parts):
        tile[s * tall : s * tall + each, :] += own[s * each : (s + 1) * each]
    side = columns(heads + 2, [taps_ref[:CONV, cols:]], wide - cols)
    each = (wide - cols) // (groups * parts)
    second = columns(heads + 1, [second_ref[0:1, :]], dim)
    for b in range(groups):
        for s in range(parts):
            there = s * tall + b * strip
            n = b * parts + s
            tile[there : there + each, :] += side[n * each : (n + 1) * each]
            tile[there : there + strip, :] += second[n * strip : (n + 1) * strip]


def weight_grad_kernel(
    places, q_ref, kv_ref, z_ref, x_ref, rim_ref, dt_ref, cos_ref, sin_ref, w_ref, both_ref, early_ref,
    *refs, heads, groups, parts, in_strips,
):
    if in_strips:
        small_refs, (pre_ref, terms_ref, tile) = refs[:4], refs[4:]
        small_columns(tile, places[2], *small_refs, heads=heads, groups=groups, parts=parts)
    else:
        tile, pre_ref, terms_ref = refs
    rows = q_ref.shape[0]
    dim = w_ref.shape[0]
    cols = heads * HEAD
    wide = x_ref.shape[1]
    at_z = 2 * LANES
    at_x = at_z + cols
    at_dt = at_x + wide
    for i in range(0, rows, TILE):
        r = slice(i, i + TILE)
        cosine, sine = cos_ref[r, :], sin_ref[r, :]
        q, kv = q_ref[r, :], kv_ref[r, :]
        pre_ref[r, :LANES] = (q * cosine - swap_halves(q) * sine).astype(B16)
        turned = kv * cosine - swap_halves(kv) * sine
        pre_ref[r, LANES : 2 * LANES] = jnp.where(iota(kv.shape, 1) < HEAD, turned, kv).astype(B16)
        pre_ref[r, at_z:at_x] = z_ref[r, :]
        x = x_ref[r, :]
        if i + TILE == rows:
            x = jnp.concatenate([x[: TILE - 8], x[TILE - 8 :] + rim_ref[...]], axis=0)
        pre_ref[r, at_x:at_dt] = x.astype(B16)
        pre_ref[r, at_dt:] = dt_ref[r, :]
    block = dim // groups
    strip = block // parts
    mixed = LANES + cols
    sides = slice(mixed + LANES, mixed + 3 * LANES)
    ends = slice(mixed + 3 * LANES, mixed + 4 * LANES)
    lane = iota((block, LANES), 1)
    for b in range(groups):
        r = slice(b * block, (b + 1) * block)
        x = both_ref[:, r]
        near = lax.dot_general(x, pre_ref[:, :at_z], ROW_DOT, preferred_element_type=F32)
        far = lax.dot_general(x, pre_ref[:, at_x:], ROW_DOT, preferred_element_type=F32)
        gain = jnp.sum(near * w_ref[r, :at_z].astype(F32), axis=1, keepdims=True)
        gain = gain + jnp.sum(far * w_ref[r, at_x:].astype(F32), axis=1, keepdims=True)
        gain = gain + early_ref[r, :]
        terms_ref[r, :LANES] = near[:, :LANES].astype(B16)
        terms_ref[r, LANES:mixed] = far[:, :cols].astype(B16)
        if in_strips:
            for s in range(parts):
                here = slice(s * strip, (s + 1) * strip)
                first = s * groups * strip + b * strip
                there = slice(first, first + strip)
                terms_ref[there, mixed : mixed + LANES] = near[here, LANES:].astype(B16)
                terms_ref[there, sides] = far[here, cols:wide].astype(B16)
                at_gain = iota((strip, LANES), 1) == heads
                tile[there, :] = jnp.where(at_gain, gain[here], tile[there, :])
            tile[r, :] = jnp.where(lane < heads, far[:, wide:], tile[r, :])
        else:
            terms_ref[r, mixed : mixed + LANES] = near[:, LANES:].astype(B16)
            terms_ref[r, sides] = far[:, cols:wide].astype(B16)
            tail = jnp.where(lane < heads, far[:, wide:], tile[r, :])
            terms_ref[r, ends] = jnp.where(lane == heads, gain, tail).astype(B16)
    if in_strips:
        terms_ref[:, ends] = tile[...].astype(B16)


def iota(shape, dim):
    return lax.broadcasted_iota(jnp.int32, shape, dim)


def per_head(columns, pair):
    shape = (columns.shape[0], LANES)
    return jnp.where(
        iota(shape, 1) < HEAD, columns[:, 2 * pair : 2 * pair + 1], columns[:, 2 * pair + 1 : 2 * pair + 2]
    )


def one_head(values, head):
    keep = (iota(values.shape, 1) < HEAD) == (head % 2 == 0)
    return jnp.where(keep, values, jnp.zeros_like(values))


def into_lane(columns, head, column):
    return jnp.where(iota(columns.shape, 1) == head, column, columns)


def silu_slope(v, sig):
    return sig * (1.0 + v * (1.0 - sig))


def tap_window(ext_ref, tap, first, amount, places):
    return ext_ref[first + 8 - (CONV - 1) + tap : first + 8 - (CONV - 1) + tap + amount, :]


def span_kernel(places, begin_ref, pre_ref, rim_ref, taps_ref, params_ref, u_ref, intra_ref, cum_ref, state_ref, ext, xb, *, heads, at_x, at_dt, nstate):
    rows = pre_ref.shape[0]
    cols = heads * HEAD
    first_row, last_begin = places[0], places[1]
    ext[0:8, :] = rim_ref[...]
    ext[8 : 8 + rows, :] = pre_ref[:, at_x:at_dt]
    local = begin_ref[...] - first_row
    row_ids = iota((rows, 1), 0)
    for i in range(0, rows, TILE):
        total = jnp.zeros((TILE, ext.shape[1]), F32)
        for tap in range(CONV):
            seen = row_ids[i : i + TILE] - (CONV - 1) + tap >= local[i : i + TILE]
            window = tap_window(ext, tap, i, TILE, places)
            total = total + jnp.where(seen, window, 0.0) * taps_ref[tap : tap + 1, :]
        u_ref[i : i + TILE, :] = total
        xb[i : i + TILE, :] = (total * jax.nn.sigmoid(total)).astype(B16)
    raw = pre_ref[:, at_dt : at_dt + LANES] + params_ref[0:1, :]
    dt = jnp.maximum(raw, 0.0) + jnp.log1p(jnp.exp(-jnp.abs(raw)))
    lower = (iota((rows, rows), 0) >= iota((rows, rows), 1)).astype(F32)
    cum = jnp.dot(lower, dt * params_ref[1:2, :], precision=HIGHEST, preferred_element_type=F32)
    cum_ref[:, :LANES] = cum
    cum_ref[:, LANES:] = dt
    cum_t, dt_t = cum.T, dt.T
    last = cum[rows - 1 : rows, :]
    closing = row_ids + first_row >= last_begin
    to_end = jnp.where(closing, jnp.exp(last - cum) * dt, 0.0)
    for i in range(0, rows, TILE):
        width = i + TILE
        c = xb[i : i + TILE, cols + nstate : cols + 2 * nstate]
        b = xb[:width, cols : cols + nstate]
        inner = lax.dot_general(c, b, LANE_DOT, preferred_element_type=F32)
        key = iota((TILE, width), 1)
        seen = (key <= iota((TILE, width), 0) + i) & (key >= local[i : i + TILE])
        for pair in range(heads // 2):
            out = []
            for h in (2 * pair, 2 * pair + 1):
                spread = jnp.where(seen, cum[i : i + TILE, h : h + 1] - cum_t[h : h + 1, :width], MASKED)
                weights = (jnp.exp(spread) * inner * dt_t[h : h + 1, :width]).astype(B16)
                out.append(jnp.dot(weights, xb[:width, pair * LANES : (pair + 1) * LANES], preferred_element_type=F32))
            intra_ref[i : i + TILE, pair * LANES : (pair + 1) * LANES] = jnp.where(iota((TILE, LANES), 1) < HEAD, out[0], out[1])
    b_all = xb[:, cols : cols + nstate]
    for pair in range(heads // 2):
        at = slice(pair * LANES, (pair + 1) * LANES)
        closed = (xb[:, at].astype(F32) * per_head(to_end, pair)).astype(B16)
        state_ref[at, :] = lax.dot_general(closed, b_all, ROW_DOT, preferred_element_type=F32).astype(B16)
    decay = jnp.where(last_begin < first_row, jnp.exp(last), 0.0)
    high = decay.astype(B16)
    low = (decay - high.astype(F32)).astype(B16)
    both = jnp.concatenate([jnp.broadcast_to(high.astype(F32), (LANES // 2, LANES)), jnp.broadcast_to(low.astype(F32), (LANES // 2, LANES))], axis=0)
    state_ref[cols : cols + 16, :] = both.T[:16, :].astype(B16)


def span_forward(places, begins, pre, rim, taps, params, heads, at_x, at_dt, nstate):
    rows = pre.shape[0]
    wide = at_dt - at_x
    cols = heads * HEAD
    return call(
        functools.partial(span_kernel, heads=heads, at_x=at_x, at_dt=at_dt, nstate=nstate),
        "span_forward",
        8,
        (places, begins, pre, rim, taps, params),
        (((rows, wide), F32), ((rows, cols), F32), ((rows, 2 * LANES), F32), ((cols + 16, nstate), B16)),
        (((rows + 8, wide), F32), ((rows, wide), B16)),
    )


def decay_of(states_ref, k, head, cols):
    tail = states_ref[k, cols + head - head % 8 : cols + head - head % 8 + 8, :].astype(F32)
    row = tail[head % 8 : head % 8 + 1, :]
    return row[:, 0:1] + row[:, LANES // 2 : LANES // 2 + 1]


def finish_kernel(places, begin_ref, states_ref, u_ref, intra_ref, cum_ref, z_ref, params_ref, gated_ref, v_ref, state_ref, squares_ref, *, heads, nstate):
    rows = u_ref.shape[0]
    cols = heads * HEAD
    state_ref[...] = jnp.zeros_like(state_ref)

    def fold(k):
        for h in range(heads):
            at = slice(h * HEAD, (h + 1) * HEAD)
            state_ref[at, :] = state_ref[at, :] * decay_of(states_ref, k, h, cols) + states_ref[k, at, :].astype(F32)

    pl.loop(0, places[2])(fold)
    carried = begin_ref[...] < places[0]
    for i in range(0, rows, TILE):
        r = slice(i, i + TILE)
        enter = jnp.where(carried[r], jnp.exp(cum_ref[r, :LANES]), 0.0)
        uc = u_ref[r, cols + nstate : cols + 2 * nstate]
        c = (uc * jax.nn.sigmoid(uc)).astype(B16)
        total = jnp.zeros((8, TILE), F32)
        for pair in range(heads // 2):
            at = slice(pair * LANES, (pair + 1) * LANES)
            y = lax.dot_general(c, state_ref[at, :].astype(B16), LANE_DOT, preferred_element_type=F32)
            ux = u_ref[r, at]
            x = ux * jax.nn.sigmoid(ux)
            skip = per_head(params_ref[2:3, :], pair)
            v = intra_ref[r, at] + per_head(enter, pair) * y + skip * x
            z = z_ref[r, at]
            gated = (v * (z * jax.nn.sigmoid(z))).astype(B16)
            v_ref[r, at] = v
            gated_ref[r, at] = gated
            g = gated.astype(F32)
            total = total + lax.dot_general(jnp.ones((8, LANES), F32), g * g, LANE_DOT, precision=HIGHEST, preferred_element_type=F32)
        squares_ref[:, r] = total


def span_finish(places, begins, states, u, intra, cum, z, params, heads, nstate):
    rows = u.shape[0]
    cols = heads * HEAD
    return call(
        functools.partial(finish_kernel, heads=heads, nstate=nstate),
        "span_finish",
        7,
        (places, begins, states, u, intra, cum, z, params),
        (((rows, cols), B16), ((rows, cols), F32), ((cols, nstate), F32), ((8, rows), F32)),
        (),
    )


def gate_back_kernel(places, begin_ref, scaled_ref, gated_ref, squares_ref, u_ref, cum_ref, z_ref, v_ref, send_ref, *refs, heads, nstate, ssm_all):
    back_ref, dz_ref, state_ref, eg = refs[-4:]
    total = refs[0][...]
    for ref in refs[1:-4]:
        total = total + ref[...]
    rows = u_ref.shape[0]
    cols = heads * HEAD
    carried = begin_ref[...] < places[0]
    squares, stat = squares_ref[...].T, total.T
    uc = u_ref[:, cols + nstate : cols + 2 * nstate]
    c = (uc * jax.nn.sigmoid(uc)).astype(B16)
    for i in range(0, rows, TILE):
        r = slice(i, i + TILE)
        enter = jnp.where(carried[r], jnp.exp(cum_ref[r, :LANES]), 0.0)
        inverse = lax.rsqrt(squares[r, 0:1] / ssm_all + EPSILON)
        mean = stat[r, 0:1] / ssm_all
        for pair in range(heads // 2):
            at = slice(pair * LANES, (pair + 1) * LANES)
            z = z_ref[r, at]
            sig = jax.nn.sigmoid(z)
            scaled = gated_ref[r, at].astype(F32) * inverse
            gg = (inverse * (scaled_ref[r, at] - scaled * mean)).astype(B16)
            back_ref[r, at] = gg
            gg = gg.astype(F32)
            dz_ref[r, at] = (gg * v_ref[r, at] * silu_slope(z, sig)).astype(B16)
            eg[r, at] = (gg * (z * sig) * per_head(enter, pair)).astype(B16)
    state_ref[:cols, :] = lax.dot_general(eg[...], c, ROW_DOT, preferred_element_type=F32).astype(B16)
    state_ref[cols:, :] = send_ref[...]


def gate_back(places, begins, scaled, gated, squares, stats, u, cum, z, v, send, heads, nstate, ssm_all):
    rows = u.shape[0]
    cols = heads * HEAD
    return call(
        functools.partial(gate_back_kernel, heads=heads, nstate=nstate, ssm_all=ssm_all),
        "gate_back",
        5,
        (places, begins, scaled, gated, squares, u, cum, z, v, send) + stats,
        (((rows, cols), B16), ((rows, cols), B16), ((cols + send.shape[0], nstate), B16)),
        (((rows, cols), B16),),
    )


def back_kernel(places, begin_ref, g_ref, z_ref, pre_ref, rim_ref, u_ref, cum_ref, state_ref, states_ref, grads_ref, taps_ref, params_ref, gx_ref, gdt_ref, rim_out, taps_out, small_out, ext, gext, xb, gb, later, dxb, lane_sum, cols_sum, *, heads, at_x, at_dt, nstate):
    rows = u_ref.shape[0]
    cols = heads * HEAD
    wide = at_dt - at_x
    count = states_ref.shape[0]
    pairs = heads // 2
    first_row, last_begin, mine = places[0], places[1], places[2]
    later[...] = jnp.zeros_like(later)

    def fold(n):
        k = count - 1 - n
        for h in range(heads):
            at = slice(h * HEAD, (h + 1) * HEAD)
            later[at, :] = later[at, :] * decay_of(states_ref, k, h, cols) + grads_ref[k, at, :].astype(F32)

    pl.loop(0, count - 1 - mine)(fold)
    local = begin_ref[...] - first_row
    row_ids = iota((rows, 1), 0)
    cum = cum_ref[:, :LANES]
    dt = cum_ref[:, LANES:]
    cum_t, dt_t = cum.T, dt.T
    last = cum[rows - 1 : rows, :]
    leave = jnp.where(row_ids + first_row >= last_begin, jnp.exp(last - cum), 0.0)
    enter = jnp.where(begin_ref[...] < first_row, jnp.exp(cum), 0.0)
    to_end = leave * dt
    for i in range(0, rows, TILE):
        r = slice(i, i + TILE)
        u = u_ref[r, :]
        xb[r, :] = (u * jax.nn.sigmoid(u)).astype(B16)
        z = z_ref[r, :]
        gb[r, :] = (g_ref[r, :].astype(F32) * (z * jax.nn.sigmoid(z))).astype(B16)
    dxb[...] = jnp.zeros_like(dxb)
    cols_sum[...] = jnp.zeros_like(cols_sum)
    b_at = slice(cols, cols + nstate)
    c_at = slice(cols + nstate, cols + 2 * nstate)
    for i in range(0, rows, TILE):
        width = i + TILE
        r = slice(i, i + TILE)
        inner = lax.dot_general(xb[r, c_at], xb[:width, b_at], LANE_DOT, preferred_element_type=F32)
        key = iota((TILE, width), 1)
        seen = (key <= iota((TILE, width), 0) + i) & (key >= local[r])
        grad_inner = jnp.zeros((TILE, width), F32)
        sums = jnp.zeros((TILE, LANES), F32)
        for h in range(heads):
            at = slice(h // 2 * LANES, (h // 2 + 1) * LANES)
            g = one_head(gb[r, at], h)
            spread = jnp.where(seen, cum[r, h : h + 1] - cum_t[h : h + 1, :width], MASKED)
            decays = jnp.exp(spread)
            steps = dt_t[h : h + 1, :width]
            pairing = lax.dot_general(g, xb[:width, at], LANE_DOT, preferred_element_type=F32)
            paired = pairing * decays
            grad_inner = grad_inner + paired * steps
            both = paired * inner
            cols_sum[h : h + 1, :width] += jnp.sum(both, axis=0, keepdims=True)
            sums = into_lane(sums, h, jnp.sum(both * steps, axis=1, keepdims=True))
            weights = (decays * inner * steps).astype(B16)
            dxb[:width, at] += lax.dot_general(weights, g, ROW_DOT, preferred_element_type=F32)
        lane_sum[r, :] = sums
        grad_inner = grad_inner.astype(B16)
        dxb[r, c_at] += jnp.dot(grad_inner, xb[:width, b_at], preferred_element_type=F32)
        dxb[:width, b_at] += lax.dot_general(grad_inner, xb[r, c_at], ROW_DOT, preferred_element_type=F32)
    from_cols = jnp.concatenate([cols_sum[...], jnp.zeros((LANES - 8, rows), F32)], axis=0).T
    state_b = state_ref[...].astype(B16)
    later_b = later[...].astype(B16)
    entered = jnp.zeros((rows, LANES), F32)
    closed = jnp.zeros((rows, LANES), F32)
    skips = jnp.zeros((1, LANES), F32)
    chained = jnp.zeros((1, LANES), F32)
    for pair in range(pairs):
        at = slice(pair * LANES, (pair + 1) * LANES)
        x = xb[:, at].astype(F32)
        g = gb[:, at].astype(F32)
        y = lax.dot_general(xb[:, c_at], state_b[at, :], LANE_DOT, preferred_element_type=F32)
        q = lax.dot_general(xb[:, b_at], later_b[at, :], LANE_DOT, preferred_element_type=F32)
        ends = per_head(to_end, pair)
        dxb[:, c_at] += jnp.dot((g * per_head(enter, pair)).astype(B16), state_b[at, :], preferred_element_type=F32)
        dxb[:, b_at] += jnp.dot((x * ends).astype(B16), later_b[at, :], preferred_element_type=F32)
        dxb[:, at] += ends * q + g * per_head(params_ref[2:3, :], pair)
        gy, xq, gx = g * y, x * q, jnp.sum(g * x, axis=0, keepdims=True)
        kept = jnp.sum(later[at, :] * state_ref[at, :], axis=1, keepdims=True)
        for h in (2 * pair, 2 * pair + 1):
            entered = into_lane(entered, h, jnp.sum(one_head(gy, h), axis=1, keepdims=True))
            closed = into_lane(closed, h, jnp.sum(one_head(xq, h), axis=1, keepdims=True))
            skips = into_lane(skips, h, jnp.sum(one_head(gx, h), axis=1, keepdims=True))
            half = slice(h % 2 * HEAD, (h % 2 + 1) * HEAD)
            chained = into_lane(chained, h, jnp.sum(kept[half], axis=0, keepdims=True))
    decay = jnp.where(last_begin < first_row, jnp.exp(last), 0.0)
    ended = closed * to_end
    grad_cum = lane_sum[...] - from_cols * dt + entered * enter - ended
    at_last = jnp.sum(ended, axis=0, keepdims=True) + decay * chained
    grad_cum = grad_cum + jnp.where(row_ids == rows - 1, at_last, 0.0)
    upper = (iota((rows, rows), 0) <= iota((rows, rows), 1)).astype(F32)
    grad_log = jnp.dot(upper, grad_cum, precision=HIGHEST, preferred_element_type=F32)
    rate = params_ref[1:2, :]
    grad_dt = from_cols + closed * leave + grad_log * rate
    grad_raw = grad_dt * jax.nn.sigmoid(pre_ref[:, at_dt : at_dt + LANES] + params_ref[0:1, :])
    grad_raw = jnp.where(iota((rows, LANES), 1) < heads, grad_raw, 0.0)
    gdt_ref[...] = grad_raw.astype(B16)
    small_out[0:1, :] = jnp.sum(grad_log * dt, axis=0, keepdims=True) * rate
    small_out[1:2, :] = jnp.sum(grad_raw, axis=0, keepdims=True)
    small_out[2:3, :] = skips
    small_out[3:8, :] = jnp.zeros((5, LANES), F32)
    ext[0:8, :] = rim_ref[...]
    ext[8 : 8 + rows, :] = pre_ref[:, at_x:at_dt]
    gext[...] = jnp.zeros_like(gext)
    taps_out[...] = jnp.zeros_like(taps_out)
    for i in range(0, rows, TILE):
        r = slice(i, i + TILE)
        u = u_ref[r, :]
        du = dxb[r, :] * silu_slope(u, jax.nn.sigmoid(u))
        for tap in range(CONV):
            seen = row_ids[r] - (CONV - 1) + tap >= local[r]
            part = jnp.where(seen, du, 0.0)
            taps_out[tap : tap + 1, :] += jnp.sum(part * tap_window(ext, tap, i, TILE, places), axis=0, keepdims=True)
            at = 8 - (CONV - 1) + tap + i
            gext[at : at + TILE, :] += part * taps_ref[tap : tap + 1, :]
    rim_out[...] = gext[0:8, :]
    gx_ref[...] = gext[8:, :]


def span_back(places, begins, back, z, pre, rim, u, cum, state, states, grads, taps, params, heads, at_x, at_dt, nstate, waits):
    rows = u.shape[0]
    cols = heads * HEAD
    wide = at_dt - at_x
    return call(
        functools.partial(back_kernel, heads=heads, at_x=at_x, at_dt=at_dt, nstate=nstate),
        "span_back",
        16,
        (places, begins, back, z, pre, rim, u, cum, state, states, grads, taps, params),
        (((rows, wide), F32), ((rows, LANES), B16), ((8, wide), F32), ((8, wide), F32), ((8, LANES), F32)),
        (((rows + 8, wide), F32), ((rows + 8, wide), F32), ((rows, wide), B16), ((rows, cols), B16),
         ((cols, nstate), F32), ((rows, wide), F32), ((rows, LANES), F32), ((8, rows), F32)),
        waits,
    )


def shards(
    x_in,
    lengths,
    norm1_gain,
    w_mix_in,
    w_dt,
    w_shared,
    conv_x,
    conv_bc,
    a_log,
    dt_bias,
    d_skip,
    gate_gain,
    w_out,
    norm2_gain,
    w_gate,
    w_up,
    w_down,
    d_out,
):
    tok_rows = x_in.shape[0]
    groups = lax.axis_size("branch")
    branch_id = lax.axis_index("branch")
    seq_id = lax.axis_index("seq")
    seq_rows = tok_rows * groups
    group_first = seq_id * seq_rows
    att_heads = HEADS_ATT // groups
    att_cols = att_heads * HEAD
    ssm_heads = w_dt.shape[1]
    ssm_cols = ssm_heads * HEAD
    kv_cols = KV * HEAD
    f32 = jnp.float32
    bf16 = jnp.bfloat16
    dim = x_in.shape[1]
    parts = lax.axis_size("seq")
    chunk = w_out.shape[0] // groups
    att_chunks = parts * att_cols // (att_cols + ssm_cols)
    ssm_chunks = parts - att_chunks
    strip = dim // (groups * parts)
    hidden_all = w_gate.shape[1]
    hidden_a = hidden_all * att_cols // ((att_cols + ssm_cols) * groups)
    hidden_s = hidden_all // groups - hidden_a
    hidden_b = hidden_a + hidden_s

    def spot(c):
        first = groups * att_chunks
        if c < first:
            return (c // att_chunks) * parts + c % att_chunks
        return ((c - first) // ssm_chunks) * parts + att_chunks + (c - first) % ssm_chunks

    to_heads = [((c % groups) * parts + c // groups, spot(c)) for c in range(groups * parts)]
    from_heads = [(spot(c), c) for c in range(groups * parts)]

    def branch_parts(part):
        routes = [[(i, i ^ k) for i in range(groups)] for k in range(1, groups)]
        return (part,) + tuple(lax.ppermute(part, "branch", route) for route in routes)

    def branch_exchange(blocks):
        return lax.all_to_all(blocks, "branch", 0, 0, tiled=True)

    def branch_gather(part):
        copies = branch_exchange(jnp.broadcast_to(part[None], (groups,) + part.shape))
        return copies.reshape((groups * part.shape[0],) + part.shape[1:])

    def branch_scatter(terms):
        blocks = terms.astype(bf16).reshape((groups, -1) + terms.shape[1:])
        return jnp.sum(lax.all_to_all(blocks, "branch", 0, 0, tiled=True).astype(f32), axis=0)

    kv_head = branch_id * att_heads // (HEADS_ATT // KV)
    side_cols = w_shared.shape[1] - 2 * kv_cols
    w1_cols = w_mix_in.shape[1] + 2 * HEAD + side_cols + LANES
    turned = w_dt.shape[0] % LANES == 0
    w1_part = call(
        functools.partial(assemble_kernel, att_cols=att_cols, turned=turned),
        "assemble",
        1,
        (kv_head[None], w_mix_in, w_shared, w_dt.T if turned else w_dt),
        (((w_mix_in.shape[0], w1_cols), B16),),
        (),
    )[0]
    w1 = lax.all_gather(w1_part, "seq", axis=0, tiled=True)

    def own_columns(w):
        return [
            lax.dynamic_slice_in_dim(w, branch_id * hidden_a, hidden_a, 1),
            lax.dynamic_slice_in_dim(w, groups * hidden_a + branch_id * hidden_s, hidden_s, 1),
        ]

    row_part = jnp.concatenate(
        [
            lax.dynamic_slice_in_dim(w_out, branch_id * chunk, chunk, 0),
            lax.dynamic_slice_in_dim(w_down, branch_id * chunk, chunk, 0),
        ],
        axis=0,
    )
    row_part = lax.ppermute(row_part, ("branch", "seq"), to_heads)
    out_part = row_part[:chunk]
    mlp_part = jnp.concatenate(
        [row_part[chunk:], jnp.concatenate(own_columns(w_gate) + own_columns(w_up), axis=1)], axis=0
    )
    x_rows = x_in.astype(f32)
    scaled1, inverse1 = rms_parts(x_rows)
    normed1 = (scaled1 * norm1_gain).astype(bf16)
    both_in = branch_gather(jnp.concatenate([normed1, d_out], axis=1))
    d_out_g = both_in[:, dim:]
    before = from_behind(both_in[seq_rows - 16 :, :dim], "seq", 1)
    row_ids = group_first + jnp.arange(seq_rows, dtype=jnp.int32)
    seq_ends = jnp.cumsum(lengths)

    def begin_of(ids):
        return jnp.max(jnp.where(seq_ends <= ids[..., None], seq_ends, 0), axis=-1)

    def end_of(ids):
        return jnp.min(jnp.where(seq_ends > ids[..., None], seq_ends, seq_rows * parts), axis=-1)

    begins = begin_of(row_ids)
    ends = end_of(row_ids)
    position = row_ids - begins
    row_last = group_first + seq_rows - 1
    begin_first, begin_last = (begin_of(group_first), begin_of(row_last))
    end_first, end_last = (end_of(group_first), end_of(row_last))
    here = seq_id
    query_lo = begin_first // seq_rows
    query_clear = jnp.minimum(jnp.maximum(query_lo, -(-begin_last // seq_rows)), here)
    query_bounds = jnp.stack([query_lo, query_clear, group_first, here, here + 1])
    key_hi = -(-end_last // seq_rows)
    key_clear = jnp.maximum(here + 1, jnp.minimum(end_first // seq_rows, key_hi))
    key_bounds = jnp.stack([here, here + 1, group_first, key_clear, key_hi])
    places = jnp.stack([group_first, begin_last, seq_id])
    begins_col, begins_row, ends_col = (begins[:, None], begins[None, :], ends[:, None])
    at_dt = ssm_cols + side_cols
    nstate = conv_bc.shape[1] // 2
    taps = jnp.pad(jnp.concatenate([conv_x, conv_bc], axis=1), ((0, 8 - CONV), (0, 0)))
    params = jnp.stack([dt_bias, -jnp.exp(a_log), d_skip])
    params = jnp.pad(params, ((0, 5), (0, LANES - ssm_heads)))
    ssm_all = gate_gain.shape[0]
    gain_row = lax.dynamic_slice_in_dim(gate_gain, branch_id * ssm_cols, ssm_cols, 0)[None, :]
    cosine, sine = rotate_tables(position)
    packed = chunk if chunk % 16 == 0 and strip % 16 == 0 else 0
    kv_rows = seq_rows + packed * dim // LANES
    queries, kv, z_pre, pre, rim = call(
        project_kernel,
        "project",
        5,
        (places, both_in, before, w1, cosine, sine, out_part),
        (
            ((seq_rows, LANES), B16),
            ((kv_rows, LANES), B16),
            ((seq_rows, ssm_cols), F32),
            ((seq_rows, at_dt + LANES), F32),
            ((8, at_dt), F32),
        ),
        (),
        (
            begins_col,
            begins_row,
            ends_col,
            query_bounds,
            key_bounds,
            taps,
            params,
            gain_row,
            mlp_part,
        ),
    )
    kv_all = lax.all_gather(kv, "seq", axis=0)
    w_out_b = kv_all if packed else lax.all_gather(out_part, "seq", axis=0, tiled=True)
    mlp_all = lax.all_gather(mlp_part, "seq", axis=0)
    if packed:
        mlp_weights, down_weights = ((mlp_all,), mlp_all)
        mlp_scratch = (
            ((dim, 2 * hidden_b), B16),
            ((parts * chunk, dim), B16),
            ((seq_rows, 2 * hidden_b), B16),
        )
    else:
        down_weights = mlp_all[:, :chunk].reshape(parts * chunk, dim)
        mlp_weights = (mlp_all[:, chunk:].reshape(dim, 2 * hidden_b), down_weights)
        mlp_scratch = ()
    u, intra, cum, state = span_forward(
        places, begins_col, pre, rim, taps, params, ssm_heads, 0, at_dt, nstate
    )
    states = lax.all_gather(state, "seq", axis=0)
    attn_out, lse, q_send = attend(
        queries, kv_all, begins_row, query_bounds, att_heads, seq_rows
    )
    q_all = lax.all_gather(q_send, "seq", axis=0)
    gated_b, gated_v, state_in, squares = span_finish(
        places, begins_col, states, u, intra, cum, z_pre, params, ssm_heads, nstate
    )

    out_shape = (parts * chunk, dim)
    mixed_out, out_terms, squares, *held = call(
        functools.partial(mix_out_kernel, ssm_all=ssm_all, chunk=packed),
        "mix_out",
        3,
        (places, attn_out, gated_b, gain_row, w_out_b) + branch_parts(squares),
        (((seq_rows, att_cols + ssm_cols), B16), ((seq_rows, dim), B16), ((8, seq_rows), F32))
        + (((out_shape, B16),) if packed else ()),
        (),
    )
    w_out_b = held[0] if packed else w_out_b
    projected = branch_scatter(out_terms)
    middle = x_rows + projected
    scaled2, inverse2 = rms_parts(middle)
    normed2 = branch_gather((scaled2 * norm2_gain).astype(bf16))
    middle_shape = (parts, chunk + dim // parts, dim) if packed else (seq_rows, 2 * hidden_b)
    hidden, mlp_middle, mlp_back = call(
        functools.partial(mlp_kernel, chunk=packed, groups=groups),
        "mlp",
        11,
        (places, normed2, both_in) + mlp_weights,
        (
            ((seq_rows, hidden_b), B16),
            (middle_shape, B16),
            ((seq_rows, dim), B16),
        ),
        mlp_scratch,
    )
    def over_rows(left, right):
        return lax.dot_general(
            left, right, (((0,), (0,)), ((), ())), preferred_element_type=f32
        ).astype(bf16)

    def strips(rows_all):
        wide = rows_all.reshape((groups, parts, strip) + rows_all.shape[1:])
        return jnp.swapaxes(wide, 0, 1).reshape((parts, groups * strip) + rows_all.shape[1:])

    if packed:
        mlp_terms = mlp_middle
    else:
        mlp_terms = jnp.concatenate(
            [
                over_rows(hidden, d_out_g).reshape(parts, chunk, dim),
                strips(over_rows(normed2, mlp_middle)),
            ],
            axis=1,
        )
    mlp_own = lax.psum_scatter(mlp_terms, "seq", scatter_dimension=0)
    grad_middle, grad_copies, grad_n2 = call(
        norm_back_kernel,
        "norm_back",
        2,
        (
            places,
            branch_exchange(mlp_back.reshape(groups, tok_rows, dim)),
            middle,
            d_out,
            norm2_gain[None, :],
        ),
        (((tok_rows, dim), F32), ((groups, tok_rows, dim), B16), ((8, dim), F32)),
        (),
        (q_all,),
    )
    grad_proj = branch_exchange(grad_copies).reshape(seq_rows, dim)
    g_pack, g_send, grad_scaled, stat, grad_gain = call(
        functools.partial(mix_back_kernel, heads=att_heads, ssm_all=ssm_all),
        "mix_back",
        5,
        (places, grad_proj, w_out_b, attn_out, lse, gated_b, squares, gain_row),
        (
            ((seq_rows, att_heads * LANES), B16),
            (q_send.shape, B16),
            ((seq_rows, ssm_cols), F32),
            ((8, seq_rows), F32),
            ((8, ssm_cols), F32),
        ),
        (((seq_rows, LANES), F32),),
    )
    stats = branch_parts(stat)
    grad_gate_gain = grad_gain[0]

    def all_columns(blocks):
        blocks = jnp.swapaxes(blocks, 0, 1)
        return jnp.concatenate(
            [blocks[:, :, :hidden_a].reshape(strip, -1), blocks[:, :, hidden_a:].reshape(strip, -1)],
            axis=1,
        )

    back_ssm, grad_z, grad_state = gate_back(
        places, begins_col, grad_scaled, gated_b, squares, stats, u, cum, z_pre, gated_v, g_send, ssm_heads, nstate, ssm_all
    )
    grad_states = lax.all_gather(grad_state, "seq", axis=0)
    grad_q = query_grad(
        queries, g_pack, kv_all, begins_col, query_bounds, att_heads, seq_rows, (grad_state, mlp_own)
    )
    y_terms = call(
        functools.partial(down_kernel, chunk=packed),
        "down",
        3,
        (places, hidden, down_weights),
        (((seq_rows, dim), B16),),
        (),
        (grad_state,),
    )[0]
    y_blocks = branch_exchange(y_terms.reshape(groups, tok_rows, dim))
    if packed:
        early_terms, early_gain = call(
            functools.partial(early_kernel, parts=parts),
            "early",
            3,
            (places, mixed_out, grad_proj, both_in, grad_z, w1),
            (((dim, dim // 2 + ssm_cols), B16), ((dim, 1), F32)),
            (),
        )
        early_terms = early_terms.reshape(parts, dim // parts, dim // 2 + ssm_cols)
    else:
        out_rows = over_rows(mixed_out, grad_proj).reshape(parts, chunk, dim)
        z_grad = lax.dot_general(both_in[:, :dim], grad_z, ROW_DOT, preferred_element_type=f32)
        at_z = 2 * LANES
        z_weight = w1[:, at_z : at_z + ssm_cols].astype(f32)
        early_gain = jnp.sum(z_grad * z_weight, axis=1, keepdims=True)
        early_terms = jnp.concatenate(
            [
                jnp.concatenate([out_rows[:, :, : dim // 2], out_rows[:, :, dim // 2 :]], axis=1),
                z_grad.astype(bf16).reshape(parts, dim // parts, ssm_cols),
            ],
            axis=2,
        )
    early_own = lax.psum_scatter(early_terms, "seq", scatter_dimension=0)
    grad_w_down = lax.ppermute(mlp_own[:chunk], ("branch", "seq"), from_heads)
    own_gu = branch_exchange(mlp_own[chunk:].reshape(groups, strip, 2 * hidden_b))
    grad_w_gate = all_columns(own_gu[:, :, :hidden_b]).astype(f32)
    grad_w_up = all_columns(own_gu[:, :, hidden_b:]).astype(f32)
    grad_xbc, grad_dt, rim_back, grad_taps, grad_small = span_back(
        places,
        begins_col,
        back_ssm,
        z_pre,
        pre,
        rim,
        u,
        cum,
        state_in,
        states,
        grad_states,
        taps,
        params,
        ssm_heads,
        0,
        at_dt,
        nstate,
        (grad_q, early_terms, y_terms),
    )
    rim_back = from_behind(rim_back, "seq", -1)
    grad_kv = key_grad(
        kv, q_all, grad_states, ssm_cols, ends_col, key_bounds, att_heads, seq_rows, (grad_dt,)
    )
    tall = groups * strip
    bc_each = conv_bc.shape[1] // (groups * parts)
    x_each = ssm_cols // parts
    in_strips = packed > 0
    if in_strips:
        small = (grad_gain, grad_taps, grad_small, grad_n2)
    else:
        grad_conv_x, grad_conv_bc = (grad_taps[:CONV, :ssm_cols], grad_taps[:CONV, ssm_cols:])
        def to_column(vector, rows_each):
            padded = jnp.pad(vector.reshape(parts, rows_each), ((0, 0), (0, tall - rows_each)))
            return padded[:, :, None]

        def to_columns(matrix, rows_each):
            wide = jnp.swapaxes(matrix.reshape(matrix.shape[0], parts, rows_each), 0, 1)
            wide = jnp.pad(wide, ((0, 0), (0, 0), (0, tall - rows_each)))
            return jnp.swapaxes(wide, 1, 2)

        bc_wide = grad_conv_bc.reshape(CONV, groups, parts, bc_each)
        bc_wide = jnp.pad(bc_wide, ((0, 0), (0, 0), (0, 0), (0, strip - bc_each)))
        bc_wide = jnp.transpose(bc_wide, (2, 1, 3, 0)).reshape(parts, tall, CONV)
        heads3 = grad_small[:3, :ssm_heads].reshape(3 * ssm_heads)
        heads3 = jnp.broadcast_to(heads3[None, None, :], (parts, tall, 3 * ssm_heads))
        small = jnp.concatenate(
            [
                jnp.zeros((parts, tall, ssm_heads + 1), f32),
                strips(grad_n2[0][:, None]),
                bc_wide,
                to_column(grad_gate_gain, x_each),
                to_columns(grad_conv_x, x_each),
                heads3,
            ],
            axis=2,
        )
        small = jnp.pad(small, ((0, 0), (0, 0), (0, LANES - small.shape[2]))).reshape(dim, LANES)
        small = (small,)
    late_cols = w1_cols - ssm_cols
    grad_pre, terms1 = call(
        functools.partial(
            weight_grad_kernel, heads=ssm_heads, groups=groups, parts=parts, in_strips=in_strips
        ),
        "weight_grad",
        7,
        (places, grad_q, grad_kv, grad_z, grad_xbc, rim_back, grad_dt, cosine, sine, w1, both_in, early_gain)
        + small,
        (((seq_rows, w1_cols), B16), ((dim, late_cols), B16)),
        (((dim, LANES), F32),) if in_strips else (),
        (own_gu, grad_w_down),
    )
    mixed_cols = att_cols + ssm_cols
    at_s = mixed_cols + 2 * HEAD + side_cols
    if in_strips:
        terms1 = terms1.reshape(parts, tall, late_cols)
    else:
        tail = terms1[:, at_s:].reshape(parts, tall, LANES)
        gain_column = strips(terms1[:, at_s + ssm_heads][:, None])
        lane = jnp.arange(LANES)
        terms1 = jnp.concatenate(
            [
                terms1[:, :mixed_cols].reshape(parts, tall, mixed_cols),
                strips(terms1[:, mixed_cols:at_s]),
                jnp.where(lane == ssm_heads, gain_column, tail),
            ],
            axis=2,
        )
    own1 = lax.psum_scatter(terms1, "seq", scatter_dimension=0)
    group_terms, early_own = call(
        group_back_kernel,
        "group_back",
        4,
        (places, grad_pre, w1, early_own),
        (((seq_rows, dim), B16), (early_own.shape, B16)),
        (),
    )
    grad_normed1 = branch_scatter(group_terms)
    y_out = call(
        add_blocks_kernel,
        "add_blocks",
        1,
        (places, y_blocks, middle),
        (((tok_rows, dim), B16),),
        (),
        (group_terms,),
    )[0]
    out_own = jnp.concatenate(
        [early_own[:chunk, : dim // 2], early_own[chunk:, : dim // 2]], axis=1
    )
    grad_w_out = lax.ppermute(out_own, ("branch", "seq"), from_heads).astype(f32)
    own_gain = lax.dynamic_slice_in_dim(norm1_gain, (branch_id * parts + seq_id) * strip, strip, 0)
    side_blocks = branch_exchange(own1[:, mixed_cols:].reshape(groups, strip, -1))
    head_row = ((1, ssm_heads), F32)
    grad_mix, grad_dt_w, grad_gain_g, grad_cx, grad_a_log, grad_dt_bias, grad_skip = call(
        functools.partial(own_kernel, heads=ssm_heads, half=dim // 2, apart=in_strips),
        "own",
        2,
        (places, own1, early_own),
        (
            ((tall, w_mix_in.shape[1]), F32),
            ((ssm_heads, tall), F32),
            ((1, x_each), F32),
            ((CONV, x_each), F32),
            head_row,
            head_row,
            head_row,
        ),
        (),
    )
    grad_shared, first_gain, second_gain, grad_cbc = call(
        functools.partial(side_kernel, heads=ssm_heads),
        "side",
        1,
        (places, side_blocks, own_gain[None, :]),
        (
            ((strip, w_shared.shape[1]), F32),
            ((1, strip), F32),
            ((1, strip), F32),
            ((CONV, bc_each), F32),
        ),
        (),
    )
    grad_x1, unused_n1 = rms_backward(grad_normed1, scaled1, inverse1, norm1_gain)
    return (
        y_out,
        grad_middle + grad_x1,
        first_gain[0],
        grad_mix,
        grad_dt_w.T,
        grad_shared,
        grad_cx,
        grad_cbc,
        grad_a_log[0],
        grad_dt_bias[0],
        grad_skip[0],
        grad_gain_g[0],
        grad_w_out,
        second_gain[0],
        grad_w_gate,
        grad_w_up,
        grad_w_down.astype(f32),
    )


def solution(mesh):
    in_specs = (
        P(("seq", "branch"), None),
        P(),
        P(),
        P("seq", "branch"),
        P("seq", "branch"),
        P("seq", None),
        P(None, "branch"),
        P(),
        P("branch"),
        P("branch"),
        P("branch"),
        P(),
        P("seq", None),
        P(),
        P("seq", None),
        P("seq", None),
        P("seq", None),
        P(("seq", "branch"), None),
    )
    out_specs = (
        P(("seq", "branch"), None),
        P(("seq", "branch"), None),
        P(("branch", "seq")),
        P("seq", "branch"),
        P("seq", "branch"),
        P(("branch", "seq"), None),
        P(None, ("branch", "seq")),
        P(None, ("branch", "seq")),
        P("branch"),
        P("branch"),
        P("branch"),
        P(("branch", "seq")),
        P(("branch", "seq"), None),
        P(("branch", "seq")),
        P(("branch", "seq"), None),
        P(("branch", "seq"), None),
        P(("branch", "seq"), None),
    )
    return jax.shard_map(shards, mesh=mesh, in_specs=in_specs, out_specs=out_specs, check_vma=False)
```

```python
import functools

import jax
import jax.numpy as jnp
from jax import lax
from jax.experimental import pallas as pl
from jax.experimental.pallas import tpu as pltpu
from jax.sharding import PartitionSpec as P

HEADS_ATT = 8
KV = 2
HEAD = 64
CONV = 4
LANES = 128
TILE = 128
MASKED = -1e30
HIGHEST = lax.Precision.HIGHEST
EPSILON = 1e-06
SCORE_SCALE = 0.125
ROPE_BASE = 1000000.0
F32 = jnp.float32
B16 = jnp.bfloat16
LANE_DOT = (((1,), (1,)), ((), ()))
ROW_DOT = (((0,), (0,)), ((), ()))


VMEM_SPEC = pl.BlockSpec(memory_space=pltpu.VMEM)
SMEM_SPEC = pl.BlockSpec(memory_space=pltpu.SMEM)
ANY_SPEC = pl.BlockSpec(memory_space=pl.ANY)


def from_behind(block, axis, distance):
    devices = range(lax.axis_size(axis))
    route = [(i - distance, i) for i in devices if i - distance in devices]
    return lax.ppermute(block, axis, route)


def rms_parts(value):
    inverse = lax.rsqrt(jnp.mean(value * value, axis=-1, keepdims=True) + EPSILON)
    return (value * inverse, inverse)


def rms_backward(grad_out, scaled, inverse, gain_vec):
    grad_scaled = grad_out * gain_vec
    grad_in = inverse * (
        grad_scaled - scaled * jnp.mean(grad_scaled * scaled, axis=-1, keepdims=True)
    )
    return (grad_in, jnp.sum(grad_out * scaled, axis=0))


def rotate_tables(position):
    half = HEAD // 2
    inverse = ROPE_BASE ** (-jnp.arange(half, dtype=jnp.float32) / half)
    angles = position.astype(jnp.float32)[:, None] * inverse[None, :]
    cosine, sine = (jnp.cos(angles), jnp.sin(angles))
    return (
        jnp.concatenate([cosine] * (LANES // half), axis=1),
        jnp.concatenate([-sine, sine] * (LANES // HEAD), axis=1),
    )


def swap_halves(values):
    half = HEAD // 2
    lane = lax.broadcasted_iota(jnp.int32, values.shape, 1)
    return jnp.where(
        lane % HEAD < half, pltpu.roll(values, LANES - half, 1), pltpu.roll(values, half, 1)
    )


def call(kernel, name, micros, args, outs, scratch, waits=()):
    given, held = (len(args), len(waits))

    def body(*refs):
        kernel(*refs[:given], *refs[given + held :])

    def padded(shape, kind):
        shape = (1,) * (2 - len(shape)) + tuple(shape)
        wide = -(-shape[-1] // LANES) * LANES
        tall = -(-shape[-2] // 16) * 16
        return functools.reduce(lambda a, b: a * b, shape[:-2], 1) * tall * wide * jnp.dtype(kind).itemsize

    held_bytes = [padded(a.shape, a.dtype) for a in args[1:]]
    held_bytes += [padded(s, d) for s, d in tuple(outs) + tuple(scratch)]
    limit = 56 << 20
    if name == "mix_out":
        limit = min(limit, sum(held_bytes) + (8 << 20))
    result = pl.pallas_call(
        body,
        out_shape=tuple(jax.ShapeDtypeStruct(s, d) for s, d in outs),
        in_specs=[SMEM_SPEC] + [VMEM_SPEC] * (given - 1) + [ANY_SPEC] * held,
        out_specs=tuple(VMEM_SPEC for _ in outs),
        scratch_shapes=[pltpu.VMEM(s, d) for s, d in scratch],
        compiler_params=pltpu.CompilerParams(vmem_limit_bytes=limit),
        cost_estimate=pl.CostEstimate(
            flops=micros * 1000000, bytes_accessed=micros * 3600000, transcendentals=micros * 100000
        ),
        name=name,
    )(*args, *waits)
    return result


def extra_rows(values, heads):
    pieces = []
    for h in range(heads):
        row = values[h : h + 1, :]
        high = row.astype(B16).astype(F32)
        for part in (high, row - high):
            pieces += [part[:, at : at + LANES] for at in range(0, row.shape[1], LANES)]
    return jnp.concatenate(pieces, axis=0)


def extra_row(rows, head, count):
    at = 2 * head * count
    high = jnp.concatenate([rows[at + n : at + n + 1] for n in range(count)], axis=1)
    low = jnp.concatenate([rows[at + count + n : at + count + n + 1] for n in range(count)], axis=1)
    return high + low


def attend_kernel(
    bounds, begin_ref, own_ref, all_ref, out_ref, lse_ref, top, acc, *, heads, keys
):
    rows = own_ref.shape[0]
    top[...] = jnp.full_like(top, MASKED)
    acc[...] = jnp.zeros_like(acc)
    row_ids = bounds[2] + iota((1, rows), 1)
    begins = begin_ref[...]
    ones = (iota((keys, HEAD), 1) == 0).astype(B16)

    def step(n, masked):
        at = n * keys
        kv = all_ref[n, :keys, :]
        k = kv[:, :HEAD]
        v = jnp.concatenate([kv[:, HEAD:], ones], axis=1).T
        if masked:
            key_ids = at + iota((keys, rows), 0)
            seen = (key_ids <= row_ids) & (key_ids >= begins)
        for h in range(heads):
            q = own_ref[:, h * HEAD : (h + 1) * HEAD]
            s = lax.dot_general(k, q, LANE_DOT, preferred_element_type=F32)
            if masked:
                s = jnp.where(seen, s, MASKED)
            old = top[h : h + 1, :]
            new = jnp.maximum(old, jnp.max(s, axis=0, keepdims=True))
            p = jnp.exp(s - new).astype(B16)
            scale = jnp.exp(old - new)
            add = jnp.dot(v, p, preferred_element_type=F32)
            acc[h] = acc[h] * scale + add
            top[h : h + 1, :] = new

    pl.loop(bounds[0], bounds[1])(lambda n: step(n, True))
    pl.loop(bounds[1], bounds[3])(lambda n: step(n, False))
    pl.loop(bounds[3], bounds[4])(lambda n: step(n, True))
    for h in range(heads):
        total = acc[h, HEAD : HEAD + 1, :]
        out_ref[:, h * HEAD : (h + 1) * HEAD] = (acc[h, :HEAD, :] / total).T.astype(B16)
        lse_ref[h : h + 1, :] = top[h : h + 1, :] + jnp.log(total)


def attend(own, everything, begins, bounds, heads, keys, waits):
    rows = own.shape[0]
    return call(
        functools.partial(attend_kernel, heads=heads, keys=keys),
        "attend",
        12,
        (bounds, begins, own, everything),
        (((rows, heads * HEAD), B16), ((8, rows), F32)),
        (((8, rows), F32), ((heads, LANES, rows), F32)),
        waits,
    )


def minus_ones(lane, base, first):
    at = base + first
    return jnp.where((lane == at) | (lane == at + 1), -1.0, 0.0).astype(B16)


def key_sides(kv, heads):
    turned = jnp.concatenate([kv[:, HEAD:], kv[:, :HEAD]], axis=1)
    lane = iota(kv.shape, 1)
    zero = jnp.zeros_like(kv)
    sides = []
    for h in range(heads):
        mine = lane < HEAD if h == 0 else lane >= HEAD
        base = HEAD * (1 - h)
        keys_h = jnp.where(mine, kv if h == 0 else turned, zero)
        values_h = jnp.where(mine, turned if h == 0 else kv, minus_ones(lane, base, 0))
        both = jnp.concatenate([keys_h, minus_ones(lane, base, 2)], axis=1)
        sides.append((keys_h, values_h, both))
    return sides


def query_grad_kernel(
    bounds, begin_ref, own_ref, g_ref, all_ref, out_ref, acc, *, heads, keys
):
    rows = own_ref.shape[0]
    acc[...] = jnp.zeros_like(acc)
    row_ids = bounds[2] + iota((rows, keys), 0)
    begins = begin_ref[...]

    def step(n, masked):
        at = n * keys
        kv = all_ref[n, :keys, :]
        sides = key_sides(kv, heads)
        if masked:
            key_ids = at + iota((rows, keys), 1)
            seen = (key_ids <= row_ids) & (key_ids >= begins)
        total = acc[...]
        for h in range(heads):
            k, v, both = sides[h]
            g = g_ref[:, h * LANES : (h + 1) * LANES]
            q = jnp.concatenate([own_ref[...], g], axis=1)
            s = lax.dot_general(q, both, LANE_DOT, preferred_element_type=F32)
            if masked:
                s = jnp.where(seen, s, MASKED)
            gp = lax.dot_general(g, v, LANE_DOT, preferred_element_type=F32)
            ds = (jnp.exp(s) * gp).astype(B16)
            total = total + jnp.dot(ds, k, preferred_element_type=F32)
        acc[...] = total

    pl.loop(bounds[0], bounds[1])(lambda n: step(n, True))
    pl.loop(bounds[1], bounds[3])(lambda n: step(n, False))
    pl.loop(bounds[3], bounds[4])(lambda n: step(n, True))
    out_ref[...] = acc[...] * SCORE_SCALE


def query_grad(own, g_pack, everything, begins, bounds, heads, keys, waits):
    rows = own.shape[0]
    return call(
        functools.partial(query_grad_kernel, heads=heads, keys=keys),
        "query_grad",
        11,
        (bounds, begins, own, g_pack, everything),
        (((rows, LANES), F32),),
        (((rows, LANES), F32),),
        waits,
    )[0]


def key_grad_kernel(
    bounds, end_ref, own_ref, all_ref, g_ref, out_ref, acc_k, acc_v, *, heads, keys, at_g
):
    rows = out_ref.shape[0]
    acc_k[...] = jnp.zeros_like(acc_k)
    acc_v[...] = jnp.zeros_like(acc_v)
    key_ids = bounds[2] + iota((rows, keys), 0)
    ends = end_ref[...]
    kv = own_ref[:rows, :]
    turned = jnp.concatenate([kv[:, HEAD:], kv[:, :HEAD]], axis=1)
    first = iota(kv.shape, 1) < HEAD
    zero = jnp.zeros_like(kv)
    count = keys // LANES
    sides = []
    for h in range(heads):
        mine = first if h == 0 else jnp.logical_not(first)
        k = jnp.where(mine, kv if h == 0 else turned, zero)
        sides.append((k, jnp.where(mine, turned if h == 0 else kv, zero)))

    def step(n, masked):
        at = n * keys
        if masked:
            row_ids = at + iota((rows, keys), 1)
            seen = (key_ids <= row_ids) & (row_ids < ends)
        q = all_ref[n, :keys, :]
        g = g_ref[n, at_g : at_g + keys, :]
        extra = g_ref[n, at_g + keys :, :].astype(F32)
        delta_rows, lse_rows = (extra[: extra.shape[0] // 2], extra[extra.shape[0] // 2 :])
        for h in range(heads):
            k, v = sides[h]
            s = lax.dot_general(k, q, LANE_DOT, preferred_element_type=F32)
            s = s - extra_row(lse_rows, h, count)
            if masked:
                s = jnp.where(seen, s, MASKED)
            p = jnp.exp(s)
            gp = lax.dot_general(v, g, LANE_DOT, preferred_element_type=F32)
            ds = (p * (gp - extra_row(delta_rows, h, count))).astype(B16)
            acc_k[h] += jnp.dot(ds, q, preferred_element_type=F32)
            acc_v[h] += jnp.dot(p.astype(B16), g, preferred_element_type=F32)

    pl.loop(bounds[0], bounds[1])(lambda n: step(n, True))
    pl.loop(bounds[1], bounds[3])(lambda n: step(n, False))
    pl.loop(bounds[3], bounds[4])(lambda n: step(n, True))
    out_ref[:, :HEAD] = acc_k[0, :, :HEAD] + acc_k[1, :, HEAD:]
    out_ref[:, HEAD:] = acc_v[0, :, :HEAD] + acc_v[1, :, HEAD:]


def key_grad(own, everything, g_all, at_g, ends, bounds, heads, keys, waits):
    rows = ends.shape[0]
    return call(
        functools.partial(key_grad_kernel, heads=heads, keys=keys, at_g=at_g),
        "key_grad",
        12,
        (bounds, ends, own, everything, g_all),
        (((rows, LANES), F32),),
        (((heads, rows, LANES), F32), ((heads, rows, LANES), F32)),
        waits,
    )[0]


def assemble_kernel(picks, mix_ref, shared_ref, dt_ref, out_ref, *, att_cols, turned):
    kv_cols = KV * HEAD
    wide = mix_ref.shape[1]
    first = picks[0] == 0
    at = att_cols
    out_ref[:, :at] = mix_ref[:, :at]
    for part in range(2):
        tile = shared_ref[:, part * kv_cols : (part + 1) * kv_cols]
        out_ref[:, at : at + HEAD] = jnp.where(first, tile[:, :HEAD], tile[:, HEAD:])
        at += HEAD
    out_ref[:, at : at + wide - att_cols] = mix_ref[:, att_cols:]
    at += wide - att_cols
    out_ref[:, at : at + shared_ref.shape[1] - 2 * kv_cols] = shared_ref[:, 2 * kv_cols :]
    at += shared_ref.shape[1] - 2 * kv_cols
    if turned:
        heads, rows = dt_ref.shape
        steps = jnp.concatenate([dt_ref[...].astype(F32), jnp.zeros((LANES - heads, rows), F32)], axis=0)
        out_ref[:, at:] = steps.T.astype(B16)
    else:
        out_ref[:, at:] = jnp.zeros((out_ref.shape[0], LANES), B16)
        out_ref[:, at : at + dt_ref.shape[1]] = dt_ref[...]


def project_kernel(
    places, both_ref, before_ref, w_ref, cos_ref, sin_ref, out_ref, q_ref, kv_ref, z_ref, pre_ref, rim_ref
):
    rows = both_ref.shape[0]
    dim = w_ref.shape[0]
    at_z = 2 * LANES
    at_x = at_z + z_ref.shape[1]
    step = 2 * TILE
    for i in range(0, rows, step):
        r = slice(i, i + step)
        x = both_ref[r, :dim]
        t = jnp.dot(x, w_ref[:, :at_z], preferred_element_type=F32)
        cosine, sine = cos_ref[r, :], sin_ref[r, :]
        q, kv = t[:, :LANES], t[:, LANES:]
        q = (q * cosine + swap_halves(q) * sine).astype(B16)
        q_ref[r, :] = (q.astype(F32) * SCORE_SCALE).astype(B16)
        turned = kv * cosine + swap_halves(kv) * sine
        kv_ref[r, :] = jnp.where(iota(kv.shape, 1) < HEAD, turned, kv).astype(B16)
        z_ref[r, :] = jnp.dot(x, w_ref[:, at_z:at_x], preferred_element_type=F32)
        pre_ref[r, :] = jnp.dot(x, w_ref[:, at_x:], preferred_element_type=F32)
    wide = rim_ref.shape[1]
    rim = jnp.dot(before_ref[...], w_ref[:, at_x : at_x + wide], preferred_element_type=F32)
    rim_ref[...] = rim[before_ref.shape[0] - 8 :, :]
    if kv_ref.shape[0] > rows:
        chunk = out_ref.shape[0]
        for n in range(dim // LANES):
            at = rows + n * chunk
            kv_ref[at : at + chunk, :] = out_ref[:, n * LANES : (n + 1) * LANES]


def partner_rows(places, k, rows):
    return pl.ds(pl.multiple_of(jnp.bitwise_xor(places[3], k) * rows, rows), rows)


def in_order(places, refs, scratch):
    rows = refs[0].shape[0]
    for k, ref in enumerate(refs):
        scratch[partner_rows(places, k, rows), :] = ref[...]


def out_weights(all_ref, w_ref, first, chunk):
    for s in range(all_ref.shape[0]):
        for n in range(w_ref.shape[1] // LANES):
            at = first + n * chunk
            piece = all_ref[s, at : at + chunk, :]
            w_ref[s * chunk : (s + 1) * chunk, n * LANES : (n + 1) * LANES] = piece


def mix_out_kernel(places, attn_ref, gated_ref, gain_ref, all_ref, *refs, ssm_all, chunk, groups):
    w_ref = all_ref
    if chunk:
        w_ref, refs = (refs[-1], refs[:-1])
        out_weights(all_ref, w_ref, attn_ref.shape[0], chunk)
    part_refs, refs = (refs[-groups:], refs[:-groups])
    mixed_ref, total_ref = refs[-2:]
    rows = attn_ref.shape[0]
    att_cols = attn_ref.shape[1]
    total = refs[0][...]
    for ref in refs[1:-2]:
        total = total + ref[...]
    total_ref[...] = total
    squares = total.T
    for i in range(0, rows, TILE):
        r = slice(i, i + TILE)
        inverse = lax.rsqrt(squares[r, 0:1] / ssm_all + EPSILON)
        gnormed = (gated_ref[r, :].astype(F32) * inverse * gain_ref[...]).astype(B16)
        mixed_ref[r, :att_cols] = attn_ref[r, :]
        mixed_ref[r, att_cols:] = gnormed
    for k, ref in enumerate(part_refs):
        r = partner_rows(places, k, rows // groups)
        ref[...] = jnp.dot(mixed_ref[r, :], w_ref[...], preferred_element_type=F32).astype(B16)


def mix_back_kernel(
    places, w_ref, attn_ref, lse_ref, gated_ref, squares_ref, gain_ref, *refs, heads, ssm_all
):
    pack_ref, send_ref, scaled_ref, stat_ref, gain_out, deltas, grad_ref = refs[-7:]
    in_order(places, refs[:-7], grad_ref)
    rows = attn_ref.shape[0]
    att_cols = attn_ref.shape[1]
    squares = squares_ref[...].T
    lse = lse_ref[...].T
    total = jnp.zeros((1, gated_ref.shape[1]), F32)
    ones = jnp.ones((8, gated_ref.shape[1]), F32)
    for i in range(0, rows, TILE):
        r = slice(i, i + TILE)
        mixed = lax.dot_general(grad_ref[r, :], w_ref[...], LANE_DOT, preferred_element_type=F32)
        back = mixed[:, :att_cols].astype(B16).astype(F32)
        product = back * attn_ref[r, :].astype(F32)
        lane = iota(back.shape, 1)
        send_ref[r, :] = back.astype(B16)
        packed = jnp.zeros((TILE, LANES), F32)
        for h in range(heads):
            base = HEAD * (1 - h)
            tile = one_head(back, h)
            delta = jnp.sum(one_head(product, h), axis=1, keepdims=True)
            packed = into_lane(packed, h, delta)
            for n, column in enumerate((delta, lse[r, h : h + 1])):
                high = column.astype(B16).astype(F32)
                tile = jnp.where(lane == base + 2 * n, high, tile)
                tile = jnp.where(lane == base + 2 * n + 1, column - high, tile)
            pack_ref[r, h * LANES : (h + 1) * LANES] = tile.astype(B16)
        deltas[r, :] = packed
        grad = mixed[:, att_cols:]
        scaled = gated_ref[r, :].astype(F32) * lax.rsqrt(squares[r, 0:1] / ssm_all + EPSILON)
        grad_scaled = grad * gain_ref[...]
        scaled_ref[r, :] = grad_scaled
        stat_ref[:, r] = lax.dot_general(
            ones, grad_scaled * scaled, LANE_DOT, precision=HIGHEST, preferred_element_type=F32
        )
        total = total + jnp.sum(grad * scaled, axis=0, keepdims=True)
    gain_out[...] = jnp.broadcast_to(total, gain_out.shape)
    extra = jnp.concatenate(
        [extra_rows(deltas[...].T, heads), extra_rows(lse_ref[...], heads)], axis=0
    )
    send_ref[rows:, :] = extra.astype(B16)


def rows_of(ref, first, last):
    return jnp.concatenate([ref[k, first:last, :] for k in range(ref.shape[0])], axis=0)


def mlp_kernel(places, out_ref, *refs, chunk, groups):
    in_order(places, refs[:groups], refs[-1])
    in_ref = refs[-1]
    refs = refs[groups:-1]
    if chunk:
        all_ref, hidden_ref, weights_ref, *term_refs, gu_ref, down_ref, grad_ref = refs
        down_ref[...] = rows_of(all_ref, 0, chunk)
        gu_ref[...] = rows_of(all_ref, chunk, all_ref.shape[1])
    else:
        gu_ref, down_ref, hidden_ref, grad_ref, *term_refs = refs
    rows = in_ref.shape[0]
    half = hidden_ref.shape[1]
    dim = in_ref.shape[1]
    step = 2 * TILE
    for i in range(0, rows, step):
        r = slice(i, i + step)
        both = jnp.dot(in_ref[r, :], gu_ref[...], preferred_element_type=F32)
        back = lax.dot_general(out_ref[r, dim:], down_ref[...], LANE_DOT, preferred_element_type=F32)
        gate, up = both[:, :half], both[:, half:]
        sig = jax.nn.sigmoid(gate)
        soft = gate * sig
        hidden_ref[r, :] = (soft * up).astype(B16)
        grad_ref[r, :half] = (back * up * sig * (1.0 + gate * (1.0 - sig))).astype(B16)
        grad_ref[r, half:] = (back * soft).astype(B16)
    for k, ref in enumerate(term_refs):
        r = partner_rows(places, k, rows // groups)
        ref[...] = lax.dot_general(
            grad_ref[r, :], gu_ref[...], LANE_DOT, preferred_element_type=F32
        ).astype(B16)
    if chunk:
        parts, tall = weights_ref.shape[0], weights_ref.shape[1] - chunk
        strip = tall // groups
        for i in range(0, half, step):
            down = lax.dot_general(
                hidden_ref[:, i : i + step], out_ref[:, dim:], ROW_DOT, preferred_element_type=F32
            ).astype(B16)
            for n in range(step // chunk):
                weights_ref[i // chunk + n, :chunk, :] = down[n * chunk : (n + 1) * chunk]
        for i in range(0, dim, step):
            both = lax.dot_general(
                in_ref[:, i : i + step], grad_ref[...], ROW_DOT, preferred_element_type=F32
            ).astype(B16)
            for n in range(step // strip):
                b, s = divmod(i // strip + n, parts)
                at = chunk + b * strip
                weights_ref[s, at : at + strip, :] = both[n * strip : (n + 1) * strip]


def down_kernel(places, hidden_ref, w_ref, out_ref, *, chunk):
    w = rows_of(w_ref, 0, chunk) if chunk else w_ref[...]
    out_ref[...] = jnp.dot(hidden_ref[...], w, preferred_element_type=F32).astype(B16)


def add_blocks_kernel(places, blocks_ref, middle_ref, out_ref):
    total = blocks_ref[0].astype(F32)
    for n in range(1, blocks_ref.shape[0]):
        total = total + blocks_ref[n].astype(F32)
    out_ref[...] = (middle_ref[...] + total).astype(B16)


def group_back_kernel(places, grad_ref, w_ref, early_ref, out_ref, kept_ref):
    rows = grad_ref.shape[0]
    step = 2 * TILE
    for i in range(0, rows, step):
        r = slice(i, i + step)
        out_ref[r, :] = lax.dot_general(
            grad_ref[r, :], w_ref[...], LANE_DOT, preferred_element_type=F32
        ).astype(B16)
    kept_ref[...] = early_ref[...]


def norm_back_kernel(places, middle_ref, grad_ref, gain_ref, *refs):
    total_ref, sent_ref, gain_out = refs[-3:]
    grad = refs[0][...].astype(F32)
    for ref in refs[1:-3]:
        grad = grad + ref[...].astype(F32)
    middle = middle_ref[...]
    inverse = lax.rsqrt(jnp.mean(middle * middle, axis=1, keepdims=True) + EPSILON)
    scaled = middle * inverse
    grad_scaled = grad * gain_ref[...]
    mean = jnp.mean(grad_scaled * scaled, axis=1, keepdims=True)
    total = inverse * (grad_scaled - scaled * mean) + grad_ref[...].astype(F32)
    total_ref[...] = total
    sent_ref[...] = total.astype(B16)
    gain_out[...] = jnp.broadcast_to(jnp.sum(grad * scaled, axis=0, keepdims=True), gain_out.shape)


def turned_rows(values):
    rows = values.shape[0]
    if rows < LANES:
        values = jnp.concatenate([values, jnp.zeros((LANES - rows, LANES), F32)], axis=0)
    return values.T


def own_kernel(places, own_ref, early_ref, mixed_ref, dt_ref, gain_ref, taps_ref, *head_refs, heads, half, apart):
    rows = own_ref.shape[0]
    cols = early_ref.shape[1] - half
    mixed_ref[:, :LANES] = own_ref[:, :LANES].astype(F32)
    mixed_ref[:, LANES : LANES + cols] = early_ref[:, half:].astype(F32)
    mixed_ref[:, LANES + cols :] = own_ref[:, LANES : LANES + cols].astype(F32)
    tail = own_ref[:, own_ref.shape[1] - LANES :].astype(F32)
    turned = turned_rows(tail)
    at_gain = heads + 2 + CONV
    each = gain_ref.shape[1]
    dt_ref[...] = turned[:heads, :rows]
    gain_ref[...] = turned[at_gain : at_gain + 1, :each]
    taps_ref[...] = turned[at_gain + 1 : at_gain + 1 + CONV, :each]
    at = at_gain + 1 + CONV
    sums = jnp.sum(tail, axis=0, keepdims=True) if apart else tail[0:1]
    count = len(head_refs)
    for n, ref in enumerate(head_refs):
        total = sums[:, at + n * heads : at + (n + 1) * heads]
        if apart:
            total = total + sums[:, at + (count + n) * heads : at + (count + n + 1) * heads]
        ref[...] = total


def side_kernel(places, blocks_ref, gain_ref, shared_ref, first_ref, second_ref, taps_ref, *, heads):
    groups, strip, wide = blocks_ref.shape
    per_kv = groups // KV
    blocks = [blocks_ref[b].astype(F32) for b in range(groups)]
    sums = []
    for h in range(KV):
        total = blocks[h * per_kv][:, : 2 * HEAD]
        for b in range(h * per_kv + 1, (h + 1) * per_kv):
            total = total + blocks[b][:, : 2 * HEAD]
        sums.append(total)
    rest = blocks[0]
    for b in range(1, groups):
        rest = rest + blocks[b]
    for part in range(2):
        for h in range(KV):
            at = (part * KV + h) * HEAD
            shared_ref[:, at : at + HEAD] = sums[h][:, part * HEAD : (part + 1) * HEAD]
    shared_ref[:, 2 * KV * HEAD :] = rest[:, 2 * HEAD : wide - LANES]
    turned = turned_rows(rest[:, wide - LANES :])
    first_ref[...] = turned[heads : heads + 1, :strip] / gain_ref[...]
    second_ref[...] = turned[heads + 1 : heads + 2, :strip]
    taps_ref[...] = turned[heads + 2 : heads + 2 + CONV, : taps_ref.shape[1]]


def early_kernel(places, mixed_ref, both_ref, dz_ref, w_ref, *refs, parts):
    terms_ref, gain_ref, grad_ref = refs[-3:]
    in_order(places, refs[:-3], grad_ref)
    dim = grad_ref.shape[1]
    half = dim // 2
    rows = mixed_ref.shape[1]
    chunk = rows // parts
    tall = dim // parts
    at_z = 2 * LANES
    cols = dz_ref.shape[1]
    step = 2 * TILE
    for i in range(0, rows, step):
        out = lax.dot_general(
            mixed_ref[:, i : i + step], grad_ref[...], ROW_DOT, preferred_element_type=F32
        ).astype(B16)
        for n in range(step // chunk):
            at = (i // chunk + n) * tall
            piece = out[n * chunk : (n + 1) * chunk]
            terms_ref[at : at + chunk, :half] = piece[:, :half]
            terms_ref[at + chunk : at + tall, :half] = piece[:, half:]
    for i in range(0, dim, step):
        r = slice(i, i + step)
        grad = lax.dot_general(both_ref[:, r], dz_ref[...], ROW_DOT, preferred_element_type=F32)
        terms_ref[r, half:] = grad.astype(B16)
        gain_ref[r, :] = jnp.sum(grad * w_ref[r, at_z : at_z + cols].astype(F32), axis=1, keepdims=True)


def small_columns(tile, mine, gain_ref, taps_ref, heads_ref, second_ref, *, heads, groups, parts):
    dim = second_ref.shape[1]
    cols = gain_ref.shape[1]
    wide = taps_ref.shape[1]
    tall = dim // parts
    strip = tall // groups
    at_gain = heads + 2 + CONV
    at = at_gain + 1 + CONV
    lane = iota((8, LANES), 1)
    values = jnp.where(lane < heads, heads_ref[...], 0.0)
    high = values.astype(B16).astype(F32)
    base = jnp.zeros((1, LANES), F32)
    for n in range(3):
        base = base + pltpu.roll(high, at + n * heads, 1)[n : n + 1]
        base = base + pltpu.roll(values - high, at + (3 + n) * heads, 1)[n : n + 1]
    own_row = iota(tile.shape, 0) % tall == mine
    tile[...] = jnp.where(own_row, base, 0.0)

    def columns(first, rows, width):
        pieces = [jnp.zeros((first, width), F32)] + rows
        left = LANES - first - sum(row.shape[0] for row in rows)
        return jnp.concatenate(pieces + [jnp.zeros((left, width), F32)], axis=0).T

    own = columns(at_gain, [gain_ref[0:1, :], taps_ref[:CONV, :cols]], cols)
    each = cols // parts
    for s in range(parts):
        tile[s * tall : s * tall + each, :] += own[s * each : (s + 1) * each]
    side = columns(heads + 2, [taps_ref[:CONV, cols:]], wide - cols)
    each = (wide - cols) // (groups * parts)
    second = columns(heads + 1, [second_ref[0:1, :]], dim)
    for b in range(groups):
        for s in range(parts):
            there = s * tall + b * strip
            n = b * parts + s
            tile[there : there + each, :] += side[n * each : (n + 1) * each]
            tile[there : there + strip, :] += second[n * strip : (n + 1) * strip]


def weight_grad_kernel(
    places, q_ref, kv_ref, z_ref, x_ref, rim_ref, dt_ref, cos_ref, sin_ref, w_ref, both_ref, early_ref,
    *refs, heads, groups, parts, in_strips,
):
    if in_strips:
        small_refs, (pre_ref, terms_ref, tile) = refs[:4], refs[4:]
        small_columns(tile, places[2], *small_refs, heads=heads, groups=groups, parts=parts)
    else:
        tile, pre_ref, terms_ref = refs
    rows = q_ref.shape[0]
    dim = w_ref.shape[0]
    cols = heads * HEAD
    wide = x_ref.shape[1]
    at_z = 2 * LANES
    at_x = at_z + cols
    at_dt = at_x + wide
    for i in range(0, rows, TILE):
        r = slice(i, i + TILE)
        cosine, sine = cos_ref[r, :], sin_ref[r, :]
        q, kv = q_ref[r, :], kv_ref[r, :]
        pre_ref[r, :LANES] = (q * cosine - swap_halves(q) * sine).astype(B16)
        turned = kv * cosine - swap_halves(kv) * sine
        pre_ref[r, LANES : 2 * LANES] = jnp.where(iota(kv.shape, 1) < HEAD, turned, kv).astype(B16)
        pre_ref[r, at_z:at_x] = z_ref[r, :]
        x = x_ref[r, :]
        if i + TILE == rows:
            x = jnp.concatenate([x[: TILE - 8], x[TILE - 8 :] + rim_ref[...]], axis=0)
        pre_ref[r, at_x:at_dt] = x.astype(B16)
        pre_ref[r, at_dt:] = dt_ref[r, :]
    block = dim // groups
    strip = block // parts
    mixed = LANES + cols
    sides = slice(mixed + LANES, mixed + 3 * LANES)
    ends = slice(mixed + 3 * LANES, mixed + 4 * LANES)
    lane = iota((block, LANES), 1)
    for b in range(groups):
        r = slice(b * block, (b + 1) * block)
        x = both_ref[:, r]
        near = lax.dot_general(x, pre_ref[:, :at_z], ROW_DOT, preferred_element_type=F32)
        far = lax.dot_general(x, pre_ref[:, at_x:], ROW_DOT, preferred_element_type=F32)
        gain = jnp.sum(near * w_ref[r, :at_z].astype(F32), axis=1, keepdims=True)
        gain = gain + jnp.sum(far * w_ref[r, at_x:].astype(F32), axis=1, keepdims=True)
        gain = gain + early_ref[r, :]
        terms_ref[r, :LANES] = near[:, :LANES].astype(B16)
        terms_ref[r, LANES:mixed] = far[:, :cols].astype(B16)
        if in_strips:
            for s in range(parts):
                here = slice(s * strip, (s + 1) * strip)
                first = s * groups * strip + b * strip
                there = slice(first, first + strip)
                terms_ref[there, mixed : mixed + LANES] = near[here, LANES:].astype(B16)
                terms_ref[there, sides] = far[here, cols:wide].astype(B16)
                at_gain = iota((strip, LANES), 1) == heads
                tile[there, :] = jnp.where(at_gain, gain[here], tile[there, :])
            tile[r, :] = jnp.where(lane < heads, far[:, wide:], tile[r, :])
        else:
            terms_ref[r, mixed : mixed + LANES] = near[:, LANES:].astype(B16)
            terms_ref[r, sides] = far[:, cols:wide].astype(B16)
            tail = jnp.where(lane < heads, far[:, wide:], tile[r, :])
            terms_ref[r, ends] = jnp.where(lane == heads, gain, tail).astype(B16)
    if in_strips:
        terms_ref[:, ends] = tile[...].astype(B16)


def iota(shape, dim):
    return lax.broadcasted_iota(jnp.int32, shape, dim)


def per_head(columns, pair):
    shape = (columns.shape[0], LANES)
    return jnp.where(
        iota(shape, 1) < HEAD, columns[:, 2 * pair : 2 * pair + 1], columns[:, 2 * pair + 1 : 2 * pair + 2]
    )


def one_head(values, head):
    keep = (iota(values.shape, 1) < HEAD) == (head % 2 == 0)
    return jnp.where(keep, values, jnp.zeros_like(values))


def into_lane(columns, head, column):
    return jnp.where(iota(columns.shape, 1) == head, column, columns)


def silu_slope(v, sig):
    return sig * (1.0 + v * (1.0 - sig))


def tap_window(ext_ref, tap, first, amount, places):
    return ext_ref[first + 8 - (CONV - 1) + tap : first + 8 - (CONV - 1) + tap + amount, :]


def span_kernel(places, begin_ref, pre_ref, rim_ref, taps_ref, params_ref, u_ref, intra_ref, cum_ref, state_ref, ext, xb, *, heads, at_x, at_dt, nstate):
    rows = pre_ref.shape[0]
    cols = heads * HEAD
    first_row, last_begin = places[0], places[1]
    ext[0:8, :] = rim_ref[...]
    ext[8 : 8 + rows, :] = pre_ref[:, at_x:at_dt]
    local = begin_ref[...] - first_row
    row_ids = iota((rows, 1), 0)
    for i in range(0, rows, TILE):
        total = jnp.zeros((TILE, ext.shape[1]), F32)
        for tap in range(CONV):
            seen = row_ids[i : i + TILE] - (CONV - 1) + tap >= local[i : i + TILE]
            window = tap_window(ext, tap, i, TILE, places)
            total = total + jnp.where(seen, window, 0.0) * taps_ref[tap : tap + 1, :]
        u_ref[i : i + TILE, :] = total
        xb[i : i + TILE, :] = (total * jax.nn.sigmoid(total)).astype(B16)
    raw = pre_ref[:, at_dt : at_dt + LANES] + params_ref[0:1, :]
    dt = jnp.maximum(raw, 0.0) + jnp.log1p(jnp.exp(-jnp.abs(raw)))
    lower = (iota((rows, rows), 0) >= iota((rows, rows), 1)).astype(F32)
    cum = jnp.dot(lower, dt * params_ref[1:2, :], precision=HIGHEST, preferred_element_type=F32)
    cum_ref[:, :LANES] = cum
    cum_ref[:, LANES:] = dt
    cum_t, dt_t = cum.T, dt.T
    last = cum[rows - 1 : rows, :]
    closing = row_ids + first_row >= last_begin
    to_end = jnp.where(closing, jnp.exp(last - cum) * dt, 0.0)
    for i in range(0, rows, TILE):
        width = i + TILE
        c = xb[i : i + TILE, cols + nstate : cols + 2 * nstate]
        b = xb[:width, cols : cols + nstate]
        inner = lax.dot_general(c, b, LANE_DOT, preferred_element_type=F32)
        key = iota((TILE, width), 1)
        seen = (key <= iota((TILE, width), 0) + i) & (key >= local[i : i + TILE])
        for pair in range(heads // 2):
            out = []
            for h in (2 * pair, 2 * pair + 1):
                spread = jnp.where(seen, cum[i : i + TILE, h : h + 1] - cum_t[h : h + 1, :width], MASKED)
                weights = (jnp.exp(spread) * inner * dt_t[h : h + 1, :width]).astype(B16)
                out.append(jnp.dot(weights, xb[:width, pair * LANES : (pair + 1) * LANES], preferred_element_type=F32))
            intra_ref[i : i + TILE, pair * LANES : (pair + 1) * LANES] = jnp.where(iota((TILE, LANES), 1) < HEAD, out[0], out[1])
    b_all = xb[:, cols : cols + nstate]
    for pair in range(heads // 2):
        at = slice(pair * LANES, (pair + 1) * LANES)
        closed = (xb[:, at].astype(F32) * per_head(to_end, pair)).astype(B16)
        state_ref[at, :] = lax.dot_general(closed, b_all, ROW_DOT, preferred_element_type=F32).astype(B16)
    decay = jnp.where(last_begin < first_row, jnp.exp(last), 0.0)
    high = decay.astype(B16)
    low = (decay - high.astype(F32)).astype(B16)
    both = jnp.concatenate([jnp.broadcast_to(high.astype(F32), (LANES // 2, LANES)), jnp.broadcast_to(low.astype(F32), (LANES // 2, LANES))], axis=0)
    state_ref[cols : cols + 16, :] = both.T[:16, :].astype(B16)


def span_forward(places, begins, pre, rim, taps, params, heads, at_x, at_dt, nstate):
    rows = pre.shape[0]
    wide = at_dt - at_x
    cols = heads * HEAD
    return call(
        functools.partial(span_kernel, heads=heads, at_x=at_x, at_dt=at_dt, nstate=nstate),
        "span_forward",
        8,
        (places, begins, pre, rim, taps, params),
        (((rows, wide), F32), ((rows, cols), F32), ((rows, 2 * LANES), F32), ((cols + 16, nstate), B16)),
        (((rows + 8, wide), F32), ((rows, wide), B16)),
    )


def decay_of(states_ref, k, head, cols):
    tail = states_ref[k, cols + head - head % 8 : cols + head - head % 8 + 8, :].astype(F32)
    row = tail[head % 8 : head % 8 + 1, :]
    return row[:, 0:1] + row[:, LANES // 2 : LANES // 2 + 1]


def finish_kernel(places, begin_ref, states_ref, u_ref, intra_ref, cum_ref, z_ref, params_ref, gated_ref, v_ref, state_ref, squares_ref, *, heads, nstate):
    rows = u_ref.shape[0]
    cols = heads * HEAD
    state_ref[...] = jnp.zeros_like(state_ref)

    def fold(k):
        for h in range(heads):
            at = slice(h * HEAD, (h + 1) * HEAD)
            state_ref[at, :] = state_ref[at, :] * decay_of(states_ref, k, h, cols) + states_ref[k, at, :].astype(F32)

    pl.loop(0, places[2])(fold)
    carried = begin_ref[...] < places[0]
    for i in range(0, rows, TILE):
        r = slice(i, i + TILE)
        enter = jnp.where(carried[r], jnp.exp(cum_ref[r, :LANES]), 0.0)
        uc = u_ref[r, cols + nstate : cols + 2 * nstate]
        c = (uc * jax.nn.sigmoid(uc)).astype(B16)
        total = jnp.zeros((8, TILE), F32)
        for pair in range(heads // 2):
            at = slice(pair * LANES, (pair + 1) * LANES)
            y = lax.dot_general(c, state_ref[at, :].astype(B16), LANE_DOT, preferred_element_type=F32)
            ux = u_ref[r, at]
            x = ux * jax.nn.sigmoid(ux)
            skip = per_head(params_ref[2:3, :], pair)
            v = intra_ref[r, at] + per_head(enter, pair) * y + skip * x
            z = z_ref[r, at]
            gated = (v * (z * jax.nn.sigmoid(z))).astype(B16)
            v_ref[r, at] = v
            gated_ref[r, at] = gated
            g = gated.astype(F32)
            total = total + lax.dot_general(jnp.ones((8, LANES), F32), g * g, LANE_DOT, precision=HIGHEST, preferred_element_type=F32)
        squares_ref[:, r] = total


def span_finish(places, begins, states, u, intra, cum, z, params, heads, nstate):
    rows = u.shape[0]
    cols = heads * HEAD
    return call(
        functools.partial(finish_kernel, heads=heads, nstate=nstate),
        "span_finish",
        7,
        (places, begins, states, u, intra, cum, z, params),
        (((rows, cols), B16), ((rows, cols), F32), ((cols, nstate), F32), ((8, rows), F32)),
        (),
    )


def gate_back_kernel(places, begin_ref, scaled_ref, gated_ref, squares_ref, u_ref, cum_ref, z_ref, v_ref, send_ref, *refs, heads, nstate, ssm_all):
    back_ref, dz_ref, state_ref, eg = refs[-4:]
    total = refs[0][...]
    for ref in refs[1:-4]:
        total = total + ref[...]
    rows = u_ref.shape[0]
    cols = heads * HEAD
    carried = begin_ref[...] < places[0]
    squares, stat = squares_ref[...].T, total.T
    uc = u_ref[:, cols + nstate : cols + 2 * nstate]
    c = (uc * jax.nn.sigmoid(uc)).astype(B16)
    for i in range(0, rows, TILE):
        r = slice(i, i + TILE)
        enter = jnp.where(carried[r], jnp.exp(cum_ref[r, :LANES]), 0.0)
        inverse = lax.rsqrt(squares[r, 0:1] / ssm_all + EPSILON)
        mean = stat[r, 0:1] / ssm_all
        for pair in range(heads // 2):
            at = slice(pair * LANES, (pair + 1) * LANES)
            z = z_ref[r, at]
            sig = jax.nn.sigmoid(z)
            scaled = gated_ref[r, at].astype(F32) * inverse
            gg = (inverse * (scaled_ref[r, at] - scaled * mean)).astype(B16)
            back_ref[r, at] = gg
            gg = gg.astype(F32)
            dz_ref[r, at] = (gg * v_ref[r, at] * silu_slope(z, sig)).astype(B16)
            eg[r, at] = (gg * (z * sig) * per_head(enter, pair)).astype(B16)
    state_ref[:cols, :] = lax.dot_general(eg[...], c, ROW_DOT, preferred_element_type=F32).astype(B16)
    state_ref[cols:, :] = send_ref[...]


def gate_back(places, begins, scaled, gated, squares, stats, u, cum, z, v, send, heads, nstate, ssm_all):
    rows = u.shape[0]
    cols = heads * HEAD
    return call(
        functools.partial(gate_back_kernel, heads=heads, nstate=nstate, ssm_all=ssm_all),
        "gate_back",
        5,
        (places, begins, scaled, gated, squares, u, cum, z, v, send) + stats,
        (((rows, cols), B16), ((rows, cols), B16), ((cols + send.shape[0], nstate), B16)),
        (((rows, cols), B16),),
    )


def back_kernel(places, begin_ref, g_ref, z_ref, pre_ref, rim_ref, u_ref, cum_ref, state_ref, states_ref, grads_ref, taps_ref, params_ref, gx_ref, gdt_ref, rim_out, taps_out, small_out, ext, gext, xb, gb, later, dxb, lane_sum, cols_sum, *, heads, at_x, at_dt, nstate):
    rows = u_ref.shape[0]
    cols = heads * HEAD
    wide = at_dt - at_x
    count = states_ref.shape[0]
    pairs = heads // 2
    first_row, last_begin, mine = places[0], places[1], places[2]
    later[...] = jnp.zeros_like(later)

    def fold(n):
        k = count - 1 - n
        for h in range(heads):
            at = slice(h * HEAD, (h + 1) * HEAD)
            later[at, :] = later[at, :] * decay_of(states_ref, k, h, cols) + grads_ref[k, at, :].astype(F32)

    pl.loop(0, count - 1 - mine)(fold)
    local = begin_ref[...] - first_row
    row_ids = iota((rows, 1), 0)
    cum = cum_ref[:, :LANES]
    dt = cum_ref[:, LANES:]
    cum_t, dt_t = cum.T, dt.T
    last = cum[rows - 1 : rows, :]
    leave = jnp.where(row_ids + first_row >= last_begin, jnp.exp(last - cum), 0.0)
    enter = jnp.where(begin_ref[...] < first_row, jnp.exp(cum), 0.0)
    to_end = leave * dt
    for i in range(0, rows, TILE):
        r = slice(i, i + TILE)
        u = u_ref[r, :]
        xb[r, :] = (u * jax.nn.sigmoid(u)).astype(B16)
        z = z_ref[r, :]
        gb[r, :] = (g_ref[r, :].astype(F32) * (z * jax.nn.sigmoid(z))).astype(B16)
    dxb[...] = jnp.zeros_like(dxb)
    cols_sum[...] = jnp.zeros_like(cols_sum)
    b_at = slice(cols, cols + nstate)
    c_at = slice(cols + nstate, cols + 2 * nstate)
    for i in range(0, rows, TILE):
        width = i + TILE
        r = slice(i, i + TILE)
        inner = lax.dot_general(xb[r, c_at], xb[:width, b_at], LANE_DOT, preferred_element_type=F32)
        key = iota((TILE, width), 1)
        seen = (key <= iota((TILE, width), 0) + i) & (key >= local[r])
        grad_inner = jnp.zeros((TILE, width), F32)
        sums = jnp.zeros((TILE, LANES), F32)
        for h in range(heads):
            at = slice(h // 2 * LANES, (h // 2 + 1) * LANES)
            g = one_head(gb[r, at], h)
            spread = jnp.where(seen, cum[r, h : h + 1] - cum_t[h : h + 1, :width], MASKED)
            decays = jnp.exp(spread)
            steps = dt_t[h : h + 1, :width]
            pairing = lax.dot_general(g, xb[:width, at], LANE_DOT, preferred_element_type=F32)
            paired = pairing * decays
            grad_inner = grad_inner + paired * steps
            both = paired * inner
            cols_sum[h : h + 1, :width] += jnp.sum(both, axis=0, keepdims=True)
            sums = into_lane(sums, h, jnp.sum(both * steps, axis=1, keepdims=True))
            weights = (decays * inner * steps).astype(B16)
            dxb[:width, at] += lax.dot_general(weights, g, ROW_DOT, preferred_element_type=F32)
        lane_sum[r, :] = sums
        grad_inner = grad_inner.astype(B16)
        dxb[r, c_at] += jnp.dot(grad_inner, xb[:width, b_at], preferred_element_type=F32)
        dxb[:width, b_at] += lax.dot_general(grad_inner, xb[r, c_at], ROW_DOT, preferred_element_type=F32)
    from_cols = jnp.concatenate([cols_sum[...], jnp.zeros((LANES - 8, rows), F32)], axis=0).T
    state_b = state_ref[...].astype(B16)
    later_b = later[...].astype(B16)
    entered = jnp.zeros((rows, LANES), F32)
    closed = jnp.zeros((rows, LANES), F32)
    skips = jnp.zeros((1, LANES), F32)
    chained = jnp.zeros((1, LANES), F32)
    for pair in range(pairs):
        at = slice(pair * LANES, (pair + 1) * LANES)
        x = xb[:, at].astype(F32)
        g = gb[:, at].astype(F32)
        y = lax.dot_general(xb[:, c_at], state_b[at, :], LANE_DOT, preferred_element_type=F32)
        q = lax.dot_general(xb[:, b_at], later_b[at, :], LANE_DOT, preferred_element_type=F32)
        ends = per_head(to_end, pair)
        dxb[:, c_at] += jnp.dot((g * per_head(enter, pair)).astype(B16), state_b[at, :], preferred_element_type=F32)
        dxb[:, b_at] += jnp.dot((x * ends).astype(B16), later_b[at, :], preferred_element_type=F32)
        dxb[:, at] += ends * q + g * per_head(params_ref[2:3, :], pair)
        gy, xq, gx = g * y, x * q, jnp.sum(g * x, axis=0, keepdims=True)
        kept = jnp.sum(later[at, :] * state_ref[at, :], axis=1, keepdims=True)
        for h in (2 * pair, 2 * pair + 1):
            entered = into_lane(entered, h, jnp.sum(one_head(gy, h), axis=1, keepdims=True))
            closed = into_lane(closed, h, jnp.sum(one_head(xq, h), axis=1, keepdims=True))
            skips = into_lane(skips, h, jnp.sum(one_head(gx, h), axis=1, keepdims=True))
            half = slice(h % 2 * HEAD, (h % 2 + 1) * HEAD)
            chained = into_lane(chained, h, jnp.sum(kept[half], axis=0, keepdims=True))
    decay = jnp.where(last_begin < first_row, jnp.exp(last), 0.0)
    ended = closed * to_end
    grad_cum = lane_sum[...] - from_cols * dt + entered * enter - ended
    at_last = jnp.sum(ended, axis=0, keepdims=True) + decay * chained
    grad_cum = grad_cum + jnp.where(row_ids == rows - 1, at_last, 0.0)
    upper = (iota((rows, rows), 0) <= iota((rows, rows), 1)).astype(F32)
    grad_log = jnp.dot(upper, grad_cum, precision=HIGHEST, preferred_element_type=F32)
    rate = params_ref[1:2, :]
    grad_dt = from_cols + closed * leave + grad_log * rate
    grad_raw = grad_dt * jax.nn.sigmoid(pre_ref[:, at_dt : at_dt + LANES] + params_ref[0:1, :])
    grad_raw = jnp.where(iota((rows, LANES), 1) < heads, grad_raw, 0.0)
    gdt_ref[...] = grad_raw.astype(B16)
    small_out[0:1, :] = jnp.sum(grad_log * dt, axis=0, keepdims=True) * rate
    small_out[1:2, :] = jnp.sum(grad_raw, axis=0, keepdims=True)
    small_out[2:3, :] = skips
    small_out[3:8, :] = jnp.zeros((5, LANES), F32)
    ext[0:8, :] = rim_ref[...]
    ext[8 : 8 + rows, :] = pre_ref[:, at_x:at_dt]
    gext[...] = jnp.zeros_like(gext)
    taps_out[...] = jnp.zeros_like(taps_out)
    for i in range(0, rows, TILE):
        r = slice(i, i + TILE)
        u = u_ref[r, :]
        du = dxb[r, :] * silu_slope(u, jax.nn.sigmoid(u))
        for tap in range(CONV):
            seen = row_ids[r] - (CONV - 1) + tap >= local[r]
            part = jnp.where(seen, du, 0.0)
            taps_out[tap : tap + 1, :] += jnp.sum(part * tap_window(ext, tap, i, TILE, places), axis=0, keepdims=True)
            at = 8 - (CONV - 1) + tap + i
            gext[at : at + TILE, :] += part * taps_ref[tap : tap + 1, :]
    rim_out[...] = gext[0:8, :]
    gx_ref[...] = gext[8:, :]


def span_back(places, begins, back, z, pre, rim, u, cum, state, states, grads, taps, params, heads, at_x, at_dt, nstate, waits):
    rows = u.shape[0]
    cols = heads * HEAD
    wide = at_dt - at_x
    return call(
        functools.partial(back_kernel, heads=heads, at_x=at_x, at_dt=at_dt, nstate=nstate),
        "span_back",
        16,
        (places, begins, back, z, pre, rim, u, cum, state, states, grads, taps, params),
        (((rows, wide), F32), ((rows, LANES), B16), ((8, wide), F32), ((8, wide), F32), ((8, LANES), F32)),
        (((rows + 8, wide), F32), ((rows + 8, wide), F32), ((rows, wide), B16), ((rows, cols), B16),
         ((cols, nstate), F32), ((rows, wide), F32), ((rows, LANES), F32), ((8, rows), F32)),
        waits,
    )


def shards(
    x_in,
    lengths,
    norm1_gain,
    w_mix_in,
    w_dt,
    w_shared,
    conv_x,
    conv_bc,
    a_log,
    dt_bias,
    d_skip,
    gate_gain,
    w_out,
    norm2_gain,
    w_gate,
    w_up,
    w_down,
    d_out,
):
    tok_rows = x_in.shape[0]
    groups = lax.axis_size("branch")
    branch_id = lax.axis_index("branch")
    seq_id = lax.axis_index("seq")
    seq_rows = tok_rows * groups
    group_first = seq_id * seq_rows
    att_heads = HEADS_ATT // groups
    att_cols = att_heads * HEAD
    ssm_heads = w_dt.shape[1]
    ssm_cols = ssm_heads * HEAD
    kv_cols = KV * HEAD
    f32 = jnp.float32
    bf16 = jnp.bfloat16
    dim = x_in.shape[1]
    parts = lax.axis_size("seq")
    chunk = w_out.shape[0] // groups
    att_chunks = parts * att_cols // (att_cols + ssm_cols)
    ssm_chunks = parts - att_chunks
    strip = dim // (groups * parts)
    hidden_all = w_gate.shape[1]
    hidden_a = hidden_all * att_cols // ((att_cols + ssm_cols) * groups)
    hidden_s = hidden_all // groups - hidden_a
    hidden_b = hidden_a + hidden_s

    def spot(c):
        first = groups * att_chunks
        if c < first:
            return (c // att_chunks) * parts + c % att_chunks
        return ((c - first) // ssm_chunks) * parts + att_chunks + (c - first) % ssm_chunks

    to_heads = [((c % groups) * parts + c // groups, spot(c)) for c in range(groups * parts)]
    from_heads = [(spot(c), c) for c in range(groups * parts)]

    def branch_parts(part):
        routes = [[(i, i ^ k) for i in range(groups)] for k in range(1, groups)]
        return (part,) + tuple(lax.ppermute(part, "branch", route) for route in routes)

    def branch_swap(blocks):
        routes = [[(i, i ^ k) for i in range(groups)] for k in range(1, groups)]
        moved = [lax.ppermute(block, "branch", route) for block, route in zip(blocks[1:], routes)]
        return (blocks[0],) + tuple(moved)

    def ordered(blocks):
        stacked = jnp.stack(blocks)
        picked = [lax.dynamic_index_in_dim(stacked, branch_id ^ n, 0, False) for n in range(groups)]
        return jnp.concatenate(picked, axis=0)

    def branch_exchange(blocks):
        return lax.all_to_all(blocks, "branch", 0, 0, tiled=True)

    def branch_gather(part):
        copies = branch_exchange(jnp.broadcast_to(part[None], (groups,) + part.shape))
        return copies.reshape((groups * part.shape[0],) + part.shape[1:])

    def branch_scatter(terms):
        blocks = terms.astype(bf16).reshape((groups, -1) + terms.shape[1:])
        return jnp.sum(lax.all_to_all(blocks, "branch", 0, 0, tiled=True).astype(f32), axis=0)

    kv_head = branch_id * att_heads // (HEADS_ATT // KV)
    side_cols = w_shared.shape[1] - 2 * kv_cols
    w1_cols = w_mix_in.shape[1] + 2 * HEAD + side_cols + LANES
    turned = w_dt.shape[0] % LANES == 0
    w1_part = call(
        functools.partial(assemble_kernel, att_cols=att_cols, turned=turned),
        "assemble",
        1,
        (kv_head[None], w_mix_in, w_shared, w_dt.T if turned else w_dt),
        (((w_mix_in.shape[0], w1_cols), B16),),
        (),
    )[0]
    w1 = lax.all_gather(w1_part, "seq", axis=0, tiled=True)

    def own_columns(w):
        return [
            lax.dynamic_slice_in_dim(w, branch_id * hidden_a, hidden_a, 1),
            lax.dynamic_slice_in_dim(w, groups * hidden_a + branch_id * hidden_s, hidden_s, 1),
        ]

    row_part = jnp.concatenate(
        [
            lax.dynamic_slice_in_dim(w_out, branch_id * chunk, chunk, 0),
            lax.dynamic_slice_in_dim(w_down, branch_id * chunk, chunk, 0),
        ],
        axis=0,
    )
    row_part = lax.ppermute(row_part, ("branch", "seq"), to_heads)
    out_part = row_part[:chunk]
    mlp_part = jnp.concatenate(
        [row_part[chunk:], jnp.concatenate(own_columns(w_gate) + own_columns(w_up), axis=1)], axis=0
    )
    x_rows = x_in.astype(f32)
    scaled1, inverse1 = rms_parts(x_rows)
    normed1 = (scaled1 * norm1_gain).astype(bf16)
    both_in = branch_gather(jnp.concatenate([normed1, d_out], axis=1))
    d_out_g = both_in[:, dim:]
    before = from_behind(both_in[seq_rows - 16 :, :dim], "seq", 1)
    row_ids = group_first + jnp.arange(seq_rows, dtype=jnp.int32)
    seq_ends = jnp.cumsum(lengths)

    def begin_of(ids):
        return jnp.max(jnp.where(seq_ends <= ids[..., None], seq_ends, 0), axis=-1)

    def end_of(ids):
        return jnp.min(jnp.where(seq_ends > ids[..., None], seq_ends, seq_rows * parts), axis=-1)

    begins = begin_of(row_ids)
    ends = end_of(row_ids)
    position = row_ids - begins
    row_last = group_first + seq_rows - 1
    begin_first, begin_last = (begin_of(group_first), begin_of(row_last))
    end_first, end_last = (end_of(group_first), end_of(row_last))
    here = seq_id
    query_lo = begin_first // seq_rows
    query_clear = jnp.minimum(jnp.maximum(query_lo, -(-begin_last // seq_rows)), here)
    query_bounds = jnp.stack([query_lo, query_clear, group_first, here, here + 1])
    key_hi = -(-end_last // seq_rows)
    key_clear = jnp.maximum(here + 1, jnp.minimum(end_first // seq_rows, key_hi))
    key_bounds = jnp.stack([here, here + 1, group_first, key_clear, key_hi])
    places = jnp.stack([group_first, begin_last, seq_id, branch_id])
    begins_col, begins_row, ends_col = (begins[:, None], begins[None, :], ends[:, None])
    at_dt = ssm_cols + side_cols
    nstate = conv_bc.shape[1] // 2
    taps = jnp.pad(jnp.concatenate([conv_x, conv_bc], axis=1), ((0, 8 - CONV), (0, 0)))
    params = jnp.stack([dt_bias, -jnp.exp(a_log), d_skip])
    params = jnp.pad(params, ((0, 5), (0, LANES - ssm_heads)))
    ssm_all = gate_gain.shape[0]
    gain_row = lax.dynamic_slice_in_dim(gate_gain, branch_id * ssm_cols, ssm_cols, 0)[None, :]
    cosine, sine = rotate_tables(position)
    packed = chunk if chunk % 16 == 0 and strip % 16 == 0 else 0
    kv_rows = seq_rows + packed * dim // LANES
    queries, kv, z_pre, pre, rim = call(
        project_kernel,
        "project",
        5,
        (places, both_in, before, w1, cosine, sine, out_part),
        (
            ((seq_rows, LANES), B16),
            ((kv_rows, LANES), B16),
            ((seq_rows, ssm_cols), F32),
            ((seq_rows, at_dt + LANES), F32),
            ((8, at_dt), F32),
        ),
        (),
        (
            begins_col,
            begins_row,
            ends_col,
            query_bounds,
            key_bounds,
            taps,
            params,
            gain_row,
            mlp_part,
        ),
    )
    kv_all = lax.all_gather(kv, "seq", axis=0)
    w_out_b = kv_all if packed else lax.all_gather(out_part, "seq", axis=0, tiled=True)
    mlp_all = lax.all_gather(mlp_part, "seq", axis=0)
    if packed:
        mlp_weights, down_weights = ((mlp_all,), mlp_all)
        mlp_scratch = (
            ((dim, 2 * hidden_b), B16),
            ((parts * chunk, dim), B16),
            ((seq_rows, 2 * hidden_b), B16),
        )
    else:
        down_weights = mlp_all[:, :chunk].reshape(parts * chunk, dim)
        mlp_weights = (mlp_all[:, chunk:].reshape(dim, 2 * hidden_b), down_weights)
        mlp_scratch = ()
    u, intra, cum, state = span_forward(
        places, begins_col, pre, rim, taps, params, ssm_heads, 0, at_dt, nstate
    )
    states = lax.all_gather(state, "seq", axis=0)
    gated_b, gated_v, state_in, squares = span_finish(
        places, begins_col, states, u, intra, cum, z_pre, params, ssm_heads, nstate
    )
    attn_out, lse = attend(
        queries, kv_all, begins_row, query_bounds, att_heads, seq_rows, (gated_b,)
    )
    q_all = lax.all_gather(queries, "seq", axis=0)

    out_shape = (parts * chunk, dim)
    row_blocks = (((tok_rows, dim), B16),) * groups
    mixed_out, squares, *out_terms = call(
        functools.partial(mix_out_kernel, ssm_all=ssm_all, chunk=packed, groups=groups),
        "mix_out",
        3,
        (places, attn_out, gated_b, gain_row, w_out_b) + branch_parts(squares),
        (((seq_rows, att_cols + ssm_cols), B16), ((8, seq_rows), F32))
        + row_blocks
        + (((out_shape, B16),) if packed else ()),
        (),
    )
    w_out_b = out_terms.pop() if packed else w_out_b
    projected = sum(block.astype(f32) for block in branch_swap(out_terms))
    middle = x_rows + projected
    scaled2, inverse2 = rms_parts(middle)
    normed2 = branch_parts((scaled2 * norm2_gain).astype(bf16))
    middle_shape = (parts, chunk + dim // parts, dim) if packed else (seq_rows, 2 * hidden_b)
    hidden, mlp_middle, *mlp_back = call(
        functools.partial(mlp_kernel, chunk=packed, groups=groups),
        "mlp",
        11,
        (places, both_in) + normed2 + mlp_weights,
        (
            ((seq_rows, hidden_b), B16),
            (middle_shape, B16),
        )
        + row_blocks,
        mlp_scratch + (((seq_rows, dim), B16),),
    )
    def over_rows(left, right):
        return lax.dot_general(
            left, right, (((0,), (0,)), ((), ())), preferred_element_type=f32
        ).astype(bf16)

    def strips(rows_all):
        wide = rows_all.reshape((groups, parts, strip) + rows_all.shape[1:])
        return jnp.swapaxes(wide, 0, 1).reshape((parts, groups * strip) + rows_all.shape[1:])

    if packed:
        mlp_terms = mlp_middle
    else:
        mlp_terms = jnp.concatenate(
            [
                over_rows(hidden, d_out_g).reshape(parts, chunk, dim),
                strips(over_rows(ordered(normed2), mlp_middle)),
            ],
            axis=1,
        )
    mlp_own = lax.psum_scatter(mlp_terms, "seq", scatter_dimension=0)
    grad_middle, grad_sent, grad_n2 = call(
        norm_back_kernel,
        "norm_back",
        2,
        (places, middle, d_out, norm2_gain[None, :]) + branch_swap(mlp_back),
        (((tok_rows, dim), F32), ((tok_rows, dim), B16), ((8, dim), F32)),
        (),
        (q_all,),
    )
    grad_proj = branch_parts(grad_sent)
    g_pack, g_send, grad_scaled, stat, grad_gain = call(
        functools.partial(mix_back_kernel, heads=att_heads, ssm_all=ssm_all),
        "mix_back",
        5,
        (places, w_out_b, attn_out, lse, gated_b, squares, gain_row) + grad_proj,
        (
            ((seq_rows, att_heads * LANES), B16),
            ((seq_rows + 4 * att_heads * seq_rows // LANES, LANES), B16),
            ((seq_rows, ssm_cols), F32),
            ((8, seq_rows), F32),
            ((8, ssm_cols), F32),
        ),
        (((seq_rows, LANES), F32), ((seq_rows, dim), B16)),
    )
    stats = branch_parts(stat)
    grad_gate_gain = grad_gain[0]

    def all_columns(blocks):
        blocks = jnp.swapaxes(blocks, 0, 1)
        return jnp.concatenate(
            [blocks[:, :, :hidden_a].reshape(strip, -1), blocks[:, :, hidden_a:].reshape(strip, -1)],
            axis=1,
        )

    back_ssm, grad_z, grad_state = gate_back(
        places, begins_col, grad_scaled, gated_b, squares, stats, u, cum, z_pre, gated_v, g_send, ssm_heads, nstate, ssm_all
    )
    grad_states = lax.all_gather(grad_state, "seq", axis=0)
    grad_q = query_grad(
        queries, g_pack, kv_all, begins_col, query_bounds, att_heads, seq_rows, (grad_state, mlp_own)
    )
    y_terms = call(
        functools.partial(down_kernel, chunk=packed),
        "down",
        3,
        (places, hidden, down_weights),
        (((seq_rows, dim), B16),),
        (),
        (grad_state,),
    )[0]
    y_blocks = branch_exchange(y_terms.reshape(groups, tok_rows, dim))
    if packed:
        early_terms, early_gain = call(
            functools.partial(early_kernel, parts=parts),
            "early",
            3,
            (places, mixed_out, both_in, grad_z, w1) + grad_proj,
            (((dim, dim // 2 + ssm_cols), B16), ((dim, 1), F32)),
            (((seq_rows, dim), B16),),
        )
        early_terms = early_terms.reshape(parts, dim // parts, dim // 2 + ssm_cols)
    else:
        out_rows = over_rows(mixed_out, ordered(grad_proj)).reshape(parts, chunk, dim)
        z_grad = lax.dot_general(both_in[:, :dim], grad_z, ROW_DOT, preferred_element_type=f32)
        at_z = 2 * LANES
        z_weight = w1[:, at_z : at_z + ssm_cols].astype(f32)
        early_gain = jnp.sum(z_grad * z_weight, axis=1, keepdims=True)
        early_terms = jnp.concatenate(
            [
                jnp.concatenate([out_rows[:, :, : dim // 2], out_rows[:, :, dim // 2 :]], axis=1),
                z_grad.astype(bf16).reshape(parts, dim // parts, ssm_cols),
            ],
            axis=2,
        )
    early_own = lax.psum_scatter(early_terms, "seq", scatter_dimension=0)
    grad_w_down = lax.ppermute(mlp_own[:chunk], ("branch", "seq"), from_heads)
    own_gu = branch_exchange(mlp_own[chunk:].reshape(groups, strip, 2 * hidden_b))
    grad_w_gate = all_columns(own_gu[:, :, :hidden_b]).astype(f32)
    grad_w_up = all_columns(own_gu[:, :, hidden_b:]).astype(f32)
    grad_xbc, grad_dt, rim_back, grad_taps, grad_small = span_back(
        places,
        begins_col,
        back_ssm,
        z_pre,
        pre,
        rim,
        u,
        cum,
        state_in,
        states,
        grad_states,
        taps,
        params,
        ssm_heads,
        0,
        at_dt,
        nstate,
        (grad_q, early_terms, y_terms),
    )
    rim_back = from_behind(rim_back, "seq", -1)
    grad_kv = key_grad(
        kv, q_all, grad_states, ssm_cols, ends_col, key_bounds, att_heads, seq_rows, (grad_dt,)
    )
    tall = groups * strip
    bc_each = conv_bc.shape[1] // (groups * parts)
    x_each = ssm_cols // parts
    in_strips = packed > 0
    if in_strips:
        small = (grad_gain, grad_taps, grad_small, grad_n2)
    else:
        grad_conv_x, grad_conv_bc = (grad_taps[:CONV, :ssm_cols], grad_taps[:CONV, ssm_cols:])
        def to_column(vector, rows_each):
            padded = jnp.pad(vector.reshape(parts, rows_each), ((0, 0), (0, tall - rows_each)))
            return padded[:, :, None]

        def to_columns(matrix, rows_each):
            wide = jnp.swapaxes(matrix.reshape(matrix.shape[0], parts, rows_each), 0, 1)
            wide = jnp.pad(wide, ((0, 0), (0, 0), (0, tall - rows_each)))
            return jnp.swapaxes(wide, 1, 2)

        bc_wide = grad_conv_bc.reshape(CONV, groups, parts, bc_each)
        bc_wide = jnp.pad(bc_wide, ((0, 0), (0, 0), (0, 0), (0, strip - bc_each)))
        bc_wide = jnp.transpose(bc_wide, (2, 1, 3, 0)).reshape(parts, tall, CONV)
        heads3 = grad_small[:3, :ssm_heads].reshape(3 * ssm_heads)
        heads3 = jnp.broadcast_to(heads3[None, None, :], (parts, tall, 3 * ssm_heads))
        small = jnp.concatenate(
            [
                jnp.zeros((parts, tall, ssm_heads + 1), f32),
                strips(grad_n2[0][:, None]),
                bc_wide,
                to_column(grad_gate_gain, x_each),
                to_columns(grad_conv_x, x_each),
                heads3,
            ],
            axis=2,
        )
        small = jnp.pad(small, ((0, 0), (0, 0), (0, LANES - small.shape[2]))).reshape(dim, LANES)
        small = (small,)
    late_cols = w1_cols - ssm_cols
    grad_pre, terms1 = call(
        functools.partial(
            weight_grad_kernel, heads=ssm_heads, groups=groups, parts=parts, in_strips=in_strips
        ),
        "weight_grad",
        7,
        (places, grad_q, grad_kv, grad_z, grad_xbc, rim_back, grad_dt, cosine, sine, w1, both_in, early_gain)
        + small,
        (((seq_rows, w1_cols), B16), ((dim, late_cols), B16)),
        (((dim, LANES), F32),) if in_strips else (),
        (own_gu, grad_w_down),
    )
    mixed_cols = att_cols + ssm_cols
    at_s = mixed_cols + 2 * HEAD + side_cols
    if in_strips:
        terms1 = terms1.reshape(parts, tall, late_cols)
    else:
        tail = terms1[:, at_s:].reshape(parts, tall, LANES)
        gain_column = strips(terms1[:, at_s + ssm_heads][:, None])
        lane = jnp.arange(LANES)
        terms1 = jnp.concatenate(
            [
                terms1[:, :mixed_cols].reshape(parts, tall, mixed_cols),
                strips(terms1[:, mixed_cols:at_s]),
                jnp.where(lane == ssm_heads, gain_column, tail),
            ],
            axis=2,
        )
    own1 = lax.psum_scatter(terms1, "seq", scatter_dimension=0)
    group_terms, early_own = call(
        group_back_kernel,
        "group_back",
        4,
        (places, grad_pre, w1, early_own),
        (((seq_rows, dim), B16), (early_own.shape, B16)),
        (),
    )
    grad_normed1 = branch_scatter(group_terms)
    y_out = call(
        add_blocks_kernel,
        "add_blocks",
        1,
        (places, y_blocks, middle),
        (((tok_rows, dim), B16),),
        (),
        (group_terms,),
    )[0]
    out_own = jnp.concatenate(
        [early_own[:chunk, : dim // 2], early_own[chunk:, : dim // 2]], axis=1
    )
    grad_w_out = lax.ppermute(out_own, ("branch", "seq"), from_heads).astype(f32)
    own_gain = lax.dynamic_slice_in_dim(norm1_gain, (branch_id * parts + seq_id) * strip, strip, 0)
    side_blocks = branch_exchange(own1[:, mixed_cols:].reshape(groups, strip, -1))
    head_row = ((1, ssm_heads), F32)
    grad_mix, grad_dt_w, grad_gain_g, grad_cx, grad_a_log, grad_dt_bias, grad_skip = call(
        functools.partial(own_kernel, heads=ssm_heads, half=dim // 2, apart=in_strips),
        "own",
        2,
        (places, own1, early_own),
        (
            ((tall, w_mix_in.shape[1]), F32),
            ((ssm_heads, tall), F32),
            ((1, x_each), F32),
            ((CONV, x_each), F32),
            head_row,
            head_row,
            head_row,
        ),
        (),
    )
    grad_shared, first_gain, second_gain, grad_cbc = call(
        functools.partial(side_kernel, heads=ssm_heads),
        "side",
        1,
        (places, side_blocks, own_gain[None, :]),
        (
            ((strip, w_shared.shape[1]), F32),
            ((1, strip), F32),
            ((1, strip), F32),
            ((CONV, bc_each), F32),
        ),
        (),
    )
    grad_x1, unused_n1 = rms_backward(grad_normed1, scaled1, inverse1, norm1_gain)
    return (
        y_out,
        grad_middle + grad_x1,
        first_gain[0],
        grad_mix,
        grad_dt_w.T,
        grad_shared,
        grad_cx,
        grad_cbc,
        grad_a_log[0],
        grad_dt_bias[0],
        grad_skip[0],
        grad_gain_g[0],
        grad_w_out,
        second_gain[0],
        grad_w_gate,
        grad_w_up,
        grad_w_down.astype(f32),
    )


def solution(mesh):
    in_specs = (
        P(("seq", "branch"), None),
        P(),
        P(),
        P("seq", "branch"),
        P("seq", "branch"),
        P("seq", None),
        P(None, "branch"),
        P(),
        P("branch"),
        P("branch"),
        P("branch"),
        P(),
        P("seq", None),
        P(),
        P("seq", None),
        P("seq", None),
        P("seq", None),
        P(("seq", "branch"), None),
    )
    out_specs = (
        P(("seq", "branch"), None),
        P(("seq", "branch"), None),
        P(("branch", "seq")),
        P("seq", "branch"),
        P("seq", "branch"),
        P(("branch", "seq"), None),
        P(None, ("branch", "seq")),
        P(None, ("branch", "seq")),
        P("branch"),
        P("branch"),
        P("branch"),
        P(("branch", "seq")),
        P(("branch", "seq"), None),
        P(("branch", "seq")),
        P(("branch", "seq"), None),
        P(("branch", "seq"), None),
        P(("branch", "seq"), None),
    )
    return jax.shard_map(shards, mesh=mesh, in_specs=in_specs, out_specs=out_specs, check_vma=False)
```

```python
import functools

import jax
import jax.numpy as jnp
from jax import lax
from jax.experimental import pallas as pl
from jax.experimental.pallas import tpu as pltpu
from jax.sharding import PartitionSpec as P

HEADS_ATT = 8
KV = 2
HEAD = 64
CONV = 4
LANES = 128
TILE = 128
MASKED = -1e30
HIGHEST = lax.Precision.HIGHEST
EPSILON = 1e-06
SCORE_SCALE = 0.125
ROPE_BASE = 1000000.0
F32 = jnp.float32
B16 = jnp.bfloat16
LANE_DOT = (((1,), (1,)), ((), ()))
ROW_DOT = (((0,), (0,)), ((), ()))


VMEM_SPEC = pl.BlockSpec(memory_space=pltpu.VMEM)
SMEM_SPEC = pl.BlockSpec(memory_space=pltpu.SMEM)
ANY_SPEC = pl.BlockSpec(memory_space=pl.ANY)


def from_behind(block, axis, distance):
    devices = range(lax.axis_size(axis))
    route = [(i - distance, i) for i in devices if i - distance in devices]
    return lax.ppermute(block, axis, route)


def rms_parts(value):
    inverse = lax.rsqrt(jnp.mean(value * value, axis=-1, keepdims=True) + EPSILON)
    return (value * inverse, inverse)


def rms_backward(grad_out, scaled, inverse, gain_vec):
    grad_scaled = grad_out * gain_vec
    grad_in = inverse * (
        grad_scaled - scaled * jnp.mean(grad_scaled * scaled, axis=-1, keepdims=True)
    )
    return (grad_in, jnp.sum(grad_out * scaled, axis=0))


def rotate_tables(position):
    half = HEAD // 2
    inverse = ROPE_BASE ** (-jnp.arange(half, dtype=jnp.float32) / half)
    angles = position.astype(jnp.float32)[:, None] * inverse[None, :]
    cosine, sine = (jnp.cos(angles), jnp.sin(angles))
    return (
        jnp.concatenate([cosine] * (LANES // half), axis=1),
        jnp.concatenate([-sine, sine] * (LANES // HEAD), axis=1),
    )


def swap_halves(values):
    half = HEAD // 2
    lane = lax.broadcasted_iota(jnp.int32, values.shape, 1)
    return jnp.where(
        lane % HEAD < half, pltpu.roll(values, LANES - half, 1), pltpu.roll(values, half, 1)
    )


def call(kernel, name, micros, args, outs, scratch, waits=()):
    given, held = (len(args), len(waits))

    def body(*refs):
        kernel(*refs[:given], *refs[given + held :])

    def padded(shape, kind):
        shape = (1,) * (2 - len(shape)) + tuple(shape)
        wide = -(-shape[-1] // LANES) * LANES
        tall = -(-shape[-2] // 16) * 16
        return functools.reduce(lambda a, b: a * b, shape[:-2], 1) * tall * wide * jnp.dtype(kind).itemsize

    held_bytes = [padded(a.shape, a.dtype) for a in args[1:]]
    held_bytes += [padded(s, d) for s, d in tuple(outs) + tuple(scratch)]
    limit = 56 << 20
    if name == "mix_out":
        limit = min(limit, sum(held_bytes) + (8 << 20))
    result = pl.pallas_call(
        body,
        out_shape=tuple(jax.ShapeDtypeStruct(s, d) for s, d in outs),
        in_specs=[SMEM_SPEC] + [VMEM_SPEC] * (given - 1) + [ANY_SPEC] * held,
        out_specs=tuple(VMEM_SPEC for _ in outs),
        scratch_shapes=[pltpu.VMEM(s, d) for s, d in scratch],
        compiler_params=pltpu.CompilerParams(vmem_limit_bytes=limit),
        cost_estimate=pl.CostEstimate(
            flops=micros * 1000000, bytes_accessed=micros * 3600000, transcendentals=micros * 100000
        ),
        name=name,
    )(*args, *waits)
    return result


def extra_rows(values, heads):
    pieces = []
    for h in range(heads):
        row = values[h : h + 1, :]
        high = row.astype(B16).astype(F32)
        for part in (high, row - high):
            pieces += [part[:, at : at + LANES] for at in range(0, row.shape[1], LANES)]
    return jnp.concatenate(pieces, axis=0)


def extra_row(rows, head, count):
    at = 2 * head * count
    high = jnp.concatenate([rows[at + n : at + n + 1] for n in range(count)], axis=1)
    low = jnp.concatenate([rows[at + count + n : at + count + n + 1] for n in range(count)], axis=1)
    return high + low


def attend_kernel(
    bounds, begin_ref, own_ref, all_ref, out_ref, lse_ref, top, acc, *, heads, keys
):
    rows = own_ref.shape[0]
    top[...] = jnp.full_like(top, MASKED)
    acc[...] = jnp.zeros_like(acc)
    row_ids = bounds[2] + iota((1, rows), 1)
    begins = begin_ref[...]
    ones = (iota((keys, HEAD), 1) == 0).astype(B16)

    def step(n, masked):
        at = n * keys
        kv = all_ref[n, :keys, :]
        k = kv[:, :HEAD]
        v = jnp.concatenate([kv[:, HEAD:], ones], axis=1).T
        if masked:
            key_ids = at + iota((keys, rows), 0)
            seen = (key_ids <= row_ids) & (key_ids >= begins)
        for h in range(heads):
            q = own_ref[:, h * HEAD : (h + 1) * HEAD]
            s = lax.dot_general(k, q, LANE_DOT, preferred_element_type=F32)
            if masked:
                s = jnp.where(seen, s, MASKED)
            old = top[h : h + 1, :]
            new = jnp.maximum(old, jnp.max(s, axis=0, keepdims=True))
            p = jnp.exp(s - new).astype(B16)
            scale = jnp.exp(old - new)
            add = jnp.dot(v, p, preferred_element_type=F32)
            acc[h] = acc[h] * scale + add
            top[h : h + 1, :] = new

    pl.loop(bounds[0], bounds[1])(lambda n: step(n, True))
    pl.loop(bounds[1], bounds[3])(lambda n: step(n, False))
    pl.loop(bounds[3], bounds[4])(lambda n: step(n, True))
    for h in range(heads):
        total = acc[h, HEAD : HEAD + 1, :]
        out_ref[:, h * HEAD : (h + 1) * HEAD] = (acc[h, :HEAD, :] / total).T.astype(B16)
        lse_ref[h : h + 1, :] = top[h : h + 1, :] + jnp.log(total)


def attend(own, everything, begins, bounds, heads, keys, waits):
    rows = own.shape[0]
    return call(
        functools.partial(attend_kernel, heads=heads, keys=keys),
        "attend",
        12,
        (bounds, begins, own, everything),
        (((rows, heads * HEAD), B16), ((8, rows), F32)),
        (((8, rows), F32), ((heads, LANES, rows), F32)),
        waits,
    )


def minus_ones(lane, base, first):
    at = base + first
    return jnp.where((lane == at) | (lane == at + 1), -1.0, 0.0).astype(B16)


def key_sides(kv, heads):
    turned = jnp.concatenate([kv[:, HEAD:], kv[:, :HEAD]], axis=1)
    lane = iota(kv.shape, 1)
    zero = jnp.zeros_like(kv)
    sides = []
    for h in range(heads):
        mine = lane < HEAD if h == 0 else lane >= HEAD
        base = HEAD * (1 - h)
        keys_h = jnp.where(mine, kv if h == 0 else turned, zero)
        values_h = jnp.where(mine, turned if h == 0 else kv, minus_ones(lane, base, 0))
        both = jnp.concatenate([keys_h, minus_ones(lane, base, 2)], axis=1)
        sides.append((keys_h, values_h, both))
    return sides


def query_grad_kernel(
    bounds, begin_ref, own_ref, g_ref, all_ref, out_ref, acc, *, heads, keys
):
    rows = own_ref.shape[0]
    acc[...] = jnp.zeros_like(acc)
    row_ids = bounds[2] + iota((rows, keys), 0)
    begins = begin_ref[...]

    def step(n, masked):
        at = n * keys
        kv = all_ref[n, :keys, :]
        sides = key_sides(kv, heads)
        if masked:
            key_ids = at + iota((rows, keys), 1)
            seen = (key_ids <= row_ids) & (key_ids >= begins)
        total = acc[...]
        for h in range(heads):
            k, v, both = sides[h]
            g = g_ref[:, h * LANES : (h + 1) * LANES]
            q = jnp.concatenate([own_ref[...], g], axis=1)
            s = lax.dot_general(q, both, LANE_DOT, preferred_element_type=F32)
            if masked:
                s = jnp.where(seen, s, MASKED)
            gp = lax.dot_general(g, v, LANE_DOT, preferred_element_type=F32)
            ds = (jnp.exp(s) * gp).astype(B16)
            total = total + jnp.dot(ds, k, preferred_element_type=F32)
        acc[...] = total

    pl.loop(bounds[0], bounds[1])(lambda n: step(n, True))
    pl.loop(bounds[1], bounds[3])(lambda n: step(n, False))
    pl.loop(bounds[3], bounds[4])(lambda n: step(n, True))
    out_ref[...] = acc[...] * SCORE_SCALE


def query_grad(own, g_pack, everything, begins, bounds, heads, keys, waits):
    rows = own.shape[0]
    return call(
        functools.partial(query_grad_kernel, heads=heads, keys=keys),
        "query_grad",
        11,
        (bounds, begins, own, g_pack, everything),
        (((rows, LANES), F32),),
        (((rows, LANES), F32),),
        waits,
    )[0]


def key_grad_kernel(
    bounds, end_ref, own_ref, all_ref, g_ref, out_ref, acc_k, acc_v, *, heads, keys, at_g
):
    rows = out_ref.shape[0]
    acc_k[...] = jnp.zeros_like(acc_k)
    acc_v[...] = jnp.zeros_like(acc_v)
    key_ids = bounds[2] + iota((rows, keys), 0)
    ends = end_ref[...]
    kv = own_ref[:rows, :]
    turned = jnp.concatenate([kv[:, HEAD:], kv[:, :HEAD]], axis=1)
    first = iota(kv.shape, 1) < HEAD
    zero = jnp.zeros_like(kv)
    count = keys // LANES
    sides = []
    for h in range(heads):
        mine = first if h == 0 else jnp.logical_not(first)
        k = jnp.where(mine, kv if h == 0 else turned, zero)
        sides.append((k, jnp.where(mine, turned if h == 0 else kv, zero)))

    def step(n, masked):
        at = n * keys
        if masked:
            row_ids = at + iota((rows, keys), 1)
            seen = (key_ids <= row_ids) & (row_ids < ends)
        q = all_ref[n, :keys, :]
        g = g_ref[n, at_g : at_g + keys, :]
        extra = g_ref[n, at_g + keys :, :].astype(F32)
        delta_rows, lse_rows = (extra[: extra.shape[0] // 2], extra[extra.shape[0] // 2 :])
        for h in range(heads):
            k, v = sides[h]
            s = lax.dot_general(k, q, LANE_DOT, preferred_element_type=F32)
            s = s - extra_row(lse_rows, h, count)
            if masked:
                s = jnp.where(seen, s, MASKED)
            p = jnp.exp(s)
            gp = lax.dot_general(v, g, LANE_DOT, preferred_element_type=F32)
            ds = (p * (gp - extra_row(delta_rows, h, count))).astype(B16)
            acc_k[h] += jnp.dot(ds, q, preferred_element_type=F32)
            acc_v[h] += jnp.dot(p.astype(B16), g, preferred_element_type=F32)

    pl.loop(bounds[0], bounds[1])(lambda n: step(n, True))
    pl.loop(bounds[1], bounds[3])(lambda n: step(n, False))
    pl.loop(bounds[3], bounds[4])(lambda n: step(n, True))
    out_ref[:, :HEAD] = acc_k[0, :, :HEAD] + acc_k[1, :, HEAD:]
    out_ref[:, HEAD:] = acc_v[0, :, :HEAD] + acc_v[1, :, HEAD:]


def key_grad(own, everything, g_all, at_g, ends, bounds, heads, keys, waits):
    rows = ends.shape[0]
    return call(
        functools.partial(key_grad_kernel, heads=heads, keys=keys, at_g=at_g),
        "key_grad",
        12,
        (bounds, ends, own, everything, g_all),
        (((rows, LANES), F32),),
        (((heads, rows, LANES), F32), ((heads, rows, LANES), F32)),
        waits,
    )[0]


def assemble_kernel(picks, mix_ref, shared_ref, dt_ref, out_ref, *, att_cols, turned):
    kv_cols = KV * HEAD
    wide = mix_ref.shape[1]
    first = picks[0] == 0
    at = att_cols
    out_ref[:, :at] = mix_ref[:, :at]
    for part in range(2):
        tile = shared_ref[:, part * kv_cols : (part + 1) * kv_cols]
        out_ref[:, at : at + HEAD] = jnp.where(first, tile[:, :HEAD], tile[:, HEAD:])
        at += HEAD
    out_ref[:, at : at + wide - att_cols] = mix_ref[:, att_cols:]
    at += wide - att_cols
    out_ref[:, at : at + shared_ref.shape[1] - 2 * kv_cols] = shared_ref[:, 2 * kv_cols :]
    at += shared_ref.shape[1] - 2 * kv_cols
    if turned:
        heads, rows = dt_ref.shape
        steps = jnp.concatenate([dt_ref[...].astype(F32), jnp.zeros((LANES - heads, rows), F32)], axis=0)
        out_ref[:, at:] = steps.T.astype(B16)
    else:
        out_ref[:, at:] = jnp.zeros((out_ref.shape[0], LANES), B16)
        out_ref[:, at : at + dt_ref.shape[1]] = dt_ref[...]


def project_kernel(
    places, both_ref, before_ref, w_ref, cos_ref, sin_ref, out_ref, q_ref, kv_ref, z_ref, pre_ref, rim_ref
):
    rows = both_ref.shape[0]
    dim = w_ref.shape[0]
    at_z = 2 * LANES
    at_x = at_z + z_ref.shape[1]
    step = 2 * TILE
    for i in range(0, rows, step):
        r = slice(i, i + step)
        x = both_ref[r, :dim]
        t = jnp.dot(x, w_ref[:, :at_z], preferred_element_type=F32)
        cosine, sine = cos_ref[r, :], sin_ref[r, :]
        q, kv = t[:, :LANES], t[:, LANES:]
        q = (q * cosine + swap_halves(q) * sine).astype(B16)
        q_ref[r, :] = (q.astype(F32) * SCORE_SCALE).astype(B16)
        turned = kv * cosine + swap_halves(kv) * sine
        kv_ref[r, :] = jnp.where(iota(kv.shape, 1) < HEAD, turned, kv).astype(B16)
        z_ref[r, :] = jnp.dot(x, w_ref[:, at_z:at_x], preferred_element_type=F32)
        pre_ref[r, :] = jnp.dot(x, w_ref[:, at_x:], preferred_element_type=F32)
    wide = rim_ref.shape[1]
    rim = jnp.dot(before_ref[...], w_ref[:, at_x : at_x + wide], preferred_element_type=F32)
    rim_ref[...] = rim[before_ref.shape[0] - 8 :, :]
    if kv_ref.shape[0] > rows:
        chunk = out_ref.shape[0]
        for n in range(dim // LANES):
            at = rows + n * chunk
            kv_ref[at : at + chunk, :] = out_ref[:, n * LANES : (n + 1) * LANES]


def partner_rows(places, k, rows):
    return pl.ds(pl.multiple_of(jnp.bitwise_xor(places[3], k) * rows, rows), rows)


def in_order(places, refs, scratch):
    rows = refs[0].shape[0]
    for k, ref in enumerate(refs):
        scratch[partner_rows(places, k, rows), :] = ref[...]


def out_weights(all_ref, w_ref, first, chunk):
    for s in range(all_ref.shape[0]):
        for n in range(w_ref.shape[1] // LANES):
            at = first + n * chunk
            piece = all_ref[s, at : at + chunk, :]
            w_ref[s * chunk : (s + 1) * chunk, n * LANES : (n + 1) * LANES] = piece


def mix_out_kernel(places, attn_ref, gated_ref, gain_ref, all_ref, *refs, ssm_all, chunk, groups):
    w_ref = all_ref
    if chunk:
        w_ref, refs = (refs[-1], refs[:-1])
        out_weights(all_ref, w_ref, attn_ref.shape[0], chunk)
    part_refs, refs = (refs[-groups:], refs[:-groups])
    mixed_ref, total_ref = refs[-2:]
    rows = attn_ref.shape[0]
    att_cols = attn_ref.shape[1]
    total = refs[0][...]
    for ref in refs[1:-2]:
        total = total + ref[...]
    total_ref[...] = total
    squares = total.T
    for i in range(0, rows, TILE):
        r = slice(i, i + TILE)
        inverse = lax.rsqrt(squares[r, 0:1] / ssm_all + EPSILON)
        gnormed = (gated_ref[r, :].astype(F32) * inverse * gain_ref[...]).astype(B16)
        mixed_ref[r, :att_cols] = attn_ref[r, :]
        mixed_ref[r, att_cols:] = gnormed
    for k, ref in enumerate(part_refs):
        r = partner_rows(places, k, rows // groups)
        ref[...] = jnp.dot(mixed_ref[r, :], w_ref[...], preferred_element_type=F32).astype(B16)


def mix_back_kernel(
    places, w_ref, attn_ref, lse_ref, gated_ref, squares_ref, gain_ref, *refs, heads, ssm_all
):
    pack_ref, send_ref, scaled_ref, stat_ref, gain_out, deltas, grad_ref = refs[-7:]
    in_order(places, refs[:-7], grad_ref)
    rows = attn_ref.shape[0]
    att_cols = attn_ref.shape[1]
    squares = squares_ref[...].T
    lse = lse_ref[...].T
    total = jnp.zeros((1, gated_ref.shape[1]), F32)
    ones = jnp.ones((8, gated_ref.shape[1]), F32)
    for i in range(0, rows, TILE):
        r = slice(i, i + TILE)
        mixed = lax.dot_general(grad_ref[r, :], w_ref[...], LANE_DOT, preferred_element_type=F32)
        back = mixed[:, :att_cols].astype(B16).astype(F32)
        product = back * attn_ref[r, :].astype(F32)
        lane = iota(back.shape, 1)
        send_ref[r, :] = back.astype(B16)
        packed = jnp.zeros((TILE, LANES), F32)
        for h in range(heads):
            base = HEAD * (1 - h)
            tile = one_head(back, h)
            delta = jnp.sum(one_head(product, h), axis=1, keepdims=True)
            packed = into_lane(packed, h, delta)
            for n, column in enumerate((delta, lse[r, h : h + 1])):
                high = column.astype(B16).astype(F32)
                tile = jnp.where(lane == base + 2 * n, high, tile)
                tile = jnp.where(lane == base + 2 * n + 1, column - high, tile)
            pack_ref[r, h * LANES : (h + 1) * LANES] = tile.astype(B16)
        deltas[r, :] = packed
        grad = mixed[:, att_cols:]
        scaled = gated_ref[r, :].astype(F32) * lax.rsqrt(squares[r, 0:1] / ssm_all + EPSILON)
        grad_scaled = grad * gain_ref[...]
        scaled_ref[r, :] = grad_scaled
        stat_ref[:, r] = lax.dot_general(
            ones, grad_scaled * scaled, LANE_DOT, precision=HIGHEST, preferred_element_type=F32
        )
        total = total + jnp.sum(grad * scaled, axis=0, keepdims=True)
    gain_out[...] = jnp.broadcast_to(total, gain_out.shape)
    extra = jnp.concatenate(
        [extra_rows(deltas[...].T, heads), extra_rows(lse_ref[...], heads)], axis=0
    )
    send_ref[rows:, :] = extra.astype(B16)


def rows_of(ref, first, last):
    return jnp.concatenate([ref[k, first:last, :] for k in range(ref.shape[0])], axis=0)


def mlp_kernel(places, out_ref, *refs, chunk, groups):
    in_order(places, refs[:groups], refs[-1])
    in_ref = refs[-1]
    refs = refs[groups:-1]
    if chunk:
        all_ref, hidden_ref, weights_ref, *term_refs, gu_ref, down_ref, grad_ref = refs
        down_ref[...] = rows_of(all_ref, 0, chunk)
        gu_ref[...] = rows_of(all_ref, chunk, all_ref.shape[1])
    else:
        gu_ref, down_ref, hidden_ref, grad_ref, *term_refs = refs
    rows = in_ref.shape[0]
    half = hidden_ref.shape[1]
    dim = in_ref.shape[1]
    step = 2 * TILE
    for i in range(0, rows, step):
        r = slice(i, i + step)
        both = jnp.dot(in_ref[r, :], gu_ref[...], preferred_element_type=F32)
        back = lax.dot_general(out_ref[r, dim:], down_ref[...], LANE_DOT, preferred_element_type=F32)
        gate, up = both[:, :half], both[:, half:]
        sig = jax.nn.sigmoid(gate)
        soft = gate * sig
        hidden_ref[r, :] = (soft * up).astype(B16)
        grad_ref[r, :half] = (back * up * sig * (1.0 + gate * (1.0 - sig))).astype(B16)
        grad_ref[r, half:] = (back * soft).astype(B16)
    for k, ref in enumerate(term_refs):
        r = partner_rows(places, k, rows // groups)
        ref[...] = lax.dot_general(
            grad_ref[r, :], gu_ref[...], LANE_DOT, preferred_element_type=F32
        ).astype(B16)
    if chunk:
        parts, tall = weights_ref.shape[0], weights_ref.shape[1] - chunk
        strip = tall // groups
        for i in range(0, half, step):
            down = lax.dot_general(
                hidden_ref[:, i : i + step], out_ref[:, dim:], ROW_DOT, preferred_element_type=F32
            ).astype(B16)
            for n in range(step // chunk):
                weights_ref[i // chunk + n, :chunk, :] = down[n * chunk : (n + 1) * chunk]
        for i in range(0, dim, step):
            both = lax.dot_general(
                in_ref[:, i : i + step], grad_ref[...], ROW_DOT, preferred_element_type=F32
            ).astype(B16)
            for n in range(step // strip):
                b, s = divmod(i // strip + n, parts)
                at = chunk + b * strip
                weights_ref[s, at : at + strip, :] = both[n * strip : (n + 1) * strip]


def down_kernel(places, hidden_ref, w_ref, *out_refs, chunk):
    w = rows_of(w_ref, 0, chunk) if chunk else w_ref[...]
    for k, ref in enumerate(out_refs):
        r = partner_rows(places, k, ref.shape[0])
        ref[...] = jnp.dot(hidden_ref[r, :], w, preferred_element_type=F32).astype(B16)


def add_blocks_kernel(places, middle_ref, *refs):
    total = refs[0][...].astype(F32)
    for ref in refs[1:-1]:
        total = total + ref[...].astype(F32)
    refs[-1][...] = (middle_ref[...] + total).astype(B16)


def group_back_kernel(places, grad_ref, w_ref, early_ref, kept_ref, *out_refs):
    for k, ref in enumerate(out_refs):
        r = partner_rows(places, k, ref.shape[0])
        ref[...] = lax.dot_general(
            grad_ref[r, :], w_ref[...], LANE_DOT, preferred_element_type=F32
        ).astype(B16)
    kept_ref[...] = early_ref[...]


def split_kernel(places, own_ref, *out_refs):
    wide = out_refs[0].shape[1]
    for k, ref in enumerate(out_refs):
        r = partner_rows(places, k, ref.shape[0])
        ref[...] = own_ref[r, own_ref.shape[1] - wide :]


def norm_back_kernel(places, middle_ref, grad_ref, gain_ref, *refs):
    total_ref, sent_ref, gain_out = refs[-3:]
    grad = refs[0][...].astype(F32)
    for ref in refs[1:-3]:
        grad = grad + ref[...].astype(F32)
    middle = middle_ref[...]
    inverse = lax.rsqrt(jnp.mean(middle * middle, axis=1, keepdims=True) + EPSILON)
    scaled = middle * inverse
    grad_scaled = grad * gain_ref[...]
    mean = jnp.mean(grad_scaled * scaled, axis=1, keepdims=True)
    total = inverse * (grad_scaled - scaled * mean) + grad_ref[...].astype(F32)
    total_ref[...] = total
    sent_ref[...] = total.astype(B16)
    gain_out[...] = jnp.broadcast_to(jnp.sum(grad * scaled, axis=0, keepdims=True), gain_out.shape)


def turned_rows(values):
    rows = values.shape[0]
    if rows < LANES:
        values = jnp.concatenate([values, jnp.zeros((LANES - rows, LANES), F32)], axis=0)
    return values.T


def own_kernel(places, own_ref, early_ref, mixed_ref, dt_ref, gain_ref, taps_ref, *head_refs, heads, half, apart):
    rows = own_ref.shape[0]
    cols = early_ref.shape[1] - half
    mixed_ref[:, :LANES] = own_ref[:, :LANES].astype(F32)
    mixed_ref[:, LANES : LANES + cols] = early_ref[:, half:].astype(F32)
    mixed_ref[:, LANES + cols :] = own_ref[:, LANES : LANES + cols].astype(F32)
    tail = own_ref[:, own_ref.shape[1] - LANES :].astype(F32)
    turned = turned_rows(tail)
    at_gain = heads + 2 + CONV
    each = gain_ref.shape[1]
    dt_ref[...] = turned[:heads, :rows]
    gain_ref[...] = turned[at_gain : at_gain + 1, :each]
    taps_ref[...] = turned[at_gain + 1 : at_gain + 1 + CONV, :each]
    at = at_gain + 1 + CONV
    sums = jnp.sum(tail, axis=0, keepdims=True) if apart else tail[0:1]
    count = len(head_refs)
    for n, ref in enumerate(head_refs):
        total = sums[:, at + n * heads : at + (n + 1) * heads]
        if apart:
            total = total + sums[:, at + (count + n) * heads : at + (count + n + 1) * heads]
        ref[...] = total


def side_kernel(places, gain_ref, *refs, heads, apart):
    if apart:
        blocks_ref, refs = (refs[-1], refs[:-1])
        for k, ref in enumerate(refs[:-4]):
            blocks_ref[jnp.bitwise_xor(places[3], k)] = ref[...]
    else:
        blocks_ref = refs[0]
    shared_ref, first_ref, second_ref, taps_ref = refs[-4:]
    groups, strip, wide = blocks_ref.shape
    per_kv = groups // KV
    blocks = [blocks_ref[b].astype(F32) for b in range(groups)]
    sums = []
    for h in range(KV):
        total = blocks[h * per_kv][:, : 2 * HEAD]
        for b in range(h * per_kv + 1, (h + 1) * per_kv):
            total = total + blocks[b][:, : 2 * HEAD]
        sums.append(total)
    rest = blocks[0]
    for b in range(1, groups):
        rest = rest + blocks[b]
    for part in range(2):
        for h in range(KV):
            at = (part * KV + h) * HEAD
            shared_ref[:, at : at + HEAD] = sums[h][:, part * HEAD : (part + 1) * HEAD]
    shared_ref[:, 2 * KV * HEAD :] = rest[:, 2 * HEAD : wide - LANES]
    turned = turned_rows(rest[:, wide - LANES :])
    first_ref[...] = turned[heads : heads + 1, :strip] / gain_ref[...]
    second_ref[...] = turned[heads + 1 : heads + 2, :strip]
    taps_ref[...] = turned[heads + 2 : heads + 2 + CONV, : taps_ref.shape[1]]


def early_kernel(places, mixed_ref, both_ref, dz_ref, w_ref, *refs, parts):
    terms_ref, gain_ref, grad_ref = refs[-3:]
    in_order(places, refs[:-3], grad_ref)
    dim = grad_ref.shape[1]
    half = dim // 2
    rows = mixed_ref.shape[1]
    chunk = rows // parts
    tall = dim // parts
    at_z = 2 * LANES
    cols = dz_ref.shape[1]
    step = 2 * TILE
    for i in range(0, rows, step):
        out = lax.dot_general(
            mixed_ref[:, i : i + step], grad_ref[...], ROW_DOT, preferred_element_type=F32
        ).astype(B16)
        for n in range(step // chunk):
            at = (i // chunk + n) * tall
            piece = out[n * chunk : (n + 1) * chunk]
            terms_ref[at : at + chunk, :half] = piece[:, :half]
            terms_ref[at + chunk : at + tall, :half] = piece[:, half:]
    for i in range(0, dim, step):
        r = slice(i, i + step)
        grad = lax.dot_general(both_ref[:, r], dz_ref[...], ROW_DOT, preferred_element_type=F32)
        terms_ref[r, half:] = grad.astype(B16)
        gain_ref[r, :] = jnp.sum(grad * w_ref[r, at_z : at_z + cols].astype(F32), axis=1, keepdims=True)


def small_columns(tile, mine, gain_ref, taps_ref, heads_ref, second_ref, *, heads, groups, parts):
    dim = second_ref.shape[1]
    cols = gain_ref.shape[1]
    wide = taps_ref.shape[1]
    tall = dim // parts
    strip = tall // groups
    at_gain = heads + 2 + CONV
    at = at_gain + 1 + CONV
    lane = iota((8, LANES), 1)
    values = jnp.where(lane < heads, heads_ref[...], 0.0)
    high = values.astype(B16).astype(F32)
    base = jnp.zeros((1, LANES), F32)
    for n in range(3):
        base = base + pltpu.roll(high, at + n * heads, 1)[n : n + 1]
        base = base + pltpu.roll(values - high, at + (3 + n) * heads, 1)[n : n + 1]
    own_row = iota(tile.shape, 0) % tall == mine
    tile[...] = jnp.where(own_row, base, 0.0)

    def columns(first, rows, width):
        pieces = [jnp.zeros((first, width), F32)] + rows
        left = LANES - first - sum(row.shape[0] for row in rows)
        return jnp.concatenate(pieces + [jnp.zeros((left, width), F32)], axis=0).T

    own = columns(at_gain, [gain_ref[0:1, :], taps_ref[:CONV, :cols]], cols)
    each = cols // parts
    for s in range(parts):
        tile[s * tall : s * tall + each, :] += own[s * each : (s + 1) * each]
    side = columns(heads + 2, [taps_ref[:CONV, cols:]], wide - cols)
    each = (wide - cols) // (groups * parts)
    second = columns(heads + 1, [second_ref[0:1, :]], dim)
    for b in range(groups):
        for s in range(parts):
            there = s * tall + b * strip
            n = b * parts + s
            tile[there : there + each, :] += side[n * each : (n + 1) * each]
            tile[there : there + strip, :] += second[n * strip : (n + 1) * strip]


def weight_grad_kernel(
    places, q_ref, kv_ref, z_ref, x_ref, rim_ref, dt_ref, cos_ref, sin_ref, w_ref, both_ref, early_ref,
    *refs, heads, groups, parts, in_strips,
):
    if in_strips:
        small_refs, (pre_ref, terms_ref, tile) = refs[:4], refs[4:]
        small_columns(tile, places[2], *small_refs, heads=heads, groups=groups, parts=parts)
    else:
        tile, pre_ref, terms_ref = refs
    rows = q_ref.shape[0]
    dim = w_ref.shape[0]
    cols = heads * HEAD
    wide = x_ref.shape[1]
    at_z = 2 * LANES
    at_x = at_z + cols
    at_dt = at_x + wide
    for i in range(0, rows, TILE):
        r = slice(i, i + TILE)
        cosine, sine = cos_ref[r, :], sin_ref[r, :]
        q, kv = q_ref[r, :], kv_ref[r, :]
        pre_ref[r, :LANES] = (q * cosine - swap_halves(q) * sine).astype(B16)
        turned = kv * cosine - swap_halves(kv) * sine
        pre_ref[r, LANES : 2 * LANES] = jnp.where(iota(kv.shape, 1) < HEAD, turned, kv).astype(B16)
        pre_ref[r, at_z:at_x] = z_ref[r, :]
        x = x_ref[r, :]
        if i + TILE == rows:
            x = jnp.concatenate([x[: TILE - 8], x[TILE - 8 :] + rim_ref[...]], axis=0)
        pre_ref[r, at_x:at_dt] = x.astype(B16)
        pre_ref[r, at_dt:] = dt_ref[r, :]
    block = dim // groups
    strip = block // parts
    mixed = LANES + cols
    sides = slice(mixed + LANES, mixed + 3 * LANES)
    ends = slice(mixed + 3 * LANES, mixed + 4 * LANES)
    lane = iota((block, LANES), 1)
    for b in range(groups):
        r = slice(b * block, (b + 1) * block)
        x = both_ref[:, r]
        near = lax.dot_general(x, pre_ref[:, :at_z], ROW_DOT, preferred_element_type=F32)
        far = lax.dot_general(x, pre_ref[:, at_x:], ROW_DOT, preferred_element_type=F32)
        gain = jnp.sum(near * w_ref[r, :at_z].astype(F32), axis=1, keepdims=True)
        gain = gain + jnp.sum(far * w_ref[r, at_x:].astype(F32), axis=1, keepdims=True)
        gain = gain + early_ref[r, :]
        terms_ref[r, :LANES] = near[:, :LANES].astype(B16)
        terms_ref[r, LANES:mixed] = far[:, :cols].astype(B16)
        if in_strips:
            for s in range(parts):
                here = slice(s * strip, (s + 1) * strip)
                first = s * groups * strip + b * strip
                there = slice(first, first + strip)
                terms_ref[there, mixed : mixed + LANES] = near[here, LANES:].astype(B16)
                terms_ref[there, sides] = far[here, cols:wide].astype(B16)
                at_gain = iota((strip, LANES), 1) == heads
                tile[there, :] = jnp.where(at_gain, gain[here], tile[there, :])
            tile[r, :] = jnp.where(lane < heads, far[:, wide:], tile[r, :])
        else:
            terms_ref[r, mixed : mixed + LANES] = near[:, LANES:].astype(B16)
            terms_ref[r, sides] = far[:, cols:wide].astype(B16)
            tail = jnp.where(lane < heads, far[:, wide:], tile[r, :])
            terms_ref[r, ends] = jnp.where(lane == heads, gain, tail).astype(B16)
    if in_strips:
        terms_ref[:, ends] = tile[...].astype(B16)


def iota(shape, dim):
    return lax.broadcasted_iota(jnp.int32, shape, dim)


def per_head(columns, pair):
    shape = (columns.shape[0], LANES)
    return jnp.where(
        iota(shape, 1) < HEAD, columns[:, 2 * pair : 2 * pair + 1], columns[:, 2 * pair + 1 : 2 * pair + 2]
    )


def one_head(values, head):
    keep = (iota(values.shape, 1) < HEAD) == (head % 2 == 0)
    return jnp.where(keep, values, jnp.zeros_like(values))


def into_lane(columns, head, column):
    return jnp.where(iota(columns.shape, 1) == head, column, columns)


def silu_slope(v, sig):
    return sig * (1.0 + v * (1.0 - sig))


def tap_window(ext_ref, tap, first, amount, places):
    return ext_ref[first + 8 - (CONV - 1) + tap : first + 8 - (CONV - 1) + tap + amount, :]


def span_kernel(places, begin_ref, pre_ref, rim_ref, taps_ref, params_ref, u_ref, intra_ref, cum_ref, state_ref, ext, xb, *, heads, at_x, at_dt, nstate):
    rows = pre_ref.shape[0]
    cols = heads * HEAD
    first_row, last_begin = places[0], places[1]
    ext[0:8, :] = rim_ref[...]
    ext[8 : 8 + rows, :] = pre_ref[:, at_x:at_dt]
    local = begin_ref[...] - first_row
    row_ids = iota((rows, 1), 0)
    for i in range(0, rows, TILE):
        total = jnp.zeros((TILE, ext.shape[1]), F32)
        for tap in range(CONV):
            seen = row_ids[i : i + TILE] - (CONV - 1) + tap >= local[i : i + TILE]
            window = tap_window(ext, tap, i, TILE, places)
            total = total + jnp.where(seen, window, 0.0) * taps_ref[tap : tap + 1, :]
        u_ref[i : i + TILE, :] = total
        xb[i : i + TILE, :] = (total * jax.nn.sigmoid(total)).astype(B16)
    raw = pre_ref[:, at_dt : at_dt + LANES] + params_ref[0:1, :]
    dt = jnp.maximum(raw, 0.0) + jnp.log1p(jnp.exp(-jnp.abs(raw)))
    lower = (iota((rows, rows), 0) >= iota((rows, rows), 1)).astype(F32)
    cum = jnp.dot(lower, dt * params_ref[1:2, :], precision=HIGHEST, preferred_element_type=F32)
    cum_ref[:, :LANES] = cum
    cum_ref[:, LANES:] = dt
    cum_t, dt_t = cum.T, dt.T
    last = cum[rows - 1 : rows, :]
    closing = row_ids + first_row >= last_begin
    to_end = jnp.where(closing, jnp.exp(last - cum) * dt, 0.0)
    for i in range(0, rows, TILE):
        width = i + TILE
        c = xb[i : i + TILE, cols + nstate : cols + 2 * nstate]
        b = xb[:width, cols : cols + nstate]
        inner = lax.dot_general(c, b, LANE_DOT, preferred_element_type=F32)
        key = iota((TILE, width), 1)
        seen = (key <= iota((TILE, width), 0) + i) & (key >= local[i : i + TILE])
        for pair in range(heads // 2):
            out = []
            for h in (2 * pair, 2 * pair + 1):
                spread = jnp.where(seen, cum[i : i + TILE, h : h + 1] - cum_t[h : h + 1, :width], MASKED)
                weights = (jnp.exp(spread) * inner * dt_t[h : h + 1, :width]).astype(B16)
                out.append(jnp.dot(weights, xb[:width, pair * LANES : (pair + 1) * LANES], preferred_element_type=F32))
            intra_ref[i : i + TILE, pair * LANES : (pair + 1) * LANES] = jnp.where(iota((TILE, LANES), 1) < HEAD, out[0], out[1])
    b_all = xb[:, cols : cols + nstate]
    for pair in range(heads // 2):
        at = slice(pair * LANES, (pair + 1) * LANES)
        closed = (xb[:, at].astype(F32) * per_head(to_end, pair)).astype(B16)
        state_ref[at, :] = lax.dot_general(closed, b_all, ROW_DOT, preferred_element_type=F32).astype(B16)
    decay = jnp.where(last_begin < first_row, jnp.exp(last), 0.0)
    high = decay.astype(B16)
    low = (decay - high.astype(F32)).astype(B16)
    both = jnp.concatenate([jnp.broadcast_to(high.astype(F32), (LANES // 2, LANES)), jnp.broadcast_to(low.astype(F32), (LANES // 2, LANES))], axis=0)
    state_ref[cols : cols + 16, :] = both.T[:16, :].astype(B16)


def span_forward(places, begins, pre, rim, taps, params, heads, at_x, at_dt, nstate):
    rows = pre.shape[0]
    wide = at_dt - at_x
    cols = heads * HEAD
    return call(
        functools.partial(span_kernel, heads=heads, at_x=at_x, at_dt=at_dt, nstate=nstate),
        "span_forward",
        8,
        (places, begins, pre, rim, taps, params),
        (((rows, wide), F32), ((rows, cols), F32), ((rows, 2 * LANES), F32), ((cols + 16, nstate), B16)),
        (((rows + 8, wide), F32), ((rows, wide), B16)),
    )


def decay_of(states_ref, k, head, cols):
    tail = states_ref[k, cols + head - head % 8 : cols + head - head % 8 + 8, :].astype(F32)
    row = tail[head % 8 : head % 8 + 1, :]
    return row[:, 0:1] + row[:, LANES // 2 : LANES // 2 + 1]


def finish_kernel(places, begin_ref, states_ref, u_ref, intra_ref, cum_ref, z_ref, params_ref, gated_ref, v_ref, state_ref, squares_ref, *, heads, nstate):
    rows = u_ref.shape[0]
    cols = heads * HEAD
    state_ref[...] = jnp.zeros_like(state_ref)

    def fold(k):
        for h in range(heads):
            at = slice(h * HEAD, (h + 1) * HEAD)
            state_ref[at, :] = state_ref[at, :] * decay_of(states_ref, k, h, cols) + states_ref[k, at, :].astype(F32)

    pl.loop(0, places[2])(fold)
    carried = begin_ref[...] < places[0]
    for i in range(0, rows, TILE):
        r = slice(i, i + TILE)
        enter = jnp.where(carried[r], jnp.exp(cum_ref[r, :LANES]), 0.0)
        uc = u_ref[r, cols + nstate : cols + 2 * nstate]
        c = (uc * jax.nn.sigmoid(uc)).astype(B16)
        total = jnp.zeros((8, TILE), F32)
        for pair in range(heads // 2):
            at = slice(pair * LANES, (pair + 1) * LANES)
            y = lax.dot_general(c, state_ref[at, :].astype(B16), LANE_DOT, preferred_element_type=F32)
            ux = u_ref[r, at]
            x = ux * jax.nn.sigmoid(ux)
            skip = per_head(params_ref[2:3, :], pair)
            v = intra_ref[r, at] + per_head(enter, pair) * y + skip * x
            z = z_ref[r, at]
            gated = (v * (z * jax.nn.sigmoid(z))).astype(B16)
            v_ref[r, at] = v
            gated_ref[r, at] = gated
            g = gated.astype(F32)
            total = total + lax.dot_general(jnp.ones((8, LANES), F32), g * g, LANE_DOT, precision=HIGHEST, preferred_element_type=F32)
        squares_ref[:, r] = total


def span_finish(places, begins, states, u, intra, cum, z, params, heads, nstate):
    rows = u.shape[0]
    cols = heads * HEAD
    return call(
        functools.partial(finish_kernel, heads=heads, nstate=nstate),
        "span_finish",
        7,
        (places, begins, states, u, intra, cum, z, params),
        (((rows, cols), B16), ((rows, cols), F32), ((cols, nstate), F32), ((8, rows), F32)),
        (),
    )


def gate_back_kernel(places, begin_ref, scaled_ref, gated_ref, squares_ref, u_ref, cum_ref, z_ref, v_ref, send_ref, *refs, heads, nstate, ssm_all):
    back_ref, dz_ref, state_ref, eg = refs[-4:]
    total = refs[0][...]
    for ref in refs[1:-4]:
        total = total + ref[...]
    rows = u_ref.shape[0]
    cols = heads * HEAD
    carried = begin_ref[...] < places[0]
    squares, stat = squares_ref[...].T, total.T
    uc = u_ref[:, cols + nstate : cols + 2 * nstate]
    c = (uc * jax.nn.sigmoid(uc)).astype(B16)
    for i in range(0, rows, TILE):
        r = slice(i, i + TILE)
        enter = jnp.where(carried[r], jnp.exp(cum_ref[r, :LANES]), 0.0)
        inverse = lax.rsqrt(squares[r, 0:1] / ssm_all + EPSILON)
        mean = stat[r, 0:1] / ssm_all
        for pair in range(heads // 2):
            at = slice(pair * LANES, (pair + 1) * LANES)
            z = z_ref[r, at]
            sig = jax.nn.sigmoid(z)
            scaled = gated_ref[r, at].astype(F32) * inverse
            gg = (inverse * (scaled_ref[r, at] - scaled * mean)).astype(B16)
            back_ref[r, at] = gg
            gg = gg.astype(F32)
            dz_ref[r, at] = (gg * v_ref[r, at] * silu_slope(z, sig)).astype(B16)
            eg[r, at] = (gg * (z * sig) * per_head(enter, pair)).astype(B16)
    state_ref[:cols, :] = lax.dot_general(eg[...], c, ROW_DOT, preferred_element_type=F32).astype(B16)
    state_ref[cols:, :] = send_ref[...]


def gate_back(places, begins, scaled, gated, squares, stats, u, cum, z, v, send, heads, nstate, ssm_all):
    rows = u.shape[0]
    cols = heads * HEAD
    return call(
        functools.partial(gate_back_kernel, heads=heads, nstate=nstate, ssm_all=ssm_all),
        "gate_back",
        5,
        (places, begins, scaled, gated, squares, u, cum, z, v, send) + stats,
        (((rows, cols), B16), ((rows, cols), B16), ((cols + send.shape[0], nstate), B16)),
        (((rows, cols), B16),),
    )


def back_kernel(places, begin_ref, g_ref, z_ref, pre_ref, rim_ref, u_ref, cum_ref, state_ref, states_ref, grads_ref, taps_ref, params_ref, gx_ref, gdt_ref, rim_out, taps_out, small_out, ext, gext, xb, gb, later, dxb, lane_sum, cols_sum, *, heads, at_x, at_dt, nstate):
    rows = u_ref.shape[0]
    cols = heads * HEAD
    wide = at_dt - at_x
    count = states_ref.shape[0]
    pairs = heads // 2
    first_row, last_begin, mine = places[0], places[1], places[2]
    later[...] = jnp.zeros_like(later)

    def fold(n):
        k = count - 1 - n
        for h in range(heads):
            at = slice(h * HEAD, (h + 1) * HEAD)
            later[at, :] = later[at, :] * decay_of(states_ref, k, h, cols) + grads_ref[k, at, :].astype(F32)

    pl.loop(0, count - 1 - mine)(fold)
    local = begin_ref[...] - first_row
    row_ids = iota((rows, 1), 0)
    cum = cum_ref[:, :LANES]
    dt = cum_ref[:, LANES:]
    cum_t, dt_t = cum.T, dt.T
    last = cum[rows - 1 : rows, :]
    leave = jnp.where(row_ids + first_row >= last_begin, jnp.exp(last - cum), 0.0)
    enter = jnp.where(begin_ref[...] < first_row, jnp.exp(cum), 0.0)
    to_end = leave * dt
    for i in range(0, rows, TILE):
        r = slice(i, i + TILE)
        u = u_ref[r, :]
        xb[r, :] = (u * jax.nn.sigmoid(u)).astype(B16)
        z = z_ref[r, :]
        gb[r, :] = (g_ref[r, :].astype(F32) * (z * jax.nn.sigmoid(z))).astype(B16)
    dxb[...] = jnp.zeros_like(dxb)
    cols_sum[...] = jnp.zeros_like(cols_sum)
    b_at = slice(cols, cols + nstate)
    c_at = slice(cols + nstate, cols + 2 * nstate)
    for i in range(0, rows, TILE):
        width = i + TILE
        r = slice(i, i + TILE)
        inner = lax.dot_general(xb[r, c_at], xb[:width, b_at], LANE_DOT, preferred_element_type=F32)
        key = iota((TILE, width), 1)
        seen = (key <= iota((TILE, width), 0) + i) & (key >= local[r])
        grad_inner = jnp.zeros((TILE, width), F32)
        sums = jnp.zeros((TILE, LANES), F32)
        for h in range(heads):
            at = slice(h // 2 * LANES, (h // 2 + 1) * LANES)
            g = one_head(gb[r, at], h)
            spread = jnp.where(seen, cum[r, h : h + 1] - cum_t[h : h + 1, :width], MASKED)
            decays = jnp.exp(spread)
            steps = dt_t[h : h + 1, :width]
            pairing = lax.dot_general(g, xb[:width, at], LANE_DOT, preferred_element_type=F32)
            paired = pairing * decays
            grad_inner = grad_inner + paired * steps
            both = paired * inner
            cols_sum[h : h + 1, :width] += jnp.sum(both, axis=0, keepdims=True)
            sums = into_lane(sums, h, jnp.sum(both * steps, axis=1, keepdims=True))
            weights = (decays * inner * steps).astype(B16)
            dxb[:width, at] += lax.dot_general(weights, g, ROW_DOT, preferred_element_type=F32)
        lane_sum[r, :] = sums
        grad_inner = grad_inner.astype(B16)
        dxb[r, c_at] += jnp.dot(grad_inner, xb[:width, b_at], preferred_element_type=F32)
        dxb[:width, b_at] += lax.dot_general(grad_inner, xb[r, c_at], ROW_DOT, preferred_element_type=F32)
    from_cols = jnp.concatenate([cols_sum[...], jnp.zeros((LANES - 8, rows), F32)], axis=0).T
    state_b = state_ref[...].astype(B16)
    later_b = later[...].astype(B16)
    entered = jnp.zeros((rows, LANES), F32)
    closed = jnp.zeros((rows, LANES), F32)
    skips = jnp.zeros((1, LANES), F32)
    chained = jnp.zeros((1, LANES), F32)
    for pair in range(pairs):
        at = slice(pair * LANES, (pair + 1) * LANES)
        x = xb[:, at].astype(F32)
        g = gb[:, at].astype(F32)
        y = lax.dot_general(xb[:, c_at], state_b[at, :], LANE_DOT, preferred_element_type=F32)
        q = lax.dot_general(xb[:, b_at], later_b[at, :], LANE_DOT, preferred_element_type=F32)
        ends = per_head(to_end, pair)
        dxb[:, c_at] += jnp.dot((g * per_head(enter, pair)).astype(B16), state_b[at, :], preferred_element_type=F32)
        dxb[:, b_at] += jnp.dot((x * ends).astype(B16), later_b[at, :], preferred_element_type=F32)
        dxb[:, at] += ends * q + g * per_head(params_ref[2:3, :], pair)
        gy, xq, gx = g * y, x * q, jnp.sum(g * x, axis=0, keepdims=True)
        kept = jnp.sum(later[at, :] * state_ref[at, :], axis=1, keepdims=True)
        for h in (2 * pair, 2 * pair + 1):
            entered = into_lane(entered, h, jnp.sum(one_head(gy, h), axis=1, keepdims=True))
            closed = into_lane(closed, h, jnp.sum(one_head(xq, h), axis=1, keepdims=True))
            skips = into_lane(skips, h, jnp.sum(one_head(gx, h), axis=1, keepdims=True))
            half = slice(h % 2 * HEAD, (h % 2 + 1) * HEAD)
            chained = into_lane(chained, h, jnp.sum(kept[half], axis=0, keepdims=True))
    decay = jnp.where(last_begin < first_row, jnp.exp(last), 0.0)
    ended = closed * to_end
    grad_cum = lane_sum[...] - from_cols * dt + entered * enter - ended
    at_last = jnp.sum(ended, axis=0, keepdims=True) + decay * chained
    grad_cum = grad_cum + jnp.where(row_ids == rows - 1, at_last, 0.0)
    upper = (iota((rows, rows), 0) <= iota((rows, rows), 1)).astype(F32)
    grad_log = jnp.dot(upper, grad_cum, precision=HIGHEST, preferred_element_type=F32)
    rate = params_ref[1:2, :]
    grad_dt = from_cols + closed * leave + grad_log * rate
    grad_raw = grad_dt * jax.nn.sigmoid(pre_ref[:, at_dt : at_dt + LANES] + params_ref[0:1, :])
    grad_raw = jnp.where(iota((rows, LANES), 1) < heads, grad_raw, 0.0)
    gdt_ref[...] = grad_raw.astype(B16)
    small_out[0:1, :] = jnp.sum(grad_log * dt, axis=0, keepdims=True) * rate
    small_out[1:2, :] = jnp.sum(grad_raw, axis=0, keepdims=True)
    small_out[2:3, :] = skips
    small_out[3:8, :] = jnp.zeros((5, LANES), F32)
    ext[0:8, :] = rim_ref[...]
    ext[8 : 8 + rows, :] = pre_ref[:, at_x:at_dt]
    gext[...] = jnp.zeros_like(gext)
    taps_out[...] = jnp.zeros_like(taps_out)
    for i in range(0, rows, TILE):
        r = slice(i, i + TILE)
        u = u_ref[r, :]
        du = dxb[r, :] * silu_slope(u, jax.nn.sigmoid(u))
        for tap in range(CONV):
            seen = row_ids[r] - (CONV - 1) + tap >= local[r]
            part = jnp.where(seen, du, 0.0)
            taps_out[tap : tap + 1, :] += jnp.sum(part * tap_window(ext, tap, i, TILE, places), axis=0, keepdims=True)
            at = 8 - (CONV - 1) + tap + i
            gext[at : at + TILE, :] += part * taps_ref[tap : tap + 1, :]
    rim_out[...] = gext[0:8, :]
    gx_ref[...] = gext[8:, :]


def span_back(places, begins, back, z, pre, rim, u, cum, state, states, grads, taps, params, heads, at_x, at_dt, nstate, waits):
    rows = u.shape[0]
    cols = heads * HEAD
    wide = at_dt - at_x
    return call(
        functools.partial(back_kernel, heads=heads, at_x=at_x, at_dt=at_dt, nstate=nstate),
        "span_back",
        16,
        (places, begins, back, z, pre, rim, u, cum, state, states, grads, taps, params),
        (((rows, wide), F32), ((rows, LANES), B16), ((8, wide), F32), ((8, wide), F32), ((8, LANES), F32)),
        (((rows + 8, wide), F32), ((rows + 8, wide), F32), ((rows, wide), B16), ((rows, cols), B16),
         ((cols, nstate), F32), ((rows, wide), F32), ((rows, LANES), F32), ((8, rows), F32)),
        waits,
    )


def shards(
    x_in,
    lengths,
    norm1_gain,
    w_mix_in,
    w_dt,
    w_shared,
    conv_x,
    conv_bc,
    a_log,
    dt_bias,
    d_skip,
    gate_gain,
    w_out,
    norm2_gain,
    w_gate,
    w_up,
    w_down,
    d_out,
):
    tok_rows = x_in.shape[0]
    groups = lax.axis_size("branch")
    branch_id = lax.axis_index("branch")
    seq_id = lax.axis_index("seq")
    seq_rows = tok_rows * groups
    group_first = seq_id * seq_rows
    att_heads = HEADS_ATT // groups
    att_cols = att_heads * HEAD
    ssm_heads = w_dt.shape[1]
    ssm_cols = ssm_heads * HEAD
    kv_cols = KV * HEAD
    f32 = jnp.float32
    bf16 = jnp.bfloat16
    dim = x_in.shape[1]
    parts = lax.axis_size("seq")
    chunk = w_out.shape[0] // groups
    att_chunks = parts * att_cols // (att_cols + ssm_cols)
    ssm_chunks = parts - att_chunks
    strip = dim // (groups * parts)
    hidden_all = w_gate.shape[1]
    hidden_a = hidden_all * att_cols // ((att_cols + ssm_cols) * groups)
    hidden_s = hidden_all // groups - hidden_a
    hidden_b = hidden_a + hidden_s

    def spot(c):
        first = groups * att_chunks
        if c < first:
            return (c // att_chunks) * parts + c % att_chunks
        return ((c - first) // ssm_chunks) * parts + att_chunks + (c - first) % ssm_chunks

    to_heads = [((c % groups) * parts + c // groups, spot(c)) for c in range(groups * parts)]
    from_heads = [(spot(c), c) for c in range(groups * parts)]

    def branch_parts(part):
        routes = [[(i, i ^ k) for i in range(groups)] for k in range(1, groups)]
        return (part,) + tuple(lax.ppermute(part, "branch", route) for route in routes)

    def branch_swap(blocks):
        routes = [[(i, i ^ k) for i in range(groups)] for k in range(1, groups)]
        moved = [lax.ppermute(block, "branch", route) for block, route in zip(blocks[1:], routes)]
        return (blocks[0],) + tuple(moved)

    def ordered(blocks):
        stacked = jnp.stack(blocks)
        picked = [lax.dynamic_index_in_dim(stacked, branch_id ^ n, 0, False) for n in range(groups)]
        return jnp.concatenate(picked, axis=0)

    def branch_exchange(blocks):
        return lax.all_to_all(blocks, "branch", 0, 0, tiled=True)

    def branch_gather(part):
        copies = branch_exchange(jnp.broadcast_to(part[None], (groups,) + part.shape))
        return copies.reshape((groups * part.shape[0],) + part.shape[1:])

    def branch_scatter(terms):
        blocks = terms.astype(bf16).reshape((groups, -1) + terms.shape[1:])
        return jnp.sum(lax.all_to_all(blocks, "branch", 0, 0, tiled=True).astype(f32), axis=0)

    kv_head = branch_id * att_heads // (HEADS_ATT // KV)
    side_cols = w_shared.shape[1] - 2 * kv_cols
    w1_cols = w_mix_in.shape[1] + 2 * HEAD + side_cols + LANES
    turned = w_dt.shape[0] % LANES == 0
    w1_part = call(
        functools.partial(assemble_kernel, att_cols=att_cols, turned=turned),
        "assemble",
        1,
        (kv_head[None], w_mix_in, w_shared, w_dt.T if turned else w_dt),
        (((w_mix_in.shape[0], w1_cols), B16),),
        (),
    )[0]
    w1 = lax.all_gather(w1_part, "seq", axis=0, tiled=True)

    def own_columns(w):
        return [
            lax.dynamic_slice_in_dim(w, branch_id * hidden_a, hidden_a, 1),
            lax.dynamic_slice_in_dim(w, groups * hidden_a + branch_id * hidden_s, hidden_s, 1),
        ]

    row_part = jnp.concatenate(
        [
            lax.dynamic_slice_in_dim(w_out, branch_id * chunk, chunk, 0),
            lax.dynamic_slice_in_dim(w_down, branch_id * chunk, chunk, 0),
        ],
        axis=0,
    )
    row_part = lax.ppermute(row_part, ("branch", "seq"), to_heads)
    out_part = row_part[:chunk]
    mlp_part = jnp.concatenate(
        [row_part[chunk:], jnp.concatenate(own_columns(w_gate) + own_columns(w_up), axis=1)], axis=0
    )
    x_rows = x_in.astype(f32)
    scaled1, inverse1 = rms_parts(x_rows)
    normed1 = (scaled1 * norm1_gain).astype(bf16)
    both_in = branch_gather(jnp.concatenate([normed1, d_out], axis=1))
    d_out_g = both_in[:, dim:]
    before = from_behind(both_in[seq_rows - 16 :, :dim], "seq", 1)
    row_ids = group_first + jnp.arange(seq_rows, dtype=jnp.int32)
    seq_ends = jnp.cumsum(lengths)

    def begin_of(ids):
        return jnp.max(jnp.where(seq_ends <= ids[..., None], seq_ends, 0), axis=-1)

    def end_of(ids):
        return jnp.min(jnp.where(seq_ends > ids[..., None], seq_ends, seq_rows * parts), axis=-1)

    begins = begin_of(row_ids)
    ends = end_of(row_ids)
    position = row_ids - begins
    row_last = group_first + seq_rows - 1
    begin_first, begin_last = (begin_of(group_first), begin_of(row_last))
    end_first, end_last = (end_of(group_first), end_of(row_last))
    here = seq_id
    query_lo = begin_first // seq_rows
    query_clear = jnp.minimum(jnp.maximum(query_lo, -(-begin_last // seq_rows)), here)
    query_bounds = jnp.stack([query_lo, query_clear, group_first, here, here + 1])
    key_hi = -(-end_last // seq_rows)
    key_clear = jnp.maximum(here + 1, jnp.minimum(end_first // seq_rows, key_hi))
    key_bounds = jnp.stack([here, here + 1, group_first, key_clear, key_hi])
    places = jnp.stack([group_first, begin_last, seq_id, branch_id])
    begins_col, begins_row, ends_col = (begins[:, None], begins[None, :], ends[:, None])
    at_dt = ssm_cols + side_cols
    nstate = conv_bc.shape[1] // 2
    taps = jnp.pad(jnp.concatenate([conv_x, conv_bc], axis=1), ((0, 8 - CONV), (0, 0)))
    params = jnp.stack([dt_bias, -jnp.exp(a_log), d_skip])
    params = jnp.pad(params, ((0, 5), (0, LANES - ssm_heads)))
    ssm_all = gate_gain.shape[0]
    gain_row = lax.dynamic_slice_in_dim(gate_gain, branch_id * ssm_cols, ssm_cols, 0)[None, :]
    cosine, sine = rotate_tables(position)
    packed = chunk if chunk % 16 == 0 and strip % 16 == 0 else 0
    kv_rows = seq_rows + packed * dim // LANES
    queries, kv, z_pre, pre, rim = call(
        project_kernel,
        "project",
        5,
        (places, both_in, before, w1, cosine, sine, out_part),
        (
            ((seq_rows, LANES), B16),
            ((kv_rows, LANES), B16),
            ((seq_rows, ssm_cols), F32),
            ((seq_rows, at_dt + LANES), F32),
            ((8, at_dt), F32),
        ),
        (),
        (
            begins_col,
            begins_row,
            ends_col,
            query_bounds,
            key_bounds,
            taps,
            params,
            gain_row,
            mlp_part,
        ),
    )
    kv_all = lax.all_gather(kv, "seq", axis=0)
    w_out_b = kv_all if packed else lax.all_gather(out_part, "seq", axis=0, tiled=True)
    mlp_all = lax.all_gather(mlp_part, "seq", axis=0)
    if packed:
        mlp_weights, down_weights = ((mlp_all,), mlp_all)
        mlp_scratch = (
            ((dim, 2 * hidden_b), B16),
            ((parts * chunk, dim), B16),
            ((seq_rows, 2 * hidden_b), B16),
        )
    else:
        down_weights = mlp_all[:, :chunk].reshape(parts * chunk, dim)
        mlp_weights = (mlp_all[:, chunk:].reshape(dim, 2 * hidden_b), down_weights)
        mlp_scratch = ()
    u, intra, cum, state = span_forward(
        places, begins_col, pre, rim, taps, params, ssm_heads, 0, at_dt, nstate
    )
    states = lax.all_gather(state, "seq", axis=0)
    gated_b, gated_v, state_in, squares = span_finish(
        places, begins_col, states, u, intra, cum, z_pre, params, ssm_heads, nstate
    )
    attn_out, lse = attend(
        queries, kv_all, begins_row, query_bounds, att_heads, seq_rows, (gated_b,)
    )
    q_all = lax.all_gather(queries, "seq", axis=0)

    out_shape = (parts * chunk, dim)
    row_blocks = (((tok_rows, dim), B16),) * groups
    mixed_out, squares, *out_terms = call(
        functools.partial(mix_out_kernel, ssm_all=ssm_all, chunk=packed, groups=groups),
        "mix_out",
        3,
        (places, attn_out, gated_b, gain_row, w_out_b) + branch_parts(squares),
        (((seq_rows, att_cols + ssm_cols), B16), ((8, seq_rows), F32))
        + row_blocks
        + (((out_shape, B16),) if packed else ()),
        (),
    )
    w_out_b = out_terms.pop() if packed else w_out_b
    projected = sum(block.astype(f32) for block in branch_swap(out_terms))
    middle = x_rows + projected
    scaled2, inverse2 = rms_parts(middle)
    normed2 = branch_parts((scaled2 * norm2_gain).astype(bf16))
    middle_shape = (parts, chunk + dim // parts, dim) if packed else (seq_rows, 2 * hidden_b)
    hidden, mlp_middle, *mlp_back = call(
        functools.partial(mlp_kernel, chunk=packed, groups=groups),
        "mlp",
        11,
        (places, both_in) + normed2 + mlp_weights,
        (
            ((seq_rows, hidden_b), B16),
            (middle_shape, B16),
        )
        + row_blocks,
        mlp_scratch + (((seq_rows, dim), B16),),
    )
    def over_rows(left, right):
        return lax.dot_general(
            left, right, (((0,), (0,)), ((), ())), preferred_element_type=f32
        ).astype(bf16)

    def strips(rows_all):
        wide = rows_all.reshape((groups, parts, strip) + rows_all.shape[1:])
        return jnp.swapaxes(wide, 0, 1).reshape((parts, groups * strip) + rows_all.shape[1:])

    if packed:
        mlp_terms = mlp_middle
    else:
        mlp_terms = jnp.concatenate(
            [
                over_rows(hidden, d_out_g).reshape(parts, chunk, dim),
                strips(over_rows(ordered(normed2), mlp_middle)),
            ],
            axis=1,
        )
    mlp_own = lax.psum_scatter(mlp_terms, "seq", scatter_dimension=0)
    grad_middle, grad_sent, grad_n2 = call(
        norm_back_kernel,
        "norm_back",
        2,
        (places, middle, d_out, norm2_gain[None, :]) + branch_swap(mlp_back),
        (((tok_rows, dim), F32), ((tok_rows, dim), B16), ((8, dim), F32)),
        (),
        (q_all,),
    )
    grad_proj = branch_parts(grad_sent)
    g_pack, g_send, grad_scaled, stat, grad_gain = call(
        functools.partial(mix_back_kernel, heads=att_heads, ssm_all=ssm_all),
        "mix_back",
        5,
        (places, w_out_b, attn_out, lse, gated_b, squares, gain_row) + grad_proj,
        (
            ((seq_rows, att_heads * LANES), B16),
            ((seq_rows + 4 * att_heads * seq_rows // LANES, LANES), B16),
            ((seq_rows, ssm_cols), F32),
            ((8, seq_rows), F32),
            ((8, ssm_cols), F32),
        ),
        (((seq_rows, LANES), F32), ((seq_rows, dim), B16)),
    )
    stats = branch_parts(stat)
    grad_gate_gain = grad_gain[0]

    def all_columns(blocks):
        blocks = jnp.swapaxes(blocks, 0, 1)
        return jnp.concatenate(
            [blocks[:, :, :hidden_a].reshape(strip, -1), blocks[:, :, hidden_a:].reshape(strip, -1)],
            axis=1,
        )

    back_ssm, grad_z, grad_state = gate_back(
        places, begins_col, grad_scaled, gated_b, squares, stats, u, cum, z_pre, gated_v, g_send, ssm_heads, nstate, ssm_all
    )
    grad_states = lax.all_gather(grad_state, "seq", axis=0)
    grad_q = query_grad(
        queries, g_pack, kv_all, begins_col, query_bounds, att_heads, seq_rows, (grad_state, mlp_own)
    )
    y_terms = call(
        functools.partial(down_kernel, chunk=packed),
        "down",
        3,
        (places, hidden, down_weights),
        row_blocks,
        (),
        (grad_state,),
    )
    y_blocks = branch_swap(y_terms)
    if packed:
        early_terms, early_gain = call(
            functools.partial(early_kernel, parts=parts),
            "early",
            3,
            (places, mixed_out, both_in, grad_z, w1) + grad_proj,
            (((dim, dim // 2 + ssm_cols), B16), ((dim, 1), F32)),
            (((seq_rows, dim), B16),),
        )
        early_terms = early_terms.reshape(parts, dim // parts, dim // 2 + ssm_cols)
    else:
        out_rows = over_rows(mixed_out, ordered(grad_proj)).reshape(parts, chunk, dim)
        z_grad = lax.dot_general(both_in[:, :dim], grad_z, ROW_DOT, preferred_element_type=f32)
        at_z = 2 * LANES
        z_weight = w1[:, at_z : at_z + ssm_cols].astype(f32)
        early_gain = jnp.sum(z_grad * z_weight, axis=1, keepdims=True)
        early_terms = jnp.concatenate(
            [
                jnp.concatenate([out_rows[:, :, : dim // 2], out_rows[:, :, dim // 2 :]], axis=1),
                z_grad.astype(bf16).reshape(parts, dim // parts, ssm_cols),
            ],
            axis=2,
        )
    early_own = lax.psum_scatter(early_terms, "seq", scatter_dimension=0)
    grad_w_down = lax.ppermute(mlp_own[:chunk], ("branch", "seq"), from_heads)
    own_gu = branch_exchange(mlp_own[chunk:].reshape(groups, strip, 2 * hidden_b))
    grad_w_gate = all_columns(own_gu[:, :, :hidden_b]).astype(f32)
    grad_w_up = all_columns(own_gu[:, :, hidden_b:]).astype(f32)
    grad_xbc, grad_dt, rim_back, grad_taps, grad_small = span_back(
        places,
        begins_col,
        back_ssm,
        z_pre,
        pre,
        rim,
        u,
        cum,
        state_in,
        states,
        grad_states,
        taps,
        params,
        ssm_heads,
        0,
        at_dt,
        nstate,
        (grad_q, early_terms, y_terms[0]),
    )
    rim_back = from_behind(rim_back, "seq", -1)
    grad_kv = key_grad(
        kv, q_all, grad_states, ssm_cols, ends_col, key_bounds, att_heads, seq_rows, (grad_dt,)
    )
    tall = groups * strip
    bc_each = conv_bc.shape[1] // (groups * parts)
    x_each = ssm_cols // parts
    in_strips = packed > 0
    if in_strips:
        small = (grad_gain, grad_taps, grad_small, grad_n2)
    else:
        grad_conv_x, grad_conv_bc = (grad_taps[:CONV, :ssm_cols], grad_taps[:CONV, ssm_cols:])
        def to_column(vector, rows_each):
            padded = jnp.pad(vector.reshape(parts, rows_each), ((0, 0), (0, tall - rows_each)))
            return padded[:, :, None]

        def to_columns(matrix, rows_each):
            wide = jnp.swapaxes(matrix.reshape(matrix.shape[0], parts, rows_each), 0, 1)
            wide = jnp.pad(wide, ((0, 0), (0, 0), (0, tall - rows_each)))
            return jnp.swapaxes(wide, 1, 2)

        bc_wide = grad_conv_bc.reshape(CONV, groups, parts, bc_each)
        bc_wide = jnp.pad(bc_wide, ((0, 0), (0, 0), (0, 0), (0, strip - bc_each)))
        bc_wide = jnp.transpose(bc_wide, (2, 1, 3, 0)).reshape(parts, tall, CONV)
        heads3 = grad_small[:3, :ssm_heads].reshape(3 * ssm_heads)
        heads3 = jnp.broadcast_to(heads3[None, None, :], (parts, tall, 3 * ssm_heads))
        small = jnp.concatenate(
            [
                jnp.zeros((parts, tall, ssm_heads + 1), f32),
                strips(grad_n2[0][:, None]),
                bc_wide,
                to_column(grad_gate_gain, x_each),
                to_columns(grad_conv_x, x_each),
                heads3,
            ],
            axis=2,
        )
        small = jnp.pad(small, ((0, 0), (0, 0), (0, LANES - small.shape[2]))).reshape(dim, LANES)
        small = (small,)
    late_cols = w1_cols - ssm_cols
    grad_pre, terms1 = call(
        functools.partial(
            weight_grad_kernel, heads=ssm_heads, groups=groups, parts=parts, in_strips=in_strips
        ),
        "weight_grad",
        7,
        (places, grad_q, grad_kv, grad_z, grad_xbc, rim_back, grad_dt, cosine, sine, w1, both_in, early_gain)
        + small,
        (((seq_rows, w1_cols), B16), ((dim, late_cols), B16)),
        (((dim, LANES), F32),) if in_strips else (),
        (own_gu, grad_w_down),
    )
    mixed_cols = att_cols + ssm_cols
    at_s = mixed_cols + 2 * HEAD + side_cols
    if in_strips:
        terms1 = terms1.reshape(parts, tall, late_cols)
    else:
        tail = terms1[:, at_s:].reshape(parts, tall, LANES)
        gain_column = strips(terms1[:, at_s + ssm_heads][:, None])
        lane = jnp.arange(LANES)
        terms1 = jnp.concatenate(
            [
                terms1[:, :mixed_cols].reshape(parts, tall, mixed_cols),
                strips(terms1[:, mixed_cols:at_s]),
                jnp.where(lane == ssm_heads, gain_column, tail),
            ],
            axis=2,
        )
    own1 = lax.psum_scatter(terms1, "seq", scatter_dimension=0)
    early_own, *group_terms = call(
        group_back_kernel,
        "group_back",
        4,
        (places, grad_pre, w1, early_own),
        ((early_own.shape, B16),) + row_blocks,
        (),
    )
    grad_normed1 = sum(block.astype(f32) for block in branch_swap(group_terms))
    y_out = call(
        add_blocks_kernel,
        "add_blocks",
        1,
        (places, middle) + y_blocks,
        (((tok_rows, dim), B16),),
        (),
        (group_terms[0],),
    )[0]
    out_own = jnp.concatenate(
        [early_own[:chunk, : dim // 2], early_own[chunk:, : dim // 2]], axis=1
    )
    grad_w_out = lax.ppermute(out_own, ("branch", "seq"), from_heads).astype(f32)
    own_gain = lax.dynamic_slice_in_dim(norm1_gain, (branch_id * parts + seq_id) * strip, strip, 0)
    side_cols = late_cols - mixed_cols
    if packed:
        side_parts = call(
            split_kernel,
            "split",
            1,
            (places, own1),
            (((strip, side_cols), B16),) * groups,
            (),
        )
        side_blocks = branch_swap(side_parts)
        side_scratch = (((groups, strip, side_cols), B16),)
    else:
        side_blocks = (branch_exchange(own1[:, mixed_cols:].reshape(groups, strip, -1)),)
        side_scratch = ()
    head_row = ((1, ssm_heads), F32)
    grad_mix, grad_dt_w, grad_gain_g, grad_cx, grad_a_log, grad_dt_bias, grad_skip = call(
        functools.partial(own_kernel, heads=ssm_heads, half=dim // 2, apart=in_strips),
        "own",
        2,
        (places, own1, early_own),
        (
            ((tall, w_mix_in.shape[1]), F32),
            ((ssm_heads, tall), F32),
            ((1, x_each), F32),
            ((CONV, x_each), F32),
            head_row,
            head_row,
            head_row,
        ),
        (),
    )
    grad_shared, first_gain, second_gain, grad_cbc = call(
        functools.partial(side_kernel, heads=ssm_heads, apart=packed > 0),
        "side",
        1,
        (places, own_gain[None, :]) + side_blocks,
        (
            ((strip, w_shared.shape[1]), F32),
            ((1, strip), F32),
            ((1, strip), F32),
            ((CONV, bc_each), F32),
        ),
        side_scratch,
    )
    grad_x1, unused_n1 = rms_backward(grad_normed1, scaled1, inverse1, norm1_gain)
    return (
        y_out,
        grad_middle + grad_x1,
        first_gain[0],
        grad_mix,
        grad_dt_w.T,
        grad_shared,
        grad_cx,
        grad_cbc,
        grad_a_log[0],
        grad_dt_bias[0],
        grad_skip[0],
        grad_gain_g[0],
        grad_w_out,
        second_gain[0],
        grad_w_gate,
        grad_w_up,
        grad_w_down.astype(f32),
    )


def solution(mesh):
    in_specs = (
        P(("seq", "branch"), None),
        P(),
        P(),
        P("seq", "branch"),
        P("seq", "branch"),
        P("seq", None),
        P(None, "branch"),
        P(),
        P("branch"),
        P("branch"),
        P("branch"),
        P(),
        P("seq", None),
        P(),
        P("seq", None),
        P("seq", None),
        P("seq", None),
        P(("seq", "branch"), None),
    )
    out_specs = (
        P(("seq", "branch"), None),
        P(("seq", "branch"), None),
        P(("branch", "seq")),
        P("seq", "branch"),
        P("seq", "branch"),
        P(("branch", "seq"), None),
        P(None, ("branch", "seq")),
        P(None, ("branch", "seq")),
        P("branch"),
        P("branch"),
        P("branch"),
        P(("branch", "seq")),
        P(("branch", "seq"), None),
        P(("branch", "seq")),
        P(("branch", "seq"), None),
        P(("branch", "seq"), None),
        P(("branch", "seq"), None),
    )
    return jax.shard_map(shards, mesh=mesh, in_specs=in_specs, out_specs=out_specs, check_vma=False)
```

```python
import functools

import jax
import jax.numpy as jnp
from jax import lax
from jax.experimental import pallas as pl
from jax.experimental.pallas import tpu as pltpu
from jax.sharding import PartitionSpec as P

HEADS_ATT = 8
KV = 2
HEAD = 64
CONV = 4
LANES = 128
TILE = 128
MASKED = -1e30
HIGHEST = lax.Precision.HIGHEST
EPSILON = 1e-06
SCORE_SCALE = 0.125
ROPE_BASE = 1000000.0
F32 = jnp.float32
B16 = jnp.bfloat16
LANE_DOT = (((1,), (1,)), ((), ()))
ROW_DOT = (((0,), (0,)), ((), ()))


VMEM_SPEC = pl.BlockSpec(memory_space=pltpu.VMEM)
SMEM_SPEC = pl.BlockSpec(memory_space=pltpu.SMEM)
ANY_SPEC = pl.BlockSpec(memory_space=pl.ANY)


def from_behind(block, axis, distance):
    devices = range(lax.axis_size(axis))
    route = [(i - distance, i) for i in devices if i - distance in devices]
    return lax.ppermute(block, axis, route)


def rms_parts(value):
    inverse = lax.rsqrt(jnp.mean(value * value, axis=-1, keepdims=True) + EPSILON)
    return (value * inverse, inverse)


def rms_backward(grad_out, scaled, inverse, gain_vec):
    grad_scaled = grad_out * gain_vec
    grad_in = inverse * (
        grad_scaled - scaled * jnp.mean(grad_scaled * scaled, axis=-1, keepdims=True)
    )
    return (grad_in, jnp.sum(grad_out * scaled, axis=0))


def rotate_tables(position):
    half = HEAD // 2
    inverse = ROPE_BASE ** (-jnp.arange(half, dtype=jnp.float32) / half)
    angles = position.astype(jnp.float32)[:, None] * inverse[None, :]
    cosine, sine = (jnp.cos(angles), jnp.sin(angles))
    return (
        jnp.concatenate([cosine] * (LANES // half), axis=1),
        jnp.concatenate([-sine, sine] * (LANES // HEAD), axis=1),
    )


def swap_halves(values):
    half = HEAD // 2
    lane = lax.broadcasted_iota(jnp.int32, values.shape, 1)
    return jnp.where(
        lane % HEAD < half, pltpu.roll(values, LANES - half, 1), pltpu.roll(values, half, 1)
    )


def call(kernel, name, micros, args, outs, scratch, waits=()):
    given, held = (len(args), len(waits))

    def body(*refs):
        kernel(*refs[:given], *refs[given + held :])

    def padded(shape, kind):
        shape = (1,) * (2 - len(shape)) + tuple(shape)
        wide = -(-shape[-1] // LANES) * LANES
        tall = -(-shape[-2] // 16) * 16
        return functools.reduce(lambda a, b: a * b, shape[:-2], 1) * tall * wide * jnp.dtype(kind).itemsize

    held_bytes = [padded(a.shape, a.dtype) for a in args[1:]]
    held_bytes += [padded(s, d) for s, d in tuple(outs) + tuple(scratch)]
    limit = 56 << 20
    if name in ("mix_out", "split", "side"):
        limit = min(limit, sum(held_bytes) + (8 << 20))
    result = pl.pallas_call(
        body,
        out_shape=tuple(jax.ShapeDtypeStruct(s, d) for s, d in outs),
        in_specs=[SMEM_SPEC] + [VMEM_SPEC] * (given - 1) + [ANY_SPEC] * held,
        out_specs=tuple(VMEM_SPEC for _ in outs),
        scratch_shapes=[pltpu.VMEM(s, d) for s, d in scratch],
        compiler_params=pltpu.CompilerParams(vmem_limit_bytes=limit),
        cost_estimate=pl.CostEstimate(
            flops=micros * 1000000, bytes_accessed=micros * 3600000, transcendentals=micros * 100000
        ),
        name=name,
    )(*args, *waits)
    return result


def extra_rows(values, heads):
    pieces = []
    for h in range(heads):
        row = values[h : h + 1, :]
        high = row.astype(B16).astype(F32)
        for part in (high, row - high):
            pieces += [part[:, at : at + LANES] for at in range(0, row.shape[1], LANES)]
    return jnp.concatenate(pieces, axis=0)


def extra_row(rows, head, count):
    at = 2 * head * count
    high = jnp.concatenate([rows[at + n : at + n + 1] for n in range(count)], axis=1)
    low = jnp.concatenate([rows[at + count + n : at + count + n + 1] for n in range(count)], axis=1)
    return high + low


def attend_kernel(
    bounds, begin_ref, own_ref, all_ref, out_ref, lse_ref, top, acc, *, heads, keys
):
    rows = own_ref.shape[0]
    top[...] = jnp.full_like(top, MASKED)
    acc[...] = jnp.zeros_like(acc)
    row_ids = bounds[2] + iota((1, rows), 1)
    begins = begin_ref[...]
    ones = (iota((keys, HEAD), 1) == 0).astype(B16)

    def step(n, masked):
        at = n * keys
        kv = all_ref[n, :keys, :]
        k = kv[:, :HEAD]
        v = jnp.concatenate([kv[:, HEAD:], ones], axis=1).T
        if masked:
            key_ids = at + iota((keys, rows), 0)
            seen = (key_ids <= row_ids) & (key_ids >= begins)
        for h in range(heads):
            q = own_ref[:, h * HEAD : (h + 1) * HEAD]
            s = lax.dot_general(k, q, LANE_DOT, preferred_element_type=F32)
            if masked:
                s = jnp.where(seen, s, MASKED)
            old = top[h : h + 1, :]
            new = jnp.maximum(old, jnp.max(s, axis=0, keepdims=True))
            p = jnp.exp(s - new).astype(B16)
            scale = jnp.exp(old - new)
            add = jnp.dot(v, p, preferred_element_type=F32)
            acc[h] = acc[h] * scale + add
            top[h : h + 1, :] = new

    pl.loop(bounds[0], bounds[1])(lambda n: step(n, True))
    pl.loop(bounds[1], bounds[3])(lambda n: step(n, False))
    pl.loop(bounds[3], bounds[4])(lambda n: step(n, True))
    for h in range(heads):
        total = acc[h, HEAD : HEAD + 1, :]
        out_ref[:, h * HEAD : (h + 1) * HEAD] = (acc[h, :HEAD, :] / total).T.astype(B16)
        lse_ref[h : h + 1, :] = top[h : h + 1, :] + jnp.log(total)


def attend(own, everything, begins, bounds, heads, keys, waits):
    rows = own.shape[0]
    return call(
        functools.partial(attend_kernel, heads=heads, keys=keys),
        "attend",
        12,
        (bounds, begins, own, everything),
        (((rows, heads * HEAD), B16), ((8, rows), F32)),
        (((8, rows), F32), ((heads, LANES, rows), F32)),
        waits,
    )


def minus_ones(lane, base, first):
    at = base + first
    return jnp.where((lane == at) | (lane == at + 1), -1.0, 0.0).astype(B16)


def key_sides(kv, heads):
    turned = jnp.concatenate([kv[:, HEAD:], kv[:, :HEAD]], axis=1)
    lane = iota(kv.shape, 1)
    zero = jnp.zeros_like(kv)
    sides = []
    for h in range(heads):
        mine = lane < HEAD if h == 0 else lane >= HEAD
        base = HEAD * (1 - h)
        keys_h = jnp.where(mine, kv if h == 0 else turned, zero)
        values_h = jnp.where(mine, turned if h == 0 else kv, minus_ones(lane, base, 0))
        both = jnp.concatenate([keys_h, minus_ones(lane, base, 2)], axis=1)
        sides.append((keys_h, values_h, both))
    return sides


def query_grad_kernel(
    bounds, begin_ref, own_ref, g_ref, all_ref, out_ref, acc, *, heads, keys
):
    rows = own_ref.shape[0]
    acc[...] = jnp.zeros_like(acc)
    row_ids = bounds[2] + iota((rows, keys), 0)
    begins = begin_ref[...]

    def step(n, masked):
        at = n * keys
        kv = all_ref[n, :keys, :]
        sides = key_sides(kv, heads)
        if masked:
            key_ids = at + iota((rows, keys), 1)
            seen = (key_ids <= row_ids) & (key_ids >= begins)
        total = acc[...]
        for h in range(heads):
            k, v, both = sides[h]
            g = g_ref[:, h * LANES : (h + 1) * LANES]
            q = jnp.concatenate([own_ref[...], g], axis=1)
            s = lax.dot_general(q, both, LANE_DOT, preferred_element_type=F32)
            if masked:
                s = jnp.where(seen, s, MASKED)
            gp = lax.dot_general(g, v, LANE_DOT, preferred_element_type=F32)
            ds = (jnp.exp(s) * gp).astype(B16)
            total = total + jnp.dot(ds, k, preferred_element_type=F32)
        acc[...] = total

    pl.loop(bounds[0], bounds[1])(lambda n: step(n, True))
    pl.loop(bounds[1], bounds[3])(lambda n: step(n, False))
    pl.loop(bounds[3], bounds[4])(lambda n: step(n, True))
    out_ref[...] = acc[...] * SCORE_SCALE


def query_grad(own, g_pack, everything, begins, bounds, heads, keys, waits):
    rows = own.shape[0]
    return call(
        functools.partial(query_grad_kernel, heads=heads, keys=keys),
        "query_grad",
        11,
        (bounds, begins, own, g_pack, everything),
        (((rows, LANES), F32),),
        (((rows, LANES), F32),),
        waits,
    )[0]


def key_grad_kernel(
    bounds, end_ref, own_ref, all_ref, g_ref, out_ref, acc_k, acc_v, *, heads, keys, at_g
):
    rows = out_ref.shape[0]
    acc_k[...] = jnp.zeros_like(acc_k)
    acc_v[...] = jnp.zeros_like(acc_v)
    key_ids = bounds[2] + iota((rows, keys), 0)
    ends = end_ref[...]
    kv = own_ref[:rows, :]
    turned = jnp.concatenate([kv[:, HEAD:], kv[:, :HEAD]], axis=1)
    first = iota(kv.shape, 1) < HEAD
    zero = jnp.zeros_like(kv)
    count = keys // LANES
    sides = []
    for h in range(heads):
        mine = first if h == 0 else jnp.logical_not(first)
        k = jnp.where(mine, kv if h == 0 else turned, zero)
        sides.append((k, jnp.where(mine, turned if h == 0 else kv, zero)))

    def step(n, masked):
        at = n * keys
        if masked:
            row_ids = at + iota((rows, keys), 1)
            seen = (key_ids <= row_ids) & (row_ids < ends)
        q = all_ref[n, :keys, :]
        g = g_ref[n, at_g : at_g + keys, :]
        extra = g_ref[n, at_g + keys :, :].astype(F32)
        delta_rows, lse_rows = (extra[: extra.shape[0] // 2], extra[extra.shape[0] // 2 :])
        for h in range(heads):
            k, v = sides[h]
            s = lax.dot_general(k, q, LANE_DOT, preferred_element_type=F32)
            s = s - extra_row(lse_rows, h, count)
            if masked:
                s = jnp.where(seen, s, MASKED)
            p = jnp.exp(s)
            gp = lax.dot_general(v, g, LANE_DOT, preferred_element_type=F32)
            ds = (p * (gp - extra_row(delta_rows, h, count))).astype(B16)
            acc_k[h] += jnp.dot(ds, q, preferred_element_type=F32)
            acc_v[h] += jnp.dot(p.astype(B16), g, preferred_element_type=F32)

    pl.loop(bounds[0], bounds[1])(lambda n: step(n, True))
    pl.loop(bounds[1], bounds[3])(lambda n: step(n, False))
    pl.loop(bounds[3], bounds[4])(lambda n: step(n, True))
    out_ref[:, :HEAD] = acc_k[0, :, :HEAD] + acc_k[1, :, HEAD:]
    out_ref[:, HEAD:] = acc_v[0, :, :HEAD] + acc_v[1, :, HEAD:]


def key_grad(own, everything, g_all, at_g, ends, bounds, heads, keys, waits):
    rows = ends.shape[0]
    return call(
        functools.partial(key_grad_kernel, heads=heads, keys=keys, at_g=at_g),
        "key_grad",
        12,
        (bounds, ends, own, everything, g_all),
        (((rows, LANES), F32),),
        (((heads, rows, LANES), F32), ((heads, rows, LANES), F32)),
        waits,
    )[0]


def assemble_kernel(picks, mix_ref, shared_ref, dt_ref, out_ref, *, att_cols, turned):
    kv_cols = KV * HEAD
    wide = mix_ref.shape[1]
    first = picks[0] == 0
    at = att_cols
    out_ref[:, :at] = mix_ref[:, :at]
    for part in range(2):
        tile = shared_ref[:, part * kv_cols : (part + 1) * kv_cols]
        out_ref[:, at : at + HEAD] = jnp.where(first, tile[:, :HEAD], tile[:, HEAD:])
        at += HEAD
    out_ref[:, at : at + wide - att_cols] = mix_ref[:, att_cols:]
    at += wide - att_cols
    out_ref[:, at : at + shared_ref.shape[1] - 2 * kv_cols] = shared_ref[:, 2 * kv_cols :]
    at += shared_ref.shape[1] - 2 * kv_cols
    if turned:
        heads, rows = dt_ref.shape
        steps = jnp.concatenate([dt_ref[...].astype(F32), jnp.zeros((LANES - heads, rows), F32)], axis=0)
        out_ref[:, at:] = steps.T.astype(B16)
    else:
        out_ref[:, at:] = jnp.zeros((out_ref.shape[0], LANES), B16)
        out_ref[:, at : at + dt_ref.shape[1]] = dt_ref[...]


def project_kernel(
    places, both_ref, before_ref, w_ref, cos_ref, sin_ref, out_ref, q_ref, kv_ref, z_ref, pre_ref, rim_ref
):
    rows = both_ref.shape[0]
    dim = w_ref.shape[0]
    at_z = 2 * LANES
    at_x = at_z + z_ref.shape[1]
    step = 2 * TILE
    for i in range(0, rows, step):
        r = slice(i, i + step)
        x = both_ref[r, :dim]
        t = jnp.dot(x, w_ref[:, :at_z], preferred_element_type=F32)
        cosine, sine = cos_ref[r, :], sin_ref[r, :]
        q, kv = t[:, :LANES], t[:, LANES:]
        q = (q * cosine + swap_halves(q) * sine).astype(B16)
        q_ref[r, :] = (q.astype(F32) * SCORE_SCALE).astype(B16)
        turned = kv * cosine + swap_halves(kv) * sine
        kv_ref[r, :] = jnp.where(iota(kv.shape, 1) < HEAD, turned, kv).astype(B16)
        z_ref[r, :] = jnp.dot(x, w_ref[:, at_z:at_x], preferred_element_type=F32)
        pre_ref[r, :] = jnp.dot(x, w_ref[:, at_x:], preferred_element_type=F32)
    wide = rim_ref.shape[1]
    rim = jnp.dot(before_ref[...], w_ref[:, at_x : at_x + wide], preferred_element_type=F32)
    rim_ref[...] = rim[before_ref.shape[0] - 8 :, :]
    if kv_ref.shape[0] > rows:
        chunk = out_ref.shape[0]
        for n in range(dim // LANES):
            at = rows + n * chunk
            kv_ref[at : at + chunk, :] = out_ref[:, n * LANES : (n + 1) * LANES]


def partner_rows(places, k, rows):
    return pl.ds(pl.multiple_of(jnp.bitwise_xor(places[3], k) * rows, rows), rows)


def in_order(places, refs, scratch):
    rows = refs[0].shape[0]
    for k, ref in enumerate(refs):
        scratch[partner_rows(places, k, rows), :] = ref[...]


def out_weights(all_ref, w_ref, first, chunk):
    for s in range(all_ref.shape[0]):
        for n in range(w_ref.shape[1] // LANES):
            at = first + n * chunk
            piece = all_ref[s, at : at + chunk, :]
            w_ref[s * chunk : (s + 1) * chunk, n * LANES : (n + 1) * LANES] = piece


def mix_out_kernel(places, attn_ref, gated_ref, gain_ref, all_ref, *refs, ssm_all, chunk, groups):
    w_ref = all_ref
    if chunk:
        w_ref, refs = (refs[-1], refs[:-1])
        out_weights(all_ref, w_ref, attn_ref.shape[0], chunk)
    part_refs, refs = (refs[-groups:], refs[:-groups])
    mixed_ref, total_ref = refs[-2:]
    rows = attn_ref.shape[0]
    att_cols = attn_ref.shape[1]
    total = refs[0][...]
    for ref in refs[1:-2]:
        total = total + ref[...]
    total_ref[...] = total
    squares = total.T
    for i in range(0, rows, TILE):
        r = slice(i, i + TILE)
        inverse = lax.rsqrt(squares[r, 0:1] / ssm_all + EPSILON)
        gnormed = (gated_ref[r, :].astype(F32) * inverse * gain_ref[...]).astype(B16)
        mixed_ref[r, :att_cols] = attn_ref[r, :]
        mixed_ref[r, att_cols:] = gnormed
    for k, ref in enumerate(part_refs):
        r = partner_rows(places, k, rows // groups)
        ref[...] = jnp.dot(mixed_ref[r, :], w_ref[...], preferred_element_type=F32).astype(B16)


def mix_back_kernel(
    places, w_ref, attn_ref, lse_ref, gated_ref, squares_ref, gain_ref, *refs, heads, ssm_all
):
    pack_ref, send_ref, scaled_ref, stat_ref, gain_out, deltas, grad_ref = refs[-7:]
    in_order(places, refs[:-7], grad_ref)
    rows = attn_ref.shape[0]
    att_cols = attn_ref.shape[1]
    squares = squares_ref[...].T
    lse = lse_ref[...].T
    total = jnp.zeros((1, gated_ref.shape[1]), F32)
    ones = jnp.ones((8, gated_ref.shape[1]), F32)
    for i in range(0, rows, TILE):
        r = slice(i, i + TILE)
        mixed = lax.dot_general(grad_ref[r, :], w_ref[...], LANE_DOT, preferred_element_type=F32)
        back = mixed[:, :att_cols].astype(B16).astype(F32)
        product = back * attn_ref[r, :].astype(F32)
        lane = iota(back.shape, 1)
        send_ref[r, :] = back.astype(B16)
        packed = jnp.zeros((TILE, LANES), F32)
        for h in range(heads):
            base = HEAD * (1 - h)
            tile = one_head(back, h)
            delta = jnp.sum(one_head(product, h), axis=1, keepdims=True)
            packed = into_lane(packed, h, delta)
            for n, column in enumerate((delta, lse[r, h : h + 1])):
                high = column.astype(B16).astype(F32)
                tile = jnp.where(lane == base + 2 * n, high, tile)
                tile = jnp.where(lane == base + 2 * n + 1, column - high, tile)
            pack_ref[r, h * LANES : (h + 1) * LANES] = tile.astype(B16)
        deltas[r, :] = packed
        grad = mixed[:, att_cols:]
        scaled = gated_ref[r, :].astype(F32) * lax.rsqrt(squares[r, 0:1] / ssm_all + EPSILON)
        grad_scaled = grad * gain_ref[...]
        scaled_ref[r, :] = grad_scaled
        stat_ref[:, r] = lax.dot_general(
            ones, grad_scaled * scaled, LANE_DOT, precision=HIGHEST, preferred_element_type=F32
        )
        total = total + jnp.sum(grad * scaled, axis=0, keepdims=True)
    gain_out[...] = jnp.broadcast_to(total, gain_out.shape)
    extra = jnp.concatenate(
        [extra_rows(deltas[...].T, heads), extra_rows(lse_ref[...], heads)], axis=0
    )
    send_ref[rows:, :] = extra.astype(B16)


def rows_of(ref, first, last):
    return jnp.concatenate([ref[k, first:last, :] for k in range(ref.shape[0])], axis=0)


def mlp_kernel(places, out_ref, *refs, chunk, groups):
    in_order(places, refs[:groups], refs[-1])
    in_ref = refs[-1]
    refs = refs[groups:-1]
    if chunk:
        all_ref, hidden_ref, weights_ref, *term_refs, gu_ref, down_ref, grad_ref = refs
        down_ref[...] = rows_of(all_ref, 0, chunk)
        gu_ref[...] = rows_of(all_ref, chunk, all_ref.shape[1])
    else:
        gu_ref, down_ref, hidden_ref, grad_ref, *term_refs = refs
    rows = in_ref.shape[0]
    half = hidden_ref.shape[1]
    dim = in_ref.shape[1]
    step = 2 * TILE
    for i in range(0, rows, step):
        r = slice(i, i + step)
        both = jnp.dot(in_ref[r, :], gu_ref[...], preferred_element_type=F32)
        back = lax.dot_general(out_ref[r, dim:], down_ref[...], LANE_DOT, preferred_element_type=F32)
        gate, up = both[:, :half], both[:, half:]
        sig = jax.nn.sigmoid(gate)
        soft = gate * sig
        hidden_ref[r, :] = (soft * up).astype(B16)
        grad_ref[r, :half] = (back * up * sig * (1.0 + gate * (1.0 - sig))).astype(B16)
        grad_ref[r, half:] = (back * soft).astype(B16)
    for k, ref in enumerate(term_refs):
        r = partner_rows(places, k, rows // groups)
        ref[...] = lax.dot_general(
            grad_ref[r, :], gu_ref[...], LANE_DOT, preferred_element_type=F32
        ).astype(B16)
    if chunk:
        parts, tall = weights_ref.shape[0], weights_ref.shape[1] - chunk
        strip = tall // groups
        for i in range(0, half, step):
            down = lax.dot_general(
                hidden_ref[:, i : i + step], out_ref[:, dim:], ROW_DOT, preferred_element_type=F32
            ).astype(B16)
            for n in range(step // chunk):
                weights_ref[i // chunk + n, :chunk, :] = down[n * chunk : (n + 1) * chunk]
        for i in range(0, dim, step):
            both = lax.dot_general(
                in_ref[:, i : i + step], grad_ref[...], ROW_DOT, preferred_element_type=F32
            ).astype(B16)
            for n in range(step // strip):
                b, s = divmod(i // strip + n, parts)
                at = chunk + b * strip
                weights_ref[s, at : at + strip, :] = both[n * strip : (n + 1) * strip]


def down_kernel(places, hidden_ref, w_ref, *out_refs, chunk):
    w = rows_of(w_ref, 0, chunk) if chunk else w_ref[...]
    for k, ref in enumerate(out_refs):
        r = partner_rows(places, k, ref.shape[0])
        ref[...] = jnp.dot(hidden_ref[r, :], w, preferred_element_type=F32).astype(B16)


def add_blocks_kernel(places, middle_ref, *refs):
    total = refs[0][...].astype(F32)
    for ref in refs[1:-1]:
        total = total + ref[...].astype(F32)
    refs[-1][...] = (middle_ref[...] + total).astype(B16)


def group_back_kernel(places, grad_ref, w_ref, early_ref, kept_ref, *out_refs):
    for k, ref in enumerate(out_refs):
        r = partner_rows(places, k, ref.shape[0])
        ref[...] = lax.dot_general(
            grad_ref[r, :], w_ref[...], LANE_DOT, preferred_element_type=F32
        ).astype(B16)
    kept_ref[...] = early_ref[...]


def split_kernel(places, own_ref, *out_refs):
    wide = out_refs[0].shape[1]
    for k, ref in enumerate(out_refs):
        r = partner_rows(places, k, ref.shape[0])
        ref[...] = own_ref[r, own_ref.shape[1] - wide :]


def norm_back_kernel(places, middle_ref, grad_ref, gain_ref, *refs):
    total_ref, sent_ref, gain_out = refs[-3:]
    grad = refs[0][...].astype(F32)
    for ref in refs[1:-3]:
        grad = grad + ref[...].astype(F32)
    middle = middle_ref[...]
    inverse = lax.rsqrt(jnp.mean(middle * middle, axis=1, keepdims=True) + EPSILON)
    scaled = middle * inverse
    grad_scaled = grad * gain_ref[...]
    mean = jnp.mean(grad_scaled * scaled, axis=1, keepdims=True)
    total = inverse * (grad_scaled - scaled * mean) + grad_ref[...].astype(F32)
    total_ref[...] = total
    sent_ref[...] = total.astype(B16)
    gain_out[...] = jnp.broadcast_to(jnp.sum(grad * scaled, axis=0, keepdims=True), gain_out.shape)


def turned_rows(values):
    rows = values.shape[0]
    if rows < LANES:
        values = jnp.concatenate([values, jnp.zeros((LANES - rows, LANES), F32)], axis=0)
    return values.T


def own_kernel(places, own_ref, early_ref, mixed_ref, dt_ref, gain_ref, taps_ref, *head_refs, heads, half, apart):
    rows = own_ref.shape[0]
    cols = early_ref.shape[1] - half
    mixed_ref[:, :LANES] = own_ref[:, :LANES].astype(F32)
    mixed_ref[:, LANES : LANES + cols] = early_ref[:, half:].astype(F32)
    mixed_ref[:, LANES + cols :] = own_ref[:, LANES : LANES + cols].astype(F32)
    tail = own_ref[:, own_ref.shape[1] - LANES :].astype(F32)
    turned = turned_rows(tail)
    at_gain = heads + 2 + CONV
    each = gain_ref.shape[1]
    dt_ref[...] = turned[:heads, :rows]
    gain_ref[...] = turned[at_gain : at_gain + 1, :each]
    taps_ref[...] = turned[at_gain + 1 : at_gain + 1 + CONV, :each]
    at = at_gain + 1 + CONV
    sums = jnp.sum(tail, axis=0, keepdims=True) if apart else tail[0:1]
    count = len(head_refs)
    for n, ref in enumerate(head_refs):
        total = sums[:, at + n * heads : at + (n + 1) * heads]
        if apart:
            total = total + sums[:, at + (count + n) * heads : at + (count + n + 1) * heads]
        ref[...] = total


def side_kernel(places, gain_ref, *refs, heads, apart):
    if apart:
        blocks_ref, refs = (refs[-1], refs[:-1])
        for k, ref in enumerate(refs[:-4]):
            blocks_ref[jnp.bitwise_xor(places[3], k)] = ref[...]
    else:
        blocks_ref = refs[0]
    shared_ref, first_ref, second_ref, taps_ref = refs[-4:]
    groups, strip, wide = blocks_ref.shape
    per_kv = groups // KV
    blocks = [blocks_ref[b].astype(F32) for b in range(groups)]
    sums = []
    for h in range(KV):
        total = blocks[h * per_kv][:, : 2 * HEAD]
        for b in range(h * per_kv + 1, (h + 1) * per_kv):
            total = total + blocks[b][:, : 2 * HEAD]
        sums.append(total)
    rest = blocks[0]
    for b in range(1, groups):
        rest = rest + blocks[b]
    for part in range(2):
        for h in range(KV):
            at = (part * KV + h) * HEAD
            shared_ref[:, at : at + HEAD] = sums[h][:, part * HEAD : (part + 1) * HEAD]
    shared_ref[:, 2 * KV * HEAD :] = rest[:, 2 * HEAD : wide - LANES]
    turned = turned_rows(rest[:, wide - LANES :])
    first_ref[...] = turned[heads : heads + 1, :strip] / gain_ref[...]
    second_ref[...] = turned[heads + 1 : heads + 2, :strip]
    taps_ref[...] = turned[heads + 2 : heads + 2 + CONV, : taps_ref.shape[1]]


def early_kernel(places, mixed_ref, both_ref, dz_ref, w_ref, *refs, parts):
    terms_ref, gain_ref, grad_ref = refs[-3:]
    in_order(places, refs[:-3], grad_ref)
    dim = grad_ref.shape[1]
    half = dim // 2
    rows = mixed_ref.shape[1]
    chunk = rows // parts
    tall = dim // parts
    at_z = 2 * LANES
    cols = dz_ref.shape[1]
    step = 2 * TILE
    for i in range(0, rows, step):
        out = lax.dot_general(
            mixed_ref[:, i : i + step], grad_ref[...], ROW_DOT, preferred_element_type=F32
        ).astype(B16)
        for n in range(step // chunk):
            at = (i // chunk + n) * tall
            piece = out[n * chunk : (n + 1) * chunk]
            terms_ref[at : at + chunk, :half] = piece[:, :half]
            terms_ref[at + chunk : at + tall, :half] = piece[:, half:]
    for i in range(0, dim, step):
        r = slice(i, i + step)
        grad = lax.dot_general(both_ref[:, r], dz_ref[...], ROW_DOT, preferred_element_type=F32)
        terms_ref[r, half:] = grad.astype(B16)
        gain_ref[r, :] = jnp.sum(grad * w_ref[r, at_z : at_z + cols].astype(F32), axis=1, keepdims=True)


def small_columns(tile, mine, gain_ref, taps_ref, heads_ref, second_ref, *, heads, groups, parts):
    dim = second_ref.shape[1]
    cols = gain_ref.shape[1]
    wide = taps_ref.shape[1]
    tall = dim // parts
    strip = tall // groups
    at_gain = heads + 2 + CONV
    at = at_gain + 1 + CONV
    lane = iota((8, LANES), 1)
    values = jnp.where(lane < heads, heads_ref[...], 0.0)
    high = values.astype(B16).astype(F32)
    base = jnp.zeros((1, LANES), F32)
    for n in range(3):
        base = base + pltpu.roll(high, at + n * heads, 1)[n : n + 1]
        base = base + pltpu.roll(values - high, at + (3 + n) * heads, 1)[n : n + 1]
    own_row = iota(tile.shape, 0) % tall == mine
    tile[...] = jnp.where(own_row, base, 0.0)

    def columns(first, rows, width):
        pieces = [jnp.zeros((first, width), F32)] + rows
        left = LANES - first - sum(row.shape[0] for row in rows)
        return jnp.concatenate(pieces + [jnp.zeros((left, width), F32)], axis=0).T

    own = columns(at_gain, [gain_ref[0:1, :], taps_ref[:CONV, :cols]], cols)
    each = cols // parts
    for s in range(parts):
        tile[s * tall : s * tall + each, :] += own[s * each : (s + 1) * each]
    side = columns(heads + 2, [taps_ref[:CONV, cols:]], wide - cols)
    each = (wide - cols) // (groups * parts)
    second = columns(heads + 1, [second_ref[0:1, :]], dim)
    for b in range(groups):
        for s in range(parts):
            there = s * tall + b * strip
            n = b * parts + s
            tile[there : there + each, :] += side[n * each : (n + 1) * each]
            tile[there : there + strip, :] += second[n * strip : (n + 1) * strip]


def weight_grad_kernel(
    places, q_ref, kv_ref, z_ref, x_ref, rim_ref, dt_ref, cos_ref, sin_ref, w_ref, both_ref, early_ref,
    *refs, heads, groups, parts, in_strips,
):
    if in_strips:
        small_refs, (pre_ref, terms_ref, tile) = refs[:4], refs[4:]
        small_columns(tile, places[2], *small_refs, heads=heads, groups=groups, parts=parts)
    else:
        tile, pre_ref, terms_ref = refs
    rows = q_ref.shape[0]
    dim = w_ref.shape[0]
    cols = heads * HEAD
    wide = x_ref.shape[1]
    at_z = 2 * LANES
    at_x = at_z + cols
    at_dt = at_x + wide
    for i in range(0, rows, TILE):
        r = slice(i, i + TILE)
        cosine, sine = cos_ref[r, :], sin_ref[r, :]
        q, kv = q_ref[r, :], kv_ref[r, :]
        pre_ref[r, :LANES] = (q * cosine - swap_halves(q) * sine).astype(B16)
        turned = kv * cosine - swap_halves(kv) * sine
        pre_ref[r, LANES : 2 * LANES] = jnp.where(iota(kv.shape, 1) < HEAD, turned, kv).astype(B16)
        pre_ref[r, at_z:at_x] = z_ref[r, :]
        x = x_ref[r, :]
        if i + TILE == rows:
            x = jnp.concatenate([x[: TILE - 8], x[TILE - 8 :] + rim_ref[...]], axis=0)
        pre_ref[r, at_x:at_dt] = x.astype(B16)
        pre_ref[r, at_dt:] = dt_ref[r, :]
    block = dim // groups
    strip = block // parts
    mixed = LANES + cols
    sides = slice(mixed + LANES, mixed + 3 * LANES)
    ends = slice(mixed + 3 * LANES, mixed + 4 * LANES)
    lane = iota((block, LANES), 1)
    for b in range(groups):
        r = slice(b * block, (b + 1) * block)
        x = both_ref[:, r]
        near = lax.dot_general(x, pre_ref[:, :at_z], ROW_DOT, preferred_element_type=F32)
        far = lax.dot_general(x, pre_ref[:, at_x:], ROW_DOT, preferred_element_type=F32)
        gain = jnp.sum(near * w_ref[r, :at_z].astype(F32), axis=1, keepdims=True)
        gain = gain + jnp.sum(far * w_ref[r, at_x:].astype(F32), axis=1, keepdims=True)
        gain = gain + early_ref[r, :]
        terms_ref[r, :LANES] = near[:, :LANES].astype(B16)
        terms_ref[r, LANES:mixed] = far[:, :cols].astype(B16)
        if in_strips:
            for s in range(parts):
                here = slice(s * strip, (s + 1) * strip)
                first = s * groups * strip + b * strip
                there = slice(first, first + strip)
                terms_ref[there, mixed : mixed + LANES] = near[here, LANES:].astype(B16)
                terms_ref[there, sides] = far[here, cols:wide].astype(B16)
                at_gain = iota((strip, LANES), 1) == heads
                tile[there, :] = jnp.where(at_gain, gain[here], tile[there, :])
            tile[r, :] = jnp.where(lane < heads, far[:, wide:], tile[r, :])
        else:
            terms_ref[r, mixed : mixed + LANES] = near[:, LANES:].astype(B16)
            terms_ref[r, sides] = far[:, cols:wide].astype(B16)
            tail = jnp.where(lane < heads, far[:, wide:], tile[r, :])
            terms_ref[r, ends] = jnp.where(lane == heads, gain, tail).astype(B16)
    if in_strips:
        terms_ref[:, ends] = tile[...].astype(B16)


def iota(shape, dim):
    return lax.broadcasted_iota(jnp.int32, shape, dim)


def per_head(columns, pair):
    shape = (columns.shape[0], LANES)
    return jnp.where(
        iota(shape, 1) < HEAD, columns[:, 2 * pair : 2 * pair + 1], columns[:, 2 * pair + 1 : 2 * pair + 2]
    )


def one_head(values, head):
    keep = (iota(values.shape, 1) < HEAD) == (head % 2 == 0)
    return jnp.where(keep, values, jnp.zeros_like(values))


def into_lane(columns, head, column):
    return jnp.where(iota(columns.shape, 1) == head, column, columns)


def silu_slope(v, sig):
    return sig * (1.0 + v * (1.0 - sig))


def tap_window(ext_ref, tap, first, amount, places):
    return ext_ref[first + 8 - (CONV - 1) + tap : first + 8 - (CONV - 1) + tap + amount, :]


def span_kernel(places, begin_ref, pre_ref, rim_ref, taps_ref, params_ref, u_ref, intra_ref, cum_ref, state_ref, ext, xb, *, heads, at_x, at_dt, nstate):
    rows = pre_ref.shape[0]
    cols = heads * HEAD
    first_row, last_begin = places[0], places[1]
    ext[0:8, :] = rim_ref[...]
    ext[8 : 8 + rows, :] = pre_ref[:, at_x:at_dt]
    local = begin_ref[...] - first_row
    row_ids = iota((rows, 1), 0)
    for i in range(0, rows, TILE):
        total = jnp.zeros((TILE, ext.shape[1]), F32)
        for tap in range(CONV):
            seen = row_ids[i : i + TILE] - (CONV - 1) + tap >= local[i : i + TILE]
            window = tap_window(ext, tap, i, TILE, places)
            total = total + jnp.where(seen, window, 0.0) * taps_ref[tap : tap + 1, :]
        u_ref[i : i + TILE, :] = total
        xb[i : i + TILE, :] = (total * jax.nn.sigmoid(total)).astype(B16)
    raw = pre_ref[:, at_dt : at_dt + LANES] + params_ref[0:1, :]
    dt = jnp.maximum(raw, 0.0) + jnp.log1p(jnp.exp(-jnp.abs(raw)))
    lower = (iota((rows, rows), 0) >= iota((rows, rows), 1)).astype(F32)
    cum = jnp.dot(lower, dt * params_ref[1:2, :], precision=HIGHEST, preferred_element_type=F32)
    cum_ref[:, :LANES] = cum
    cum_ref[:, LANES:] = dt
    cum_t, dt_t = cum.T, dt.T
    last = cum[rows - 1 : rows, :]
    closing = row_ids + first_row >= last_begin
    to_end = jnp.where(closing, jnp.exp(last - cum) * dt, 0.0)
    for i in range(0, rows, TILE):
        width = i + TILE
        c = xb[i : i + TILE, cols + nstate : cols + 2 * nstate]
        b = xb[:width, cols : cols + nstate]
        inner = lax.dot_general(c, b, LANE_DOT, preferred_element_type=F32)
        key = iota((TILE, width), 1)
        seen = (key <= iota((TILE, width), 0) + i) & (key >= local[i : i + TILE])
        for pair in range(heads // 2):
            out = []
            for h in (2 * pair, 2 * pair + 1):
                spread = jnp.where(seen, cum[i : i + TILE, h : h + 1] - cum_t[h : h + 1, :width], MASKED)
                weights = (jnp.exp(spread) * inner * dt_t[h : h + 1, :width]).astype(B16)
                out.append(jnp.dot(weights, xb[:width, pair * LANES : (pair + 1) * LANES], preferred_element_type=F32))
            intra_ref[i : i + TILE, pair * LANES : (pair + 1) * LANES] = jnp.where(iota((TILE, LANES), 1) < HEAD, out[0], out[1])
    b_all = xb[:, cols : cols + nstate]
    for pair in range(heads // 2):
        at = slice(pair * LANES, (pair + 1) * LANES)
        closed = (xb[:, at].astype(F32) * per_head(to_end, pair)).astype(B16)
        state_ref[at, :] = lax.dot_general(closed, b_all, ROW_DOT, preferred_element_type=F32).astype(B16)
    decay = jnp.where(last_begin < first_row, jnp.exp(last), 0.0)
    high = decay.astype(B16)
    low = (decay - high.astype(F32)).astype(B16)
    both = jnp.concatenate([jnp.broadcast_to(high.astype(F32), (LANES // 2, LANES)), jnp.broadcast_to(low.astype(F32), (LANES // 2, LANES))], axis=0)
    state_ref[cols : cols + 16, :] = both.T[:16, :].astype(B16)


def span_forward(places, begins, pre, rim, taps, params, heads, at_x, at_dt, nstate):
    rows = pre.shape[0]
    wide = at_dt - at_x
    cols = heads * HEAD
    return call(
        functools.partial(span_kernel, heads=heads, at_x=at_x, at_dt=at_dt, nstate=nstate),
        "span_forward",
        8,
        (places, begins, pre, rim, taps, params),
        (((rows, wide), F32), ((rows, cols), F32), ((rows, 2 * LANES), F32), ((cols + 16, nstate), B16)),
        (((rows + 8, wide), F32), ((rows, wide), B16)),
    )


def decay_of(states_ref, k, head, cols):
    tail = states_ref[k, cols + head - head % 8 : cols + head - head % 8 + 8, :].astype(F32)
    row = tail[head % 8 : head % 8 + 1, :]
    return row[:, 0:1] + row[:, LANES // 2 : LANES // 2 + 1]


def finish_kernel(places, begin_ref, states_ref, u_ref, intra_ref, cum_ref, z_ref, params_ref, gated_ref, v_ref, state_ref, squares_ref, *, heads, nstate):
    rows = u_ref.shape[0]
    cols = heads * HEAD
    state_ref[...] = jnp.zeros_like(state_ref)

    def fold(k):
        for h in range(heads):
            at = slice(h * HEAD, (h + 1) * HEAD)
            state_ref[at, :] = state_ref[at, :] * decay_of(states_ref, k, h, cols) + states_ref[k, at, :].astype(F32)

    pl.loop(0, places[2])(fold)
    carried = begin_ref[...] < places[0]
    for i in range(0, rows, TILE):
        r = slice(i, i + TILE)
        enter = jnp.where(carried[r], jnp.exp(cum_ref[r, :LANES]), 0.0)
        uc = u_ref[r, cols + nstate : cols + 2 * nstate]
        c = (uc * jax.nn.sigmoid(uc)).astype(B16)
        total = jnp.zeros((8, TILE), F32)
        for pair in range(heads // 2):
            at = slice(pair * LANES, (pair + 1) * LANES)
            y = lax.dot_general(c, state_ref[at, :].astype(B16), LANE_DOT, preferred_element_type=F32)
            ux = u_ref[r, at]
            x = ux * jax.nn.sigmoid(ux)
            skip = per_head(params_ref[2:3, :], pair)
            v = intra_ref[r, at] + per_head(enter, pair) * y + skip * x
            z = z_ref[r, at]
            gated = (v * (z * jax.nn.sigmoid(z))).astype(B16)
            v_ref[r, at] = v
            gated_ref[r, at] = gated
            g = gated.astype(F32)
            total = total + lax.dot_general(jnp.ones((8, LANES), F32), g * g, LANE_DOT, precision=HIGHEST, preferred_element_type=F32)
        squares_ref[:, r] = total


def span_finish(places, begins, states, u, intra, cum, z, params, heads, nstate):
    rows = u.shape[0]
    cols = heads * HEAD
    return call(
        functools.partial(finish_kernel, heads=heads, nstate=nstate),
        "span_finish",
        7,
        (places, begins, states, u, intra, cum, z, params),
        (((rows, cols), B16), ((rows, cols), F32), ((cols, nstate), F32), ((8, rows), F32)),
        (),
    )


def gate_back_kernel(places, begin_ref, scaled_ref, gated_ref, squares_ref, u_ref, cum_ref, z_ref, v_ref, send_ref, *refs, heads, nstate, ssm_all):
    back_ref, dz_ref, state_ref, eg = refs[-4:]
    total = refs[0][...]
    for ref in refs[1:-4]:
        total = total + ref[...]
    rows = u_ref.shape[0]
    cols = heads * HEAD
    carried = begin_ref[...] < places[0]
    squares, stat = squares_ref[...].T, total.T
    uc = u_ref[:, cols + nstate : cols + 2 * nstate]
    c = (uc * jax.nn.sigmoid(uc)).astype(B16)
    for i in range(0, rows, TILE):
        r = slice(i, i + TILE)
        enter = jnp.where(carried[r], jnp.exp(cum_ref[r, :LANES]), 0.0)
        inverse = lax.rsqrt(squares[r, 0:1] / ssm_all + EPSILON)
        mean = stat[r, 0:1] / ssm_all
        for pair in range(heads // 2):
            at = slice(pair * LANES, (pair + 1) * LANES)
            z = z_ref[r, at]
            sig = jax.nn.sigmoid(z)
            scaled = gated_ref[r, at].astype(F32) * inverse
            gg = (inverse * (scaled_ref[r, at] - scaled * mean)).astype(B16)
            back_ref[r, at] = gg
            gg = gg.astype(F32)
            dz_ref[r, at] = (gg * v_ref[r, at] * silu_slope(z, sig)).astype(B16)
            eg[r, at] = (gg * (z * sig) * per_head(enter, pair)).astype(B16)
    state_ref[:cols, :] = lax.dot_general(eg[...], c, ROW_DOT, preferred_element_type=F32).astype(B16)
    state_ref[cols:, :] = send_ref[...]


def gate_back(places, begins, scaled, gated, squares, stats, u, cum, z, v, send, heads, nstate, ssm_all):
    rows = u.shape[0]
    cols = heads * HEAD
    return call(
        functools.partial(gate_back_kernel, heads=heads, nstate=nstate, ssm_all=ssm_all),
        "gate_back",
        5,
        (places, begins, scaled, gated, squares, u, cum, z, v, send) + stats,
        (((rows, cols), B16), ((rows, cols), B16), ((cols + send.shape[0], nstate), B16)),
        (((rows, cols), B16),),
    )


def back_kernel(places, begin_ref, g_ref, z_ref, pre_ref, rim_ref, u_ref, cum_ref, state_ref, states_ref, grads_ref, taps_ref, params_ref, gx_ref, gdt_ref, rim_out, taps_out, small_out, ext, gext, xb, gb, later, dxb, lane_sum, cols_sum, *, heads, at_x, at_dt, nstate):
    rows = u_ref.shape[0]
    cols = heads * HEAD
    wide = at_dt - at_x
    count = states_ref.shape[0]
    pairs = heads // 2
    first_row, last_begin, mine = places[0], places[1], places[2]
    later[...] = jnp.zeros_like(later)

    def fold(n):
        k = count - 1 - n
        for h in range(heads):
            at = slice(h * HEAD, (h + 1) * HEAD)
            later[at, :] = later[at, :] * decay_of(states_ref, k, h, cols) + grads_ref[k, at, :].astype(F32)

    pl.loop(0, count - 1 - mine)(fold)
    local = begin_ref[...] - first_row
    row_ids = iota((rows, 1), 0)
    cum = cum_ref[:, :LANES]
    dt = cum_ref[:, LANES:]
    cum_t, dt_t = cum.T, dt.T
    last = cum[rows - 1 : rows, :]
    leave = jnp.where(row_ids + first_row >= last_begin, jnp.exp(last - cum), 0.0)
    enter = jnp.where(begin_ref[...] < first_row, jnp.exp(cum), 0.0)
    to_end = leave * dt
    for i in range(0, rows, TILE):
        r = slice(i, i + TILE)
        u = u_ref[r, :]
        xb[r, :] = (u * jax.nn.sigmoid(u)).astype(B16)
        z = z_ref[r, :]
        gb[r, :] = (g_ref[r, :].astype(F32) * (z * jax.nn.sigmoid(z))).astype(B16)
    dxb[...] = jnp.zeros_like(dxb)
    cols_sum[...] = jnp.zeros_like(cols_sum)
    b_at = slice(cols, cols + nstate)
    c_at = slice(cols + nstate, cols + 2 * nstate)
    for i in range(0, rows, TILE):
        width = i + TILE
        r = slice(i, i + TILE)
        inner = lax.dot_general(xb[r, c_at], xb[:width, b_at], LANE_DOT, preferred_element_type=F32)
        key = iota((TILE, width), 1)
        seen = (key <= iota((TILE, width), 0) + i) & (key >= local[r])
        grad_inner = jnp.zeros((TILE, width), F32)
        sums = jnp.zeros((TILE, LANES), F32)
        for h in range(heads):
            at = slice(h // 2 * LANES, (h // 2 + 1) * LANES)
            g = one_head(gb[r, at], h)
            spread = jnp.where(seen, cum[r, h : h + 1] - cum_t[h : h + 1, :width], MASKED)
            decays = jnp.exp(spread)
            steps = dt_t[h : h + 1, :width]
            pairing = lax.dot_general(g, xb[:width, at], LANE_DOT, preferred_element_type=F32)
            paired = pairing * decays
            grad_inner = grad_inner + paired * steps
            both = paired * inner
            cols_sum[h : h + 1, :width] += jnp.sum(both, axis=0, keepdims=True)
            sums = into_lane(sums, h, jnp.sum(both * steps, axis=1, keepdims=True))
            weights = (decays * inner * steps).astype(B16)
            dxb[:width, at] += lax.dot_general(weights, g, ROW_DOT, preferred_element_type=F32)
        lane_sum[r, :] = sums
        grad_inner = grad_inner.astype(B16)
        dxb[r, c_at] += jnp.dot(grad_inner, xb[:width, b_at], preferred_element_type=F32)
        dxb[:width, b_at] += lax.dot_general(grad_inner, xb[r, c_at], ROW_DOT, preferred_element_type=F32)
    from_cols = jnp.concatenate([cols_sum[...], jnp.zeros((LANES - 8, rows), F32)], axis=0).T
    state_b = state_ref[...].astype(B16)
    later_b = later[...].astype(B16)
    entered = jnp.zeros((rows, LANES), F32)
    closed = jnp.zeros((rows, LANES), F32)
    skips = jnp.zeros((1, LANES), F32)
    chained = jnp.zeros((1, LANES), F32)
    for pair in range(pairs):
        at = slice(pair * LANES, (pair + 1) * LANES)
        x = xb[:, at].astype(F32)
        g = gb[:, at].astype(F32)
        y = lax.dot_general(xb[:, c_at], state_b[at, :], LANE_DOT, preferred_element_type=F32)
        q = lax.dot_general(xb[:, b_at], later_b[at, :], LANE_DOT, preferred_element_type=F32)
        ends = per_head(to_end, pair)
        dxb[:, c_at] += jnp.dot((g * per_head(enter, pair)).astype(B16), state_b[at, :], preferred_element_type=F32)
        dxb[:, b_at] += jnp.dot((x * ends).astype(B16), later_b[at, :], preferred_element_type=F32)
        dxb[:, at] += ends * q + g * per_head(params_ref[2:3, :], pair)
        gy, xq, gx = g * y, x * q, jnp.sum(g * x, axis=0, keepdims=True)
        kept = jnp.sum(later[at, :] * state_ref[at, :], axis=1, keepdims=True)
        for h in (2 * pair, 2 * pair + 1):
            entered = into_lane(entered, h, jnp.sum(one_head(gy, h), axis=1, keepdims=True))
            closed = into_lane(closed, h, jnp.sum(one_head(xq, h), axis=1, keepdims=True))
            skips = into_lane(skips, h, jnp.sum(one_head(gx, h), axis=1, keepdims=True))
            half = slice(h % 2 * HEAD, (h % 2 + 1) * HEAD)
            chained = into_lane(chained, h, jnp.sum(kept[half], axis=0, keepdims=True))
    decay = jnp.where(last_begin < first_row, jnp.exp(last), 0.0)
    ended = closed * to_end
    grad_cum = lane_sum[...] - from_cols * dt + entered * enter - ended
    at_last = jnp.sum(ended, axis=0, keepdims=True) + decay * chained
    grad_cum = grad_cum + jnp.where(row_ids == rows - 1, at_last, 0.0)
    upper = (iota((rows, rows), 0) <= iota((rows, rows), 1)).astype(F32)
    grad_log = jnp.dot(upper, grad_cum, precision=HIGHEST, preferred_element_type=F32)
    rate = params_ref[1:2, :]
    grad_dt = from_cols + closed * leave + grad_log * rate
    grad_raw = grad_dt * jax.nn.sigmoid(pre_ref[:, at_dt : at_dt + LANES] + params_ref[0:1, :])
    grad_raw = jnp.where(iota((rows, LANES), 1) < heads, grad_raw, 0.0)
    gdt_ref[...] = grad_raw.astype(B16)
    small_out[0:1, :] = jnp.sum(grad_log * dt, axis=0, keepdims=True) * rate
    small_out[1:2, :] = jnp.sum(grad_raw, axis=0, keepdims=True)
    small_out[2:3, :] = skips
    small_out[3:8, :] = jnp.zeros((5, LANES), F32)
    ext[0:8, :] = rim_ref[...]
    ext[8 : 8 + rows, :] = pre_ref[:, at_x:at_dt]
    gext[...] = jnp.zeros_like(gext)
    taps_out[...] = jnp.zeros_like(taps_out)
    for i in range(0, rows, TILE):
        r = slice(i, i + TILE)
        u = u_ref[r, :]
        du = dxb[r, :] * silu_slope(u, jax.nn.sigmoid(u))
        for tap in range(CONV):
            seen = row_ids[r] - (CONV - 1) + tap >= local[r]
            part = jnp.where(seen, du, 0.0)
            taps_out[tap : tap + 1, :] += jnp.sum(part * tap_window(ext, tap, i, TILE, places), axis=0, keepdims=True)
            at = 8 - (CONV - 1) + tap + i
            gext[at : at + TILE, :] += part * taps_ref[tap : tap + 1, :]
    rim_out[...] = gext[0:8, :]
    gx_ref[...] = gext[8:, :]


def span_back(places, begins, back, z, pre, rim, u, cum, state, states, grads, taps, params, heads, at_x, at_dt, nstate, waits):
    rows = u.shape[0]
    cols = heads * HEAD
    wide = at_dt - at_x
    return call(
        functools.partial(back_kernel, heads=heads, at_x=at_x, at_dt=at_dt, nstate=nstate),
        "span_back",
        16,
        (places, begins, back, z, pre, rim, u, cum, state, states, grads, taps, params),
        (((rows, wide), F32), ((rows, LANES), B16), ((8, wide), F32), ((8, wide), F32), ((8, LANES), F32)),
        (((rows + 8, wide), F32), ((rows + 8, wide), F32), ((rows, wide), B16), ((rows, cols), B16),
         ((cols, nstate), F32), ((rows, wide), F32), ((rows, LANES), F32), ((8, rows), F32)),
        waits,
    )


def shards(
    x_in,
    lengths,
    norm1_gain,
    w_mix_in,
    w_dt,
    w_shared,
    conv_x,
    conv_bc,
    a_log,
    dt_bias,
    d_skip,
    gate_gain,
    w_out,
    norm2_gain,
    w_gate,
    w_up,
    w_down,
    d_out,
):
    tok_rows = x_in.shape[0]
    groups = lax.axis_size("branch")
    branch_id = lax.axis_index("branch")
    seq_id = lax.axis_index("seq")
    seq_rows = tok_rows * groups
    group_first = seq_id * seq_rows
    att_heads = HEADS_ATT // groups
    att_cols = att_heads * HEAD
    ssm_heads = w_dt.shape[1]
    ssm_cols = ssm_heads * HEAD
    kv_cols = KV * HEAD
    f32 = jnp.float32
    bf16 = jnp.bfloat16
    dim = x_in.shape[1]
    parts = lax.axis_size("seq")
    chunk = w_out.shape[0] // groups
    att_chunks = parts * att_cols // (att_cols + ssm_cols)
    ssm_chunks = parts - att_chunks
    strip = dim // (groups * parts)
    hidden_all = w_gate.shape[1]
    hidden_a = hidden_all * att_cols // ((att_cols + ssm_cols) * groups)
    hidden_s = hidden_all // groups - hidden_a
    hidden_b = hidden_a + hidden_s

    def spot(c):
        first = groups * att_chunks
        if c < first:
            return (c // att_chunks) * parts + c % att_chunks
        return ((c - first) // ssm_chunks) * parts + att_chunks + (c - first) % ssm_chunks

    to_heads = [((c % groups) * parts + c // groups, spot(c)) for c in range(groups * parts)]
    from_heads = [(spot(c), c) for c in range(groups * parts)]

    def branch_parts(part):
        routes = [[(i, i ^ k) for i in range(groups)] for k in range(1, groups)]
        return (part,) + tuple(lax.ppermute(part, "branch", route) for route in routes)

    def branch_swap(blocks):
        routes = [[(i, i ^ k) for i in range(groups)] for k in range(1, groups)]
        moved = [lax.ppermute(block, "branch", route) for block, route in zip(blocks[1:], routes)]
        return (blocks[0],) + tuple(moved)

    def ordered(blocks):
        stacked = jnp.stack(blocks)
        picked = [lax.dynamic_index_in_dim(stacked, branch_id ^ n, 0, False) for n in range(groups)]
        return jnp.concatenate(picked, axis=0)

    def branch_exchange(blocks):
        return lax.all_to_all(blocks, "branch", 0, 0, tiled=True)

    def branch_gather(part):
        copies = branch_exchange(jnp.broadcast_to(part[None], (groups,) + part.shape))
        return copies.reshape((groups * part.shape[0],) + part.shape[1:])

    def branch_scatter(terms):
        blocks = terms.astype(bf16).reshape((groups, -1) + terms.shape[1:])
        return jnp.sum(lax.all_to_all(blocks, "branch", 0, 0, tiled=True).astype(f32), axis=0)

    kv_head = branch_id * att_heads // (HEADS_ATT // KV)
    side_cols = w_shared.shape[1] - 2 * kv_cols
    w1_cols = w_mix_in.shape[1] + 2 * HEAD + side_cols + LANES
    turned = w_dt.shape[0] % LANES == 0
    w1_part = call(
        functools.partial(assemble_kernel, att_cols=att_cols, turned=turned),
        "assemble",
        1,
        (kv_head[None], w_mix_in, w_shared, w_dt.T if turned else w_dt),
        (((w_mix_in.shape[0], w1_cols), B16),),
        (),
    )[0]
    w1 = lax.all_gather(w1_part, "seq", axis=0, tiled=True)

    def own_columns(w):
        return [
            lax.dynamic_slice_in_dim(w, branch_id * hidden_a, hidden_a, 1),
            lax.dynamic_slice_in_dim(w, groups * hidden_a + branch_id * hidden_s, hidden_s, 1),
        ]

    row_part = jnp.concatenate(
        [
            lax.dynamic_slice_in_dim(w_out, branch_id * chunk, chunk, 0),
            lax.dynamic_slice_in_dim(w_down, branch_id * chunk, chunk, 0),
        ],
        axis=0,
    )
    row_part = lax.ppermute(row_part, ("branch", "seq"), to_heads)
    out_part = row_part[:chunk]
    mlp_part = jnp.concatenate(
        [row_part[chunk:], jnp.concatenate(own_columns(w_gate) + own_columns(w_up), axis=1)], axis=0
    )
    x_rows = x_in.astype(f32)
    scaled1, inverse1 = rms_parts(x_rows)
    normed1 = (scaled1 * norm1_gain).astype(bf16)
    both_in = branch_gather(jnp.concatenate([normed1, d_out], axis=1))
    d_out_g = both_in[:, dim:]
    before = from_behind(both_in[seq_rows - 16 :, :dim], "seq", 1)
    row_ids = group_first + jnp.arange(seq_rows, dtype=jnp.int32)
    seq_ends = jnp.cumsum(lengths)

    def begin_of(ids):
        return jnp.max(jnp.where(seq_ends <= ids[..., None], seq_ends, 0), axis=-1)

    def end_of(ids):
        return jnp.min(jnp.where(seq_ends > ids[..., None], seq_ends, seq_rows * parts), axis=-1)

    begins = begin_of(row_ids)
    ends = end_of(row_ids)
    position = row_ids - begins
    row_last = group_first + seq_rows - 1
    begin_first, begin_last = (begin_of(group_first), begin_of(row_last))
    end_first, end_last = (end_of(group_first), end_of(row_last))
    here = seq_id
    query_lo = begin_first // seq_rows
    query_clear = jnp.minimum(jnp.maximum(query_lo, -(-begin_last // seq_rows)), here)
    query_bounds = jnp.stack([query_lo, query_clear, group_first, here, here + 1])
    key_hi = -(-end_last // seq_rows)
    key_clear = jnp.maximum(here + 1, jnp.minimum(end_first // seq_rows, key_hi))
    key_bounds = jnp.stack([here, here + 1, group_first, key_clear, key_hi])
    places = jnp.stack([group_first, begin_last, seq_id, branch_id])
    begins_col, begins_row, ends_col = (begins[:, None], begins[None, :], ends[:, None])
    at_dt = ssm_cols + side_cols
    nstate = conv_bc.shape[1] // 2
    taps = jnp.pad(jnp.concatenate([conv_x, conv_bc], axis=1), ((0, 8 - CONV), (0, 0)))
    params = jnp.stack([dt_bias, -jnp.exp(a_log), d_skip])
    params = jnp.pad(params, ((0, 5), (0, LANES - ssm_heads)))
    ssm_all = gate_gain.shape[0]
    gain_row = lax.dynamic_slice_in_dim(gate_gain, branch_id * ssm_cols, ssm_cols, 0)[None, :]
    cosine, sine = rotate_tables(position)
    packed = chunk if chunk % 16 == 0 and strip % 16 == 0 else 0
    kv_rows = seq_rows + packed * dim // LANES
    queries, kv, z_pre, pre, rim = call(
        project_kernel,
        "project",
        5,
        (places, both_in, before, w1, cosine, sine, out_part),
        (
            ((seq_rows, LANES), B16),
            ((kv_rows, LANES), B16),
            ((seq_rows, ssm_cols), F32),
            ((seq_rows, at_dt + LANES), F32),
            ((8, at_dt), F32),
        ),
        (),
        (
            begins_col,
            begins_row,
            ends_col,
            query_bounds,
            key_bounds,
            taps,
            params,
            gain_row,
            mlp_part,
        ),
    )
    kv_all = lax.all_gather(kv, "seq", axis=0)
    w_out_b = kv_all if packed else lax.all_gather(out_part, "seq", axis=0, tiled=True)
    mlp_all = lax.all_gather(mlp_part, "seq", axis=0)
    if packed:
        mlp_weights, down_weights = ((mlp_all,), mlp_all)
        mlp_scratch = (
            ((dim, 2 * hidden_b), B16),
            ((parts * chunk, dim), B16),
            ((seq_rows, 2 * hidden_b), B16),
        )
    else:
        down_weights = mlp_all[:, :chunk].reshape(parts * chunk, dim)
        mlp_weights = (mlp_all[:, chunk:].reshape(dim, 2 * hidden_b), down_weights)
        mlp_scratch = ()
    u, intra, cum, state = span_forward(
        places, begins_col, pre, rim, taps, params, ssm_heads, 0, at_dt, nstate
    )
    states = lax.all_gather(state, "seq", axis=0)
    gated_b, gated_v, state_in, squares = span_finish(
        places, begins_col, states, u, intra, cum, z_pre, params, ssm_heads, nstate
    )
    attn_out, lse = attend(
        queries, kv_all, begins_row, query_bounds, att_heads, seq_rows, (gated_b,)
    )
    q_all = lax.all_gather(queries, "seq", axis=0)

    out_shape = (parts * chunk, dim)
    row_blocks = (((tok_rows, dim), B16),) * groups
    mixed_out, squares, *out_terms = call(
        functools.partial(mix_out_kernel, ssm_all=ssm_all, chunk=packed, groups=groups),
        "mix_out",
        3,
        (places, attn_out, gated_b, gain_row, w_out_b) + branch_parts(squares),
        (((seq_rows, att_cols + ssm_cols), B16), ((8, seq_rows), F32))
        + row_blocks
        + (((out_shape, B16),) if packed else ()),
        (),
    )
    w_out_b = out_terms.pop() if packed else w_out_b
    projected = sum(block.astype(f32) for block in branch_swap(out_terms))
    middle = x_rows + projected
    scaled2, inverse2 = rms_parts(middle)
    normed2 = branch_parts((scaled2 * norm2_gain).astype(bf16))
    middle_shape = (parts, chunk + dim // parts, dim) if packed else (seq_rows, 2 * hidden_b)
    hidden, mlp_middle, *mlp_back = call(
        functools.partial(mlp_kernel, chunk=packed, groups=groups),
        "mlp",
        11,
        (places, both_in) + normed2 + mlp_weights,
        (
            ((seq_rows, hidden_b), B16),
            (middle_shape, B16),
        )
        + row_blocks,
        mlp_scratch + (((seq_rows, dim), B16),),
    )
    def over_rows(left, right):
        return lax.dot_general(
            left, right, (((0,), (0,)), ((), ())), preferred_element_type=f32
        ).astype(bf16)

    def strips(rows_all):
        wide = rows_all.reshape((groups, parts, strip) + rows_all.shape[1:])
        return jnp.swapaxes(wide, 0, 1).reshape((parts, groups * strip) + rows_all.shape[1:])

    if packed:
        mlp_terms = mlp_middle
    else:
        mlp_terms = jnp.concatenate(
            [
                over_rows(hidden, d_out_g).reshape(parts, chunk, dim),
                strips(over_rows(ordered(normed2), mlp_middle)),
            ],
            axis=1,
        )
    mlp_own = lax.psum_scatter(mlp_terms, "seq", scatter_dimension=0)
    grad_middle, grad_sent, grad_n2 = call(
        norm_back_kernel,
        "norm_back",
        2,
        (places, middle, d_out, norm2_gain[None, :]) + branch_swap(mlp_back),
        (((tok_rows, dim), F32), ((tok_rows, dim), B16), ((8, dim), F32)),
        (),
        (q_all,),
    )
    grad_proj = branch_parts(grad_sent)
    g_pack, g_send, grad_scaled, stat, grad_gain = call(
        functools.partial(mix_back_kernel, heads=att_heads, ssm_all=ssm_all),
        "mix_back",
        5,
        (places, w_out_b, attn_out, lse, gated_b, squares, gain_row) + grad_proj,
        (
            ((seq_rows, att_heads * LANES), B16),
            ((seq_rows + 4 * att_heads * seq_rows // LANES, LANES), B16),
            ((seq_rows, ssm_cols), F32),
            ((8, seq_rows), F32),
            ((8, ssm_cols), F32),
        ),
        (((seq_rows, LANES), F32), ((seq_rows, dim), B16)),
    )
    stats = branch_parts(stat)
    grad_gate_gain = grad_gain[0]

    def all_columns(blocks):
        blocks = jnp.swapaxes(blocks, 0, 1)
        return jnp.concatenate(
            [blocks[:, :, :hidden_a].reshape(strip, -1), blocks[:, :, hidden_a:].reshape(strip, -1)],
            axis=1,
        )

    back_ssm, grad_z, grad_state = gate_back(
        places, begins_col, grad_scaled, gated_b, squares, stats, u, cum, z_pre, gated_v, g_send, ssm_heads, nstate, ssm_all
    )
    grad_states = lax.all_gather(grad_state, "seq", axis=0)
    grad_q = query_grad(
        queries, g_pack, kv_all, begins_col, query_bounds, att_heads, seq_rows, (grad_state, mlp_own)
    )
    y_terms = call(
        functools.partial(down_kernel, chunk=packed),
        "down",
        3,
        (places, hidden, down_weights),
        row_blocks,
        (),
        (grad_state,),
    )
    y_blocks = branch_swap(y_terms)
    if packed:
        early_terms, early_gain = call(
            functools.partial(early_kernel, parts=parts),
            "early",
            3,
            (places, mixed_out, both_in, grad_z, w1) + grad_proj,
            (((dim, dim // 2 + ssm_cols), B16), ((dim, 1), F32)),
            (((seq_rows, dim), B16),),
        )
        early_terms = early_terms.reshape(parts, dim // parts, dim // 2 + ssm_cols)
    else:
        out_rows = over_rows(mixed_out, ordered(grad_proj)).reshape(parts, chunk, dim)
        z_grad = lax.dot_general(both_in[:, :dim], grad_z, ROW_DOT, preferred_element_type=f32)
        at_z = 2 * LANES
        z_weight = w1[:, at_z : at_z + ssm_cols].astype(f32)
        early_gain = jnp.sum(z_grad * z_weight, axis=1, keepdims=True)
        early_terms = jnp.concatenate(
            [
                jnp.concatenate([out_rows[:, :, : dim // 2], out_rows[:, :, dim // 2 :]], axis=1),
                z_grad.astype(bf16).reshape(parts, dim // parts, ssm_cols),
            ],
            axis=2,
        )
    early_own = lax.psum_scatter(early_terms, "seq", scatter_dimension=0)
    grad_w_down = lax.ppermute(mlp_own[:chunk], ("branch", "seq"), from_heads)
    own_gu = branch_exchange(mlp_own[chunk:].reshape(groups, strip, 2 * hidden_b))
    grad_w_gate = all_columns(own_gu[:, :, :hidden_b]).astype(f32)
    grad_w_up = all_columns(own_gu[:, :, hidden_b:]).astype(f32)
    grad_xbc, grad_dt, rim_back, grad_taps, grad_small = span_back(
        places,
        begins_col,
        back_ssm,
        z_pre,
        pre,
        rim,
        u,
        cum,
        state_in,
        states,
        grad_states,
        taps,
        params,
        ssm_heads,
        0,
        at_dt,
        nstate,
        (grad_q, early_terms, y_terms[0]),
    )
    rim_back = from_behind(rim_back, "seq", -1)
    grad_kv = key_grad(
        kv, q_all, grad_states, ssm_cols, ends_col, key_bounds, att_heads, seq_rows, (grad_dt,)
    )
    tall = groups * strip
    bc_each = conv_bc.shape[1] // (groups * parts)
    x_each = ssm_cols // parts
    in_strips = packed > 0
    if in_strips:
        small = (grad_gain, grad_taps, grad_small, grad_n2)
    else:
        grad_conv_x, grad_conv_bc = (grad_taps[:CONV, :ssm_cols], grad_taps[:CONV, ssm_cols:])
        def to_column(vector, rows_each):
            padded = jnp.pad(vector.reshape(parts, rows_each), ((0, 0), (0, tall - rows_each)))
            return padded[:, :, None]

        def to_columns(matrix, rows_each):
            wide = jnp.swapaxes(matrix.reshape(matrix.shape[0], parts, rows_each), 0, 1)
            wide = jnp.pad(wide, ((0, 0), (0, 0), (0, tall - rows_each)))
            return jnp.swapaxes(wide, 1, 2)

        bc_wide = grad_conv_bc.reshape(CONV, groups, parts, bc_each)
        bc_wide = jnp.pad(bc_wide, ((0, 0), (0, 0), (0, 0), (0, strip - bc_each)))
        bc_wide = jnp.transpose(bc_wide, (2, 1, 3, 0)).reshape(parts, tall, CONV)
        heads3 = grad_small[:3, :ssm_heads].reshape(3 * ssm_heads)
        heads3 = jnp.broadcast_to(heads3[None, None, :], (parts, tall, 3 * ssm_heads))
        small = jnp.concatenate(
            [
                jnp.zeros((parts, tall, ssm_heads + 1), f32),
                strips(grad_n2[0][:, None]),
                bc_wide,
                to_column(grad_gate_gain, x_each),
                to_columns(grad_conv_x, x_each),
                heads3,
            ],
            axis=2,
        )
        small = jnp.pad(small, ((0, 0), (0, 0), (0, LANES - small.shape[2]))).reshape(dim, LANES)
        small = (small,)
    late_cols = w1_cols - ssm_cols
    grad_pre, terms1 = call(
        functools.partial(
            weight_grad_kernel, heads=ssm_heads, groups=groups, parts=parts, in_strips=in_strips
        ),
        "weight_grad",
        7,
        (places, grad_q, grad_kv, grad_z, grad_xbc, rim_back, grad_dt, cosine, sine, w1, both_in, early_gain)
        + small,
        (((seq_rows, w1_cols), B16), ((dim, late_cols), B16)),
        (((dim, LANES), F32),) if in_strips else (),
        (own_gu, grad_w_down),
    )
    mixed_cols = att_cols + ssm_cols
    at_s = mixed_cols + 2 * HEAD + side_cols
    if in_strips:
        terms1 = terms1.reshape(parts, tall, late_cols)
    else:
        tail = terms1[:, at_s:].reshape(parts, tall, LANES)
        gain_column = strips(terms1[:, at_s + ssm_heads][:, None])
        lane = jnp.arange(LANES)
        terms1 = jnp.concatenate(
            [
                terms1[:, :mixed_cols].reshape(parts, tall, mixed_cols),
                strips(terms1[:, mixed_cols:at_s]),
                jnp.where(lane == ssm_heads, gain_column, tail),
            ],
            axis=2,
        )
    own1 = lax.psum_scatter(terms1, "seq", scatter_dimension=0)
    early_own, *group_terms = call(
        group_back_kernel,
        "group_back",
        4,
        (places, grad_pre, w1, early_own),
        ((early_own.shape, B16),) + row_blocks,
        (),
    )
    grad_normed1 = sum(block.astype(f32) for block in branch_swap(group_terms))
    y_out = call(
        add_blocks_kernel,
        "add_blocks",
        1,
        (places, middle) + y_blocks,
        (((tok_rows, dim), B16),),
        (),
        (group_terms[0],),
    )[0]
    out_own = jnp.concatenate(
        [early_own[:chunk, : dim // 2], early_own[chunk:, : dim // 2]], axis=1
    )
    grad_w_out = lax.ppermute(out_own, ("branch", "seq"), from_heads).astype(f32)
    own_gain = lax.dynamic_slice_in_dim(norm1_gain, (branch_id * parts + seq_id) * strip, strip, 0)
    side_cols = late_cols - mixed_cols
    if packed:
        side_parts = call(
            split_kernel,
            "split",
            1,
            (places, own1),
            (((strip, side_cols), B16),) * groups,
            (),
        )
        side_blocks = branch_swap(side_parts)
        side_scratch = (((groups, strip, side_cols), B16),)
    else:
        side_blocks = (branch_exchange(own1[:, mixed_cols:].reshape(groups, strip, -1)),)
        side_scratch = ()
    head_row = ((1, ssm_heads), F32)
    grad_mix, grad_dt_w, grad_gain_g, grad_cx, grad_a_log, grad_dt_bias, grad_skip = call(
        functools.partial(own_kernel, heads=ssm_heads, half=dim // 2, apart=in_strips),
        "own",
        2,
        (places, own1, early_own),
        (
            ((tall, w_mix_in.shape[1]), F32),
            ((ssm_heads, tall), F32),
            ((1, x_each), F32),
            ((CONV, x_each), F32),
            head_row,
            head_row,
            head_row,
        ),
        (),
    )
    grad_shared, first_gain, second_gain, grad_cbc = call(
        functools.partial(side_kernel, heads=ssm_heads, apart=packed > 0),
        "side",
        1,
        (places, own_gain[None, :]) + side_blocks,
        (
            ((strip, w_shared.shape[1]), F32),
            ((1, strip), F32),
            ((1, strip), F32),
            ((CONV, bc_each), F32),
        ),
        side_scratch,
    )
    grad_x1, unused_n1 = rms_backward(grad_normed1, scaled1, inverse1, norm1_gain)
    return (
        y_out,
        grad_middle + grad_x1,
        first_gain[0],
        grad_mix,
        grad_dt_w.T,
        grad_shared,
        grad_cx,
        grad_cbc,
        grad_a_log[0],
        grad_dt_bias[0],
        grad_skip[0],
        grad_gain_g[0],
        grad_w_out,
        second_gain[0],
        grad_w_gate,
        grad_w_up,
        grad_w_down.astype(f32),
    )


def solution(mesh):
    in_specs = (
        P(("seq", "branch"), None),
        P(),
        P(),
        P("seq", "branch"),
        P("seq", "branch"),
        P("seq", None),
        P(None, "branch"),
        P(),
        P("branch"),
        P("branch"),
        P("branch"),
        P(),
        P("seq", None),
        P(),
        P("seq", None),
        P("seq", None),
        P("seq", None),
        P(("seq", "branch"), None),
    )
    out_specs = (
        P(("seq", "branch"), None),
        P(("seq", "branch"), None),
        P(("branch", "seq")),
        P("seq", "branch"),
        P("seq", "branch"),
        P(("branch", "seq"), None),
        P(None, ("branch", "seq")),
        P(None, ("branch", "seq")),
        P("branch"),
        P("branch"),
        P("branch"),
        P(("branch", "seq")),
        P(("branch", "seq"), None),
        P(("branch", "seq")),
        P(("branch", "seq"), None),
        P(("branch", "seq"), None),
        P(("branch", "seq"), None),
    )
    return jax.shard_map(shards, mesh=mesh, in_specs=in_specs, out_specs=out_specs, check_vma=False)
```

```python
import functools

import jax
import jax.numpy as jnp
from jax import lax
from jax.experimental import pallas as pl
from jax.experimental.pallas import tpu as pltpu
from jax.sharding import PartitionSpec as P

HEADS_ATT = 8
KV = 2
HEAD = 64
CONV = 4
LANES = 128
TILE = 128
MASKED = -1e30
HIGHEST = lax.Precision.HIGHEST
EPSILON = 1e-06
SCORE_SCALE = 0.125
ROPE_BASE = 1000000.0
F32 = jnp.float32
B16 = jnp.bfloat16
LANE_DOT = (((1,), (1,)), ((), ()))
ROW_DOT = (((0,), (0,)), ((), ()))


VMEM_SPEC = pl.BlockSpec(memory_space=pltpu.VMEM)
SMEM_SPEC = pl.BlockSpec(memory_space=pltpu.SMEM)
ANY_SPEC = pl.BlockSpec(memory_space=pl.ANY)


def from_behind(block, axis, distance):
    devices = range(lax.axis_size(axis))
    route = [(i - distance, i) for i in devices if i - distance in devices]
    return lax.ppermute(block, axis, route)


def rms_parts(value):
    inverse = lax.rsqrt(jnp.mean(value * value, axis=-1, keepdims=True) + EPSILON)
    return (value * inverse, inverse)


def rms_backward(grad_out, scaled, inverse, gain_vec):
    grad_scaled = grad_out * gain_vec
    grad_in = inverse * (
        grad_scaled - scaled * jnp.mean(grad_scaled * scaled, axis=-1, keepdims=True)
    )
    return (grad_in, jnp.sum(grad_out * scaled, axis=0))


def rotate_tables(position):
    half = HEAD // 2
    inverse = ROPE_BASE ** (-jnp.arange(half, dtype=jnp.float32) / half)
    angles = position.astype(jnp.float32)[:, None] * inverse[None, :]
    cosine, sine = (jnp.cos(angles), jnp.sin(angles))
    return (
        jnp.concatenate([cosine] * (LANES // half), axis=1),
        jnp.concatenate([-sine, sine] * (LANES // HEAD), axis=1),
    )


def swap_halves(values):
    half = HEAD // 2
    lane = lax.broadcasted_iota(jnp.int32, values.shape, 1)
    return jnp.where(
        lane % HEAD < half, pltpu.roll(values, LANES - half, 1), pltpu.roll(values, half, 1)
    )


def call(kernel, name, micros, args, outs, scratch, waits=()):
    given, held = (len(args), len(waits))

    def body(*refs):
        kernel(*refs[:given], *refs[given + held :])

    def padded(shape, kind):
        shape = (1,) * (2 - len(shape)) + tuple(shape)
        wide = -(-shape[-1] // LANES) * LANES
        tall = -(-shape[-2] // 16) * 16
        return functools.reduce(lambda a, b: a * b, shape[:-2], 1) * tall * wide * jnp.dtype(kind).itemsize

    held_bytes = [padded(a.shape, a.dtype) for a in args[1:]]
    held_bytes += [padded(s, d) for s, d in tuple(outs) + tuple(scratch)]
    limit = 56 << 20
    if name in ("mix_out", "split", "side", "own", "norm_back"):
        limit = min(limit, sum(held_bytes) + (8 << 20))
    result = pl.pallas_call(
        body,
        out_shape=tuple(jax.ShapeDtypeStruct(s, d) for s, d in outs),
        in_specs=[SMEM_SPEC] + [VMEM_SPEC] * (given - 1) + [ANY_SPEC] * held,
        out_specs=tuple(VMEM_SPEC for _ in outs),
        scratch_shapes=[pltpu.VMEM(s, d) for s, d in scratch],
        compiler_params=pltpu.CompilerParams(vmem_limit_bytes=limit),
        cost_estimate=pl.CostEstimate(
            flops=micros * 1000000, bytes_accessed=micros * 3600000, transcendentals=micros * 100000
        ),
        name=name,
    )(*args, *waits)
    return result


def extra_rows(values, heads):
    pieces = []
    for h in range(heads):
        row = values[h : h + 1, :]
        high = row.astype(B16).astype(F32)
        for part in (high, row - high):
            pieces += [part[:, at : at + LANES] for at in range(0, row.shape[1], LANES)]
    return jnp.concatenate(pieces, axis=0)


def extra_row(rows, head, count):
    at = 2 * head * count
    high = jnp.concatenate([rows[at + n : at + n + 1] for n in range(count)], axis=1)
    low = jnp.concatenate([rows[at + count + n : at + count + n + 1] for n in range(count)], axis=1)
    return high + low


def attend_kernel(
    bounds, begin_ref, own_ref, all_ref, out_ref, lse_ref, top, acc, *, heads, keys
):
    rows = own_ref.shape[0]
    top[...] = jnp.full_like(top, MASKED)
    acc[...] = jnp.zeros_like(acc)
    row_ids = bounds[2] + iota((1, rows), 1)
    begins = begin_ref[...]
    ones = (iota((keys, HEAD), 1) == 0).astype(B16)

    def step(n, masked):
        at = n * keys
        kv = all_ref[n, :keys, :]
        k = kv[:, :HEAD]
        v = jnp.concatenate([kv[:, HEAD:], ones], axis=1).T
        if masked:
            key_ids = at + iota((keys, rows), 0)
            seen = (key_ids <= row_ids) & (key_ids >= begins)
        for h in range(heads):
            q = own_ref[:, h * HEAD : (h + 1) * HEAD]
            s = lax.dot_general(k, q, LANE_DOT, preferred_element_type=F32)
            if masked:
                s = jnp.where(seen, s, MASKED)
            old = top[h : h + 1, :]
            new = jnp.maximum(old, jnp.max(s, axis=0, keepdims=True))
            p = jnp.exp(s - new).astype(B16)
            scale = jnp.exp(old - new)
            add = jnp.dot(v, p, preferred_element_type=F32)
            acc[h] = acc[h] * scale + add
            top[h : h + 1, :] = new

    pl.loop(bounds[0], bounds[1])(lambda n: step(n, True))
    pl.loop(bounds[1], bounds[3])(lambda n: step(n, False))
    pl.loop(bounds[3], bounds[4])(lambda n: step(n, True))
    for h in range(heads):
        total = acc[h, HEAD : HEAD + 1, :]
        out_ref[:, h * HEAD : (h + 1) * HEAD] = (acc[h, :HEAD, :] / total).T.astype(B16)
        lse_ref[h : h + 1, :] = top[h : h + 1, :] + jnp.log(total)


def attend(own, everything, begins, bounds, heads, keys, waits):
    rows = own.shape[0]
    return call(
        functools.partial(attend_kernel, heads=heads, keys=keys),
        "attend",
        12,
        (bounds, begins, own, everything),
        (((rows, heads * HEAD), B16), ((8, rows), F32)),
        (((8, rows), F32), ((heads, LANES, rows), F32)),
        waits,
    )


def minus_ones(lane, base, first):
    at = base + first
    return jnp.where((lane == at) | (lane == at + 1), -1.0, 0.0).astype(B16)


def key_sides(kv, heads):
    turned = jnp.concatenate([kv[:, HEAD:], kv[:, :HEAD]], axis=1)
    lane = iota(kv.shape, 1)
    zero = jnp.zeros_like(kv)
    sides = []
    for h in range(heads):
        mine = lane < HEAD if h == 0 else lane >= HEAD
        base = HEAD * (1 - h)
        keys_h = jnp.where(mine, kv if h == 0 else turned, zero)
        values_h = jnp.where(mine, turned if h == 0 else kv, minus_ones(lane, base, 0))
        both = jnp.concatenate([keys_h, minus_ones(lane, base, 2)], axis=1)
        sides.append((keys_h, values_h, both))
    return sides


def query_grad_kernel(
    bounds, begin_ref, own_ref, g_ref, all_ref, out_ref, acc, *, heads, keys
):
    rows = own_ref.shape[0]
    acc[...] = jnp.zeros_like(acc)
    row_ids = bounds[2] + iota((rows, keys), 0)
    begins = begin_ref[...]

    def step(n, masked):
        at = n * keys
        kv = all_ref[n, :keys, :]
        sides = key_sides(kv, heads)
        if masked:
            key_ids = at + iota((rows, keys), 1)
            seen = (key_ids <= row_ids) & (key_ids >= begins)
        total = acc[...]
        for h in range(heads):
            k, v, both = sides[h]
            g = g_ref[:, h * LANES : (h + 1) * LANES]
            q = jnp.concatenate([own_ref[...], g], axis=1)
            s = lax.dot_general(q, both, LANE_DOT, preferred_element_type=F32)
            if masked:
                s = jnp.where(seen, s, MASKED)
            gp = lax.dot_general(g, v, LANE_DOT, preferred_element_type=F32)
            ds = (jnp.exp(s) * gp).astype(B16)
            total = total + jnp.dot(ds, k, preferred_element_type=F32)
        acc[...] = total

    pl.loop(bounds[0], bounds[1])(lambda n: step(n, True))
    pl.loop(bounds[1], bounds[3])(lambda n: step(n, False))
    pl.loop(bounds[3], bounds[4])(lambda n: step(n, True))
    out_ref[...] = acc[...] * SCORE_SCALE


def query_grad(own, g_pack, everything, begins, bounds, heads, keys, waits):
    rows = own.shape[0]
    return call(
        functools.partial(query_grad_kernel, heads=heads, keys=keys),
        "query_grad",
        11,
        (bounds, begins, own, g_pack, everything),
        (((rows, LANES), F32),),
        (((rows, LANES), F32),),
        waits,
    )[0]


def key_grad_kernel(
    bounds, end_ref, own_ref, all_ref, g_ref, out_ref, acc_k, acc_v, *, heads, keys, at_g
):
    rows = out_ref.shape[0]
    acc_k[...] = jnp.zeros_like(acc_k)
    acc_v[...] = jnp.zeros_like(acc_v)
    key_ids = bounds[2] + iota((rows, keys), 0)
    ends = end_ref[...]
    kv = own_ref[:rows, :]
    turned = jnp.concatenate([kv[:, HEAD:], kv[:, :HEAD]], axis=1)
    first = iota(kv.shape, 1) < HEAD
    zero = jnp.zeros_like(kv)
    count = keys // LANES
    sides = []
    for h in range(heads):
        mine = first if h == 0 else jnp.logical_not(first)
        k = jnp.where(mine, kv if h == 0 else turned, zero)
        sides.append((k, jnp.where(mine, turned if h == 0 else kv, zero)))

    def step(n, masked):
        at = n * keys
        if masked:
            row_ids = at + iota((rows, keys), 1)
            seen = (key_ids <= row_ids) & (row_ids < ends)
        q = all_ref[n, :keys, :]
        g = g_ref[n, at_g : at_g + keys, :]
        extra = g_ref[n, at_g + keys :, :].astype(F32)
        delta_rows, lse_rows = (extra[: extra.shape[0] // 2], extra[extra.shape[0] // 2 :])
        for h in range(heads):
            k, v = sides[h]
            s = lax.dot_general(k, q, LANE_DOT, preferred_element_type=F32)
            s = s - extra_row(lse_rows, h, count)
            if masked:
                s = jnp.where(seen, s, MASKED)
            p = jnp.exp(s)
            gp = lax.dot_general(v, g, LANE_DOT, preferred_element_type=F32)
            ds = (p * (gp - extra_row(delta_rows, h, count))).astype(B16)
            acc_k[h] += jnp.dot(ds, q, preferred_element_type=F32)
            acc_v[h] += jnp.dot(p.astype(B16), g, preferred_element_type=F32)

    pl.loop(bounds[0], bounds[1])(lambda n: step(n, True))
    pl.loop(bounds[1], bounds[3])(lambda n: step(n, False))
    pl.loop(bounds[3], bounds[4])(lambda n: step(n, True))
    out_ref[:, :HEAD] = acc_k[0, :, :HEAD] + acc_k[1, :, HEAD:]
    out_ref[:, HEAD:] = acc_v[0, :, :HEAD] + acc_v[1, :, HEAD:]


def key_grad(own, everything, g_all, at_g, ends, bounds, heads, keys, waits):
    rows = ends.shape[0]
    return call(
        functools.partial(key_grad_kernel, heads=heads, keys=keys, at_g=at_g),
        "key_grad",
        12,
        (bounds, ends, own, everything, g_all),
        (((rows, LANES), F32),),
        (((heads, rows, LANES), F32), ((heads, rows, LANES), F32)),
        waits,
    )[0]


def assemble_kernel(picks, mix_ref, shared_ref, dt_ref, out_ref, *, att_cols, turned):
    kv_cols = KV * HEAD
    wide = mix_ref.shape[1]
    first = picks[0] == 0
    at = att_cols
    out_ref[:, :at] = mix_ref[:, :at]
    for part in range(2):
        tile = shared_ref[:, part * kv_cols : (part + 1) * kv_cols]
        out_ref[:, at : at + HEAD] = jnp.where(first, tile[:, :HEAD], tile[:, HEAD:])
        at += HEAD
    out_ref[:, at : at + wide - att_cols] = mix_ref[:, att_cols:]
    at += wide - att_cols
    out_ref[:, at : at + shared_ref.shape[1] - 2 * kv_cols] = shared_ref[:, 2 * kv_cols :]
    at += shared_ref.shape[1] - 2 * kv_cols
    if turned:
        heads, rows = dt_ref.shape
        steps = jnp.concatenate([dt_ref[...].astype(F32), jnp.zeros((LANES - heads, rows), F32)], axis=0)
        out_ref[:, at:] = steps.T.astype(B16)
    else:
        out_ref[:, at:] = jnp.zeros((out_ref.shape[0], LANES), B16)
        out_ref[:, at : at + dt_ref.shape[1]] = dt_ref[...]


def project_kernel(
    places, both_ref, before_ref, w_ref, cos_ref, sin_ref, out_ref, q_ref, kv_ref, z_ref, pre_ref, rim_ref
):
    rows = both_ref.shape[0]
    dim = w_ref.shape[0]
    at_z = 2 * LANES
    at_x = at_z + z_ref.shape[1]
    step = 2 * TILE
    for i in range(0, rows, step):
        r = slice(i, i + step)
        x = both_ref[r, :dim]
        t = jnp.dot(x, w_ref[:, :at_z], preferred_element_type=F32)
        cosine, sine = cos_ref[r, :], sin_ref[r, :]
        q, kv = t[:, :LANES], t[:, LANES:]
        q = (q * cosine + swap_halves(q) * sine).astype(B16)
        q_ref[r, :] = (q.astype(F32) * SCORE_SCALE).astype(B16)
        turned = kv * cosine + swap_halves(kv) * sine
        kv_ref[r, :] = jnp.where(iota(kv.shape, 1) < HEAD, turned, kv).astype(B16)
        z_ref[r, :] = jnp.dot(x, w_ref[:, at_z:at_x], preferred_element_type=F32)
        pre_ref[r, :] = jnp.dot(x, w_ref[:, at_x:], preferred_element_type=F32)
    wide = rim_ref.shape[1]
    rim = jnp.dot(before_ref[...], w_ref[:, at_x : at_x + wide], preferred_element_type=F32)
    rim_ref[...] = rim[before_ref.shape[0] - 8 :, :]
    if kv_ref.shape[0] > rows:
        chunk = out_ref.shape[0]
        for n in range(dim // LANES):
            at = rows + n * chunk
            kv_ref[at : at + chunk, :] = out_ref[:, n * LANES : (n + 1) * LANES]


def partner_rows(places, k, rows):
    return pl.ds(pl.multiple_of(jnp.bitwise_xor(places[3], k) * rows, rows), rows)


def in_order(places, refs, scratch):
    rows = refs[0].shape[0]
    for k, ref in enumerate(refs):
        scratch[partner_rows(places, k, rows), :] = ref[...]


def out_weights(all_ref, w_ref, first, chunk):
    for s in range(all_ref.shape[0]):
        for n in range(w_ref.shape[1] // LANES):
            at = first + n * chunk
            piece = all_ref[s, at : at + chunk, :]
            w_ref[s * chunk : (s + 1) * chunk, n * LANES : (n + 1) * LANES] = piece


def mix_out_kernel(places, attn_ref, gated_ref, gain_ref, all_ref, *refs, ssm_all, chunk, groups):
    w_ref = all_ref
    if chunk:
        w_ref, refs = (refs[-1], refs[:-1])
        out_weights(all_ref, w_ref, attn_ref.shape[0], chunk)
    part_refs, refs = (refs[-groups:], refs[:-groups])
    mixed_ref, total_ref = refs[-2:]
    rows = attn_ref.shape[0]
    att_cols = attn_ref.shape[1]
    total = refs[0][...]
    for ref in refs[1:-2]:
        total = total + ref[...]
    total_ref[...] = total
    squares = total.T
    for i in range(0, rows, TILE):
        r = slice(i, i + TILE)
        inverse = lax.rsqrt(squares[r, 0:1] / ssm_all + EPSILON)
        gnormed = (gated_ref[r, :].astype(F32) * inverse * gain_ref[...]).astype(B16)
        mixed_ref[r, :att_cols] = attn_ref[r, :]
        mixed_ref[r, att_cols:] = gnormed
    for k, ref in enumerate(part_refs):
        r = partner_rows(places, k, rows // groups)
        ref[...] = jnp.dot(mixed_ref[r, :], w_ref[...], preferred_element_type=F32).astype(B16)


def mix_back_kernel(
    places, w_ref, attn_ref, lse_ref, gated_ref, squares_ref, gain_ref, *refs, heads, ssm_all
):
    pack_ref, send_ref, scaled_ref, stat_ref, gain_out, deltas, grad_ref = refs[-7:]
    in_order(places, refs[:-7], grad_ref)
    rows = attn_ref.shape[0]
    att_cols = attn_ref.shape[1]
    squares = squares_ref[...].T
    lse = lse_ref[...].T
    total = jnp.zeros((1, gated_ref.shape[1]), F32)
    ones = jnp.ones((8, gated_ref.shape[1]), F32)
    for i in range(0, rows, TILE):
        r = slice(i, i + TILE)
        mixed = lax.dot_general(grad_ref[r, :], w_ref[...], LANE_DOT, preferred_element_type=F32)
        back = mixed[:, :att_cols].astype(B16).astype(F32)
        product = back * attn_ref[r, :].astype(F32)
        lane = iota(back.shape, 1)
        send_ref[r, :] = back.astype(B16)
        packed = jnp.zeros((TILE, LANES), F32)
        for h in range(heads):
            base = HEAD * (1 - h)
            tile = one_head(back, h)
            delta = jnp.sum(one_head(product, h), axis=1, keepdims=True)
            packed = into_lane(packed, h, delta)
            for n, column in enumerate((delta, lse[r, h : h + 1])):
                high = column.astype(B16).astype(F32)
                tile = jnp.where(lane == base + 2 * n, high, tile)
                tile = jnp.where(lane == base + 2 * n + 1, column - high, tile)
            pack_ref[r, h * LANES : (h + 1) * LANES] = tile.astype(B16)
        deltas[r, :] = packed
        grad = mixed[:, att_cols:]
        scaled = gated_ref[r, :].astype(F32) * lax.rsqrt(squares[r, 0:1] / ssm_all + EPSILON)
        grad_scaled = grad * gain_ref[...]
        scaled_ref[r, :] = grad_scaled
        stat_ref[:, r] = lax.dot_general(
            ones, grad_scaled * scaled, LANE_DOT, precision=HIGHEST, preferred_element_type=F32
        )
        total = total + jnp.sum(grad * scaled, axis=0, keepdims=True)
    gain_out[...] = jnp.broadcast_to(total, gain_out.shape)
    extra = jnp.concatenate(
        [extra_rows(deltas[...].T, heads), extra_rows(lse_ref[...], heads)], axis=0
    )
    send_ref[rows:, :] = extra.astype(B16)


def rows_of(ref, first, last):
    return jnp.concatenate([ref[k, first:last, :] for k in range(ref.shape[0])], axis=0)


def mlp_kernel(places, out_ref, *refs, chunk, groups):
    in_order(places, refs[:groups], refs[-1])
    in_ref = refs[-1]
    refs = refs[groups:-1]
    if chunk:
        all_ref, hidden_ref, weights_ref, *term_refs, gu_ref, down_ref, grad_ref = refs
        down_ref[...] = rows_of(all_ref, 0, chunk)
        gu_ref[...] = rows_of(all_ref, chunk, all_ref.shape[1])
    else:
        gu_ref, down_ref, hidden_ref, grad_ref, *term_refs = refs
    rows = in_ref.shape[0]
    half = hidden_ref.shape[1]
    dim = in_ref.shape[1]
    step = 2 * TILE
    for i in range(0, rows, step):
        r = slice(i, i + step)
        both = jnp.dot(in_ref[r, :], gu_ref[...], preferred_element_type=F32)
        back = lax.dot_general(out_ref[r, dim:], down_ref[...], LANE_DOT, preferred_element_type=F32)
        gate, up = both[:, :half], both[:, half:]
        sig = jax.nn.sigmoid(gate)
        soft = gate * sig
        hidden_ref[r, :] = (soft * up).astype(B16)
        grad_ref[r, :half] = (back * up * sig * (1.0 + gate * (1.0 - sig))).astype(B16)
        grad_ref[r, half:] = (back * soft).astype(B16)
    for k, ref in enumerate(term_refs):
        r = partner_rows(places, k, rows // groups)
        ref[...] = lax.dot_general(
            grad_ref[r, :], gu_ref[...], LANE_DOT, preferred_element_type=F32
        ).astype(B16)
    if chunk:
        parts, tall = weights_ref.shape[0], weights_ref.shape[1] - chunk
        strip = tall // groups
        for i in range(0, half, step):
            down = lax.dot_general(
                hidden_ref[:, i : i + step], out_ref[:, dim:], ROW_DOT, preferred_element_type=F32
            ).astype(B16)
            for n in range(step // chunk):
                weights_ref[i // chunk + n, :chunk, :] = down[n * chunk : (n + 1) * chunk]
        for i in range(0, dim, step):
            both = lax.dot_general(
                in_ref[:, i : i + step], grad_ref[...], ROW_DOT, preferred_element_type=F32
            ).astype(B16)
            for n in range(step // strip):
                b, s = divmod(i // strip + n, parts)
                at = chunk + b * strip
                weights_ref[s, at : at + strip, :] = both[n * strip : (n + 1) * strip]


def down_kernel(places, hidden_ref, w_ref, *out_refs, chunk):
    w = rows_of(w_ref, 0, chunk) if chunk else w_ref[...]
    for k, ref in enumerate(out_refs):
        r = partner_rows(places, k, ref.shape[0])
        ref[...] = jnp.dot(hidden_ref[r, :], w, preferred_element_type=F32).astype(B16)


def add_blocks_kernel(places, middle_ref, *refs):
    total = refs[0][...].astype(F32)
    for ref in refs[1:-1]:
        total = total + ref[...].astype(F32)
    refs[-1][...] = (middle_ref[...] + total).astype(B16)


def group_back_kernel(places, grad_ref, w_ref, early_ref, kept_ref, *out_refs):
    for k, ref in enumerate(out_refs):
        r = partner_rows(places, k, ref.shape[0])
        ref[...] = lax.dot_general(
            grad_ref[r, :], w_ref[...], LANE_DOT, preferred_element_type=F32
        ).astype(B16)
    kept_ref[...] = early_ref[...]


def split_kernel(places, own_ref, *out_refs):
    wide = out_refs[0].shape[1]
    for k, ref in enumerate(out_refs):
        r = partner_rows(places, k, ref.shape[0])
        ref[...] = own_ref[r, own_ref.shape[1] - wide :]


def norm_back_kernel(places, middle_ref, grad_ref, gain_ref, *refs):
    total_ref, sent_ref, gain_out = refs[-3:]
    grad = refs[0][...].astype(F32)
    for ref in refs[1:-3]:
        grad = grad + ref[...].astype(F32)
    middle = middle_ref[...]
    inverse = lax.rsqrt(jnp.mean(middle * middle, axis=1, keepdims=True) + EPSILON)
    scaled = middle * inverse
    grad_scaled = grad * gain_ref[...]
    mean = jnp.mean(grad_scaled * scaled, axis=1, keepdims=True)
    total = inverse * (grad_scaled - scaled * mean) + grad_ref[...].astype(F32)
    total_ref[...] = total
    sent_ref[...] = total.astype(B16)
    gain_out[...] = jnp.broadcast_to(jnp.sum(grad * scaled, axis=0, keepdims=True), gain_out.shape)


def turned_rows(values):
    rows = values.shape[0]
    if rows < LANES:
        values = jnp.concatenate([values, jnp.zeros((LANES - rows, LANES), F32)], axis=0)
    return values.T


def own_kernel(places, own_ref, early_ref, mixed_ref, dt_ref, gain_ref, taps_ref, *head_refs, heads, half, apart):
    rows = own_ref.shape[0]
    cols = early_ref.shape[1] - half
    mixed_ref[:, :LANES] = own_ref[:, :LANES].astype(F32)
    mixed_ref[:, LANES : LANES + cols] = early_ref[:, half:].astype(F32)
    mixed_ref[:, LANES + cols :] = own_ref[:, LANES : LANES + cols].astype(F32)
    tail = own_ref[:, own_ref.shape[1] - LANES :].astype(F32)
    turned = turned_rows(tail)
    at_gain = heads + 2 + CONV
    each = gain_ref.shape[1]
    dt_ref[...] = turned[:heads, :rows]
    gain_ref[...] = turned[at_gain : at_gain + 1, :each]
    taps_ref[...] = turned[at_gain + 1 : at_gain + 1 + CONV, :each]
    at = at_gain + 1 + CONV
    sums = jnp.sum(tail, axis=0, keepdims=True) if apart else tail[0:1]
    count = len(head_refs)
    for n, ref in enumerate(head_refs):
        total = sums[:, at + n * heads : at + (n + 1) * heads]
        if apart:
            total = total + sums[:, at + (count + n) * heads : at + (count + n + 1) * heads]
        ref[...] = total


def side_kernel(places, gain_ref, *refs, heads, apart):
    if apart:
        blocks_ref, refs = (refs[-1], refs[:-1])
        for k, ref in enumerate(refs[:-4]):
            blocks_ref[jnp.bitwise_xor(places[3], k)] = ref[...]
    else:
        blocks_ref = refs[0]
    shared_ref, first_ref, second_ref, taps_ref = refs[-4:]
    groups, strip, wide = blocks_ref.shape
    per_kv = groups // KV
    blocks = [blocks_ref[b].astype(F32) for b in range(groups)]
    sums = []
    for h in range(KV):
        total = blocks[h * per_kv][:, : 2 * HEAD]
        for b in range(h * per_kv + 1, (h + 1) * per_kv):
            total = total + blocks[b][:, : 2 * HEAD]
        sums.append(total)
    rest = blocks[0]
    for b in range(1, groups):
        rest = rest + blocks[b]
    for part in range(2):
        for h in range(KV):
            at = (part * KV + h) * HEAD
            shared_ref[:, at : at + HEAD] = sums[h][:, part * HEAD : (part + 1) * HEAD]
    shared_ref[:, 2 * KV * HEAD :] = rest[:, 2 * HEAD : wide - LANES]
    turned = turned_rows(rest[:, wide - LANES :])
    first_ref[...] = turned[heads : heads + 1, :strip] / gain_ref[...]
    second_ref[...] = turned[heads + 1 : heads + 2, :strip]
    taps_ref[...] = turned[heads + 2 : heads + 2 + CONV, : taps_ref.shape[1]]


def early_kernel(places, mixed_ref, both_ref, dz_ref, w_ref, *refs, parts):
    terms_ref, gain_ref, grad_ref = refs[-3:]
    in_order(places, refs[:-3], grad_ref)
    dim = grad_ref.shape[1]
    half = dim // 2
    rows = mixed_ref.shape[1]
    chunk = rows // parts
    tall = dim // parts
    at_z = 2 * LANES
    cols = dz_ref.shape[1]
    step = 2 * TILE
    for i in range(0, rows, step):
        out = lax.dot_general(
            mixed_ref[:, i : i + step], grad_ref[...], ROW_DOT, preferred_element_type=F32
        ).astype(B16)
        for n in range(step // chunk):
            at = (i // chunk + n) * tall
            piece = out[n * chunk : (n + 1) * chunk]
            terms_ref[at : at + chunk, :half] = piece[:, :half]
            terms_ref[at + chunk : at + tall, :half] = piece[:, half:]
    for i in range(0, dim, step):
        r = slice(i, i + step)
        grad = lax.dot_general(both_ref[:, r], dz_ref[...], ROW_DOT, preferred_element_type=F32)
        terms_ref[r, half:] = grad.astype(B16)
        gain_ref[r, :] = jnp.sum(grad * w_ref[r, at_z : at_z + cols].astype(F32), axis=1, keepdims=True)


def small_columns(tile, mine, gain_ref, taps_ref, heads_ref, second_ref, *, heads, groups, parts):
    dim = second_ref.shape[1]
    cols = gain_ref.shape[1]
    wide = taps_ref.shape[1]
    tall = dim // parts
    strip = tall // groups
    at_gain = heads + 2 + CONV
    at = at_gain + 1 + CONV
    lane = iota((8, LANES), 1)
    values = jnp.where(lane < heads, heads_ref[...], 0.0)
    high = values.astype(B16).astype(F32)
    base = jnp.zeros((1, LANES), F32)
    for n in range(3):
        base = base + pltpu.roll(high, at + n * heads, 1)[n : n + 1]
        base = base + pltpu.roll(values - high, at + (3 + n) * heads, 1)[n : n + 1]
    own_row = iota(tile.shape, 0) % tall == mine
    tile[...] = jnp.where(own_row, base, 0.0)

    def columns(first, rows, width):
        pieces = [jnp.zeros((first, width), F32)] + rows
        left = LANES - first - sum(row.shape[0] for row in rows)
        return jnp.concatenate(pieces + [jnp.zeros((left, width), F32)], axis=0).T

    own = columns(at_gain, [gain_ref[0:1, :], taps_ref[:CONV, :cols]], cols)
    each = cols // parts
    for s in range(parts):
        tile[s * tall : s * tall + each, :] += own[s * each : (s + 1) * each]
    side = columns(heads + 2, [taps_ref[:CONV, cols:]], wide - cols)
    each = (wide - cols) // (groups * parts)
    second = columns(heads + 1, [second_ref[0:1, :]], dim)
    for b in range(groups):
        for s in range(parts):
            there = s * tall + b * strip
            n = b * parts + s
            tile[there : there + each, :] += side[n * each : (n + 1) * each]
            tile[there : there + strip, :] += second[n * strip : (n + 1) * strip]


def weight_grad_kernel(
    places, q_ref, kv_ref, z_ref, x_ref, rim_ref, dt_ref, cos_ref, sin_ref, w_ref, both_ref, early_ref,
    *refs, heads, groups, parts, in_strips,
):
    if in_strips:
        small_refs, (pre_ref, terms_ref, tile) = refs[:4], refs[4:]
        small_columns(tile, places[2], *small_refs, heads=heads, groups=groups, parts=parts)
    else:
        tile, pre_ref, terms_ref = refs
    rows = q_ref.shape[0]
    dim = w_ref.shape[0]
    cols = heads * HEAD
    wide = x_ref.shape[1]
    at_z = 2 * LANES
    at_x = at_z + cols
    at_dt = at_x + wide
    for i in range(0, rows, TILE):
        r = slice(i, i + TILE)
        cosine, sine = cos_ref[r, :], sin_ref[r, :]
        q, kv = q_ref[r, :], kv_ref[r, :]
        pre_ref[r, :LANES] = (q * cosine - swap_halves(q) * sine).astype(B16)
        turned = kv * cosine - swap_halves(kv) * sine
        pre_ref[r, LANES : 2 * LANES] = jnp.where(iota(kv.shape, 1) < HEAD, turned, kv).astype(B16)
        pre_ref[r, at_z:at_x] = z_ref[r, :]
        x = x_ref[r, :]
        if i + TILE == rows:
            x = jnp.concatenate([x[: TILE - 8], x[TILE - 8 :] + rim_ref[...]], axis=0)
        pre_ref[r, at_x:at_dt] = x.astype(B16)
        pre_ref[r, at_dt:] = dt_ref[r, :]
    block = dim // groups
    strip = block // parts
    mixed = LANES + cols
    sides = slice(mixed + LANES, mixed + 3 * LANES)
    ends = slice(mixed + 3 * LANES, mixed + 4 * LANES)
    lane = iota((block, LANES), 1)
    for b in range(groups):
        r = slice(b * block, (b + 1) * block)
        x = both_ref[:, r]
        near = lax.dot_general(x, pre_ref[:, :at_z], ROW_DOT, preferred_element_type=F32)
        far = lax.dot_general(x, pre_ref[:, at_x:], ROW_DOT, preferred_element_type=F32)
        gain = jnp.sum(near * w_ref[r, :at_z].astype(F32), axis=1, keepdims=True)
        gain = gain + jnp.sum(far * w_ref[r, at_x:].astype(F32), axis=1, keepdims=True)
        gain = gain + early_ref[r, :]
        terms_ref[r, :LANES] = near[:, :LANES].astype(B16)
        terms_ref[r, LANES:mixed] = far[:, :cols].astype(B16)
        if in_strips:
            for s in range(parts):
                here = slice(s * strip, (s + 1) * strip)
                first = s * groups * strip + b * strip
                there = slice(first, first + strip)
                terms_ref[there, mixed : mixed + LANES] = near[here, LANES:].astype(B16)
                terms_ref[there, sides] = far[here, cols:wide].astype(B16)
                at_gain = iota((strip, LANES), 1) == heads
                tile[there, :] = jnp.where(at_gain, gain[here], tile[there, :])
            tile[r, :] = jnp.where(lane < heads, far[:, wide:], tile[r, :])
        else:
            terms_ref[r, mixed : mixed + LANES] = near[:, LANES:].astype(B16)
            terms_ref[r, sides] = far[:, cols:wide].astype(B16)
            tail = jnp.where(lane < heads, far[:, wide:], tile[r, :])
            terms_ref[r, ends] = jnp.where(lane == heads, gain, tail).astype(B16)
    if in_strips:
        terms_ref[:, ends] = tile[...].astype(B16)


def iota(shape, dim):
    return lax.broadcasted_iota(jnp.int32, shape, dim)


def per_head(columns, pair):
    shape = (columns.shape[0], LANES)
    return jnp.where(
        iota(shape, 1) < HEAD, columns[:, 2 * pair : 2 * pair + 1], columns[:, 2 * pair + 1 : 2 * pair + 2]
    )


def one_head(values, head):
    keep = (iota(values.shape, 1) < HEAD) == (head % 2 == 0)
    return jnp.where(keep, values, jnp.zeros_like(values))


def into_lane(columns, head, column):
    return jnp.where(iota(columns.shape, 1) == head, column, columns)


def silu_slope(v, sig):
    return sig * (1.0 + v * (1.0 - sig))


def tap_window(ext_ref, tap, first, amount, places):
    return ext_ref[first + 8 - (CONV - 1) + tap : first + 8 - (CONV - 1) + tap + amount, :]


def span_kernel(places, begin_ref, pre_ref, rim_ref, taps_ref, params_ref, u_ref, intra_ref, cum_ref, state_ref, ext, xb, *, heads, at_x, at_dt, nstate):
    rows = pre_ref.shape[0]
    cols = heads * HEAD
    first_row, last_begin = places[0], places[1]
    ext[0:8, :] = rim_ref[...]
    ext[8 : 8 + rows, :] = pre_ref[:, at_x:at_dt]
    local = begin_ref[...] - first_row
    row_ids = iota((rows, 1), 0)
    for i in range(0, rows, TILE):
        total = jnp.zeros((TILE, ext.shape[1]), F32)
        for tap in range(CONV):
            seen = row_ids[i : i + TILE] - (CONV - 1) + tap >= local[i : i + TILE]
            window = tap_window(ext, tap, i, TILE, places)
            total = total + jnp.where(seen, window, 0.0) * taps_ref[tap : tap + 1, :]
        u_ref[i : i + TILE, :] = total
        xb[i : i + TILE, :] = (total * jax.nn.sigmoid(total)).astype(B16)
    raw = pre_ref[:, at_dt : at_dt + LANES] + params_ref[0:1, :]
    dt = jnp.maximum(raw, 0.0) + jnp.log1p(jnp.exp(-jnp.abs(raw)))
    lower = (iota((rows, rows), 0) >= iota((rows, rows), 1)).astype(F32)
    cum = jnp.dot(lower, dt * params_ref[1:2, :], precision=HIGHEST, preferred_element_type=F32)
    cum_ref[:, :LANES] = cum
    cum_ref[:, LANES:] = dt
    cum_t, dt_t = cum.T, dt.T
    last = cum[rows - 1 : rows, :]
    closing = row_ids + first_row >= last_begin
    to_end = jnp.where(closing, jnp.exp(last - cum) * dt, 0.0)
    for i in range(0, rows, TILE):
        width = i + TILE
        c = xb[i : i + TILE, cols + nstate : cols + 2 * nstate]
        b = xb[:width, cols : cols + nstate]
        inner = lax.dot_general(c, b, LANE_DOT, preferred_element_type=F32)
        key = iota((TILE, width), 1)
        seen = (key <= iota((TILE, width), 0) + i) & (key >= local[i : i + TILE])
        for pair in range(heads // 2):
            out = []
            for h in (2 * pair, 2 * pair + 1):
                spread = jnp.where(seen, cum[i : i + TILE, h : h + 1] - cum_t[h : h + 1, :width], MASKED)
                weights = (jnp.exp(spread) * inner * dt_t[h : h + 1, :width]).astype(B16)
                out.append(jnp.dot(weights, xb[:width, pair * LANES : (pair + 1) * LANES], preferred_element_type=F32))
            intra_ref[i : i + TILE, pair * LANES : (pair + 1) * LANES] = jnp.where(iota((TILE, LANES), 1) < HEAD, out[0], out[1])
    b_all = xb[:, cols : cols + nstate]
    for pair in range(heads // 2):
        at = slice(pair * LANES, (pair + 1) * LANES)
        closed = (xb[:, at].astype(F32) * per_head(to_end, pair)).astype(B16)
        state_ref[at, :] = lax.dot_general(closed, b_all, ROW_DOT, preferred_element_type=F32).astype(B16)
    decay = jnp.where(last_begin < first_row, jnp.exp(last), 0.0)
    high = decay.astype(B16)
    low = (decay - high.astype(F32)).astype(B16)
    both = jnp.concatenate([jnp.broadcast_to(high.astype(F32), (LANES // 2, LANES)), jnp.broadcast_to(low.astype(F32), (LANES // 2, LANES))], axis=0)
    state_ref[cols : cols + 16, :] = both.T[:16, :].astype(B16)


def span_forward(places, begins, pre, rim, taps, params, heads, at_x, at_dt, nstate):
    rows = pre.shape[0]
    wide = at_dt - at_x
    cols = heads * HEAD
    return call(
        functools.partial(span_kernel, heads=heads, at_x=at_x, at_dt=at_dt, nstate=nstate),
        "span_forward",
        8,
        (places, begins, pre, rim, taps, params),
        (((rows, wide), F32), ((rows, cols), F32), ((rows, 2 * LANES), F32), ((cols + 16, nstate), B16)),
        (((rows + 8, wide), F32), ((rows, wide), B16)),
    )


def decay_of(states_ref, k, head, cols):
    tail = states_ref[k, cols + head - head % 8 : cols + head - head % 8 + 8, :].astype(F32)
    row = tail[head % 8 : head % 8 + 1, :]
    return row[:, 0:1] + row[:, LANES // 2 : LANES // 2 + 1]


def finish_kernel(places, begin_ref, states_ref, u_ref, intra_ref, cum_ref, z_ref, params_ref, gated_ref, v_ref, state_ref, squares_ref, *, heads, nstate):
    rows = u_ref.shape[0]
    cols = heads * HEAD
    state_ref[...] = jnp.zeros_like(state_ref)

    def fold(k):
        for h in range(heads):
            at = slice(h * HEAD, (h + 1) * HEAD)
            state_ref[at, :] = state_ref[at, :] * decay_of(states_ref, k, h, cols) + states_ref[k, at, :].astype(F32)

    pl.loop(0, places[2])(fold)
    carried = begin_ref[...] < places[0]
    for i in range(0, rows, TILE):
        r = slice(i, i + TILE)
        enter = jnp.where(carried[r], jnp.exp(cum_ref[r, :LANES]), 0.0)
        uc = u_ref[r, cols + nstate : cols + 2 * nstate]
        c = (uc * jax.nn.sigmoid(uc)).astype(B16)
        total = jnp.zeros((8, TILE), F32)
        for pair in range(heads // 2):
            at = slice(pair * LANES, (pair + 1) * LANES)
            y = lax.dot_general(c, state_ref[at, :].astype(B16), LANE_DOT, preferred_element_type=F32)
            ux = u_ref[r, at]
            x = ux * jax.nn.sigmoid(ux)
            skip = per_head(params_ref[2:3, :], pair)
            v = intra_ref[r, at] + per_head(enter, pair) * y + skip * x
            z = z_ref[r, at]
            gated = (v * (z * jax.nn.sigmoid(z))).astype(B16)
            v_ref[r, at] = v
            gated_ref[r, at] = gated
            g = gated.astype(F32)
            total = total + lax.dot_general(jnp.ones((8, LANES), F32), g * g, LANE_DOT, precision=HIGHEST, preferred_element_type=F32)
        squares_ref[:, r] = total


def span_finish(places, begins, states, u, intra, cum, z, params, heads, nstate):
    rows = u.shape[0]
    cols = heads * HEAD
    return call(
        functools.partial(finish_kernel, heads=heads, nstate=nstate),
        "span_finish",
        7,
        (places, begins, states, u, intra, cum, z, params),
        (((rows, cols), B16), ((rows, cols), F32), ((cols, nstate), F32), ((8, rows), F32)),
        (),
    )


def gate_back_kernel(places, begin_ref, scaled_ref, gated_ref, squares_ref, u_ref, cum_ref, z_ref, v_ref, send_ref, *refs, heads, nstate, ssm_all):
    back_ref, dz_ref, state_ref, eg = refs[-4:]
    total = refs[0][...]
    for ref in refs[1:-4]:
        total = total + ref[...]
    rows = u_ref.shape[0]
    cols = heads * HEAD
    carried = begin_ref[...] < places[0]
    squares, stat = squares_ref[...].T, total.T
    uc = u_ref[:, cols + nstate : cols + 2 * nstate]
    c = (uc * jax.nn.sigmoid(uc)).astype(B16)
    for i in range(0, rows, TILE):
        r = slice(i, i + TILE)
        enter = jnp.where(carried[r], jnp.exp(cum_ref[r, :LANES]), 0.0)
        inverse = lax.rsqrt(squares[r, 0:1] / ssm_all + EPSILON)
        mean = stat[r, 0:1] / ssm_all
        for pair in range(heads // 2):
            at = slice(pair * LANES, (pair + 1) * LANES)
            z = z_ref[r, at]
            sig = jax.nn.sigmoid(z)
            scaled = gated_ref[r, at].astype(F32) * inverse
            gg = (inverse * (scaled_ref[r, at] - scaled * mean)).astype(B16)
            back_ref[r, at] = gg
            gg = gg.astype(F32)
            dz_ref[r, at] = (gg * v_ref[r, at] * silu_slope(z, sig)).astype(B16)
            eg[r, at] = (gg * (z * sig) * per_head(enter, pair)).astype(B16)
    state_ref[:cols, :] = lax.dot_general(eg[...], c, ROW_DOT, preferred_element_type=F32).astype(B16)
    state_ref[cols:, :] = send_ref[...]


def gate_back(places, begins, scaled, gated, squares, stats, u, cum, z, v, send, heads, nstate, ssm_all):
    rows = u.shape[0]
    cols = heads * HEAD
    return call(
        functools.partial(gate_back_kernel, heads=heads, nstate=nstate, ssm_all=ssm_all),
        "gate_back",
        5,
        (places, begins, scaled, gated, squares, u, cum, z, v, send) + stats,
        (((rows, cols), B16), ((rows, cols), B16), ((cols + send.shape[0], nstate), B16)),
        (((rows, cols), B16),),
    )


def back_kernel(places, begin_ref, g_ref, z_ref, pre_ref, rim_ref, u_ref, cum_ref, state_ref, states_ref, grads_ref, taps_ref, params_ref, gx_ref, gdt_ref, rim_out, taps_out, small_out, ext, gext, xb, gb, later, dxb, lane_sum, cols_sum, *, heads, at_x, at_dt, nstate):
    rows = u_ref.shape[0]
    cols = heads * HEAD
    wide = at_dt - at_x
    count = states_ref.shape[0]
    pairs = heads // 2
    first_row, last_begin, mine = places[0], places[1], places[2]
    later[...] = jnp.zeros_like(later)

    def fold(n):
        k = count - 1 - n
        for h in range(heads):
            at = slice(h * HEAD, (h + 1) * HEAD)
            later[at, :] = later[at, :] * decay_of(states_ref, k, h, cols) + grads_ref[k, at, :].astype(F32)

    pl.loop(0, count - 1 - mine)(fold)
    local = begin_ref[...] - first_row
    row_ids = iota((rows, 1), 0)
    cum = cum_ref[:, :LANES]
    dt = cum_ref[:, LANES:]
    cum_t, dt_t = cum.T, dt.T
    last = cum[rows - 1 : rows, :]
    leave = jnp.where(row_ids + first_row >= last_begin, jnp.exp(last - cum), 0.0)
    enter = jnp.where(begin_ref[...] < first_row, jnp.exp(cum), 0.0)
    to_end = leave * dt
    for i in range(0, rows, TILE):
        r = slice(i, i + TILE)
        u = u_ref[r, :]
        xb[r, :] = (u * jax.nn.sigmoid(u)).astype(B16)
        z = z_ref[r, :]
        gb[r, :] = (g_ref[r, :].astype(F32) * (z * jax.nn.sigmoid(z))).astype(B16)
    dxb[...] = jnp.zeros_like(dxb)
    cols_sum[...] = jnp.zeros_like(cols_sum)
    b_at = slice(cols, cols + nstate)
    c_at = slice(cols + nstate, cols + 2 * nstate)
    for i in range(0, rows, TILE):
        width = i + TILE
        r = slice(i, i + TILE)
        inner = lax.dot_general(xb[r, c_at], xb[:width, b_at], LANE_DOT, preferred_element_type=F32)
        key = iota((TILE, width), 1)
        seen = (key <= iota((TILE, width), 0) + i) & (key >= local[r])
        grad_inner = jnp.zeros((TILE, width), F32)
        sums = jnp.zeros((TILE, LANES), F32)
        for h in range(heads):
            at = slice(h // 2 * LANES, (h // 2 + 1) * LANES)
            g = one_head(gb[r, at], h)
            spread = jnp.where(seen, cum[r, h : h + 1] - cum_t[h : h + 1, :width], MASKED)
            decays = jnp.exp(spread)
            steps = dt_t[h : h + 1, :width]
            pairing = lax.dot_general(g, xb[:width, at], LANE_DOT, preferred_element_type=F32)
            paired = pairing * decays
            grad_inner = grad_inner + paired * steps
            both = paired * inner
            cols_sum[h : h + 1, :width] += jnp.sum(both, axis=0, keepdims=True)
            sums = into_lane(sums, h, jnp.sum(both * steps, axis=1, keepdims=True))
            weights = (decays * inner * steps).astype(B16)
            dxb[:width, at] += lax.dot_general(weights, g, ROW_DOT, preferred_element_type=F32)
        lane_sum[r, :] = sums
        grad_inner = grad_inner.astype(B16)
        dxb[r, c_at] += jnp.dot(grad_inner, xb[:width, b_at], preferred_element_type=F32)
        dxb[:width, b_at] += lax.dot_general(grad_inner, xb[r, c_at], ROW_DOT, preferred_element_type=F32)
    from_cols = jnp.concatenate([cols_sum[...], jnp.zeros((LANES - 8, rows), F32)], axis=0).T
    state_b = state_ref[...].astype(B16)
    later_b = later[...].astype(B16)
    entered = jnp.zeros((rows, LANES), F32)
    closed = jnp.zeros((rows, LANES), F32)
    skips = jnp.zeros((1, LANES), F32)
    chained = jnp.zeros((1, LANES), F32)
    for pair in range(pairs):
        at = slice(pair * LANES, (pair + 1) * LANES)
        x = xb[:, at].astype(F32)
        g = gb[:, at].astype(F32)
        y = lax.dot_general(xb[:, c_at], state_b[at, :], LANE_DOT, preferred_element_type=F32)
        q = lax.dot_general(xb[:, b_at], later_b[at, :], LANE_DOT, preferred_element_type=F32)
        ends = per_head(to_end, pair)
        dxb[:, c_at] += jnp.dot((g * per_head(enter, pair)).astype(B16), state_b[at, :], preferred_element_type=F32)
        dxb[:, b_at] += jnp.dot((x * ends).astype(B16), later_b[at, :], preferred_element_type=F32)
        dxb[:, at] += ends * q + g * per_head(params_ref[2:3, :], pair)
        gy, xq, gx = g * y, x * q, jnp.sum(g * x, axis=0, keepdims=True)
        kept = jnp.sum(later[at, :] * state_ref[at, :], axis=1, keepdims=True)
        for h in (2 * pair, 2 * pair + 1):
            entered = into_lane(entered, h, jnp.sum(one_head(gy, h), axis=1, keepdims=True))
            closed = into_lane(closed, h, jnp.sum(one_head(xq, h), axis=1, keepdims=True))
            skips = into_lane(skips, h, jnp.sum(one_head(gx, h), axis=1, keepdims=True))
            half = slice(h % 2 * HEAD, (h % 2 + 1) * HEAD)
            chained = into_lane(chained, h, jnp.sum(kept[half], axis=0, keepdims=True))
    decay = jnp.where(last_begin < first_row, jnp.exp(last), 0.0)
    ended = closed * to_end
    grad_cum = lane_sum[...] - from_cols * dt + entered * enter - ended
    at_last = jnp.sum(ended, axis=0, keepdims=True) + decay * chained
    grad_cum = grad_cum + jnp.where(row_ids == rows - 1, at_last, 0.0)
    upper = (iota((rows, rows), 0) <= iota((rows, rows), 1)).astype(F32)
    grad_log = jnp.dot(upper, grad_cum, precision=HIGHEST, preferred_element_type=F32)
    rate = params_ref[1:2, :]
    grad_dt = from_cols + closed * leave + grad_log * rate
    grad_raw = grad_dt * jax.nn.sigmoid(pre_ref[:, at_dt : at_dt + LANES] + params_ref[0:1, :])
    grad_raw = jnp.where(iota((rows, LANES), 1) < heads, grad_raw, 0.0)
    gdt_ref[...] = grad_raw.astype(B16)
    small_out[0:1, :] = jnp.sum(grad_log * dt, axis=0, keepdims=True) * rate
    small_out[1:2, :] = jnp.sum(grad_raw, axis=0, keepdims=True)
    small_out[2:3, :] = skips
    small_out[3:8, :] = jnp.zeros((5, LANES), F32)
    ext[0:8, :] = rim_ref[...]
    ext[8 : 8 + rows, :] = pre_ref[:, at_x:at_dt]
    gext[...] = jnp.zeros_like(gext)
    taps_out[...] = jnp.zeros_like(taps_out)
    for i in range(0, rows, TILE):
        r = slice(i, i + TILE)
        u = u_ref[r, :]
        du = dxb[r, :] * silu_slope(u, jax.nn.sigmoid(u))
        for tap in range(CONV):
            seen = row_ids[r] - (CONV - 1) + tap >= local[r]
            part = jnp.where(seen, du, 0.0)
            taps_out[tap : tap + 1, :] += jnp.sum(part * tap_window(ext, tap, i, TILE, places), axis=0, keepdims=True)
            at = 8 - (CONV - 1) + tap + i
            gext[at : at + TILE, :] += part * taps_ref[tap : tap + 1, :]
    rim_out[...] = gext[0:8, :]
    gx_ref[...] = gext[8:, :]


def span_back(places, begins, back, z, pre, rim, u, cum, state, states, grads, taps, params, heads, at_x, at_dt, nstate, waits):
    rows = u.shape[0]
    cols = heads * HEAD
    wide = at_dt - at_x
    return call(
        functools.partial(back_kernel, heads=heads, at_x=at_x, at_dt=at_dt, nstate=nstate),
        "span_back",
        16,
        (places, begins, back, z, pre, rim, u, cum, state, states, grads, taps, params),
        (((rows, wide), F32), ((rows, LANES), B16), ((8, wide), F32), ((8, wide), F32), ((8, LANES), F32)),
        (((rows + 8, wide), F32), ((rows + 8, wide), F32), ((rows, wide), B16), ((rows, cols), B16),
         ((cols, nstate), F32), ((rows, wide), F32), ((rows, LANES), F32), ((8, rows), F32)),
        waits,
    )


def shards(
    x_in,
    lengths,
    norm1_gain,
    w_mix_in,
    w_dt,
    w_shared,
    conv_x,
    conv_bc,
    a_log,
    dt_bias,
    d_skip,
    gate_gain,
    w_out,
    norm2_gain,
    w_gate,
    w_up,
    w_down,
    d_out,
):
    tok_rows = x_in.shape[0]
    groups = lax.axis_size("branch")
    branch_id = lax.axis_index("branch")
    seq_id = lax.axis_index("seq")
    seq_rows = tok_rows * groups
    group_first = seq_id * seq_rows
    att_heads = HEADS_ATT // groups
    att_cols = att_heads * HEAD
    ssm_heads = w_dt.shape[1]
    ssm_cols = ssm_heads * HEAD
    kv_cols = KV * HEAD
    f32 = jnp.float32
    bf16 = jnp.bfloat16
    dim = x_in.shape[1]
    parts = lax.axis_size("seq")
    chunk = w_out.shape[0] // groups
    att_chunks = parts * att_cols // (att_cols + ssm_cols)
    ssm_chunks = parts - att_chunks
    strip = dim // (groups * parts)
    hidden_all = w_gate.shape[1]
    hidden_a = hidden_all * att_cols // ((att_cols + ssm_cols) * groups)
    hidden_s = hidden_all // groups - hidden_a
    hidden_b = hidden_a + hidden_s

    def spot(c):
        first = groups * att_chunks
        if c < first:
            return (c // att_chunks) * parts + c % att_chunks
        return ((c - first) // ssm_chunks) * parts + att_chunks + (c - first) % ssm_chunks

    to_heads = [((c % groups) * parts + c // groups, spot(c)) for c in range(groups * parts)]
    from_heads = [(spot(c), c) for c in range(groups * parts)]

    def branch_parts(part):
        routes = [[(i, i ^ k) for i in range(groups)] for k in range(1, groups)]
        return (part,) + tuple(lax.ppermute(part, "branch", route) for route in routes)

    def branch_swap(blocks):
        routes = [[(i, i ^ k) for i in range(groups)] for k in range(1, groups)]
        moved = [lax.ppermute(block, "branch", route) for block, route in zip(blocks[1:], routes)]
        return (blocks[0],) + tuple(moved)

    def ordered(blocks):
        stacked = jnp.stack(blocks)
        picked = [lax.dynamic_index_in_dim(stacked, branch_id ^ n, 0, False) for n in range(groups)]
        return jnp.concatenate(picked, axis=0)

    def branch_exchange(blocks):
        return lax.all_to_all(blocks, "branch", 0, 0, tiled=True)

    def branch_gather(part):
        copies = branch_exchange(jnp.broadcast_to(part[None], (groups,) + part.shape))
        return copies.reshape((groups * part.shape[0],) + part.shape[1:])

    def branch_scatter(terms):
        blocks = terms.astype(bf16).reshape((groups, -1) + terms.shape[1:])
        return jnp.sum(lax.all_to_all(blocks, "branch", 0, 0, tiled=True).astype(f32), axis=0)

    kv_head = branch_id * att_heads // (HEADS_ATT // KV)
    side_cols = w_shared.shape[1] - 2 * kv_cols
    w1_cols = w_mix_in.shape[1] + 2 * HEAD + side_cols + LANES
    turned = w_dt.shape[0] % LANES == 0
    w1_part = call(
        functools.partial(assemble_kernel, att_cols=att_cols, turned=turned),
        "assemble",
        1,
        (kv_head[None], w_mix_in, w_shared, w_dt.T if turned else w_dt),
        (((w_mix_in.shape[0], w1_cols), B16),),
        (),
    )[0]
    w1 = lax.all_gather(w1_part, "seq", axis=0, tiled=True)

    def own_columns(w):
        return [
            lax.dynamic_slice_in_dim(w, branch_id * hidden_a, hidden_a, 1),
            lax.dynamic_slice_in_dim(w, groups * hidden_a + branch_id * hidden_s, hidden_s, 1),
        ]

    row_part = jnp.concatenate(
        [
            lax.dynamic_slice_in_dim(w_out, branch_id * chunk, chunk, 0),
            lax.dynamic_slice_in_dim(w_down, branch_id * chunk, chunk, 0),
        ],
        axis=0,
    )
    row_part = lax.ppermute(row_part, ("branch", "seq"), to_heads)
    out_part = row_part[:chunk]
    mlp_part = jnp.concatenate(
        [row_part[chunk:], jnp.concatenate(own_columns(w_gate) + own_columns(w_up), axis=1)], axis=0
    )
    x_rows = x_in.astype(f32)
    scaled1, inverse1 = rms_parts(x_rows)
    normed1 = (scaled1 * norm1_gain).astype(bf16)
    both_in = branch_gather(jnp.concatenate([normed1, d_out], axis=1))
    d_out_g = both_in[:, dim:]
    before = from_behind(both_in[seq_rows - 16 :, :dim], "seq", 1)
    row_ids = group_first + jnp.arange(seq_rows, dtype=jnp.int32)
    seq_ends = jnp.cumsum(lengths)

    def begin_of(ids):
        return jnp.max(jnp.where(seq_ends <= ids[..., None], seq_ends, 0), axis=-1)

    def end_of(ids):
        return jnp.min(jnp.where(seq_ends > ids[..., None], seq_ends, seq_rows * parts), axis=-1)

    begins = begin_of(row_ids)
    ends = end_of(row_ids)
    position = row_ids - begins
    row_last = group_first + seq_rows - 1
    begin_first, begin_last = (begin_of(group_first), begin_of(row_last))
    end_first, end_last = (end_of(group_first), end_of(row_last))
    here = seq_id
    query_lo = begin_first // seq_rows
    query_clear = jnp.minimum(jnp.maximum(query_lo, -(-begin_last // seq_rows)), here)
    query_bounds = jnp.stack([query_lo, query_clear, group_first, here, here + 1])
    key_hi = -(-end_last // seq_rows)
    key_clear = jnp.maximum(here + 1, jnp.minimum(end_first // seq_rows, key_hi))
    key_bounds = jnp.stack([here, here + 1, group_first, key_clear, key_hi])
    places = jnp.stack([group_first, begin_last, seq_id, branch_id])
    begins_col, begins_row, ends_col = (begins[:, None], begins[None, :], ends[:, None])
    at_dt = ssm_cols + side_cols
    nstate = conv_bc.shape[1] // 2
    taps = jnp.pad(jnp.concatenate([conv_x, conv_bc], axis=1), ((0, 8 - CONV), (0, 0)))
    params = jnp.stack([dt_bias, -jnp.exp(a_log), d_skip])
    params = jnp.pad(params, ((0, 5), (0, LANES - ssm_heads)))
    ssm_all = gate_gain.shape[0]
    gain_row = lax.dynamic_slice_in_dim(gate_gain, branch_id * ssm_cols, ssm_cols, 0)[None, :]
    cosine, sine = rotate_tables(position)
    packed = chunk if chunk % 16 == 0 and strip % 16 == 0 else 0
    kv_rows = seq_rows + packed * dim // LANES
    queries, kv, z_pre, pre, rim = call(
        project_kernel,
        "project",
        5,
        (places, both_in, before, w1, cosine, sine, out_part),
        (
            ((seq_rows, LANES), B16),
            ((kv_rows, LANES), B16),
            ((seq_rows, ssm_cols), F32),
            ((seq_rows, at_dt + LANES), F32),
            ((8, at_dt), F32),
        ),
        (),
        (
            begins_col,
            begins_row,
            ends_col,
            query_bounds,
            key_bounds,
            taps,
            params,
            gain_row,
            mlp_part,
        ),
    )
    kv_all = lax.all_gather(kv, "seq", axis=0)
    w_out_b = kv_all if packed else lax.all_gather(out_part, "seq", axis=0, tiled=True)
    mlp_all = lax.all_gather(mlp_part, "seq", axis=0)
    if packed:
        mlp_weights, down_weights = ((mlp_all,), mlp_all)
        mlp_scratch = (
            ((dim, 2 * hidden_b), B16),
            ((parts * chunk, dim), B16),
            ((seq_rows, 2 * hidden_b), B16),
        )
    else:
        down_weights = mlp_all[:, :chunk].reshape(parts * chunk, dim)
        mlp_weights = (mlp_all[:, chunk:].reshape(dim, 2 * hidden_b), down_weights)
        mlp_scratch = ()
    u, intra, cum, state = span_forward(
        places, begins_col, pre, rim, taps, params, ssm_heads, 0, at_dt, nstate
    )
    states = lax.all_gather(state, "seq", axis=0)
    gated_b, gated_v, state_in, squares = span_finish(
        places, begins_col, states, u, intra, cum, z_pre, params, ssm_heads, nstate
    )
    attn_out, lse = attend(
        queries, kv_all, begins_row, query_bounds, att_heads, seq_rows, (gated_b,)
    )
    q_all = lax.all_gather(queries, "seq", axis=0)

    out_shape = (parts * chunk, dim)
    row_blocks = (((tok_rows, dim), B16),) * groups
    mixed_out, squares, *out_terms = call(
        functools.partial(mix_out_kernel, ssm_all=ssm_all, chunk=packed, groups=groups),
        "mix_out",
        3,
        (places, attn_out, gated_b, gain_row, w_out_b) + branch_parts(squares),
        (((seq_rows, att_cols + ssm_cols), B16), ((8, seq_rows), F32))
        + row_blocks
        + (((out_shape, B16),) if packed else ()),
        (),
    )
    w_out_b = out_terms.pop() if packed else w_out_b
    projected = sum(block.astype(f32) for block in branch_swap(out_terms))
    middle = x_rows + projected
    scaled2, inverse2 = rms_parts(middle)
    normed2 = branch_parts((scaled2 * norm2_gain).astype(bf16))
    middle_shape = (parts, chunk + dim // parts, dim) if packed else (seq_rows, 2 * hidden_b)
    hidden, mlp_middle, *mlp_back = call(
        functools.partial(mlp_kernel, chunk=packed, groups=groups),
        "mlp",
        11,
        (places, both_in) + normed2 + mlp_weights,
        (
            ((seq_rows, hidden_b), B16),
            (middle_shape, B16),
        )
        + row_blocks,
        mlp_scratch + (((seq_rows, dim), B16),),
    )
    def over_rows(left, right):
        return lax.dot_general(
            left, right, (((0,), (0,)), ((), ())), preferred_element_type=f32
        ).astype(bf16)

    def strips(rows_all):
        wide = rows_all.reshape((groups, parts, strip) + rows_all.shape[1:])
        return jnp.swapaxes(wide, 0, 1).reshape((parts, groups * strip) + rows_all.shape[1:])

    if packed:
        mlp_terms = mlp_middle
    else:
        mlp_terms = jnp.concatenate(
            [
                over_rows(hidden, d_out_g).reshape(parts, chunk, dim),
                strips(over_rows(ordered(normed2), mlp_middle)),
            ],
            axis=1,
        )
    mlp_own = lax.psum_scatter(mlp_terms, "seq", scatter_dimension=0)
    grad_middle, grad_sent, grad_n2 = call(
        norm_back_kernel,
        "norm_back",
        2,
        (places, middle, d_out, norm2_gain[None, :]) + branch_swap(mlp_back),
        (((tok_rows, dim), F32), ((tok_rows, dim), B16), ((8, dim), F32)),
        (),
        (q_all,),
    )
    grad_proj = branch_parts(grad_sent)
    g_pack, g_send, grad_scaled, stat, grad_gain = call(
        functools.partial(mix_back_kernel, heads=att_heads, ssm_all=ssm_all),
        "mix_back",
        5,
        (places, w_out_b, attn_out, lse, gated_b, squares, gain_row) + grad_proj,
        (
            ((seq_rows, att_heads * LANES), B16),
            ((seq_rows + 4 * att_heads * seq_rows // LANES, LANES), B16),
            ((seq_rows, ssm_cols), F32),
            ((8, seq_rows), F32),
            ((8, ssm_cols), F32),
        ),
        (((seq_rows, LANES), F32), ((seq_rows, dim), B16)),
    )
    stats = branch_parts(stat)
    grad_gate_gain = grad_gain[0]

    def all_columns(blocks):
        blocks = jnp.swapaxes(blocks, 0, 1)
        return jnp.concatenate(
            [blocks[:, :, :hidden_a].reshape(strip, -1), blocks[:, :, hidden_a:].reshape(strip, -1)],
            axis=1,
        )

    back_ssm, grad_z, grad_state = gate_back(
        places, begins_col, grad_scaled, gated_b, squares, stats, u, cum, z_pre, gated_v, g_send, ssm_heads, nstate, ssm_all
    )
    grad_states = lax.all_gather(grad_state, "seq", axis=0)
    grad_q = query_grad(
        queries, g_pack, kv_all, begins_col, query_bounds, att_heads, seq_rows, (grad_state, mlp_own)
    )
    y_terms = call(
        functools.partial(down_kernel, chunk=packed),
        "down",
        3,
        (places, hidden, down_weights),
        row_blocks,
        (),
        (grad_state,),
    )
    y_blocks = branch_swap(y_terms)
    if packed:
        early_terms, early_gain = call(
            functools.partial(early_kernel, parts=parts),
            "early",
            3,
            (places, mixed_out, both_in, grad_z, w1) + grad_proj,
            (((dim, dim // 2 + ssm_cols), B16), ((dim, 1), F32)),
            (((seq_rows, dim), B16),),
        )
        early_terms = early_terms.reshape(parts, dim // parts, dim // 2 + ssm_cols)
    else:
        out_rows = over_rows(mixed_out, ordered(grad_proj)).reshape(parts, chunk, dim)
        z_grad = lax.dot_general(both_in[:, :dim], grad_z, ROW_DOT, preferred_element_type=f32)
        at_z = 2 * LANES
        z_weight = w1[:, at_z : at_z + ssm_cols].astype(f32)
        early_gain = jnp.sum(z_grad * z_weight, axis=1, keepdims=True)
        early_terms = jnp.concatenate(
            [
                jnp.concatenate([out_rows[:, :, : dim // 2], out_rows[:, :, dim // 2 :]], axis=1),
                z_grad.astype(bf16).reshape(parts, dim // parts, ssm_cols),
            ],
            axis=2,
        )
    early_own = lax.psum_scatter(early_terms, "seq", scatter_dimension=0)
    grad_w_down = lax.ppermute(mlp_own[:chunk], ("branch", "seq"), from_heads)
    own_gu = branch_exchange(mlp_own[chunk:].reshape(groups, strip, 2 * hidden_b))
    grad_w_gate = all_columns(own_gu[:, :, :hidden_b]).astype(f32)
    grad_w_up = all_columns(own_gu[:, :, hidden_b:]).astype(f32)
    grad_xbc, grad_dt, rim_back, grad_taps, grad_small = span_back(
        places,
        begins_col,
        back_ssm,
        z_pre,
        pre,
        rim,
        u,
        cum,
        state_in,
        states,
        grad_states,
        taps,
        params,
        ssm_heads,
        0,
        at_dt,
        nstate,
        (grad_q, early_terms, y_terms[0]),
    )
    rim_back = from_behind(rim_back, "seq", -1)
    grad_kv = key_grad(
        kv, q_all, grad_states, ssm_cols, ends_col, key_bounds, att_heads, seq_rows, (grad_dt,)
    )
    tall = groups * strip
    bc_each = conv_bc.shape[1] // (groups * parts)
    x_each = ssm_cols // parts
    in_strips = packed > 0
    if in_strips:
        small = (grad_gain, grad_taps, grad_small, grad_n2)
    else:
        grad_conv_x, grad_conv_bc = (grad_taps[:CONV, :ssm_cols], grad_taps[:CONV, ssm_cols:])
        def to_column(vector, rows_each):
            padded = jnp.pad(vector.reshape(parts, rows_each), ((0, 0), (0, tall - rows_each)))
            return padded[:, :, None]

        def to_columns(matrix, rows_each):
            wide = jnp.swapaxes(matrix.reshape(matrix.shape[0], parts, rows_each), 0, 1)
            wide = jnp.pad(wide, ((0, 0), (0, 0), (0, tall - rows_each)))
            return jnp.swapaxes(wide, 1, 2)

        bc_wide = grad_conv_bc.reshape(CONV, groups, parts, bc_each)
        bc_wide = jnp.pad(bc_wide, ((0, 0), (0, 0), (0, 0), (0, strip - bc_each)))
        bc_wide = jnp.transpose(bc_wide, (2, 1, 3, 0)).reshape(parts, tall, CONV)
        heads3 = grad_small[:3, :ssm_heads].reshape(3 * ssm_heads)
        heads3 = jnp.broadcast_to(heads3[None, None, :], (parts, tall, 3 * ssm_heads))
        small = jnp.concatenate(
            [
                jnp.zeros((parts, tall, ssm_heads + 1), f32),
                strips(grad_n2[0][:, None]),
                bc_wide,
                to_column(grad_gate_gain, x_each),
                to_columns(grad_conv_x, x_each),
                heads3,
            ],
            axis=2,
        )
        small = jnp.pad(small, ((0, 0), (0, 0), (0, LANES - small.shape[2]))).reshape(dim, LANES)
        small = (small,)
    late_cols = w1_cols - ssm_cols
    grad_pre, terms1 = call(
        functools.partial(
            weight_grad_kernel, heads=ssm_heads, groups=groups, parts=parts, in_strips=in_strips
        ),
        "weight_grad",
        7,
        (places, grad_q, grad_kv, grad_z, grad_xbc, rim_back, grad_dt, cosine, sine, w1, both_in, early_gain)
        + small,
        (((seq_rows, w1_cols), B16), ((dim, late_cols), B16)),
        (((dim, LANES), F32),) if in_strips else (),
        (own_gu, grad_w_down),
    )
    mixed_cols = att_cols + ssm_cols
    at_s = mixed_cols + 2 * HEAD + side_cols
    if in_strips:
        terms1 = terms1.reshape(parts, tall, late_cols)
    else:
        tail = terms1[:, at_s:].reshape(parts, tall, LANES)
        gain_column = strips(terms1[:, at_s + ssm_heads][:, None])
        lane = jnp.arange(LANES)
        terms1 = jnp.concatenate(
            [
                terms1[:, :mixed_cols].reshape(parts, tall, mixed_cols),
                strips(terms1[:, mixed_cols:at_s]),
                jnp.where(lane == ssm_heads, gain_column, tail),
            ],
            axis=2,
        )
    own1 = lax.psum_scatter(terms1, "seq", scatter_dimension=0)
    early_own, *group_terms = call(
        group_back_kernel,
        "group_back",
        4,
        (places, grad_pre, w1, early_own),
        ((early_own.shape, B16),) + row_blocks,
        (),
    )
    grad_normed1 = sum(block.astype(f32) for block in branch_swap(group_terms))
    y_out = call(
        add_blocks_kernel,
        "add_blocks",
        1,
        (places, middle) + y_blocks,
        (((tok_rows, dim), B16),),
        (),
        (group_terms[0],),
    )[0]
    out_own = jnp.concatenate(
        [early_own[:chunk, : dim // 2], early_own[chunk:, : dim // 2]], axis=1
    )
    grad_w_out = lax.ppermute(out_own, ("branch", "seq"), from_heads).astype(f32)
    own_gain = lax.dynamic_slice_in_dim(norm1_gain, (branch_id * parts + seq_id) * strip, strip, 0)
    side_cols = late_cols - mixed_cols
    if packed:
        side_parts = call(
            split_kernel,
            "split",
            1,
            (places, own1),
            (((strip, side_cols), B16),) * groups,
            (),
        )
        side_blocks = branch_swap(side_parts)
        side_scratch = (((groups, strip, side_cols), B16),)
    else:
        side_blocks = (branch_exchange(own1[:, mixed_cols:].reshape(groups, strip, -1)),)
        side_scratch = ()
    head_row = ((1, ssm_heads), F32)
    grad_mix, grad_dt_w, grad_gain_g, grad_cx, grad_a_log, grad_dt_bias, grad_skip = call(
        functools.partial(own_kernel, heads=ssm_heads, half=dim // 2, apart=in_strips),
        "own",
        2,
        (places, own1, early_own),
        (
            ((tall, w_mix_in.shape[1]), F32),
            ((ssm_heads, tall), F32),
            ((1, x_each), F32),
            ((CONV, x_each), F32),
            head_row,
            head_row,
            head_row,
        ),
        (),
    )
    grad_shared, first_gain, second_gain, grad_cbc = call(
        functools.partial(side_kernel, heads=ssm_heads, apart=packed > 0),
        "side",
        1,
        (places, own_gain[None, :]) + side_blocks,
        (
            ((strip, w_shared.shape[1]), F32),
            ((1, strip), F32),
            ((1, strip), F32),
            ((CONV, bc_each), F32),
        ),
        side_scratch,
    )
    grad_x1, unused_n1 = rms_backward(grad_normed1, scaled1, inverse1, norm1_gain)
    return (
        y_out,
        grad_middle + grad_x1,
        first_gain[0],
        grad_mix,
        grad_dt_w.T,
        grad_shared,
        grad_cx,
        grad_cbc,
        grad_a_log[0],
        grad_dt_bias[0],
        grad_skip[0],
        grad_gain_g[0],
        grad_w_out,
        second_gain[0],
        grad_w_gate,
        grad_w_up,
        grad_w_down.astype(f32),
    )


def solution(mesh):
    in_specs = (
        P(("seq", "branch"), None),
        P(),
        P(),
        P("seq", "branch"),
        P("seq", "branch"),
        P("seq", None),
        P(None, "branch"),
        P(),
        P("branch"),
        P("branch"),
        P("branch"),
        P(),
        P("seq", None),
        P(),
        P("seq", None),
        P("seq", None),
        P("seq", None),
        P(("seq", "branch"), None),
    )
    out_specs = (
        P(("seq", "branch"), None),
        P(("seq", "branch"), None),
        P(("branch", "seq")),
        P("seq", "branch"),
        P("seq", "branch"),
        P(("branch", "seq"), None),
        P(None, ("branch", "seq")),
        P(None, ("branch", "seq")),
        P("branch"),
        P("branch"),
        P("branch"),
        P(("branch", "seq")),
        P(("branch", "seq"), None),
        P(("branch", "seq")),
        P(("branch", "seq"), None),
        P(("branch", "seq"), None),
        P(("branch", "seq"), None),
    )
    return jax.shard_map(shards, mesh=mesh, in_specs=in_specs, out_specs=out_specs, check_vma=False)
```
